32 devices in a mesh: freq: 16 (over z, y, core), chan: 2 (over x).
Axes of the slice: x: 2, y: 2, z: 4, core: 2. Of those that a mesh axis runs over, the one named last changes fastest.
Arguments:
- tokens: bfloat16 [2, 4096, 768], P(None, 'freq', 'chan'), may hold values from -6 to 6
- cotangent: bfloat16 [2, 4096, 768], P(None, 'freq', 'chan'), may hold values from -6 to 6
- first_gain: float32 [768], P('chan'), may hold values from 0.5 to 1.5
- second_gain: float32 [768], P('chan'), may hold values from 0.5 to 1.5
- w_value: bfloat16 [768, 768], P('freq', 'chan'), may hold values from -0.21875 to 0.21875
- w_gate: bfloat16 [768, 768], P('freq', 'chan'), may hold values from -0.21875 to 0.21875
- w_out: bfloat16 [768, 768], P('freq', 'chan'), may hold values from -0.375 to 0.375
- w_up: bfloat16 [768, 3072], P('freq', 'chan'), may hold values from -0.21875 to 0.21875
- w_down: bfloat16 [768, 3072], P('freq', 'chan'), may hold values from -0.1875 to 0.1875
- raw_kernel: float32 [768, 2048], P('chan', 'freq'), may hold values from -0.3 to 0.3
- lengths: int32 [768], P('chan'), may hold values from 512 to 2048, as said below
Outputs:
- output: bfloat16 [2, 4096, 768], P(None, 'freq', 'chan')
- grad_input: float32 [2, 4096, 768], P(None, 'freq', 'chan')
- grad_value: float32 [768, 768], P('freq', 'chan')
- grad_gate: float32 [768, 768], P('freq', 'chan')
- grad_out: float32 [768, 768], P('freq', 'chan')
- grad_up: float32 [768, 3072], P('freq', 'chan')
- grad_down: float32 [768, 3072], P('freq', 'chan')
- grad_first: float32 [384, 2], P('freq', 'chan')
- grad_second: float32 [384, 2], P('freq', 'chan')
- grad_kernel: float32 [768, 2048], P('chan', 'freq')
The draws below stay inside these ranges and needn't reach their ends.
Inputs may be any that keep to these rules, and one draw needn't show every extreme that they name: `lengths`: in each half of the 768 channels at least one kernel has all 2048 taps live.
All inputs are finite; a program needn't handle non-finite values.
Results may differ from the reference program's by a relative error of at most 0.017.
Values may be sent and summed in bfloat16 or wider, within the bound.
A program may use at most 192 MiB of HBM per device.

```python
import jax
import jax.numpy as jnp
from jax import lax

D = 768
FF = 3072
K = 2048
SEQS = 2
SEQ_LEN = 4096
N_CHAN = 2


def draw_lengths(key, part):
    key = jax.random.fold_in(key, 11)
    key_values, key_lower, key_upper = jax.random.split(key, 3)
    values = jax.random.randint(key_values, (D,), K // 4, K + 1)
    lower_pick = jax.random.randint(key_lower, (), 0, D // 2)
    upper_pick = jax.random.randint(key_upper, (), D // 2, D)
    values = values.at[lower_pick].set(K).at[upper_pick].set(K)
    return values.astype(jnp.int32)


def spiked(values, stream_key, source, target, blocks, factor):
    def block_of(position):
        return (jnp.arange(values.shape[position]) // (values.shape[position] // blocks)).reshape((-1,) + (1,) * (values.ndim - 1 - position))

    near = jax.random.permutation(stream_key, blocks)[block_of(target)]
    other_side = (block_of(target) + blocks // 2) % blocks
    return jnp.where((block_of(source) == near) | (block_of(source) == other_side), factor * values, values)


def block_scale(stream_key, dims, shards, least, high):
    def one(dim, parts):
        steps = jax.random.uniform(jax.random.fold_in(jax.random.fold_in(stream_key, 6), dim), (parts,), jnp.float32, least / len(shards), high / len(shards))
        return jnp.repeat(jnp.exp(steps), dims[dim] // parts).reshape((-1,) + (1,) * (len(dims) - dim - 1))

    level = one(*shards[0])
    for cut in shards[1:]:
        level = level * one(*cut)
    return level


def bell_draw(own_key, dims, scale, limit, pieces=(), kind=jnp.bfloat16):
    gain = block_scale(own_key, dims, pieces, -0.22, 0.18) if pieces else 1.0
    values = jax.random.normal(own_key, dims, jnp.float32) * scale * gain
    return jnp.minimum(jnp.maximum(values, -limit), limit).astype(kind)


def heavy_noise(rng, extent, scale, bound, cuts, heavy, held_as=jnp.bfloat16):
    values = scale * jax.random.normal(rng, extent, jnp.float32)
    if cuts:
        values = values * block_scale(rng, extent, cuts, -0.22, 0.18)
    return jnp.clip(spiked(values, jax.random.fold_in(rng, 3), *heavy), -bound, bound).astype(held_as)


def setup_inputs(seed: int = 0) -> dict:
    seeds = jax.random.split(jax.random.key(seed), 12)
    return {
        "tokens": bell_draw(seeds[0], (SEQS, SEQ_LEN, D), 1.0, 6.0, ((1, 16), (2, 2))),
        "cotangent": heavy_noise(seeds[1], (SEQS, SEQ_LEN, D), 1.0, 6.0, ((1, 16), (2, 2)), (1, 2, 16, 2.0)),
        "first_gain": jnp.clip(1.0 + 0.1 * jax.random.normal(seeds[2], (D,), jnp.float32), 0.5, 1.5),
        "second_gain": jnp.clip(1.0 + 0.1 * jax.random.normal(seeds[3], (D,), jnp.float32), 0.5, 1.5),
        "w_value": bell_draw(seeds[4], (D, D), D ** -0.5, 0.21875, ((0, 16), (1, 2))),
        "w_gate": bell_draw(seeds[5], (D, D), D ** -0.5, 0.21875, ((0, 16), (1, 2))),
        "w_out": bell_draw(seeds[6], (D, D), (D // 3) ** -0.5, 0.375, ((0, 16), (1, 2))),
        "w_up": bell_draw(seeds[7], (D, FF), D ** -0.5, 0.21875, ((0, 16), (1, 2))),
        "w_down": bell_draw(seeds[8], (D, FF), (FF // 3) ** -0.5, 0.1875, ((0, 16), (1, 2))),
        "raw_kernel": bell_draw(seeds[9], (D, K), 0.05, 0.3, ((0, 2), (1, 16)), jnp.float32),
        "lengths": draw_lengths(jax.random.fold_in(seeds[11], 71), 0),
    }


THRESH = 0.003
EPSILON = 1e-05
HIGHEST = lax.Precision.HIGHEST

@jax.custom_vjp
def low(v):
    return lax.optimization_barrier(v.astype(jnp.bfloat16)).astype(jnp.float32)

@jax.custom_vjp
def low_back(v):
    return v

def low_keep(v):
    return (low(v), None)

def low_pass(kept, grad):
    return (grad,)

def back_keep(v):
    return (v, None)

def back_low(kept, grad):
    return (low(grad),)
low.defvjp(low_keep, low_pass)
low_back.defvjp(back_keep, back_low)

def norm_rows(values, gain_row):
    center = lax.optimization_barrier(jnp.mean(values, axis=-1, keepdims=True))
    shifted = values - center
    spread = lax.optimization_barrier(jnp.mean(shifted * shifted, axis=-1, keepdims=True))
    return shifted * lax.rsqrt(spread + EPSILON) * gain_row

def shape_kernel(raw_taps, lengths):
    padded = jnp.pad(raw_taps, ((0, 0), (1, 1)))
    pooled = (padded[:, :-2] + padded[:, 1:-1] + padded[:, 2:]) / 3.0
    shrunk = pooled - THRESH * jnp.tanh(pooled / THRESH)
    tap_index = lax.broadcasted_iota(jnp.int32, raw_taps.shape, 1)
    live_taps = (tap_index < lengths[:, None]).astype(raw_taps.dtype)
    return shrunk * live_taps

def causal_conv(signal, kernel):
    seq_length = signal.shape[0]
    padded_size = 2 * seq_length
    signal_spec = jnp.fft.rfft(signal, n=padded_size, axis=0)
    kernel_spec = jnp.fft.rfft(kernel, n=padded_size, axis=1).T
    return jnp.fft.irfft(signal_spec * kernel_spec, n=padded_size, axis=0)[:seq_length]

def forward(sequence, first_gain, second_gain, w_value, w_gate, w_out, w_up, w_down, raw_kernel, lengths):
    kernel = shape_kernel(raw_kernel, lengths)
    input1 = low(norm_rows(sequence, first_gain))
    value_low = low(low_back(jnp.dot(input1, w_value, precision=HIGHEST, preferred_element_type=jnp.float32)))
    gate_proj = low_back(jnp.dot(input1, w_gate, precision=HIGHEST, preferred_element_type=jnp.float32))
    mixed = low(low_back(causal_conv(value_low, kernel)))
    inner_low = low(mixed * jax.nn.silu(gate_proj))
    branch = low_back(jnp.dot(inner_low, w_out.T, precision=HIGHEST, preferred_element_type=jnp.float32))
    residual = sequence + branch
    input2 = low(norm_rows(residual, second_gain))
    hidden = low_back(jnp.dot(input2, w_up, precision=HIGHEST, preferred_element_type=jnp.float32))
    activated = low(jax.nn.gelu(hidden))
    return residual + jnp.dot(activated, w_down.T, precision=HIGHEST, preferred_element_type=jnp.float32)

def reference(tokens, cotangent, first_gain, second_gain, w_value, w_gate, w_out, w_up, w_down, raw_kernel, lengths):
    params = tuple((p.astype(jnp.float32) for p in (first_gain, second_gain, w_value, w_gate, w_out, w_up, w_down, raw_kernel)))

    def one_sequence(carry, pair):
        sequence, seq_cot = pair

        def closed(seq_in, *weights):
            return forward(seq_in, *weights, lengths)
        result, pull = jax.vjp(closed, sequence.astype(jnp.float32), *params)
        grads = pull(seq_cot.astype(jnp.float32))
        carry = tuple((c + g for c, g in zip(carry, grads[1:])))
        return (carry, (result.astype(jnp.bfloat16), grads[0]))
    zeros = tuple((jnp.zeros_like(p) for p in params))
    sums, (output, grad_input) = lax.scan(one_sequence, zeros, (tokens, cotangent))
    grad_first = sums[0].reshape(N_CHAN, D // N_CHAN).T
    grad_second = sums[1].reshape(N_CHAN, D // N_CHAN).T
    return (output, grad_input, sums[2], sums[3], sums[4], sums[5], sums[6], grad_first, grad_second, sums[7])
```

```python
import functools
import math

import jax
import jax.numpy as jnp
import numpy as np
from jax import lax
from jax.experimental import pallas as pl
from jax.experimental.pallas import tpu as pltpu
from jax.sharding import PartitionSpec as P

THRESH = 0.003
EPSILON = 1e-05
LANES = 128
MESH = pl.DeviceIdType.MESH
F32 = jnp.float32
BF16 = jnp.bfloat16


def bit_sizes(freq_count):
    return [1 << i for i in reversed(range(freq_count.bit_length() - 1))]


class Place:
    def __init__(self, freq_count):
        self.freq_count = freq_count
        self.freq = lax.axis_index("freq")
        self.chan = lax.axis_index("chan")
        self.bits = bit_sizes(freq_count)
        self.coords = [self.chan] + [lax.rem(self.freq // b, 2) for b in self.bits]
        self.dims = len(self.coords)

    def partner(self, dim):
        if dim == 0:
            return (self.freq, 1 - self.chan)
        bit = self.bits[dim - 1]
        return (self.freq + bit - 2 * bit * self.coords[dim], self.chan)


def greet(devices):
    barrier = pltpu.get_barrier_semaphore()
    for device in devices:
        pl.semaphore_signal(barrier, inc=1, device_id=device, device_id_type=MESH)
    pl.semaphore_wait(barrier, len(devices))


def greet_all(place):
    barrier = pltpu.get_barrier_semaphore()
    count = 2 * place.freq_count
    me = place.chan * place.freq_count + place.freq

    def one(step, carry):
        other = lax.rem(me + step, count)
        pl.semaphore_signal(
            barrier,
            inc=1,
            device_id=(lax.rem(other, place.freq_count), other // place.freq_count),
            device_id_type=MESH,
        )
        return carry

    lax.fori_loop(1, count, one, 0)
    pl.semaphore_wait(barrier, count - 1)


def gather_orders(dims):
    top = list(range(1, dims - 2))
    return (top + [0, dims - 2, dims - 1], top + [dims - 2, 0, dims - 1])


class Gather:
    def __init__(self, place, buffer, order, send, recv):
        self.place, self.buffer, self.order, self.send, self.recv = place, buffer, order, send, recv

    def index(self, step):
        done = self.order[:step]
        return tuple(
            slice(None) if dim in done else coord for dim, coord in enumerate(self.place.coords)
        )

    def copy(self, step):
        region = self.buffer.at[self.index(step)]
        return pltpu.make_async_remote_copy(
            src_ref=region,
            dst_ref=region,
            send_sem=self.send.at[step],
            recv_sem=self.recv.at[step],
            device_id=self.place.partner(self.order[step]),
            device_id_type=MESH,
        )

    def start(self, step):
        self.copy(step).start()

    def wait(self, step):
        self.copy(step).wait()


def front_kernel(freq_count, tokens, cotangent, gains, *refs):
    shards, refs = refs[:5], refs[5:]
    x_out, g_out, gain_out = refs[:3]
    buffers, refs = refs[3:8], refs[8:]
    w_send, w_recv, x_send, x_recv, local = refs
    place = Place(freq_count)
    orders = gather_orders(place.dims)
    which = (0, 1, 0, 0, 1)
    own = []
    for k in range(5):
        copy = pltpu.make_async_copy(
            shards[k], buffers[k].at[tuple(place.coords)], local.at[k]
        )
        copy.start()
        own.append(copy)
    chan = place.chan
    for k, (source, target) in enumerate(
        ((tokens.at[chan], x_out.at[chan]), (cotangent.at[chan], g_out.at[chan]), (gains, gain_out.at[chan]))
    ):
        copy = pltpu.make_async_copy(source, target, local.at[5 + k])
        copy.start()
        own.append(copy)
    greet([place.partner(dim) for dim in range(place.dims)])
    swaps = []
    for k, (source, target) in enumerate(
        (
            (tokens.at[1 - chan], x_out.at[chan]),
            (cotangent.at[1 - chan], g_out.at[chan]),
            (gains, gain_out.at[chan]),
        )
    ):
        swaps.append(
            pltpu.make_async_remote_copy(
                src_ref=source,
                dst_ref=target,
                send_sem=x_send.at[k],
                recv_sem=x_recv.at[k],
                device_id=place.partner(0),
                device_id_type=MESH,
            )
        )
    for swap in swaps:
        swap.start()
    gathers = [
        Gather(place, buffers[k], orders[which[k]], w_send.at[k], w_recv.at[k]) for k in range(5)
    ]
    for k in range(5):
        own[k].wait()
        gathers[k].start(0)
    for step in range(1, place.dims + 1):
        for gather in gathers:
            gather.wait(step - 1)
            if step < place.dims:
                gather.start(step)
    for swap in swaps:
        swap.wait()
    for copy in own[5:]:
        copy.wait()


VMEM_SPEC = pl.BlockSpec(memory_space=pltpu.VMEM)


def front(freq_count, tokens, cotangent, gains, shards):
    lead = (2,) * (1 + len(bit_sizes(freq_count)))
    _, here, half = tokens.shape
    dims = len(lead)
    out_shape = [
        jax.ShapeDtypeStruct((2, here, half), BF16),
        jax.ShapeDtypeStruct((2, here, half), BF16),
        jax.ShapeDtypeStruct((2,) + gains.shape, F32),
    ] + [jax.ShapeDtypeStruct(lead + w.shape, BF16) for w in shards]
    return pl.pallas_call(
        functools.partial(front_kernel, freq_count),
        out_shape=out_shape,
        in_specs=[VMEM_SPEC] * 8,
        out_specs=[VMEM_SPEC] * 8,
        scratch_shapes=[
            pltpu.SemaphoreType.DMA((5, dims)),
            pltpu.SemaphoreType.DMA((5, dims)),
            pltpu.SemaphoreType.DMA((3,)),
            pltpu.SemaphoreType.DMA((3,)),
            pltpu.SemaphoreType.DMA((8,)),
        ],
        compiler_params=pltpu.CompilerParams(
            collective_id=0, has_side_effects=True, vmem_limit_bytes=60 << 20
        ),
        name="front",
    )(tokens, cotangent, gains, *shards)


class Reduce:
    def __init__(self, place, total, landing, order, send, recv):
        self.place, self.total, self.landing, self.order = place, total, landing, order
        self.send, self.recv = send, recv

    def region(self, step, coord_of):
        fixed = self.order[:step]
        out = []
        for dim, coord in enumerate(self.place.coords):
            if dim in fixed:
                out.append(coord)
            elif dim == self.order[step]:
                out.append(coord_of(coord))
            else:
                out.append(slice(None))
        return tuple(out)

    def copy(self, step):
        return pltpu.make_async_remote_copy(
            src_ref=self.total.at[self.region(step, lambda c: 1 - c)],
            dst_ref=self.landing[step],
            send_sem=self.send.at[step],
            recv_sem=self.recv.at[step],
            device_id=self.place.partner(self.order[step]),
            device_id_type=MESH,
        )

    def start(self, step):
        self.copy(step).start()

    def wait(self, step):
        self.copy(step).wait()

    def add(self, step, out=None):
        kept = self.region(step, lambda c: c)
        free = [dim for dim, at in enumerate(kept) if isinstance(at, slice)]
        landing = self.landing[step]

        def one(turn, carry):
            where, there = list(kept), []
            for place, dim in enumerate(free):
                at = lax.rem(turn // (1 << (len(free) - 1 - place)), 2)
                where[dim] = at
                there.append(at)
            where, there = tuple(where), tuple(there)
            total = self.total[where].astype(F32) + landing[there].astype(F32)
            if out is None:
                self.total[where] = total.astype(BF16)
            else:
                out[...] = total
            return carry

        if free:
            lax.fori_loop(0, 1 << len(free), one, 0)
        else:
            one(0, 0)


def back_kernel(freq_count, *refs):
    grads, refs = refs[:5], refs[5:]
    out_rows, grad_rows, refs = refs[0], refs[1], refs[2:]
    results, refs = refs[:5], refs[5:]
    output, grad_input, refs = refs[0], refs[1], refs[2:]
    place = Place(freq_count)
    dims = place.dims
    landing = [refs[k * dims : (k + 1) * dims] for k in range(5)]
    refs = refs[5 * dims :]
    grad_send, grad_land, w_send, w_recv, x_send, x_recv, local = refs
    orders = [tuple(reversed(order)) for order in gather_orders(dims)]
    which = (0, 1, 0, 0, 1)
    chan = place.chan
    greet([place.partner(dim) for dim in range(dims)])
    reduces = [
        Reduce(place, grads[k], landing[k], orders[which[k]], w_send.at[k], w_recv.at[k])
        for k in range(5)
    ]
    turn = (4, 3, 2, 1, 0)
    for k in turn:
        reduces[k].start(0)
    grad_send[...] = grad_rows[1 - chan].astype(BF16)
    swaps = []
    for k, (source, target) in enumerate(
        ((out_rows.at[1 - chan], output.at[chan]), (grad_send, grad_land))
    ):
        swaps.append(
            pltpu.make_async_remote_copy(
                src_ref=source,
                dst_ref=target,
                send_sem=x_send.at[k],
                recv_sem=x_recv.at[k],
                device_id=place.partner(0),
                device_id_type=MESH,
            )
        )
        swaps[-1].start()
    copy = pltpu.make_async_copy(out_rows.at[chan], output.at[chan], local)
    copy.start()
    grad_input[chan] = grad_rows[chan]
    for step in range(1, dims + 1):
        for k in turn:
            reduces[k].wait(step - 1)
            if step < dims:
                reduces[k].add(step - 1)
                reduces[k].start(step)
            else:
                reduces[k].add(step - 1, results[k])
    copy.wait()
    for swap in swaps:
        swap.wait()
    grad_input[1 - chan] = grad_land[...].astype(F32)


def back(freq_count, grads, out_rows, grad_rows):
    dims = 1 + len(bit_sizes(freq_count))
    tails = [g.shape[-2:] for g in grads]
    _, here, half = out_rows.shape
    landings = []
    for tail in tails:
        landings += [pltpu.VMEM((2,) * (dims - 1 - step) + tail, BF16) for step in range(dims)]
    return pl.pallas_call(
        functools.partial(back_kernel, freq_count),
        out_shape=[jax.ShapeDtypeStruct(tail, F32) for tail in tails]
        + [
            jax.ShapeDtypeStruct((2, here, half), BF16),
            jax.ShapeDtypeStruct((2, here, half), F32),
        ],
        in_specs=[VMEM_SPEC] * 7,
        out_specs=[VMEM_SPEC] * 7,
        scratch_shapes=landings
        + [
            pltpu.VMEM((here, half), BF16),
            pltpu.VMEM((here, half), BF16),
            pltpu.SemaphoreType.DMA((5, dims)),
            pltpu.SemaphoreType.DMA((5, dims)),
            pltpu.SemaphoreType.DMA((2,)),
            pltpu.SemaphoreType.DMA((2,)),
            pltpu.SemaphoreType.DMA,
        ],
        compiler_params=pltpu.CompilerParams(
            collective_id=3, has_side_effects=True, vmem_limit_bytes=60 << 20
        ),
        name="back",
    )(*grads, out_rows, grad_rows)


class Sizes:
    def __init__(self, freq_count, here, half, taps):
        self.freq_count = freq_count
        self.here = here
        self.cols = here // LANES
        self.channels = half // freq_count
        self.chunk = self.cols * self.channels
        self.devices = 2 * freq_count
        self.tap_rows = taps // LANES
        self.rows = here * freq_count // LANES + self.tap_rows
        self.size = self.rows * LANES


def conv_tables(sizes):
    rows, size = sizes.rows, sizes.size
    f = np.arange(rows)
    fi = np.arange(sizes.freq_count)
    a_of, imag = [], []
    for col in range(sizes.cols):
        for seq in range(2):
            for block in fi:
                a_of.append(block * sizes.cols + col)
                imag.append(seq)
    a_of, imag = np.array(a_of), np.array(imag)
    angle = 2 * np.pi * np.outer(f, a_of) / rows
    cos, sin = np.cos(angle), np.sin(angle)
    into = np.concatenate([np.where(imag, sin, cos), np.where(imag, cos, -sin)], axis=0)
    outof = np.concatenate([np.where(imag, sin, cos), np.where(imag, cos, -sin)], axis=0).T / size
    taps = np.arange(sizes.tap_rows)
    angle = 2 * np.pi * np.outer(f, taps) / rows
    taps_into = np.concatenate([np.cos(angle), -np.sin(angle)], axis=0)
    taps_outof = taps_into.T / size
    b = np.arange(LANES)
    angle = 2 * np.pi * np.outer(f, b) / size
    turn = np.stack([np.cos(angle), np.sin(angle)])
    angle = 2 * np.pi * np.outer(b, b) / LANES
    cos, sin = np.cos(angle), np.sin(angle)
    ahead = np.block([[cos, -sin], [sin, cos]])
    return (
        jnp.asarray(into, BF16),
        jnp.asarray(outof, BF16),
        jnp.asarray(taps_into, BF16),
        jnp.asarray(taps_outof, BF16),
        jnp.asarray(turn, F32),
        jnp.asarray(ahead, BF16),
        jnp.asarray(ahead.T, BF16),
    )


def dot(left, right):
    return jnp.dot(left, right, preferred_element_type=F32)


def spectrum_into(sizes, load, into, turn, ahead, inner, spectrum):
    rows = sizes.rows

    def one(pair, carry):
        both = jnp.concatenate([load(2 * pair), load(2 * pair + 1)], axis=1).astype(BF16)
        part = dot(into[...], both)
        for side in range(2):
            real = part[:rows, side * LANES : (side + 1) * LANES]
            imag = part[rows:, side * LANES : (side + 1) * LANES]
            turned = jnp.concatenate(
                [real * turn[0] + imag * turn[1], imag * turn[0] - real * turn[1]], axis=1
            )
            start = pl.multiple_of((2 * pair + side) * rows, 16)
            inner[pl.ds(start, rows), :] = turned.astype(BF16)
        return carry

    lax.fori_loop(0, sizes.channels // 2, one, 0)
    tile = sizes.channels * rows // 4

    def two(step, carry):
        at = pl.ds(pl.multiple_of(step * tile, 16), tile)
        spectrum[at, :] = dot(inner[at, :], ahead[...])
        return carry

    lax.fori_loop(0, 4, two, 0)


def signal_from(sizes, product, outof, turn, behind, inner, store):
    rows = sizes.rows
    tile = sizes.channels * rows // 4

    def one(step, carry):
        at = pl.ds(pl.multiple_of(step * tile, 16), tile)
        inner[at, :] = dot(product(at), behind[...]).astype(BF16)
        return carry

    lax.fori_loop(0, 4, one, 0)

    def two(pair, carry):
        sides = []
        for side in range(2):
            start = pl.multiple_of((2 * pair + side) * rows, 16)
            back = inner[pl.ds(start, rows), :].astype(F32)
            real, imag = back[:, :LANES], back[:, LANES:]
            sides.append(
                jnp.concatenate(
                    [real * turn[0] - imag * turn[1], imag * turn[0] + real * turn[1]], axis=0
                ).astype(BF16)
            )
        got = dot(outof[...], jnp.concatenate(sides, axis=1))
        for side in range(2):
            store(2 * pair + side, got[:, side * LANES : (side + 1) * LANES])
        return carry

    lax.fori_loop(0, sizes.channels // 2, two, 0)


def times(left, right, conj):
    a, b = left[:, :LANES], left[:, LANES:]
    c, d = right[:, :LANES], right[:, LANES:]
    if conj:
        return jnp.concatenate([a * c + b * d, b * c - a * d], axis=1).astype(BF16)
    return jnp.concatenate([a * c - b * d, a * d + b * c], axis=1).astype(BF16)


class Exchange:
    def __init__(self, place, source, target, send, recv):
        self.place, self.source, self.target = place, source, target
        self.send, self.recv = send, recv
        self.count = 2 * place.freq_count
        self.me = place.chan * place.freq_count + place.freq

    def each(self, action):
        freq_count = self.place.freq_count

        def one(step, carry):
            other = lax.rem(self.me + step, self.count)
            origin = lax.rem(self.me + self.count - step, self.count)
            action(step, other, origin, (lax.rem(other, freq_count), other // freq_count))
            return carry

        lax.fori_loop(1, self.count, one, 0)

    def start(self):
        def action(step, other, origin, device):
            pltpu.make_async_remote_copy(
                src_ref=self.source.at[other],
                dst_ref=self.target.at[self.me],
                send_sem=self.send.at[step],
                recv_sem=self.recv.at[step],
                device_id=device,
                device_id_type=MESH,
            ).start()

        self.each(action)
        self.target[self.me] = self.source[self.me]

    def wait(self):
        def action(step, other, origin, device):
            pltpu.make_async_remote_copy(
                src_ref=self.source.at[other],
                dst_ref=self.target.at[origin],
                send_sem=self.send.at[step],
                recv_sem=self.recv.at[step],
                device_id=device,
                device_id_type=MESH,
            ).wait()

        self.each(action)


class PlaneExchange:
    def __init__(self, place, source, target, send, recv):
        self.place, self.source, self.target = place, source, target
        self.send, self.recv = send, recv

    def each(self, action):
        count, me = self.place.freq_count, self.place.freq

        def one(step, carry):
            action(step, lax.rem(me + step, count), lax.rem(me + count - step, count))
            return carry

        lax.fori_loop(1, count, one, 0)

    def start(self):
        def action(step, other, origin):
            pltpu.make_async_remote_copy(
                src_ref=self.source(other),
                dst_ref=self.target(self.place.freq),
                send_sem=self.send.at[step],
                recv_sem=self.recv.at[step],
                device_id=(other, self.place.chan),
                device_id_type=MESH,
            ).start()

        self.each(action)

    def wait(self):
        def action(step, other, origin):
            pltpu.make_async_remote_copy(
                src_ref=self.source(other),
                dst_ref=self.target(origin),
                send_sem=self.send.at[step],
                recv_sem=self.recv.at[step],
                device_id=(other, self.place.chan),
                device_id_type=MESH,
            ).wait()

        self.each(action)


def to_chunks(sizes, rows):
    turned = rows.T.reshape(sizes.devices, sizes.channels, sizes.here)
    pieces = [turned[:, :, col * LANES : (col + 1) * LANES] for col in range(sizes.cols)]
    return jnp.concatenate(pieces, axis=1).astype(BF16)


def from_chunks(sizes, chunks):
    wide = chunks.astype(F32)
    pieces = [
        wide[:, col * sizes.channels : (col + 1) * sizes.channels, :].reshape(
            sizes.devices * sizes.channels, LANES
        )
        for col in range(sizes.cols)
    ]
    return jnp.concatenate(pieces, axis=1).T


def chunk_loader(sizes, ref):
    def load(channel):
        pieces = [
            ref[pl.ds(col * sizes.channels + channel, sizes.devices, stride=sizes.chunk), :]
            for col in range(sizes.cols)
        ]
        return jnp.concatenate(pieces, axis=0)

    return load


def chunk_storer(sizes, ref):
    def store(channel, values):
        for col in range(sizes.cols):
            ref[pl.ds(col * sizes.channels + channel, sizes.devices, stride=sizes.chunk), :] = values[
                col * sizes.devices : (col + 1) * sizes.devices
            ]

    return store


def widen(sizes, chunks, ref):
    def one(step, carry):
        ref[pl.ds(pl.multiple_of(step * sizes.chunk, 8), sizes.chunk), :] = chunks[step].astype(F32)
        return carry

    lax.fori_loop(0, sizes.devices, one, 0)


def narrow(sizes, ref, chunks):
    def one(step, carry):
        chunks[step] = ref[pl.ds(pl.multiple_of(step * sizes.chunk, 8), sizes.chunk), :].astype(BF16)
        return carry

    lax.fori_loop(0, sizes.devices, one, 0)


def pooled_taps(taps):
    lane = lax.broadcasted_iota(jnp.int32, taps.shape, 2)
    zero = jnp.zeros_like(taps[:1])
    after = pltpu.roll(taps, LANES - 1, 2)
    before = pltpu.roll(taps, 1, 2)
    after = jnp.where(lane == LANES - 1, jnp.concatenate([after[1:], zero], axis=0), after)
    before = jnp.where(lane == 0, jnp.concatenate([zero, before[:-1]], axis=0), before)
    return (before + taps + after) / 3.0


def live_mask(shape, lengths):
    tap = lax.broadcasted_iota(jnp.int32, shape, 0) * LANES + lax.broadcasted_iota(
        jnp.int32, shape, 2
    )
    return (tap < lengths[None]).astype(F32)


def conv_kernel(
    sizes, raw_kernel, lengths, value, into, outof, taps_into, turn, ahead, behind,
    mixed, taps, kernel_spec, value_spec, sent, landed, wide, inner, tap_wide,
    t_send, t_recv, a_send, a_recv, b_send, b_recv,
):
    place = Place(sizes.freq_count)
    channels = sizes.channels
    greet_all(place)
    tap_move = PlaneExchange(
        place,
        lambda g: raw_kernel.at[pl.ds(pl.multiple_of(g * channels, 8), channels)],
        lambda g: taps.at[g],
        t_send,
        t_recv,
    )
    tap_move.start()
    taps[place.freq] = raw_kernel[pl.ds(pl.multiple_of(place.freq * channels, 8), channels)]
    sent[...] = to_chunks(sizes, value[...])
    there = Exchange(place, sent, landed, a_send, a_recv)
    there.start()
    tap_move.wait()
    pooled = pooled_taps(taps[...])
    shrunk = (pooled - THRESH * jnp.tanh(pooled / THRESH)) * live_mask(pooled.shape, lengths[...])
    tap_wide[...] = shrunk.reshape(sizes.tap_rows * channels, LANES)
    spectrum_into(
        sizes,
        lambda c: tap_wide[pl.ds(c, sizes.tap_rows, stride=channels), :],
        taps_into, turn, ahead, inner, kernel_spec,
    )
    there.wait()
    widen(sizes, landed, wide)
    spectrum_into(sizes, chunk_loader(sizes, wide), into, turn, ahead, inner, value_spec)
    signal_from(
        sizes,
        lambda at: times(value_spec[at, :], kernel_spec[at, :], False),
        outof, turn, behind, inner, chunk_storer(sizes, wide),
    )
    narrow(sizes, wide, sent)
    back_again = Exchange(place, sent, mixed, b_send, b_recv)
    back_again.start()
    back_again.wait()


def conv_scratch(sizes):
    chunks = (sizes.devices, sizes.chunk, LANES)
    return [
        pltpu.VMEM(chunks, BF16),
        pltpu.VMEM(chunks, BF16),
        pltpu.VMEM((sizes.devices * sizes.chunk, LANES), F32),
        pltpu.VMEM((sizes.channels * sizes.rows, 2 * LANES), BF16),
        pltpu.VMEM((sizes.tap_rows * sizes.channels, LANES), F32),
    ] + [
        pltpu.SemaphoreType.DMA((count,))
        for count in (sizes.freq_count,) * 2 + (sizes.devices,) * 4
    ]


def conv_forward(sizes, raw_kernel, lengths, value, tables):
    into, outof, taps_into, _, turn, ahead, behind = tables
    spec = jax.ShapeDtypeStruct((sizes.channels * sizes.rows, 2 * LANES), F32)
    return pl.pallas_call(
        functools.partial(conv_kernel, sizes),
        out_shape=[
            jax.ShapeDtypeStruct((sizes.devices, sizes.chunk, LANES), BF16),
            jax.ShapeDtypeStruct((sizes.tap_rows, sizes.channels, LANES), F32),
            spec,
            spec,
        ],
        in_specs=[VMEM_SPEC] * 9,
        out_specs=[VMEM_SPEC] * 4,
        scratch_shapes=conv_scratch(sizes),
        compiler_params=pltpu.CompilerParams(
            collective_id=1, has_side_effects=True, vmem_limit_bytes=60 << 20
        ),
        name="conv",
    )(raw_kernel, lengths, value, into, outof, taps_into, turn, ahead, behind)


def conv_back_kernel(
    sizes, lengths, taps, kernel_spec, value_spec, grad_mixed, into, outof, taps_outof, turn, ahead, behind,
    grad_signal, grad_kernel, sent, landed, wide, inner, tap_wide, grad_spec, tap_grad,
    t_send, t_recv, a_send, a_recv, b_send, b_recv,
):
    place = Place(sizes.freq_count)
    channels = sizes.channels
    greet_all(place)
    sent[...] = to_chunks(sizes, grad_mixed[...])
    there = Exchange(place, sent, landed, a_send, a_recv)
    there.start()
    there.wait()
    widen(sizes, landed, wide)
    spectrum_into(sizes, chunk_loader(sizes, wide), into, turn, ahead, inner, grad_spec)
    signal_from(
        sizes,
        lambda at: times(grad_spec[at, :], kernel_spec[at, :], True),
        outof, turn, behind, inner, chunk_storer(sizes, wide),
    )
    narrow(sizes, wide, sent)
    back_again = Exchange(place, sent, grad_signal, b_send, b_recv)
    back_again.start()

    def store(channel, values):
        tap_wide[pl.ds(channel, sizes.tap_rows, stride=channels), :] = values

    signal_from(
        sizes,
        lambda at: times(grad_spec[at, :], value_spec[at, :], True),
        taps_outof, turn, behind, inner, store,
    )
    pooled = pooled_taps(taps[...])
    bent = jnp.tanh(pooled / THRESH)
    grad_taps = tap_wide[...].reshape(pooled.shape)
    tap_grad[...] = pooled_taps(grad_taps * live_mask(pooled.shape, lengths[...]) * bent * bent)
    tap_move = PlaneExchange(
        place,
        lambda g: tap_grad.at[g],
        lambda g: grad_kernel.at[pl.ds(pl.multiple_of(g * channels, 8), channels)],
        t_send,
        t_recv,
    )
    tap_move.start()
    grad_kernel[pl.ds(pl.multiple_of(place.freq * channels, 8), channels)] = tap_grad[place.freq]
    tap_move.wait()
    back_again.wait()


def conv_backward(sizes, lengths, taps, kernel_spec, value_spec, grad_mixed, tables):
    into, outof, _, taps_outof, turn, ahead, behind = tables
    scratch = conv_scratch(sizes)
    scratch[5:5] = [
        pltpu.VMEM(value_spec.shape, F32),
        pltpu.VMEM(taps.shape, F32),
    ]
    return pl.pallas_call(
        functools.partial(conv_back_kernel, sizes),
        out_shape=[
            jax.ShapeDtypeStruct((sizes.devices, sizes.chunk, LANES), BF16),
            jax.ShapeDtypeStruct((sizes.channels * sizes.freq_count, LANES), F32),
        ],
        in_specs=[VMEM_SPEC] * 11,
        out_specs=[VMEM_SPEC] * 2,
        scratch_shapes=scratch,
        compiler_params=pltpu.CompilerParams(
            collective_id=2, has_side_effects=True, vmem_limit_bytes=60 << 20
        ),
        name="conv_back",
    )(lengths, taps, kernel_spec, value_spec, grad_mixed, into, outof, taps_outof, turn, ahead, behind)


def norm(values, gain):
    center = jnp.mean(values, axis=-1, keepdims=True)
    shifted = values - center
    scale = lax.rsqrt(jnp.mean(shifted * shifted, axis=-1, keepdims=True) + EPSILON)
    normed = shifted * scale
    return normed, scale, (normed * gain).astype(BF16)


def norm_back(grad_rows, normed, scale, gain):
    scaled = grad_rows * gain
    plain = jnp.mean(scaled, axis=-1, keepdims=True)
    cross = jnp.mean(scaled * normed, axis=-1, keepdims=True)
    return scale * (scaled - plain - normed * cross)


def halves(values):
    return jnp.stack(jnp.split(values, 2, axis=-1))


def one_sequence(
    tokens, cotangent, first_gain, second_gain, w_value, w_gate, w_out, w_up, w_down, raw_kernel, lengths
):
    freq_count = lax.axis_size("freq")
    _, here, half = tokens.shape
    sizes = Sizes(freq_count, here, half, raw_kernel.shape[1] * freq_count)
    tables = conv_tables(sizes)
    gains = jnp.zeros((8, half), F32).at[0].set(first_gain).at[1].set(second_gain)
    shards = (w_value, w_gate, w_out, w_up, w_down)
    x2, g2, gain2, *full = front(freq_count, tokens, cotangent, gains, shards)
    full = [w.reshape((2, -1, w.shape[-1])) for w in full]
    full_value, full_gate, full_out, full_up, full_down = full
    rows = jnp.concatenate([x2[0], x2[1]], axis=1).astype(F32)
    grad_rows = jnp.concatenate([g2[0], g2[1]], axis=1)
    first = jnp.concatenate([gain2[0, 0], gain2[1, 0]])
    second = jnp.concatenate([gain2[0, 1], gain2[1, 1]])

    def split(values):
        return values.reshape(values.shape[0], 2, -1)

    def project(equation, left, right):
        return jnp.einsum(equation, left, right, preferred_element_type=F32)

    normed1, scale1, input1 = norm(rows, first)
    value = project("td,cde->tce", input1, full_value).reshape(here, -1)
    gate = project("td,cde->tce", input1, full_gate).reshape(here, -1)
    my_lengths = lax.dynamic_slice_in_dim(
        lengths, lax.axis_index("freq") * sizes.channels, sizes.channels
    )
    my_lengths = jnp.broadcast_to(my_lengths[:, None], (sizes.channels, LANES))
    mixed_chunks, taps, kernel_spec, value_spec = conv_forward(
        sizes, raw_kernel, my_lengths, value, tables
    )
    mixed = from_chunks(sizes, mixed_chunks)
    gate_act, gate_pull = jax.vjp(jax.nn.silu, gate)
    inner = (mixed * gate_act).astype(BF16)
    residual = rows + project("tce,coe->to", split(inner), full_out)
    normed2, scale2, input2 = norm(residual, second)
    hidden = project("td,cdf->tcf", input2, full_up)
    activated, act_pull = jax.vjp(jax.nn.gelu, hidden)
    activated = activated.astype(BF16)
    output = (residual + project("tcf,cof->to", activated, full_down)).astype(BF16)
    grad_act = project("to,cof->tcf", grad_rows, full_down)
    down_grad = project("to,tcf->cof", grad_rows, activated).astype(BF16)
    grad_hidden = act_pull(grad_act)[0].astype(BF16)
    up_grad = project("td,tcf->cdf", input2, grad_hidden).astype(BF16)
    grad_in2 = project("tcf,cdf->td", grad_hidden, full_up)
    second_grad = jnp.sum(grad_in2 * normed2, axis=0)
    grad_residual = grad_rows.astype(F32) + norm_back(grad_in2, normed2, scale2, second)
    grad_branch = grad_residual.astype(BF16)
    grad_inner = project("to,coe->tce", grad_branch, full_out).reshape(here, -1)
    out_grad = project("to,tce->coe", grad_branch, split(inner)).astype(BF16)
    signal_chunks, grad_kernel = conv_backward(
        sizes, my_lengths, taps, kernel_spec, value_spec, grad_inner * gate_act, tables
    )
    grad_signal = from_chunks(sizes, signal_chunks).astype(BF16)
    grad_gate_rows = gate_pull(grad_inner * mixed)[0].astype(BF16)
    value_grad = project("td,tce->cde", input1, split(grad_signal)).astype(BF16)
    gate_grad = project("td,tce->cde", input1, split(grad_gate_rows)).astype(BF16)
    grad_in1 = project("tce,cde->td", split(grad_signal), full_value) + project(
        "tce,cde->td", split(grad_gate_rows), full_gate
    )
    first_grad = jnp.sum(grad_in1 * normed1, axis=0)
    grad_input = grad_residual + norm_back(grad_in1, normed1, scale1, first)
    lead = (2,) * (1 + len(bit_sizes(freq_count)))
    grads = [
        g.reshape(lead + shard.shape)
        for g, shard in zip((value_grad, gate_grad, out_grad, up_grad, down_grad), shards)
    ]
    *owned, output, grad_input = back(freq_count, grads, halves(output), halves(grad_input))
    gain_grads = lax.psum(jnp.stack([first_grad, second_grad]), ("freq", "chan"))
    start = lax.axis_index("chan") * half + lax.axis_index("freq") * sizes.channels
    gain_grads = lax.dynamic_slice_in_dim(gain_grads, start, sizes.channels, axis=1)
    return (output, grad_input, *owned, gain_grads[0][:, None], gain_grads[1][:, None], grad_kernel)


def fits(mesh):
    freq_count = mesh.shape["freq"]
    return lambda tokens, w_value, raw_kernel: (
        mesh.shape["chan"] == 2
        and tokens.shape[0] == 2
        and freq_count >= 4
        and freq_count & (freq_count - 1) == 0
        and w_value.shape[0] % (16 * freq_count) == 0
        and w_value.shape[1] % (16 * freq_count) == 0
        and tokens.shape[1] % (LANES * freq_count) == 0
        and raw_kernel.shape[1] == LANES * freq_count
        and (tokens.shape[1] + raw_kernel.shape[1]) // LANES % 16 == 0
    )


D = 768
SEQ_MB = 1
MICRO = 2


HIGHEST = lax.Precision.HIGHEST


def circle(height, breadth, period):
    first_index = lax.broadcasted_iota(jnp.int32, (height, breadth), 0)
    second_index = lax.broadcasted_iota(jnp.int32, (height, breadth), 1)
    phase_angle = (first_index * second_index % period).astype(jnp.float32) * (
        2.0 * math.pi / period
    )
    return (jnp.cos(phase_angle), jnp.sin(phase_angle))


def make_tables(padded_size):
    inner_size = 128
    outer_size = padded_size // inner_size
    outer_cos, outer_sin = circle(outer_size, outer_size, outer_size)
    inner_cos, inner_sin = circle(inner_size, inner_size, inner_size)
    twist_cos, twist_sin = circle(outer_size, inner_size, padded_size)
    return (outer_cos, outer_sin, inner_cos, inner_sin, twist_cos, twist_sin)


def spectrum(signal, padded_size, tables):
    outer_cos, outer_sin, inner_cos, inner_sin, twist_cos, twist_sin = tables
    inner_size = inner_cos.shape[0]
    pad_width = [(0, 0)] * (signal.ndim - 1) + [(0, padded_size - signal.shape[-1])]
    grid_values = jnp.pad(signal, pad_width).reshape(
        signal.shape[:-1] + (padded_size // inner_size, inner_size)
    )
    part_real = jnp.einsum("...ab,fa->...fb", grid_values, outer_cos, precision=HIGHEST)
    part_imag = -jnp.einsum("...ab,fa->...fb", grid_values, outer_sin, precision=HIGHEST)
    turned_real = part_real * twist_cos + part_imag * twist_sin
    turned_imag = part_imag * twist_cos - part_real * twist_sin
    spec_real = jnp.einsum(
        "...fb,bg->...fg", turned_real, inner_cos, precision=HIGHEST
    ) + jnp.einsum("...fb,bg->...fg", turned_imag, inner_sin, precision=HIGHEST)
    spec_imag = jnp.einsum(
        "...fb,bg->...fg", turned_imag, inner_cos, precision=HIGHEST
    ) - jnp.einsum("...fb,bg->...fg", turned_real, inner_sin, precision=HIGHEST)
    return (spec_real, spec_imag)


def signal_of(spec_real, spec_imag, keep_count, tables):
    outer_cos, outer_sin, inner_cos, inner_sin, twist_cos, twist_sin = tables
    padded_size = spec_real.shape[-1] * spec_real.shape[-2]
    back_real = jnp.einsum("...fg,bg->...fb", spec_real, inner_cos, precision=HIGHEST) - jnp.einsum(
        "...fg,bg->...fb", spec_imag, inner_sin, precision=HIGHEST
    )
    back_imag = jnp.einsum("...fg,bg->...fb", spec_imag, inner_cos, precision=HIGHEST) + jnp.einsum(
        "...fg,bg->...fb", spec_real, inner_sin, precision=HIGHEST
    )
    turned_real = back_real * twist_cos - back_imag * twist_sin
    turned_imag = back_imag * twist_cos + back_real * twist_sin
    grid_values = (
        jnp.einsum("...fb,af->...ab", turned_real, outer_cos, precision=HIGHEST)
        - jnp.einsum("...fb,af->...ab", turned_imag, outer_sin, precision=HIGHEST)
    ) / padded_size
    flat_values = grid_values.reshape(grid_values.shape[:-2] + (padded_size,))
    return flat_values[..., :keep_count]


def shape_kernel(raw_taps, live_taps):
    padded = jnp.pad(raw_taps, ((0, 0), (1, 1)))
    pooled = (padded[:, :-2] + padded[:, 1:-1] + padded[:, 2:]) / 3.0
    return (pooled - THRESH * jnp.tanh(pooled / THRESH)) * live_taps


def row_norm(values):
    row_width = values.shape[-1] * lax.axis_size("chan")
    row_total, row_square = lax.psum(
        (jnp.sum(values, axis=-1), jnp.sum(values * values, axis=-1)), "chan"
    )
    center = row_total / row_width
    spread = row_square / row_width - center * center
    scale = lax.rsqrt(spread + EPSILON)[..., None]
    return ((values - center[..., None]) * scale, scale)


def row_back(grad_rows, normed, scale, gain_row):
    row_width = grad_rows.shape[-1] * lax.axis_size("chan")
    scaled = grad_rows * gain_row
    sum_plain, sum_cross = lax.psum(
        (jnp.sum(scaled, axis=-1), jnp.sum(scaled * normed, axis=-1)), "chan"
    )
    return scale * (
        scaled - sum_plain[..., None] / row_width - normed * sum_cross[..., None] / row_width
    )


def features(values):
    return lax.all_gather(values, "chan", axis=2, tiled=True)


def partial_sum(values):
    return lax.psum_scatter(
        values.astype(jnp.bfloat16), "chan", scatter_dimension=2, tiled=True
    ).astype(jnp.float32)


def to_channels(values):
    return lax.all_to_all(
        jnp.swapaxes(values, 1, 2), "freq", split_axis=1, concat_axis=2, tiled=True
    )


def to_tokens(values):
    arrived = lax.all_to_all(values, "freq", split_axis=2, concat_axis=1, tiled=True)
    return jnp.swapaxes(arrived, 1, 2)


def by_features(
    tokens,
    cotangent,
    first_gain,
    second_gain,
    w_value,
    w_gate,
    w_out,
    w_up,
    w_down,
    raw_kernel,
    lengths,
):
    full_value, full_gate, full_out, full_up, full_down = (
        lax.all_gather(w_value, "freq", axis=0, tiled=True),
        lax.all_gather(w_gate, "freq", axis=0, tiled=True),
        lax.all_gather(w_out, "freq", axis=0, tiled=True),
        lax.all_gather(w_up, "freq", axis=0, tiled=True),
        lax.all_gather(w_down, "freq", axis=0, tiled=True),
    )
    freq_count = lax.axis_size("freq")
    chan_width = tokens.shape[2]
    channels = chan_width // freq_count
    seq_length = tokens.shape[1] * freq_count
    padded_size = 2 * seq_length
    tables = make_tables(padded_size)
    kernel_rows = lax.all_to_all(raw_kernel, "freq", split_axis=0, concat_axis=1, tiled=True)
    tap_count = kernel_rows.shape[1]
    my_lengths = lax.dynamic_slice_in_dim(lengths, lax.axis_index("freq") * channels, channels)
    tap_index = lax.broadcasted_iota(jnp.int32, (channels, tap_count), 1)
    live_taps = (tap_index < my_lengths[:, None]).astype(jnp.float32)
    kernel, kernel_pull = jax.vjp(functools.partial(shape_kernel, live_taps=live_taps), kernel_rows)
    kernel_real, kernel_imag = spectrum(kernel, padded_size, tables)
    hidden_width = full_up.shape[1]
    shard_factor = 1
    totals = (
        jnp.zeros((D // shard_factor, chan_width), jnp.float32),
        jnp.zeros((D // shard_factor, chan_width), jnp.float32),
        jnp.zeros((D // shard_factor, chan_width), jnp.float32),
        jnp.zeros((D // shard_factor, hidden_width), jnp.float32),
        jnp.zeros((D // shard_factor, hidden_width), jnp.float32),
        jnp.zeros((chan_width // shard_factor, 1), jnp.float32),
        jnp.zeros((chan_width // shard_factor, 1), jnp.float32),
    )
    kernel_grad = jnp.zeros((channels, tap_count), jnp.float32)
    outputs = []
    input_grads = []
    for micro_index in range(MICRO):
        rows_here = tokens[micro_index * SEQ_MB : (micro_index + 1) * SEQ_MB].astype(jnp.float32)
        first_normed, first_scale = row_norm(rows_here)
        input1 = features((first_normed * first_gain).astype(jnp.bfloat16))
        value_low = jnp.einsum(
            "bld,de->ble", input1, full_value, preferred_element_type=jnp.float32
        ).astype(jnp.bfloat16)
        gate_proj = jnp.einsum("bld,de->ble", input1, full_gate, preferred_element_type=jnp.float32)
        signal = to_channels(value_low).astype(jnp.float32)
        signal_real, signal_imag = spectrum(signal, padded_size, tables)
        mixed = signal_of(
            signal_real * kernel_real - signal_imag * kernel_imag,
            signal_real * kernel_imag + signal_imag * kernel_real,
            seq_length,
            tables,
        )
        mixed_rows = to_tokens(mixed.astype(jnp.bfloat16)).astype(jnp.float32)
        gate_act, gate_pull = jax.vjp(jax.nn.silu, gate_proj)
        inner_low = (mixed_rows * gate_act).astype(jnp.bfloat16)
        residual = rows_here + partial_sum(
            jnp.einsum("ble,oe->blo", inner_low, full_out, preferred_element_type=jnp.float32)
        )
        second_normed, second_scale = row_norm(residual)
        input2 = features((second_normed * second_gain).astype(jnp.bfloat16))
        hidden = jnp.einsum("bld,df->blf", input2, full_up, preferred_element_type=jnp.float32)
        activated, act_pull = jax.vjp(jax.nn.gelu, hidden)
        act_low = activated.astype(jnp.bfloat16)
        result = residual + partial_sum(
            jnp.einsum("blf,of->blo", act_low, full_down, preferred_element_type=jnp.float32)
        )
        outputs.append(result.astype(jnp.bfloat16))
        grad_rows_out = cotangent[micro_index * SEQ_MB : (micro_index + 1) * SEQ_MB]
        grad_full = features(grad_rows_out)
        grad_act = jnp.einsum(
            "blo,of->blf", grad_full, full_down, preferred_element_type=jnp.float32
        )
        down_grad = jnp.einsum(
            "blo,blf->of", grad_full, act_low, preferred_element_type=jnp.float32
        )
        grad_hidden = act_pull(grad_act)[0].astype(jnp.bfloat16)
        up_grad = jnp.einsum("bld,blf->df", input2, grad_hidden, preferred_element_type=jnp.float32)
        grad_in2 = partial_sum(
            jnp.einsum("blf,df->bld", grad_hidden, full_up, preferred_element_type=jnp.float32)
        )
        second_grad = jnp.sum(grad_in2 * second_normed, axis=(0, 1))
        grad_residual = grad_rows_out.astype(jnp.float32) + row_back(
            grad_in2, second_normed, second_scale, second_gain
        )
        grad_branch = features(grad_residual.astype(jnp.bfloat16))
        grad_inner = jnp.einsum(
            "blo,oe->ble", grad_branch, full_out, preferred_element_type=jnp.float32
        )
        out_grad = jnp.einsum(
            "blo,ble->oe", grad_branch, inner_low, preferred_element_type=jnp.float32
        )
        grad_mixed = to_channels((grad_inner * gate_act).astype(jnp.bfloat16)).astype(jnp.float32)
        grad_real, grad_imag = spectrum(grad_mixed, padded_size, tables)
        grad_signal = signal_of(
            grad_real * kernel_real + grad_imag * kernel_imag,
            grad_imag * kernel_real - grad_real * kernel_imag,
            seq_length,
            tables,
        )
        kernel_grad = kernel_grad + jnp.sum(
            signal_of(
                grad_real * signal_real + grad_imag * signal_imag,
                grad_imag * signal_real - grad_real * signal_imag,
                tap_count,
                tables,
            ),
            axis=0,
        )
        grad_signal_rows = to_tokens(grad_signal.astype(jnp.bfloat16))
        grad_gate_rows = gate_pull(grad_inner * mixed_rows)[0].astype(jnp.bfloat16)
        value_grad = jnp.einsum(
            "bld,ble->de", input1, grad_signal_rows, preferred_element_type=jnp.float32
        )
        gate_grad = jnp.einsum(
            "bld,ble->de", input1, grad_gate_rows, preferred_element_type=jnp.float32
        )
        grad_in1 = partial_sum(
            jnp.einsum(
                "ble,de->bld", grad_signal_rows, full_value, preferred_element_type=jnp.float32
            )
            + jnp.einsum(
                "ble,de->bld", grad_gate_rows, full_gate, preferred_element_type=jnp.float32
            )
        )
        first_grad = jnp.sum(grad_in1 * first_normed, axis=(0, 1))
        input_grads.append(
            grad_residual + row_back(grad_in1, first_normed, first_scale, first_gain)
        )
        local_terms = (
            value_grad,
            gate_grad,
            out_grad,
            up_grad,
            down_grad,
            first_grad[:, None],
            second_grad[:, None],
        )
        totals = tuple((left + right for left, right in zip(totals, local_terms)))
    totals = lax.psum_scatter(totals, "freq", scatter_dimension=0, tiled=True)
    raw_grad = kernel_pull(kernel_grad)[0]
    grad_kernel = lax.all_to_all(raw_grad, "freq", split_axis=1, concat_axis=0, tiled=True)
    output = jnp.concatenate(outputs, axis=0)
    grad_input = jnp.concatenate(input_grads, axis=0)
    return (
        output,
        grad_input,
        totals[0],
        totals[1],
        totals[2],
        totals[3],
        totals[4],
        totals[5],
        totals[6],
        grad_kernel,
    )


def solution(mesh):
    specs = dict(
        mesh=mesh,
        in_specs=(
            P(None, "freq", "chan"),
            P(None, "freq", "chan"),
            P("chan"),
            P("chan"),
            P("freq", "chan"),
            P("freq", "chan"),
            P("freq", "chan"),
            P("freq", "chan"),
            P("freq", "chan"),
            P("chan", "freq"),
            P("chan"),
        ),
        out_specs=(
            P(None, "freq", "chan"),
            P(None, "freq", "chan"),
            P("freq", "chan"),
            P("freq", "chan"),
            P("freq", "chan"),
            P("freq", "chan"),
            P("freq", "chan"),
            P("freq", "chan"),
            P("freq", "chan"),
            P("chan", "freq"),
        ),
        check_vma=False,
    )

    def step(*args):
        whole = fits(mesh)(args[0], args[4], args[9])
        return jax.shard_map(one_sequence if whole else by_features, **specs)(*args)

    return step
```

```python
import functools
import math

import jax
import jax.numpy as jnp
import numpy as np
from jax import lax
from jax.experimental import pallas as pl
from jax.experimental.pallas import tpu as pltpu
from jax.sharding import PartitionSpec as P

THRESH = 0.003
EPSILON = 1e-05
LANES = 128
MESH = pl.DeviceIdType.MESH
F32 = jnp.float32
BF16 = jnp.bfloat16


def bit_sizes(freq_count):
    return [1 << i for i in reversed(range(freq_count.bit_length() - 1))]


class Place:
    def __init__(self, freq_count):
        self.freq_count = freq_count
        self.freq = lax.axis_index("freq")
        self.chan = lax.axis_index("chan")
        self.bits = bit_sizes(freq_count)
        self.coords = [self.chan] + [lax.rem(self.freq // b, 2) for b in self.bits]
        self.dims = len(self.coords)
        self.core = self.coords[-1]

    def other(self, flipped):
        freq, chan = self.freq, self.chan
        for dim in flipped:
            if dim == 0:
                chan = 1 - chan
            else:
                bit = self.bits[dim - 1]
                freq = freq + bit - 2 * bit * self.coords[dim]
        return (freq, chan)


def flips(dims):
    return [
        tuple(dim for at, dim in enumerate(dims) if mask >> at & 1) for mask in range(1, 1 << len(dims))
    ]


def remote(source, target, send, recv, device):
    return pltpu.make_async_remote_copy(
        src_ref=source,
        dst_ref=target,
        send_sem=send,
        recv_sem=recv,
        device_id=device,
        device_id_type=MESH,
    )


def greet_all(place):
    barrier = pltpu.get_barrier_semaphore()
    count = 2 * place.freq_count
    me = place.chan * place.freq_count + place.freq

    def one(step, carry):
        other = lax.rem(me + step, count)
        pl.semaphore_signal(
            barrier,
            inc=1,
            device_id=(lax.rem(other, place.freq_count), other // place.freq_count),
            device_id_type=MESH,
        )
        return carry

    lax.fori_loop(1, count, one, 0)
    pl.semaphore_wait(barrier, count - 1)


class Gather:
    def __init__(self, place, buffer, phases, send, recv, columns=None):
        self.place, self.buffer, self.phases, self.send, self.recv = place, buffer, phases, send, recv
        self.columns = (slice(None), slice(None)) if columns is None else (slice(None), columns)

    def copies(self, phase):
        done = [dim for dims in self.phases[:phase] for dim in dims]
        index = tuple(
            slice(None) if dim in done else coord for dim, coord in enumerate(self.place.coords)
        )
        region = self.buffer.at[index + self.columns]
        base = sum(len(flips(dims)) for dims in self.phases[:phase])
        return [
            remote(region, region, self.send.at[base + k], self.recv.at[base + k], self.place.other(flipped))
            for k, flipped in enumerate(flips(self.phases[phase]))
        ]

    def start(self, phase):
        for copy in self.copies(phase):
            copy.start()

    def wait(self, phase):
        for copy in self.copies(phase):
            copy.wait()

    def go_on(self, phase):
        self.wait(phase)
        if phase + 1 < len(self.phases):
            self.start(phase + 1)


class Reduce:
    def __init__(self, place, total, landing, phases, send, recv, out, columns=None):
        self.place, self.total, self.landing, self.phases = place, total, landing, phases
        self.send, self.recv, self.out = send, recv, out
        self.coords = place.coords[:-1]
        self.columns = (slice(None), slice(None)) if columns is None else (slice(None), columns)

    def region(self, phase, flipped):
        fixed = [dim for dims in self.phases[: phase + 1] for dim in dims]
        return tuple(
            (1 - coord if dim in flipped else coord) if dim in fixed else slice(None)
            for dim, coord in enumerate(self.coords)
        )

    def copies(self, phase):
        base = sum(len(flips(dims)) for dims in self.phases[:phase])
        return [
            remote(
                self.total.at[self.region(phase, flipped) + self.columns],
                self.landing[phase].at[k],
                self.send.at[base + k],
                self.recv.at[base + k],
                self.place.other(flipped),
            )
            for k, flipped in enumerate(flips(self.phases[phase]))
        ]

    def start(self, phase):
        for copy in self.copies(phase):
            copy.start()

    def finish(self, phase):
        for copy in self.copies(phase):
            copy.wait()
        kept = self.region(phase, ())
        free = [dim for dim, at in enumerate(kept) if isinstance(at, slice)]
        landing = self.landing[phase]
        last = phase + 1 == len(self.phases)

        def one(turn, carry):
            where, there = list(kept), []
            for at, dim in enumerate(free):
                bit = lax.rem(turn // (1 << (len(free) - 1 - at)), 2)
                where[dim] = bit
                there.append(bit)
            where = tuple(where) + self.columns
            total = self.total[where].astype(F32)
            for k in range(len(flips(self.phases[phase]))):
                total = total + landing[(k,) + tuple(there)].astype(F32)
            if last:
                self.out[self.columns] = total
            else:
                self.total[where] = total.astype(BF16)
            return carry

        if free:
            lax.fori_loop(0, 1 << len(free), one, 0)
        else:
            one(0, 0)

    def go_on(self, phase):
        self.finish(phase)
        if phase + 1 < len(self.phases):
            self.start(phase + 1)


def landing_shapes(phases, dims, rows, columns):
    shapes, free = [], dims - 1
    for group in phases:
        free -= len(group)
        shapes.append((len(flips(group)),) + (2,) * free + (rows, columns))
    return shapes


class Spread:
    def __init__(self, place, total, landing, phases, send, recv):
        self.place, self.total, self.landing, self.phases = place, total, landing, phases
        self.send, self.recv = send, recv

    def copies(self, phase):
        base = sum(len(flips(dims)) for dims in self.phases[:phase])
        return [
            remote(
                self.total.at[phase],
                self.landing.at[base + k],
                self.send.at[base + k],
                self.recv.at[base + k],
                self.place.other(flipped),
            )
            for k, flipped in enumerate(flips(self.phases[phase]))
        ]

    def start(self, phase):
        for copy in self.copies(phase):
            copy.start()

    def go_on(self, phase):
        copies = self.copies(phase)
        base = sum(len(flips(dims)) for dims in self.phases[:phase])
        for copy in copies:
            copy.wait()
        total = self.total[phase]
        for k in range(len(copies)):
            total = total + self.landing[base + k]
        self.total[phase + 1] = total
        if phase + 1 < len(self.phases):
            self.start(phase + 1)


class Sizes:
    def __init__(self, freq_count, here, half, taps):
        self.freq_count = freq_count
        self.here = here
        self.cols = here // LANES
        self.channels = half // freq_count
        self.chunk = self.cols * self.channels
        self.devices = 2 * freq_count
        self.tap_rows = taps // LANES
        self.rows = here * freq_count // LANES + self.tap_rows
        self.size = self.rows * LANES


def conv_tables(sizes):
    rows, size = sizes.rows, sizes.size
    f = np.arange(rows)
    fi = np.arange(sizes.freq_count)
    a_of, imag = [], []
    for col in range(sizes.cols):
        for seq in range(2):
            for block in fi:
                a_of.append(block * sizes.cols + col)
                imag.append(seq)
    a_of, imag = np.array(a_of), np.array(imag)
    angle = 2 * np.pi * np.outer(f, a_of) / rows
    cos, sin = np.cos(angle), np.sin(angle)
    into = np.concatenate([np.where(imag, sin, cos), np.where(imag, cos, -sin)], axis=0)
    outof = np.concatenate([np.where(imag, sin, cos), np.where(imag, cos, -sin)], axis=0).T / size
    taps = np.arange(sizes.tap_rows)
    angle = 2 * np.pi * np.outer(f, taps) / rows
    taps_into = np.concatenate([np.cos(angle), -np.sin(angle)], axis=0)
    taps_outof = taps_into.T / size
    b = np.arange(LANES)
    angle = 2 * np.pi * np.outer(f, b) / size
    turn = np.stack([np.cos(angle), np.sin(angle)])
    angle = 2 * np.pi * np.outer(b, b) / LANES
    cos, sin = np.cos(angle), np.sin(angle)
    ahead = np.block([[cos, -sin], [sin, cos]])
    return (
        jnp.asarray(into, BF16),
        jnp.asarray(outof, BF16),
        jnp.asarray(taps_into, BF16),
        jnp.asarray(taps_outof, BF16),
        jnp.asarray(turn, F32),
        jnp.asarray(ahead, BF16),
        jnp.asarray(ahead.T, BF16),
    )


def dot(left, right):
    return jnp.dot(left, right, preferred_element_type=F32)


def spectrum_into(sizes, load, into, turn, ahead, inner, spectrum):
    rows = sizes.rows

    def one(pair, carry):
        both = jnp.concatenate([load(2 * pair), load(2 * pair + 1)], axis=1).astype(BF16)
        part = dot(into[...], both)
        for side in range(2):
            real = part[:rows, side * LANES : (side + 1) * LANES]
            imag = part[rows:, side * LANES : (side + 1) * LANES]
            turned = jnp.concatenate(
                [real * turn[0] + imag * turn[1], imag * turn[0] - real * turn[1]], axis=1
            )
            start = pl.multiple_of((2 * pair + side) * rows, 16)
            inner[pl.ds(start, rows), :] = turned.astype(BF16)
        return carry

    lax.fori_loop(0, sizes.channels // 2, one, 0)
    tile = sizes.channels * rows // 4

    def two(step, carry):
        at = pl.ds(pl.multiple_of(step * tile, 16), tile)
        spectrum[at, :] = dot(inner[at, :], ahead[...])
        return carry

    lax.fori_loop(0, 4, two, 0)


def signal_from(sizes, product, outof, turn, behind, inner, store):
    rows = sizes.rows
    tile = sizes.channels * rows // 4

    def one(step, carry):
        at = pl.ds(pl.multiple_of(step * tile, 16), tile)
        inner[at, :] = dot(product(at), behind[...]).astype(BF16)
        return carry

    lax.fori_loop(0, 4, one, 0)

    def two(pair, carry):
        sides = []
        for side in range(2):
            start = pl.multiple_of((2 * pair + side) * rows, 16)
            back = inner[pl.ds(start, rows), :].astype(F32)
            real, imag = back[:, :LANES], back[:, LANES:]
            sides.append(
                jnp.concatenate(
                    [real * turn[0] - imag * turn[1], imag * turn[0] + real * turn[1]], axis=0
                ).astype(BF16)
            )
        got = dot(outof[...], jnp.concatenate(sides, axis=1))
        for side in range(2):
            store(2 * pair + side, got[:, side * LANES : (side + 1) * LANES])
        return carry

    lax.fori_loop(0, sizes.channels // 2, two, 0)


def times(left, right, conj):
    a, b = left[:, :LANES], left[:, LANES:]
    c, d = right[:, :LANES], right[:, LANES:]
    if conj:
        return jnp.concatenate([a * c + b * d, b * c - a * d], axis=1).astype(BF16)
    return jnp.concatenate([a * c - b * d, a * d + b * c], axis=1).astype(BF16)


class Exchange:
    def __init__(self, place, source, target, send, recv):
        self.place, self.source, self.target = place, source, target
        self.send, self.recv = send, recv
        self.count = 2 * place.freq_count
        self.me = place.chan * place.freq_count + place.freq

    def each(self, action):
        freq_count = self.place.freq_count

        def one(step, carry):
            other = lax.rem(self.me + step, self.count)
            origin = lax.rem(self.me + self.count - step, self.count)
            action(step, other, origin, (lax.rem(other, freq_count), other // freq_count))
            return carry

        lax.fori_loop(1, self.count, one, 0)

    def start(self):
        def action(step, other, origin, device):
            pltpu.make_async_remote_copy(
                src_ref=self.source.at[other],
                dst_ref=self.target.at[self.me],
                send_sem=self.send.at[step],
                recv_sem=self.recv.at[step],
                device_id=device,
                device_id_type=MESH,
            ).start()

        self.each(action)
        self.target[self.me] = self.source[self.me]

    def wait(self):
        def action(step, other, origin, device):
            pltpu.make_async_remote_copy(
                src_ref=self.source.at[other],
                dst_ref=self.target.at[origin],
                send_sem=self.send.at[step],
                recv_sem=self.recv.at[step],
                device_id=device,
                device_id_type=MESH,
            ).wait()

        self.each(action)


class PlaneExchange:
    def __init__(self, place, source, target, send, recv):
        self.place, self.source, self.target = place, source, target
        self.send, self.recv = send, recv

    def each(self, action):
        count, me = self.place.freq_count, self.place.freq

        def one(step, carry):
            action(step, lax.rem(me + step, count), lax.rem(me + count - step, count))
            return carry

        lax.fori_loop(1, count, one, 0)

    def start(self):
        def action(step, other, origin):
            pltpu.make_async_remote_copy(
                src_ref=self.source(other),
                dst_ref=self.target(self.place.freq),
                send_sem=self.send.at[step],
                recv_sem=self.recv.at[step],
                device_id=(other, self.place.chan),
                device_id_type=MESH,
            ).start()

        self.each(action)

    def wait(self):
        def action(step, other, origin):
            pltpu.make_async_remote_copy(
                src_ref=self.source(other),
                dst_ref=self.target(origin),
                send_sem=self.send.at[step],
                recv_sem=self.recv.at[step],
                device_id=(other, self.place.chan),
                device_id_type=MESH,
            ).wait()

        self.each(action)


def to_chunks(sizes, rows):
    turned = rows.T.reshape(sizes.devices, sizes.channels, sizes.here)
    pieces = [turned[:, :, col * LANES : (col + 1) * LANES] for col in range(sizes.cols)]
    return jnp.concatenate(pieces, axis=1).astype(BF16)


def from_chunks(sizes, chunks):
    wide = chunks.astype(F32)
    pieces = [
        wide[:, col * sizes.channels : (col + 1) * sizes.channels, :].reshape(
            sizes.devices * sizes.channels, LANES
        )
        for col in range(sizes.cols)
    ]
    return jnp.concatenate(pieces, axis=1).T


def chunk_loader(sizes, ref):
    def load(channel):
        pieces = [
            ref[pl.ds(col * sizes.channels + channel, sizes.devices, stride=sizes.chunk), :]
            for col in range(sizes.cols)
        ]
        return jnp.concatenate(pieces, axis=0)

    return load


def chunk_storer(sizes, ref):
    def store(channel, values):
        for col in range(sizes.cols):
            ref[pl.ds(col * sizes.channels + channel, sizes.devices, stride=sizes.chunk), :] = values[
                col * sizes.devices : (col + 1) * sizes.devices
            ]

    return store


def widen(sizes, chunks, ref):
    def one(step, carry):
        ref[pl.ds(pl.multiple_of(step * sizes.chunk, 8), sizes.chunk), :] = chunks[step].astype(F32)
        return carry

    lax.fori_loop(0, sizes.devices, one, 0)


def narrow(sizes, ref, chunks):
    def one(step, carry):
        chunks[step] = ref[pl.ds(pl.multiple_of(step * sizes.chunk, 8), sizes.chunk), :].astype(BF16)
        return carry

    lax.fori_loop(0, sizes.devices, one, 0)


def pooled_taps(taps):
    lane = lax.broadcasted_iota(jnp.int32, taps.shape, 2)
    zero = jnp.zeros_like(taps[:1])
    after = pltpu.roll(taps, LANES - 1, 2)
    before = pltpu.roll(taps, 1, 2)
    after = jnp.where(lane == LANES - 1, jnp.concatenate([after[1:], zero], axis=0), after)
    before = jnp.where(lane == 0, jnp.concatenate([zero, before[:-1]], axis=0), before)
    return (before + taps + after) / 3.0


def live_mask(shape, lengths):
    tap = lax.broadcasted_iota(jnp.int32, shape, 0) * LANES + lax.broadcasted_iota(
        jnp.int32, shape, 2
    )
    return (tap < lengths[None]).astype(F32)


VMEM_SPEC = pl.BlockSpec(memory_space=pltpu.VMEM)
ANY_SPEC = pl.BlockSpec(memory_space=pl.ANY)
GELU_SCALE = math.sqrt(2.0 / math.pi)
GELU_CUBE = 0.044715


def dot_nt(left, right):
    return lax.dot_general(left, right, (((1,), (1,)), ((), ())), preferred_element_type=F32)


def norm(values):
    center = jnp.mean(values, axis=-1, keepdims=True)
    shifted = values - center
    scale = lax.rsqrt(jnp.mean(shifted * shifted, axis=-1, keepdims=True) + EPSILON)
    return shifted * scale, scale


def norm_back(grad_rows, normed, scale, gain):
    scaled = grad_rows * gain
    plain = jnp.mean(scaled, axis=-1, keepdims=True)
    cross = jnp.mean(scaled * normed, axis=-1, keepdims=True)
    return scale * (scaled - plain - normed * cross)


class Names:
    def __init__(self, names, refs):
        for name, ref in zip(names, refs, strict=True):
            setattr(self, name, ref)


class Plan:
    inputs = (
        "tokens", "cotangent", "pack", "raw_kernel",
        "s_value", "s_gate", "s_out", "s_up", "s_down",
        "into", "outof", "taps_into", "taps_outof", "turn", "ahead", "behind",
    )
    outputs = (
        "output", "grad_input", "r_value", "r_gate", "r_out", "r_up", "r_down", "gain_sums", "grad_kernel",
    )

    def __init__(self, sizes, ff_half):
        self.sizes = sizes
        here, channels, freq_count = sizes.here, sizes.channels, sizes.freq_count
        half = channels * freq_count
        width = 2 * half
        self.here, self.half, self.width, self.ff_half = here, half, width, ff_half
        dims = 1 + len(bit_sizes(freq_count))
        self.dims = dims
        self.rows = rows = width // freq_count
        self.lead = lead = (2,) * dims
        core, y, top = dims - 1, dims - 2, tuple(range(1, dims - 2))
        self.core_dim = core
        self.gather_phases = dict(
            value=(top, (0, y), (core,)),
            gate=(top, (0,), (y,), (core,)),
            out=(top, (y,), (0,), (core,)),
            up=(top, (0,), (y,), (core,)),
            down=(top, (y,), (0,), (core,)),
        )
        self.reduce_phases = dict(
            value=((0, y), top),
            gate=((0,), (y,), top),
            out=((y,), (0,), top),
            up=((0,), (y,), top),
            down=((y,), (0,), top),
        )
        self.spread_phases = ((core,), (0, y), top)
        self.pieces = 2
        self.piece = ff_half // self.pieces
        self.tile = half
        self.per_piece = self.piece // self.tile
        self.tiles = 2 * ff_half // self.tile
        names, shapes = [], []

        def add(name, shape, kind):
            names.append(name)
            shapes.append(pltpu.VMEM(shape, kind))

        def sems(name, *shape):
            names.append(name)
            shapes.append(pltpu.SemaphoreType.DMA(shape))

        for name in ("x_buf", "g_buf", "out_send", "gin_send"):
            add(name, (2, here, half), BF16)
        add("gin_land", (here, half), BF16)
        add("packs", (2, 8, half), F32)
        add("turned_pack", (half, 8), F32)
        self.weight_names = ("value", "gate", "out", "up", "down")
        columns = dict(value=half, gate=half, out=half, up=ff_half, down=ff_half)
        self.columns = columns
        for name in self.weight_names:
            add("w_" + name, lead + (rows, columns[name]), BF16)
            add("g_" + name, lead[:-1] + (rows, columns[name]), BF16)
            pieces = self.pieces if name in ("up", "down") else 1
            for piece in range(pieces):
                landing = landing_shapes(self.reduce_phases[name], dims, rows, columns[name] // pieces)
                for phase, shape in enumerate(landing):
                    add(f"l_{name}{piece}{phase}", shape, BF16)
                for what in ("gs", "gr", "rs", "rr"):
                    sems(f"{what}_{name}{piece}", 8)
        spec = (channels * sizes.rows, 2 * LANES)
        for name in ("kernel_spec", "value_spec", "grad_spec"):
            add(name, spec, F32)
        add("inner", spec, BF16)
        add("taps", (sizes.tap_rows, channels, LANES), F32)
        add("tap_grad", (sizes.tap_rows, channels, LANES), F32)
        add("tap_wide", (sizes.tap_rows * channels, LANES), F32)
        chunks = (sizes.devices, sizes.chunk, LANES)
        for name in ("sent", "sent_back", "landed1", "landed2", "landed3", "landed4"):
            add(name, chunks, BF16)
        add("wide", (sizes.devices * sizes.chunk, LANES), F32)
        for name in ("t1", "t2"):
            sems(name + "_send", freq_count)
            sems(name + "_recv", freq_count)
        for name in ("a1", "a2", "a3", "a4"):
            sems(name + "_send", sizes.devices)
            sems(name + "_recv", sizes.devices)
        for name in ("normed1", "gate", "mixed", "residual", "normed2", "out_sum", "in2_sum", "grad_res"):
            add(name, (here, width), F32)
        for name in ("scale1", "scale2"):
            add(name, (here, 1), F32)
        for name in ("input1", "input2", "grad_rows", "branch_rows"):
            add(name, (here, width), BF16)
        for name in ("input1", "input2", "grad_rows", "branch_rows"):
            add("t_" + name, (width // (2 * rows), 2, rows, here), BF16)
            add("twin_" + name, (width // (2 * rows), rows, here), BF16)
        for name in ("inner_rows", "signal_rows", "gate_rows"):
            add(name, (2, here, half), BF16)
            add("twin_" + name, (2, here, half), BF16)
        for name in ("act", "hid"):
            add(name, (self.tiles, here, self.tile), BF16)
            add("twin_" + name, (self.tiles, here, self.tile), BF16)
        for name in ("act", "hid"):
            sems(f"{name}_send", self.tiles)
            sems(f"{name}_recv", self.tiles)
        sems("twin_send", 7)
        sems("twin_recv", 7)
        add("gain_total", (len(self.spread_phases) + 1, 2 * width // LANES + 4, LANES), F32)
        add("gain_land", (1 + 3 + 3, 2 * width // LANES + 4, LANES), F32)
        sems("gain_send", 8)
        sems("gain_recv", 8)
        sems("swap_send", 5)
        sems("swap_recv", 5)
        sems("local", 10)
        self.names, self.scratch = names, shapes


def row_tiles(count, body, tile=64):
    def one(step, carry):
        body(pl.ds(pl.multiple_of(step * tile, tile), tile))
        return carry

    lax.fori_loop(0, count // tile, one, 0)


def block_kernel(plan, *refs):
    sizes = plan.sizes
    here, half, width, channels = plan.here, plan.half, plan.width, sizes.channels
    k = Names(plan.inputs + plan.outputs + tuple(plan.names), refs)
    place = Place(sizes.freq_count)
    chan, core = place.chan, place.core
    twin = place.other((plan.core_dim,))
    across = place.other((0,))

    def whole(ref, lead, columns=slice(None)):
        value = ref[(lead,) + (slice(None),) * plan.dims + (columns,)]
        return value.reshape(width, value.shape[-1])

    own = []
    for at, name in enumerate(plan.weight_names):
        buffer = getattr(k, "w_" + name).at[tuple(place.coords)]
        own.append(pltpu.make_async_copy(getattr(k, "s_" + name), buffer, k.local.at[at]))
    moves = (
        (k.tokens.at[chan], k.x_buf.at[chan]),
        (k.cotangent.at[chan], k.g_buf.at[chan]),
        (k.pack, k.packs.at[chan]),
        (k.raw_kernel.at[pl.ds(pl.multiple_of(place.freq * channels, 8), channels)], k.taps.at[place.freq]),
    )
    for at, (source, target) in enumerate(moves):
        own.append(pltpu.make_async_copy(source, target, k.local.at[5 + at]))
    for copy in own:
        copy.start()
    greet_all(place)
    swaps = [
        remote(source, target, k.swap_send.at[at], k.swap_recv.at[at], across)
        for at, (source, target) in enumerate(
            (
                (k.tokens.at[1 - chan], k.x_buf.at[chan]),
                (k.pack, k.packs.at[chan]),
                (k.cotangent.at[1 - chan], k.g_buf.at[chan]),
            )
        )
    ]
    swaps[0].start()
    swaps[1].start()
    gathers = {}
    for name in plan.weight_names:
        buffer = getattr(k, "w_" + name)
        pieces = plan.pieces if name in ("up", "down") else 1
        for piece in range(pieces):
            size = plan.columns[name] // pieces
            gathers[name + str(piece)] = Gather(
                place,
                buffer,
                plan.gather_phases[name],
                getattr(k, f"gs_{name}{piece}"),
                getattr(k, f"gr_{name}{piece}"),
                pl.ds(piece * size, size) if pieces > 1 else None,
            )
    own[0].wait()
    gathers["value0"].start(0)
    own[1].wait()
    gathers["gate0"].start(0)
    tap_move = PlaneExchange(
        place,
        lambda g: k.raw_kernel.at[pl.ds(pl.multiple_of(g * channels, 8), channels)],
        lambda g: k.taps.at[g],
        k.t1_send,
        k.t1_recv,
    )
    tap_move.start()
    own[2].wait()
    gathers["out0"].start(0)
    swaps[2].start()
    own[3].wait()
    own[4].wait()
    own[5].wait()
    own[7].wait()
    gathers["value0"].go_on(0)
    gathers["up0"].start(0)
    swaps[0].wait()
    swaps[1].wait()

    def gain_row(row):
        return jnp.concatenate([k.packs[0, row : row + 1, :], k.packs[1, row : row + 1, :]], axis=1)

    first_gain, second_gain = gain_row(0), gain_row(1)

    def first_norm(at):
        rows = jnp.concatenate([k.x_buf[0, at, :], k.x_buf[1, at, :]], axis=1).astype(F32)
        normed, scale = norm(rows)
        k.normed1[at, :] = normed
        k.scale1[at, :] = scale
        k.input1[at, :] = (normed * first_gain).astype(BF16)

    row_tiles(here, first_norm)
    gathers["gate0"].go_on(0)
    gathers["out0"].go_on(0)
    gathers["value0"].go_on(1)
    gathers["down0"].start(0)

    def turn_rows(name):
        turned = getattr(k, name)[...].astype(F32).T.astype(BF16)
        target = getattr(k, "t_" + name)
        target[...] = turned.reshape(target.shape)

    twins = {}

    def share_turned(name, at):
        turn_rows(name)
        twins[name] = remote(
            getattr(k, "t_" + name).at[:, 1 - core],
            getattr(k, "twin_" + name),
            k.twin_send.at[at],
            k.twin_recv.at[at],
            twin,
        )
        twins[name].start()

    def share_rows(name, at):
        twins[name] = remote(
            getattr(k, name), getattr(k, "twin_" + name), k.twin_send.at[at], k.twin_recv.at[at], twin
        )
        twins[name].start()

    share_turned("input1", 0)
    gathers["value0"].go_on(2)

    value = jnp.concatenate(
        [dot(k.input1[...], whole(k.w_value, 0)), dot(k.input1[...], whole(k.w_value, 1))], axis=1
    )
    k.sent[...] = to_chunks(sizes, value)
    move1 = Exchange(place, k.sent, k.landed1, k.a1_send, k.a1_recv)
    move1.start()
    gathers["gate0"].go_on(1)
    gathers["out0"].go_on(1)
    gathers["up0"].go_on(0)
    gathers["up1"].start(0)
    tap_move.wait()
    own[8].wait()
    k.turned_pack[...] = k.packs[chan].T
    lengths = k.turned_pack[pl.ds(pl.multiple_of(place.freq * channels, 8), channels), 2:3]
    live = live_mask(k.taps.shape, lengths)
    pooled = pooled_taps(k.taps[...])
    shrunk = (pooled - THRESH * jnp.tanh(pooled / THRESH)) * live
    k.tap_wide[...] = shrunk.reshape(sizes.tap_rows * channels, LANES)
    spectrum_into(
        sizes,
        lambda c: k.tap_wide[pl.ds(c, sizes.tap_rows, stride=channels), :],
        k.taps_into, k.turn, k.ahead, k.inner, k.kernel_spec,
    )
    swaps[2].wait()
    own[6].wait()
    k.grad_rows[...] = jnp.concatenate([k.g_buf[0], k.g_buf[1]], axis=1)
    share_turned("grad_rows", 2)
    gathers["gate0"].go_on(2)
    gathers["out0"].go_on(2)
    gathers["up0"].go_on(1)
    gathers["gate0"].go_on(3)
    for c in range(2):
        k.gate[:, c * half : (c + 1) * half] = dot(k.input1[...], whole(k.w_gate, c))
    move1.wait()

    widen(sizes, k.landed1, k.wide)
    spectrum_into(sizes, chunk_loader(sizes, k.wide), k.into, k.turn, k.ahead, k.inner, k.value_spec)
    signal_from(
        sizes,
        lambda at: times(k.value_spec[at, :], k.kernel_spec[at, :], False),
        k.outof, k.turn, k.behind, k.inner, chunk_storer(sizes, k.wide),
    )
    narrow(sizes, k.wide, k.sent_back)
    move2 = Exchange(place, k.sent_back, k.landed2, k.a2_send, k.a2_recv)
    move2.start()
    gathers["down0"].go_on(0)
    gathers["down1"].start(0)
    gathers["up1"].go_on(0)
    gathers["up0"].go_on(2)
    gathers["out0"].go_on(3)
    gathers["down0"].go_on(1)
    gathers["up1"].go_on(1)
    gathers["up0"].go_on(3)
    move2.wait()

    def from_chunk_columns(chunks, col):
        wide = chunks[:, col * channels : (col + 1) * channels, :].astype(F32)
        return wide.reshape(width, LANES).T

    for col in range(sizes.cols):
        k.mixed[col * LANES : (col + 1) * LANES, :] = from_chunk_columns(k.landed2, col)

    def make_inner(at):
        gate = k.gate[at, :]
        inner = (k.mixed[at, :] * (gate * jax.nn.sigmoid(gate))).astype(BF16)
        k.inner_rows[0, at, :] = inner[:, :half]
        k.inner_rows[1, at, :] = inner[:, half:]

    row_tiles(here, make_inner)
    share_rows("inner_rows", 4)
    k.residual[...] = dot_nt(k.inner_rows[0], whole(k.w_out, 0)) + dot_nt(
        k.inner_rows[1], whole(k.w_out, 1)
    )

    def second_norm(at):
        rows = jnp.concatenate([k.x_buf[0, at, :], k.x_buf[1, at, :]], axis=1).astype(F32)
        residual = k.residual[at, :] + rows
        normed, scale = norm(residual)
        k.residual[at, :] = residual
        k.normed2[at, :] = normed
        k.scale2[at, :] = scale
        k.input2[at, :] = (normed * second_gain).astype(BF16)

    row_tiles(here, second_norm)
    share_turned("input2", 1)
    gathers["down1"].go_on(0)
    gathers["down0"].go_on(2)
    gathers["up1"].go_on(2)
    gathers["down1"].go_on(1)
    gathers["down0"].go_on(3)
    gathers["up1"].go_on(3)
    gathers["down1"].go_on(2)
    gathers["down1"].go_on(3)

    k.out_sum[...] = jnp.zeros_like(k.out_sum)
    k.in2_sum[...] = jnp.zeros_like(k.in2_sum)
    per_half = plan.tiles // 2

    def twin_copy(name, tile):
        return remote(
            getattr(k, name).at[tile],
            getattr(k, "twin_" + name).at[tile],
            getattr(k, name + "_send").at[tile],
            getattr(k, name + "_recv").at[tile],
            twin,
        )

    def feed_forward(tile, carry):
        columns = pl.ds(pl.multiple_of(lax.rem(tile, per_half) * plan.tile, LANES), plan.tile)
        up = whole(k.w_up, tile // per_half, columns)
        hidden = dot(k.input2[...], up)
        square = hidden * hidden
        bent = jnp.tanh(GELU_SCALE * hidden * (1.0 + GELU_CUBE * square))
        act = (0.5 * hidden * (1.0 + bent)).astype(BF16)
        slope = 0.5 * (1.0 + bent) + (0.5 * GELU_SCALE) * hidden * (1.0 - bent * bent) * (
            1.0 + 3.0 * GELU_CUBE * square
        )
        down = whole(k.w_down, tile // per_half, columns)
        grad = (dot(k.grad_rows[...], down) * slope).astype(BF16)
        k.act[tile] = act
        k.hid[tile] = grad
        twin_copy("act", tile).start()
        twin_copy("hid", tile).start()
        k.in2_sum[...] += dot_nt(grad, up)
        k.out_sum[...] += dot_nt(act, down)
        return carry

    lax.fori_loop(0, plan.tiles, feed_forward, 0)

    gain_rows = 2 * width // LANES
    k.gain_total[0] = jnp.zeros_like(k.gain_total[0])

    def add_gain(row, sums):
        for at in range(width // LANES):
            base = row * (width // LANES) + at
            k.gain_total[0, base : base + 1, :] += sums[:, at * LANES : (at + 1) * LANES]

    def second_back(at):
        grad = k.in2_sum[at, :]
        normed = k.normed2[at, :]
        add_gain(1, jnp.sum(grad * normed, axis=0, keepdims=True))
        result = k.grad_rows[at, :].astype(F32) + norm_back(grad, normed, k.scale2[at, :], second_gain)
        k.grad_res[at, :] = result
        k.branch_rows[at, :] = result.astype(BF16)

    row_tiles(here, second_back)
    for c in range(2):
        k.in2_sum[:, c * half : (c + 1) * half] = dot(k.branch_rows[...], whole(k.w_out, c))

    def gate_back(at):
        gate = k.gate[at, :]
        grad = k.in2_sum[at, :]
        sig = jax.nn.sigmoid(gate)
        rows = (grad * k.mixed[at, :] * (sig * (1.0 + gate * (1.0 - sig)))).astype(BF16)
        k.gate_rows[0, at, :] = rows[:, :half]
        k.gate_rows[1, at, :] = rows[:, half:]
        k.normed2[at, :] = grad * (gate * sig)

    row_tiles(here, gate_back)
    k.sent[...] = to_chunks(sizes, k.normed2[...])
    move3 = Exchange(place, k.sent, k.landed3, k.a3_send, k.a3_recv)
    move3.start()
    share_rows("gate_rows", 6)
    share_turned("branch_rows", 3)

    reduces = {}
    for name in plan.weight_names:
        pieces = plan.pieces if name in ("up", "down") else 1
        for piece in range(pieces):
            size = plan.columns[name] // pieces
            reduces[name + str(piece)] = Reduce(
                place,
                getattr(k, "g_" + name),
                [getattr(k, f"l_{name}{piece}{phase}") for phase in range(len(plan.reduce_phases[name]))],
                plan.reduce_phases[name],
                getattr(k, f"rs_{name}{piece}"),
                getattr(k, f"rr_{name}{piece}"),
                getattr(k, "r_" + name),
                pl.ds(piece * size, size) if pieces > 1 else None,
            )

    def left(name):
        mine = getattr(k, "t_" + name)[:, core]
        rows = width // 2
        return jnp.concatenate(
            [mine.reshape(rows, here), getattr(k, "twin_" + name)[...].reshape(rows, here)], axis=1
        )

    def tile_grads(name, left_name, right_name, piece):
        grads, right = getattr(k, "g_" + name), getattr(k, right_name)
        twin_right = getattr(k, "twin_" + right_name)
        count = plan.per_piece

        def one(turn, carry):
            lead, at = turn // count, lax.rem(turn, count)
            tile = lead * per_half + piece * count + at
            got = dot(left(left_name), jnp.concatenate([right[tile], twin_right[tile]], axis=0))
            columns = pl.ds(pl.multiple_of((piece * count + at) * plan.tile, LANES), plan.tile)
            index = (lead,) + (slice(None),) * (plan.dims - 1) + (columns,)
            grads[index] = got.astype(BF16).reshape((2,) * (plan.dims - 2) + (plan.rows, plan.tile))
            return carry

        lax.fori_loop(0, 2 * count, one, 0)

    def row_grads(name, left_name, right_name):
        grads, right = getattr(k, "g_" + name), getattr(k, right_name)
        twin_right = getattr(k, "twin_" + right_name)
        for c in range(2):
            got = dot(left(left_name), jnp.concatenate([right[c], twin_right[c]], axis=0))
            grads[c] = got.astype(BF16).reshape((2,) * (plan.dims - 2) + (plan.rows, half))

    def wait_tiles(tile, carry):
        twin_copy("act", tile).wait()
        twin_copy("hid", tile).wait()
        return carry

    lax.fori_loop(0, plan.tiles, wait_tiles, 0)
    twins["input2"].wait()
    twins["grad_rows"].wait()
    tile_grads("up", "input2", "hid", 0)
    reduces["up0"].start(0)
    tile_grads("down", "grad_rows", "act", 0)
    reduces["down0"].start(0)
    tile_grads("up", "input2", "hid", 1)
    reduces["up1"].start(0)
    tile_grads("down", "grad_rows", "act", 1)
    reduces["down1"].start(0)

    def make_output(at):
        rows = (k.residual[at, :] + k.out_sum[at, :]).astype(BF16)
        k.out_send[0, at, :] = rows[:, :half]
        k.out_send[1, at, :] = rows[:, half:]

    row_tiles(here, make_output)
    swap_out = remote(
        k.out_send.at[1 - chan], k.output.at[chan], k.swap_send.at[3], k.swap_recv.at[3], across
    )
    swap_out.start()
    k.output[chan] = k.out_send[chan]
    twins["inner_rows"].wait()
    twins["branch_rows"].wait()
    row_grads("out", "branch_rows", "inner_rows")
    reduces["out0"].start(0)
    twins["gate_rows"].wait()
    twins["input1"].wait()
    row_grads("gate", "input1", "gate_rows")
    reduces["gate0"].start(0)
    move3.wait()

    widen(sizes, k.landed3, k.wide)
    spectrum_into(sizes, chunk_loader(sizes, k.wide), k.into, k.turn, k.ahead, k.inner, k.grad_spec)
    signal_from(
        sizes,
        lambda at: times(k.grad_spec[at, :], k.kernel_spec[at, :], True),
        k.outof, k.turn, k.behind, k.inner, chunk_storer(sizes, k.wide),
    )
    narrow(sizes, k.wide, k.sent_back)
    move4 = Exchange(place, k.sent_back, k.landed4, k.a4_send, k.a4_recv)
    move4.start()

    def store_taps(channel, values):
        k.tap_wide[pl.ds(channel, sizes.tap_rows, stride=channels), :] = values

    reduces["up0"].go_on(0)
    reduces["down0"].go_on(0)
    signal_from(
        sizes,
        lambda at: times(k.grad_spec[at, :], k.value_spec[at, :], True),
        k.taps_outof, k.turn, k.behind, k.inner, store_taps,
    )
    pooled = pooled_taps(k.taps[...])
    bent = jnp.tanh(pooled / THRESH)
    k.tap_grad[...] = pooled_taps(k.tap_wide[...].reshape(pooled.shape) * live * bent * bent)
    tap_back = PlaneExchange(
        place,
        lambda g: k.tap_grad.at[g],
        lambda g: k.grad_kernel.at[pl.ds(pl.multiple_of(g * channels, 8), channels)],
        k.t2_send,
        k.t2_recv,
    )
    tap_back.start()
    k.grad_kernel[pl.ds(pl.multiple_of(place.freq * channels, 8), channels)] = k.tap_grad[place.freq]
    reduces["up1"].go_on(0)
    reduces["down1"].go_on(0)
    reduces["out0"].go_on(0)
    reduces["gate0"].go_on(0)
    move4.wait()

    for col in range(sizes.cols):
        rows = from_chunk_columns(k.landed4, col).astype(BF16)
        for c in range(2):
            k.signal_rows[c, col * LANES : (col + 1) * LANES, :] = rows[:, c * half : (c + 1) * half]
    share_rows("signal_rows", 5)
    k.out_sum[...] = sum(
        dot_nt(rows[c], whole(weight, c))
        for rows, weight in ((k.signal_rows, k.w_value), (k.gate_rows, k.w_gate))
        for c in range(2)
    )
    twins["signal_rows"].wait()
    row_grads("value", "input1", "signal_rows")
    reduces["value0"].start(0)

    def first_back(at):
        grad = k.out_sum[at, :]
        normed = k.normed1[at, :]
        add_gain(0, jnp.sum(grad * normed, axis=0, keepdims=True))
        result = k.grad_res[at, :] + norm_back(grad, normed, k.scale1[at, :], first_gain)
        k.grad_res[at, :] = result
        k.gin_send[0, at, :] = result[:, :half].astype(BF16)
        k.gin_send[1, at, :] = result[:, half:].astype(BF16)

    row_tiles(here, first_back)
    swap_gin = remote(
        k.gin_send.at[1 - chan], k.gin_land, k.swap_send.at[4], k.swap_recv.at[4], across
    )
    swap_gin.start()
    spread = Spread(place, k.gain_total, k.gain_land, plan.spread_phases, k.gain_send, k.gain_recv)
    spread.start(0)
    k.grad_input[chan] = jnp.where(chan == 0, k.grad_res[:, :half], k.grad_res[:, half:])
    for name in ("up0", "down0", "up1", "down1", "out0", "gate0"):
        reduces[name].go_on(1)
    spread.go_on(0)
    reduces["value0"].go_on(0)
    spread.go_on(1)
    for name in ("up0", "down0", "up1", "down1", "out0", "gate0"):
        reduces[name].go_on(2)
    spread.go_on(2)
    k.gain_sums[...] = k.gain_total[len(plan.spread_phases)]
    tap_back.wait()
    swap_out.wait()
    swap_gin.wait()
    k.grad_input[1 - chan] = k.gin_land[...].astype(F32)
    reduces["value0"].go_on(1)


def copy_kernel(count, *refs):
    sources, targets, sems = refs[:count], refs[count : 2 * count], refs[-1]
    copies = [pltpu.make_async_copy(sources[n], targets[n], sems.at[n]) for n in range(count)]
    for copy in copies:
        copy.start()
    for copy in copies:
        copy.wait()


def settle(arrays):
    return pl.pallas_call(
        functools.partial(copy_kernel, len(arrays)),
        out_shape=[jax.ShapeDtypeStruct(a.shape, a.dtype) for a in arrays],
        in_specs=[ANY_SPEC] * len(arrays),
        out_specs=[ANY_SPEC] * len(arrays),
        scratch_shapes=[pltpu.SemaphoreType.DMA((len(arrays),))],
        name="settle",
    )(*arrays)


def one_sequence(
    tokens, cotangent, first_gain, second_gain, w_value, w_gate, w_out, w_up, w_down, raw_kernel, lengths
):
    freq_count = lax.axis_size("freq")
    _, here, half = tokens.shape
    sizes = Sizes(freq_count, here, half, raw_kernel.shape[1] * freq_count)
    plan = Plan(sizes, w_up.shape[1])
    pack = jnp.concatenate(
        [jnp.stack([first_gain, second_gain, lengths.astype(F32)]), jnp.zeros((5, half), F32)]
    )
    shards = (w_value, w_gate, w_out, w_up, w_down)
    tables = conv_tables(sizes)
    out_shape = (
        [jax.ShapeDtypeStruct((2, here, half), BF16), jax.ShapeDtypeStruct((2, here, half), F32)]
        + [jax.ShapeDtypeStruct(w.shape, F32) for w in shards]
        + [
            jax.ShapeDtypeStruct((4 * half // LANES + 4, LANES), F32),
            jax.ShapeDtypeStruct(raw_kernel.shape, F32),
        ]
    )
    results = pl.pallas_call(
        functools.partial(block_kernel, plan),
        out_shape=out_shape,
        in_specs=[ANY_SPEC] * 9 + [VMEM_SPEC] * len(tables),
        out_specs=[VMEM_SPEC] * len(out_shape),
        scratch_shapes=plan.scratch,
        compiler_params=pltpu.CompilerParams(
            collective_id=0, has_side_effects=True, vmem_limit_bytes=63 << 20
        ),
        name="block",
    )(tokens, cotangent, pack, raw_kernel, *shards, *tables)
    *arrays, gain_sums, grad_kernel = results
    arrays = settle([*arrays, grad_kernel])
    sums = gain_sums.reshape(-1)[: 4 * half].reshape(2, 2 * half)
    start = lax.axis_index("chan") * half + lax.axis_index("freq") * sizes.channels
    sums = lax.dynamic_slice_in_dim(sums, start, sizes.channels, axis=1)
    return (*arrays[:-1], sums[0][:, None], sums[1][:, None], arrays[-1])


def fits(mesh):
    freq_count = mesh.shape["freq"]
    return lambda tokens, w_value, raw_kernel: (
        mesh.shape["chan"] == 2
        and tokens.shape[0] == 2
        and freq_count >= 8
        and freq_count & (freq_count - 1) == 0
        and w_value.shape[0] % (16 * freq_count) == 0
        and w_value.shape[1] % (16 * freq_count) == 0
        and w_value.shape[1] % 256 == 0
        and tokens.shape[1] % (LANES * freq_count) == 0
        and raw_kernel.shape[1] == LANES * freq_count
        and (tokens.shape[1] + raw_kernel.shape[1]) // LANES % 16 == 0
    )


D = 768
SEQ_MB = 1
MICRO = 2


HIGHEST = lax.Precision.HIGHEST


def circle(height, breadth, period):
    first_index = lax.broadcasted_iota(jnp.int32, (height, breadth), 0)
    second_index = lax.broadcasted_iota(jnp.int32, (height, breadth), 1)
    phase_angle = (first_index * second_index % period).astype(jnp.float32) * (
        2.0 * math.pi / period
    )
    return (jnp.cos(phase_angle), jnp.sin(phase_angle))


def make_tables(padded_size):
    inner_size = 128
    outer_size = padded_size // inner_size
    outer_cos, outer_sin = circle(outer_size, outer_size, outer_size)
    inner_cos, inner_sin = circle(inner_size, inner_size, inner_size)
    twist_cos, twist_sin = circle(outer_size, inner_size, padded_size)
    return (outer_cos, outer_sin, inner_cos, inner_sin, twist_cos, twist_sin)


def spectrum(signal, padded_size, tables):
    outer_cos, outer_sin, inner_cos, inner_sin, twist_cos, twist_sin = tables
    inner_size = inner_cos.shape[0]
    pad_width = [(0, 0)] * (signal.ndim - 1) + [(0, padded_size - signal.shape[-1])]
    grid_values = jnp.pad(signal, pad_width).reshape(
        signal.shape[:-1] + (padded_size // inner_size, inner_size)
    )
    part_real = jnp.einsum("...ab,fa->...fb", grid_values, outer_cos, precision=HIGHEST)
    part_imag = -jnp.einsum("...ab,fa->...fb", grid_values, outer_sin, precision=HIGHEST)
    turned_real = part_real * twist_cos + part_imag * twist_sin
    turned_imag = part_imag * twist_cos - part_real * twist_sin
    spec_real = jnp.einsum(
        "...fb,bg->...fg", turned_real, inner_cos, precision=HIGHEST
    ) + jnp.einsum("...fb,bg->...fg", turned_imag, inner_sin, precision=HIGHEST)
    spec_imag = jnp.einsum(
        "...fb,bg->...fg", turned_imag, inner_cos, precision=HIGHEST
    ) - jnp.einsum("...fb,bg->...fg", turned_real, inner_sin, precision=HIGHEST)
    return (spec_real, spec_imag)


def signal_of(spec_real, spec_imag, keep_count, tables):
    outer_cos, outer_sin, inner_cos, inner_sin, twist_cos, twist_sin = tables
    padded_size = spec_real.shape[-1] * spec_real.shape[-2]
    back_real = jnp.einsum("...fg,bg->...fb", spec_real, inner_cos, precision=HIGHEST) - jnp.einsum(
        "...fg,bg->...fb", spec_imag, inner_sin, precision=HIGHEST
    )
    back_imag = jnp.einsum("...fg,bg->...fb", spec_imag, inner_cos, precision=HIGHEST) + jnp.einsum(
        "...fg,bg->...fb", spec_real, inner_sin, precision=HIGHEST
    )
    turned_real = back_real * twist_cos - back_imag * twist_sin
    turned_imag = back_imag * twist_cos + back_real * twist_sin
    grid_values = (
        jnp.einsum("...fb,af->...ab", turned_real, outer_cos, precision=HIGHEST)
        - jnp.einsum("...fb,af->...ab", turned_imag, outer_sin, precision=HIGHEST)
    ) / padded_size
    flat_values = grid_values.reshape(grid_values.shape[:-2] + (padded_size,))
    return flat_values[..., :keep_count]


def shape_kernel(raw_taps, live_taps):
    padded = jnp.pad(raw_taps, ((0, 0), (1, 1)))
    pooled = (padded[:, :-2] + padded[:, 1:-1] + padded[:, 2:]) / 3.0
    return (pooled - THRESH * jnp.tanh(pooled / THRESH)) * live_taps


def row_norm(values):
    row_width = values.shape[-1] * lax.axis_size("chan")
    row_total, row_square = lax.psum(
        (jnp.sum(values, axis=-1), jnp.sum(values * values, axis=-1)), "chan"
    )
    center = row_total / row_width
    spread = row_square / row_width - center * center
    scale = lax.rsqrt(spread + EPSILON)[..., None]
    return ((values - center[..., None]) * scale, scale)


def row_back(grad_rows, normed, scale, gain_row):
    row_width = grad_rows.shape[-1] * lax.axis_size("chan")
    scaled = grad_rows * gain_row
    sum_plain, sum_cross = lax.psum(
        (jnp.sum(scaled, axis=-1), jnp.sum(scaled * normed, axis=-1)), "chan"
    )
    return scale * (
        scaled - sum_plain[..., None] / row_width - normed * sum_cross[..., None] / row_width
    )


def features(values):
    return lax.all_gather(values, "chan", axis=2, tiled=True)


def partial_sum(values):
    return lax.psum_scatter(
        values.astype(jnp.bfloat16), "chan", scatter_dimension=2, tiled=True
    ).astype(jnp.float32)


def to_channels(values):
    return lax.all_to_all(
        jnp.swapaxes(values, 1, 2), "freq", split_axis=1, concat_axis=2, tiled=True
    )


def to_tokens(values):
    arrived = lax.all_to_all(values, "freq", split_axis=2, concat_axis=1, tiled=True)
    return jnp.swapaxes(arrived, 1, 2)


def by_features(
    tokens,
    cotangent,
    first_gain,
    second_gain,
    w_value,
    w_gate,
    w_out,
    w_up,
    w_down,
    raw_kernel,
    lengths,
):
    full_value, full_gate, full_out, full_up, full_down = (
        lax.all_gather(w_value, "freq", axis=0, tiled=True),
        lax.all_gather(w_gate, "freq", axis=0, tiled=True),
        lax.all_gather(w_out, "freq", axis=0, tiled=True),
        lax.all_gather(w_up, "freq", axis=0, tiled=True),
        lax.all_gather(w_down, "freq", axis=0, tiled=True),
    )
    freq_count = lax.axis_size("freq")
    chan_width = tokens.shape[2]
    channels = chan_width // freq_count
    seq_length = tokens.shape[1] * freq_count
    padded_size = 2 * seq_length
    tables = make_tables(padded_size)
    kernel_rows = lax.all_to_all(raw_kernel, "freq", split_axis=0, concat_axis=1, tiled=True)
    tap_count = kernel_rows.shape[1]
    my_lengths = lax.dynamic_slice_in_dim(lengths, lax.axis_index("freq") * channels, channels)
    tap_index = lax.broadcasted_iota(jnp.int32, (channels, tap_count), 1)
    live_taps = (tap_index < my_lengths[:, None]).astype(jnp.float32)
    kernel, kernel_pull = jax.vjp(functools.partial(shape_kernel, live_taps=live_taps), kernel_rows)
    kernel_real, kernel_imag = spectrum(kernel, padded_size, tables)
    hidden_width = full_up.shape[1]
    shard_factor = 1
    totals = (
        jnp.zeros((D // shard_factor, chan_width), jnp.float32),
        jnp.zeros((D // shard_factor, chan_width), jnp.float32),
        jnp.zeros((D // shard_factor, chan_width), jnp.float32),
        jnp.zeros((D // shard_factor, hidden_width), jnp.float32),
        jnp.zeros((D // shard_factor, hidden_width), jnp.float32),
        jnp.zeros((chan_width // shard_factor, 1), jnp.float32),
        jnp.zeros((chan_width // shard_factor, 1), jnp.float32),
    )
    kernel_grad = jnp.zeros((channels, tap_count), jnp.float32)
    outputs = []
    input_grads = []
    for micro_index in range(MICRO):
        rows_here = tokens[micro_index * SEQ_MB : (micro_index + 1) * SEQ_MB].astype(jnp.float32)
        first_normed, first_scale = row_norm(rows_here)
        input1 = features((first_normed * first_gain).astype(jnp.bfloat16))
        value_low = jnp.einsum(
            "bld,de->ble", input1, full_value, preferred_element_type=jnp.float32
        ).astype(jnp.bfloat16)
        gate_proj = jnp.einsum("bld,de->ble", input1, full_gate, preferred_element_type=jnp.float32)
        signal = to_channels(value_low).astype(jnp.float32)
        signal_real, signal_imag = spectrum(signal, padded_size, tables)
        mixed = signal_of(
            signal_real * kernel_real - signal_imag * kernel_imag,
            signal_real * kernel_imag + signal_imag * kernel_real,
            seq_length,
            tables,
        )
        mixed_rows = to_tokens(mixed.astype(jnp.bfloat16)).astype(jnp.float32)
        gate_act, gate_pull = jax.vjp(jax.nn.silu, gate_proj)
        inner_low = (mixed_rows * gate_act).astype(jnp.bfloat16)
        residual = rows_here + partial_sum(
            jnp.einsum("ble,oe->blo", inner_low, full_out, preferred_element_type=jnp.float32)
        )
        second_normed, second_scale = row_norm(residual)
        input2 = features((second_normed * second_gain).astype(jnp.bfloat16))
        hidden = jnp.einsum("bld,df->blf", input2, full_up, preferred_element_type=jnp.float32)
        activated, act_pull = jax.vjp(jax.nn.gelu, hidden)
        act_low = activated.astype(jnp.bfloat16)
        result = residual + partial_sum(
            jnp.einsum("blf,of->blo", act_low, full_down, preferred_element_type=jnp.float32)
        )
        outputs.append(result.astype(jnp.bfloat16))
        grad_rows_out = cotangent[micro_index * SEQ_MB : (micro_index + 1) * SEQ_MB]
        grad_full = features(grad_rows_out)
        grad_act = jnp.einsum(
            "blo,of->blf", grad_full, full_down, preferred_element_type=jnp.float32
        )
        down_grad = jnp.einsum(
            "blo,blf->of", grad_full, act_low, preferred_element_type=jnp.float32
        )
        grad_hidden = act_pull(grad_act)[0].astype(jnp.bfloat16)
        up_grad = jnp.einsum("bld,blf->df", input2, grad_hidden, preferred_element_type=jnp.float32)
        grad_in2 = partial_sum(
            jnp.einsum("blf,df->bld", grad_hidden, full_up, preferred_element_type=jnp.float32)
        )
        second_grad = jnp.sum(grad_in2 * second_normed, axis=(0, 1))
        grad_residual = grad_rows_out.astype(jnp.float32) + row_back(
            grad_in2, second_normed, second_scale, second_gain
        )
        grad_branch = features(grad_residual.astype(jnp.bfloat16))
        grad_inner = jnp.einsum(
            "blo,oe->ble", grad_branch, full_out, preferred_element_type=jnp.float32
        )
        out_grad = jnp.einsum(
            "blo,ble->oe", grad_branch, inner_low, preferred_element_type=jnp.float32
        )
        grad_mixed = to_channels((grad_inner * gate_act).astype(jnp.bfloat16)).astype(jnp.float32)
        grad_real, grad_imag = spectrum(grad_mixed, padded_size, tables)
        grad_signal = signal_of(
            grad_real * kernel_real + grad_imag * kernel_imag,
            grad_imag * kernel_real - grad_real * kernel_imag,
            seq_length,
            tables,
        )
        kernel_grad = kernel_grad + jnp.sum(
            signal_of(
                grad_real * signal_real + grad_imag * signal_imag,
                grad_imag * signal_real - grad_real * signal_imag,
                tap_count,
                tables,
            ),
            axis=0,
        )
        grad_signal_rows = to_tokens(grad_signal.astype(jnp.bfloat16))
        grad_gate_rows = gate_pull(grad_inner * mixed_rows)[0].astype(jnp.bfloat16)
        value_grad = jnp.einsum(
            "bld,ble->de", input1, grad_signal_rows, preferred_element_type=jnp.float32
        )
        gate_grad = jnp.einsum(
            "bld,ble->de", input1, grad_gate_rows, preferred_element_type=jnp.float32
        )
        grad_in1 = partial_sum(
            jnp.einsum(
                "ble,de->bld", grad_signal_rows, full_value, preferred_element_type=jnp.float32
            )
            + jnp.einsum(
                "ble,de->bld", grad_gate_rows, full_gate, preferred_element_type=jnp.float32
            )
        )
        first_grad = jnp.sum(grad_in1 * first_normed, axis=(0, 1))
        input_grads.append(
            grad_residual + row_back(grad_in1, first_normed, first_scale, first_gain)
        )
        local_terms = (
            value_grad,
            gate_grad,
            out_grad,
            up_grad,
            down_grad,
            first_grad[:, None],
            second_grad[:, None],
        )
        totals = tuple((left + right for left, right in zip(totals, local_terms)))
    totals = lax.psum_scatter(totals, "freq", scatter_dimension=0, tiled=True)
    raw_grad = kernel_pull(kernel_grad)[0]
    grad_kernel = lax.all_to_all(raw_grad, "freq", split_axis=1, concat_axis=0, tiled=True)
    output = jnp.concatenate(outputs, axis=0)
    grad_input = jnp.concatenate(input_grads, axis=0)
    return (
        output,
        grad_input,
        totals[0],
        totals[1],
        totals[2],
        totals[3],
        totals[4],
        totals[5],
        totals[6],
        grad_kernel,
    )


def solution(mesh):
    specs = dict(
        mesh=mesh,
        in_specs=(
            P(None, "freq", "chan"),
            P(None, "freq", "chan"),
            P("chan"),
            P("chan"),
            P("freq", "chan"),
            P("freq", "chan"),
            P("freq", "chan"),
            P("freq", "chan"),
            P("freq", "chan"),
            P("chan", "freq"),
            P("chan"),
        ),
        out_specs=(
            P(None, "freq", "chan"),
            P(None, "freq", "chan"),
            P("freq", "chan"),
            P("freq", "chan"),
            P("freq", "chan"),
            P("freq", "chan"),
            P("freq", "chan"),
            P("freq", "chan"),
            P("freq", "chan"),
            P("chan", "freq"),
        ),
        check_vma=False,
    )

    def step(*args):
        whole = fits(mesh)(args[0], args[4], args[9])
        return jax.shard_map(one_sequence if whole else by_features, **specs)(*args)

    return step
```

```python
import functools
import math

import jax
import jax.numpy as jnp
import numpy as np
from jax import lax
from jax.experimental import pallas as pl
from jax.experimental.pallas import tpu as pltpu
from jax.sharding import PartitionSpec as P

THRESH = 0.003
EPSILON = 1e-05
LANES = 128
MESH = pl.DeviceIdType.MESH
F32 = jnp.float32
BF16 = jnp.bfloat16


def bit_sizes(freq_count):
    return [1 << i for i in reversed(range(freq_count.bit_length() - 1))]


class Place:
    def __init__(self, freq_count):
        self.freq_count = freq_count
        self.freq = lax.axis_index("freq")
        self.chan = lax.axis_index("chan")
        self.bits = bit_sizes(freq_count)
        self.coords = [self.chan] + [lax.rem(self.freq // b, 2) for b in self.bits]
        self.dims = len(self.coords)
        self.core = self.coords[-1]

    def other(self, flipped):
        freq, chan = self.freq, self.chan
        for dim in flipped:
            if dim == 0:
                chan = 1 - chan
            else:
                bit = self.bits[dim - 1]
                freq = freq + bit - 2 * bit * self.coords[dim]
        return (freq, chan)


def flips(dims):
    return [
        tuple(dim for at, dim in enumerate(dims) if mask >> at & 1) for mask in range(1, 1 << len(dims))
    ]


def remote(source, target, send, recv, device):
    return pltpu.make_async_remote_copy(
        src_ref=source,
        dst_ref=target,
        send_sem=send,
        recv_sem=recv,
        device_id=device,
        device_id_type=MESH,
    )


def greet_all(place):
    barrier = pltpu.get_barrier_semaphore()
    count = 2 * place.freq_count
    me = place.chan * place.freq_count + place.freq

    def one(step, carry):
        other = lax.rem(me + step, count)
        pl.semaphore_signal(
            barrier,
            inc=1,
            device_id=(lax.rem(other, place.freq_count), other // place.freq_count),
            device_id_type=MESH,
        )
        return carry

    lax.fori_loop(1, count, one, 0)
    pl.semaphore_wait(barrier, count - 1)


class Gather:
    def __init__(self, place, buffer, phases, send, recv, columns=None):
        self.place, self.buffer, self.phases, self.send, self.recv = place, buffer, phases, send, recv
        self.columns = (slice(None), slice(None)) if columns is None else (slice(None), columns)

    def copies(self, phase):
        done = [dim for dims in self.phases[:phase] for dim in dims]
        index = tuple(
            slice(None) if dim in done else coord for dim, coord in enumerate(self.place.coords)
        )
        region = self.buffer.at[index + self.columns]
        base = sum(len(flips(dims)) for dims in self.phases[:phase])
        return [
            remote(region, region, self.send.at[base + k], self.recv.at[base + k], self.place.other(flipped))
            for k, flipped in enumerate(flips(self.phases[phase]))
        ]

    def start(self, phase):
        for copy in self.copies(phase):
            copy.start()

    def wait(self, phase):
        for copy in self.copies(phase):
            copy.wait()

    def go_on(self, phase):
        self.wait(phase)
        if phase + 1 < len(self.phases):
            self.start(phase + 1)


class Reduce:
    def __init__(self, place, total, landing, phases, send, recv, out, columns=None):
        self.place, self.total, self.landing, self.phases = place, total, landing, phases
        self.send, self.recv, self.out = send, recv, out
        self.coords = place.coords[:-1]
        self.columns = (slice(None), slice(None)) if columns is None else (slice(None), columns)

    def region(self, phase, flipped):
        fixed = [dim for dims in self.phases[: phase + 1] for dim in dims]
        return tuple(
            (1 - coord if dim in flipped else coord) if dim in fixed else slice(None)
            for dim, coord in enumerate(self.coords)
        )

    def copies(self, phase):
        base = sum(len(flips(dims)) for dims in self.phases[:phase])
        return [
            remote(
                self.total.at[self.region(phase, flipped) + self.columns],
                self.landing[phase].at[k],
                self.send.at[base + k],
                self.recv.at[base + k],
                self.place.other(flipped),
            )
            for k, flipped in enumerate(flips(self.phases[phase]))
        ]

    def start(self, phase):
        for copy in self.copies(phase):
            copy.start()

    def finish(self, phase):
        for copy in self.copies(phase):
            copy.wait()
        kept = self.region(phase, ())
        free = [dim for dim, at in enumerate(kept) if isinstance(at, slice)]
        landing = self.landing[phase]
        last = phase + 1 == len(self.phases)

        def one(turn, carry):
            where, there = list(kept), []
            for at, dim in enumerate(free):
                bit = lax.rem(turn // (1 << (len(free) - 1 - at)), 2)
                where[dim] = bit
                there.append(bit)
            where = tuple(where) + self.columns
            total = self.total[where].astype(F32)
            for k in range(len(flips(self.phases[phase]))):
                total = total + landing[(k,) + tuple(there)].astype(F32)
            if last:
                self.out[self.columns] = total
            else:
                self.total[where] = total.astype(BF16)
            return carry

        if free:
            lax.fori_loop(0, 1 << len(free), one, 0)
        else:
            one(0, 0)

    def go_on(self, phase):
        self.finish(phase)
        if phase + 1 < len(self.phases):
            self.start(phase + 1)


def landing_shapes(phases, dims, rows, columns):
    shapes, free = [], dims - 1
    for group in phases:
        free -= len(group)
        shapes.append((len(flips(group)),) + (2,) * free + (rows, columns))
    return shapes


class Spread:
    def __init__(self, place, total, landing, phases, send, recv):
        self.place, self.total, self.landing, self.phases = place, total, landing, phases
        self.send, self.recv = send, recv

    def copies(self, phase):
        base = sum(len(flips(dims)) for dims in self.phases[:phase])
        return [
            remote(
                self.total.at[phase],
                self.landing.at[base + k],
                self.send.at[base + k],
                self.recv.at[base + k],
                self.place.other(flipped),
            )
            for k, flipped in enumerate(flips(self.phases[phase]))
        ]

    def start(self, phase):
        for copy in self.copies(phase):
            copy.start()

    def go_on(self, phase):
        copies = self.copies(phase)
        base = sum(len(flips(dims)) for dims in self.phases[:phase])
        for copy in copies:
            copy.wait()
        total = self.total[phase]
        for k in range(len(copies)):
            total = total + self.landing[base + k]
        self.total[phase + 1] = total
        if phase + 1 < len(self.phases):
            self.start(phase + 1)


class Sizes:
    def __init__(self, freq_count, here, half, taps):
        self.freq_count = freq_count
        self.here = here
        self.cols = here // LANES
        self.channels = half // freq_count
        self.chunk = self.cols * self.channels
        self.devices = 2 * freq_count
        self.tap_rows = taps // LANES
        self.rows = here * freq_count // LANES + self.tap_rows
        self.size = self.rows * LANES


def conv_tables(sizes):
    rows, size = sizes.rows, sizes.size
    f = np.arange(rows)
    fi = np.arange(sizes.freq_count)
    a_of, imag = [], []
    for col in range(sizes.cols):
        for seq in range(2):
            for block in fi:
                a_of.append(block * sizes.cols + col)
                imag.append(seq)
    a_of, imag = np.array(a_of), np.array(imag)
    angle = 2 * np.pi * np.outer(f, a_of) / rows
    cos, sin = np.cos(angle), np.sin(angle)
    into = np.concatenate([np.where(imag, sin, cos), np.where(imag, cos, -sin)], axis=0)
    outof = np.concatenate([np.where(imag, sin, cos), np.where(imag, cos, -sin)], axis=0).T / size
    taps = np.arange(sizes.tap_rows)
    angle = 2 * np.pi * np.outer(f, taps) / rows
    taps_into = np.concatenate([np.cos(angle), -np.sin(angle)], axis=0)
    taps_outof = taps_into.T / size
    b = np.arange(LANES)
    angle = 2 * np.pi * np.outer(f, b) / size
    turn = np.stack([np.cos(angle), np.sin(angle)])
    angle = 2 * np.pi * np.outer(b, b) / LANES
    cos, sin = np.cos(angle), np.sin(angle)
    ahead = np.block([[cos, -sin], [sin, cos]])
    return (
        jnp.asarray(into, BF16),
        jnp.asarray(outof, BF16),
        jnp.asarray(taps_into, BF16),
        jnp.asarray(taps_outof, BF16),
        jnp.asarray(turn, F32),
        jnp.asarray(ahead, BF16),
        jnp.asarray(ahead.T, BF16),
    )


def dot(left, right):
    return jnp.dot(left, right, preferred_element_type=F32)


def spectrum_into(sizes, load, into, turn, ahead, inner, spectrum):
    rows = sizes.rows

    def one(pair, carry):
        both = jnp.concatenate([load(2 * pair), load(2 * pair + 1)], axis=1).astype(BF16)
        part = dot(into[...], both)
        for side in range(2):
            real = part[:rows, side * LANES : (side + 1) * LANES]
            imag = part[rows:, side * LANES : (side + 1) * LANES]
            turned = jnp.concatenate(
                [real * turn[0] + imag * turn[1], imag * turn[0] - real * turn[1]], axis=1
            )
            start = pl.multiple_of((2 * pair + side) * rows, 16)
            inner[pl.ds(start, rows), :] = turned.astype(BF16)
        return carry

    lax.fori_loop(0, sizes.channels // 2, one, 0)
    tile = sizes.channels * rows // 4

    def two(step, carry):
        at = pl.ds(pl.multiple_of(step * tile, 16), tile)
        spectrum[at, :] = dot(inner[at, :], ahead[...])
        return carry

    lax.fori_loop(0, 4, two, 0)


def signal_from(sizes, product, outof, turn, behind, inner, store):
    rows = sizes.rows
    tile = sizes.channels * rows // 4

    def one(step, carry):
        at = pl.ds(pl.multiple_of(step * tile, 16), tile)
        inner[at, :] = dot(product(at), behind[...]).astype(BF16)
        return carry

    lax.fori_loop(0, 4, one, 0)

    def two(pair, carry):
        sides = []
        for side in range(2):
            start = pl.multiple_of((2 * pair + side) * rows, 16)
            back = inner[pl.ds(start, rows), :].astype(F32)
            real, imag = back[:, :LANES], back[:, LANES:]
            sides.append(
                jnp.concatenate(
                    [real * turn[0] - imag * turn[1], imag * turn[0] + real * turn[1]], axis=0
                ).astype(BF16)
            )
        got = dot(outof[...], jnp.concatenate(sides, axis=1))
        for side in range(2):
            store(2 * pair + side, got[:, side * LANES : (side + 1) * LANES])
        return carry

    lax.fori_loop(0, sizes.channels // 2, two, 0)


def times(left, right, conj):
    a, b = left[:, :LANES], left[:, LANES:]
    c, d = right[:, :LANES], right[:, LANES:]
    if conj:
        return jnp.concatenate([a * c + b * d, b * c - a * d], axis=1).astype(BF16)
    return jnp.concatenate([a * c - b * d, a * d + b * c], axis=1).astype(BF16)


class Exchange:
    def __init__(self, place, source, target, send, recv):
        self.place, self.source, self.target = place, source, target
        self.send, self.recv = send, recv
        self.count = 2 * place.freq_count
        self.me = place.chan * place.freq_count + place.freq

    def each(self, action):
        freq_count = self.place.freq_count

        def one(step, carry):
            other = lax.rem(self.me + step, self.count)
            origin = lax.rem(self.me + self.count - step, self.count)
            action(step, other, origin, (lax.rem(other, freq_count), other // freq_count))
            return carry

        lax.fori_loop(1, self.count, one, 0)

    def start(self):
        def action(step, other, origin, device):
            pltpu.make_async_remote_copy(
                src_ref=self.source.at[other],
                dst_ref=self.target.at[self.me],
                send_sem=self.send.at[step],
                recv_sem=self.recv.at[step],
                device_id=device,
                device_id_type=MESH,
            ).start()

        self.each(action)
        self.target[self.me] = self.source[self.me]

    def wait(self):
        def action(step, other, origin, device):
            pltpu.make_async_remote_copy(
                src_ref=self.source.at[other],
                dst_ref=self.target.at[origin],
                send_sem=self.send.at[step],
                recv_sem=self.recv.at[step],
                device_id=device,
                device_id_type=MESH,
            ).wait()

        self.each(action)


class PlaneExchange:
    def __init__(self, place, source, target, send, recv):
        self.place, self.source, self.target = place, source, target
        self.send, self.recv = send, recv

    def each(self, action):
        count, me = self.place.freq_count, self.place.freq

        def one(step, carry):
            action(step, lax.rem(me + step, count), lax.rem(me + count - step, count))
            return carry

        lax.fori_loop(1, count, one, 0)

    def start(self):
        def action(step, other, origin):
            pltpu.make_async_remote_copy(
                src_ref=self.source(other),
                dst_ref=self.target(self.place.freq),
                send_sem=self.send.at[step],
                recv_sem=self.recv.at[step],
                device_id=(other, self.place.chan),
                device_id_type=MESH,
            ).start()

        self.each(action)

    def wait(self):
        def action(step, other, origin):
            pltpu.make_async_remote_copy(
                src_ref=self.source(other),
                dst_ref=self.target(origin),
                send_sem=self.send.at[step],
                recv_sem=self.recv.at[step],
                device_id=(other, self.place.chan),
                device_id_type=MESH,
            ).wait()

        self.each(action)


def to_chunks(sizes, rows):
    turned = rows.T.reshape(sizes.devices, sizes.channels, sizes.here)
    pieces = [turned[:, :, col * LANES : (col + 1) * LANES] for col in range(sizes.cols)]
    return jnp.concatenate(pieces, axis=1).astype(BF16)


def from_chunks(sizes, chunks):
    wide = chunks.astype(F32)
    pieces = [
        wide[:, col * sizes.channels : (col + 1) * sizes.channels, :].reshape(
            sizes.devices * sizes.channels, LANES
        )
        for col in range(sizes.cols)
    ]
    return jnp.concatenate(pieces, axis=1).T


def chunk_loader(sizes, ref):
    def load(channel):
        pieces = [
            ref[pl.ds(col * sizes.channels + channel, sizes.devices, stride=sizes.chunk), :]
            for col in range(sizes.cols)
        ]
        return jnp.concatenate(pieces, axis=0)

    return load


def chunk_storer(sizes, ref):
    def store(channel, values):
        for col in range(sizes.cols):
            ref[pl.ds(col * sizes.channels + channel, sizes.devices, stride=sizes.chunk), :] = values[
                col * sizes.devices : (col + 1) * sizes.devices
            ]

    return store


def widen(sizes, chunks, ref):
    def one(step, carry):
        ref[pl.ds(pl.multiple_of(step * sizes.chunk, 8), sizes.chunk), :] = chunks[step].astype(F32)
        return carry

    lax.fori_loop(0, sizes.devices, one, 0)


def narrow(sizes, ref, chunks):
    def one(step, carry):
        chunks[step] = ref[pl.ds(pl.multiple_of(step * sizes.chunk, 8), sizes.chunk), :].astype(BF16)
        return carry

    lax.fori_loop(0, sizes.devices, one, 0)


def pooled_taps(taps):
    lane = lax.broadcasted_iota(jnp.int32, taps.shape, 2)
    zero = jnp.zeros_like(taps[:1])
    after = pltpu.roll(taps, LANES - 1, 2)
    before = pltpu.roll(taps, 1, 2)
    after = jnp.where(lane == LANES - 1, jnp.concatenate([after[1:], zero], axis=0), after)
    before = jnp.where(lane == 0, jnp.concatenate([zero, before[:-1]], axis=0), before)
    return (before + taps + after) / 3.0


def live_mask(shape, lengths):
    tap = lax.broadcasted_iota(jnp.int32, shape, 0) * LANES + lax.broadcasted_iota(
        jnp.int32, shape, 2
    )
    return (tap < lengths[None]).astype(F32)


VMEM_SPEC = pl.BlockSpec(memory_space=pltpu.VMEM)
ANY_SPEC = pl.BlockSpec(memory_space=pl.ANY)
GELU_SCALE = math.sqrt(2.0 / math.pi)
GELU_CUBE = 0.044715


def dot_nt(left, right):
    return lax.dot_general(left, right, (((1,), (1,)), ((), ())), preferred_element_type=F32)


def norm(values):
    center = jnp.mean(values, axis=-1, keepdims=True)
    shifted = values - center
    scale = lax.rsqrt(jnp.mean(shifted * shifted, axis=-1, keepdims=True) + EPSILON)
    return shifted * scale, scale


def norm_back(grad_rows, normed, scale, gain):
    scaled = grad_rows * gain
    plain = jnp.mean(scaled, axis=-1, keepdims=True)
    cross = jnp.mean(scaled * normed, axis=-1, keepdims=True)
    return scale * (scaled - plain - normed * cross)


class Names:
    def __init__(self, names, refs):
        for name, ref in zip(names, refs, strict=True):
            setattr(self, name, ref)


class Plan:
    inputs = (
        "tokens", "cotangent", "pack", "raw_kernel",
        "s_value", "s_gate", "s_out", "s_up", "s_down",
        "into", "outof", "taps_into", "taps_outof", "turn", "ahead", "behind",
    )
    outputs = (
        "output", "grad_input", "r_value", "r_gate", "r_out", "r_up", "r_down", "gain_sums", "grad_kernel",
    )

    def __init__(self, sizes, ff_half):
        self.sizes = sizes
        here, channels, freq_count = sizes.here, sizes.channels, sizes.freq_count
        half = channels * freq_count
        width = 2 * half
        self.here, self.half, self.width, self.ff_half = here, half, width, ff_half
        dims = 1 + len(bit_sizes(freq_count))
        self.dims = dims
        self.rows = rows = width // freq_count
        self.lead = lead = (2,) * dims
        core, y, top = dims - 1, dims - 2, tuple(range(1, dims - 2))
        self.core_dim = core
        self.gather_phases = dict(
            value=(top, (0, y), (core,)),
            gate=(top, (0,), (y,), (core,)),
            out=(top, (y,), (0,), (core,)),
            up=(top, (0,), (y,), (core,)),
            down=(top, (y,), (0,), (core,)),
        )
        self.reduce_phases = dict(
            value=((0, y), top),
            gate=((0,), (y,), top),
            out=((y,), (0,), top),
            up=((0,), (y,), top),
            down=((y,), (0,), top),
        )
        self.spread_phases = ((core,), (0, y), top)
        self.pieces = 2
        self.piece = ff_half // self.pieces
        self.tile = half
        self.per_piece = self.piece // self.tile
        self.tiles = 2 * ff_half // self.tile
        names, shapes = [], []

        def add(name, shape, kind):
            names.append(name)
            shapes.append(pltpu.VMEM(shape, kind))

        def sems(name, *shape):
            names.append(name)
            shapes.append(pltpu.SemaphoreType.DMA(shape))

        for name in ("x_buf", "g_buf", "out_send", "gin_send"):
            add(name, (2, here, half), BF16)
        add("gin_land", (here, half), BF16)
        add("packs", (2, 8, half), F32)
        add("turned_pack", (half, 8), F32)
        self.weight_names = ("value", "gate", "out", "up", "down")
        columns = dict(value=half, gate=half, out=half, up=ff_half, down=ff_half)
        self.columns = columns
        for name in self.weight_names:
            add("w_" + name, lead + (rows, columns[name]), BF16)
            add("g_" + name, lead[:-1] + (rows, columns[name]), BF16)
            pieces = self.pieces if name in ("up", "down") else 1
            for piece in range(pieces):
                landing = landing_shapes(self.reduce_phases[name], dims, rows, columns[name] // pieces)
                for phase, shape in enumerate(landing):
                    add(f"l_{name}{piece}{phase}", shape, BF16)
                for what in ("gs", "gr", "rs", "rr"):
                    sems(f"{what}_{name}{piece}", 8)
        spec = (channels * sizes.rows, 2 * LANES)
        for name in ("kernel_spec", "value_spec", "grad_spec"):
            add(name, spec, F32)
        add("inner", spec, BF16)
        add("taps", (sizes.tap_rows, channels, LANES), F32)
        add("tap_grad", (sizes.tap_rows, channels, LANES), F32)
        add("tap_wide", (sizes.tap_rows * channels, LANES), F32)
        chunks = (sizes.devices, sizes.chunk, LANES)
        for name in ("sent", "sent_back", "landed1", "landed2", "landed3", "landed4"):
            add(name, chunks, BF16)
        add("wide", (sizes.devices * sizes.chunk, LANES), F32)
        for name in ("t1", "t2"):
            sems(name + "_send", freq_count)
            sems(name + "_recv", freq_count)
        for name in ("a1", "a2", "a3", "a4"):
            sems(name + "_send", sizes.devices)
            sems(name + "_recv", sizes.devices)
        for name in ("normed1", "gate", "mixed", "residual", "normed2", "out_sum", "in2_sum", "grad_res"):
            add(name, (here, width), F32)
        for name in ("scale1", "scale2"):
            add(name, (here, 1), F32)
        for name in ("input1", "input2", "grad_rows", "branch_rows"):
            add(name, (here, width), BF16)
        for name in ("input1", "input2", "grad_rows", "branch_rows"):
            add("t_" + name, (width // (2 * rows), 2, rows, here), BF16)
            add("twin_" + name, (width // (2 * rows), rows, here), BF16)
        for name in ("inner_rows", "signal_rows", "gate_rows"):
            add(name, (2, here, half), BF16)
            add("twin_" + name, (2, here, half), BF16)
        for name in ("act", "hid"):
            add(name, (self.tiles, here, self.tile), BF16)
            add("twin_" + name, (self.tiles, here, self.tile), BF16)
        for name in ("act", "hid"):
            sems(f"{name}_send", self.tiles)
            sems(f"{name}_recv", self.tiles)
        sems("twin_send", 7)
        sems("twin_recv", 7)
        add("gain_total", (len(self.spread_phases) + 1, 2 * width // LANES + 4, LANES), F32)
        add("gain_land", (1 + 3 + 3, 2 * width // LANES + 4, LANES), F32)
        sems("gain_send", 8)
        sems("gain_recv", 8)
        sems("swap_send", 5)
        sems("swap_recv", 5)
        sems("local", 10)
        sems("leave", len(self.outputs))
        add("v_output", (2, here, half), BF16)
        add("v_grad_input", (2, here, half), F32)
        for name in self.weight_names:
            add("v_r_" + name, (rows, columns[name]), F32)
        add("v_grad_kernel", (half, LANES), F32)
        self.names, self.scratch = names, shapes


def row_tiles(count, body, tile=64):
    def one(step, carry):
        body(pl.ds(pl.multiple_of(step * tile, tile), tile))
        return carry

    lax.fori_loop(0, count // tile, one, 0)


def block_kernel(plan, *refs):
    sizes = plan.sizes
    here, half, width, channels = plan.here, plan.half, plan.width, sizes.channels
    k = Names(plan.inputs + plan.outputs + tuple(plan.names), refs)
    place = Place(sizes.freq_count)
    chan, core = place.chan, place.core
    twin = place.other((plan.core_dim,))
    across = place.other((0,))

    def whole(ref, lead, columns=slice(None)):
        value = ref[(lead,) + (slice(None),) * plan.dims + (columns,)]
        return value.reshape(width, value.shape[-1])

    leaving = []

    def leave(name):
        source = getattr(k, "v_" + name) if name != "gain_sums" else k.gain_total.at[len(plan.spread_phases)]
        at = plan.outputs.index(name)
        leaving.append(pltpu.make_async_copy(source, getattr(k, name), k.leave.at[at]))
        leaving[-1].start()

    own = []
    for at, name in enumerate(plan.weight_names):
        buffer = getattr(k, "w_" + name).at[tuple(place.coords)]
        own.append(pltpu.make_async_copy(getattr(k, "s_" + name), buffer, k.local.at[at]))
    moves = (
        (k.tokens.at[chan], k.x_buf.at[chan]),
        (k.cotangent.at[chan], k.g_buf.at[chan]),
        (k.pack, k.packs.at[chan]),
        (k.raw_kernel.at[pl.ds(pl.multiple_of(place.freq * channels, 8), channels)], k.taps.at[place.freq]),
    )
    for at, (source, target) in enumerate(moves):
        own.append(pltpu.make_async_copy(source, target, k.local.at[5 + at]))
    for copy in own:
        copy.start()
    greet_all(place)
    swaps = [
        remote(source, target, k.swap_send.at[at], k.swap_recv.at[at], across)
        for at, (source, target) in enumerate(
            (
                (k.tokens.at[1 - chan], k.x_buf.at[chan]),
                (k.pack, k.packs.at[chan]),
                (k.cotangent.at[1 - chan], k.g_buf.at[chan]),
            )
        )
    ]
    swaps[0].start()
    swaps[1].start()
    gathers = {}
    for name in plan.weight_names:
        buffer = getattr(k, "w_" + name)
        pieces = plan.pieces if name in ("up", "down") else 1
        for piece in range(pieces):
            size = plan.columns[name] // pieces
            gathers[name + str(piece)] = Gather(
                place,
                buffer,
                plan.gather_phases[name],
                getattr(k, f"gs_{name}{piece}"),
                getattr(k, f"gr_{name}{piece}"),
                pl.ds(piece * size, size) if pieces > 1 else None,
            )
    own[0].wait()
    gathers["value0"].start(0)
    own[1].wait()
    gathers["gate0"].start(0)
    tap_move = PlaneExchange(
        place,
        lambda g: k.raw_kernel.at[pl.ds(pl.multiple_of(g * channels, 8), channels)],
        lambda g: k.taps.at[g],
        k.t1_send,
        k.t1_recv,
    )
    tap_move.start()
    own[2].wait()
    gathers["out0"].start(0)
    swaps[2].start()
    own[3].wait()
    own[4].wait()
    own[5].wait()
    own[7].wait()
    gathers["value0"].go_on(0)
    gathers["up0"].start(0)
    swaps[0].wait()
    swaps[1].wait()

    def gain_row(row):
        return jnp.concatenate([k.packs[0, row : row + 1, :], k.packs[1, row : row + 1, :]], axis=1)

    first_gain, second_gain = gain_row(0), gain_row(1)

    def first_norm(at):
        rows = jnp.concatenate([k.x_buf[0, at, :], k.x_buf[1, at, :]], axis=1).astype(F32)
        normed, scale = norm(rows)
        k.normed1[at, :] = normed
        k.scale1[at, :] = scale
        k.input1[at, :] = (normed * first_gain).astype(BF16)

    row_tiles(here, first_norm)
    gathers["gate0"].go_on(0)
    gathers["out0"].go_on(0)
    gathers["value0"].go_on(1)
    gathers["down0"].start(0)

    def turn_rows(name):
        turned = getattr(k, name)[...].astype(F32).T.astype(BF16)
        target = getattr(k, "t_" + name)
        target[...] = turned.reshape(target.shape)

    twins = {}

    def share_turned(name, at):
        turn_rows(name)
        twins[name] = remote(
            getattr(k, "t_" + name).at[:, 1 - core],
            getattr(k, "twin_" + name),
            k.twin_send.at[at],
            k.twin_recv.at[at],
            twin,
        )
        twins[name].start()

    def share_rows(name, at):
        twins[name] = remote(
            getattr(k, name), getattr(k, "twin_" + name), k.twin_send.at[at], k.twin_recv.at[at], twin
        )
        twins[name].start()

    share_turned("input1", 0)
    gathers["value0"].go_on(2)

    value = jnp.concatenate(
        [dot(k.input1[...], whole(k.w_value, 0)), dot(k.input1[...], whole(k.w_value, 1))], axis=1
    )
    k.sent[...] = to_chunks(sizes, value)
    move1 = Exchange(place, k.sent, k.landed1, k.a1_send, k.a1_recv)
    move1.start()
    gathers["gate0"].go_on(1)
    gathers["out0"].go_on(1)
    gathers["up0"].go_on(0)
    gathers["up1"].start(0)
    tap_move.wait()
    own[8].wait()
    k.turned_pack[...] = k.packs[chan].T
    lengths = k.turned_pack[pl.ds(pl.multiple_of(place.freq * channels, 8), channels), 2:3]
    live = live_mask(k.taps.shape, lengths)
    pooled = pooled_taps(k.taps[...])
    shrunk = (pooled - THRESH * jnp.tanh(pooled / THRESH)) * live
    k.tap_wide[...] = shrunk.reshape(sizes.tap_rows * channels, LANES)
    spectrum_into(
        sizes,
        lambda c: k.tap_wide[pl.ds(c, sizes.tap_rows, stride=channels), :],
        k.taps_into, k.turn, k.ahead, k.inner, k.kernel_spec,
    )
    swaps[2].wait()
    own[6].wait()
    k.grad_rows[...] = jnp.concatenate([k.g_buf[0], k.g_buf[1]], axis=1)
    share_turned("grad_rows", 2)
    gathers["gate0"].go_on(2)
    gathers["out0"].go_on(2)
    gathers["up0"].go_on(1)
    gathers["gate0"].go_on(3)
    for c in range(2):
        k.gate[:, c * half : (c + 1) * half] = dot(k.input1[...], whole(k.w_gate, c))
    move1.wait()

    widen(sizes, k.landed1, k.wide)
    spectrum_into(sizes, chunk_loader(sizes, k.wide), k.into, k.turn, k.ahead, k.inner, k.value_spec)
    signal_from(
        sizes,
        lambda at: times(k.value_spec[at, :], k.kernel_spec[at, :], False),
        k.outof, k.turn, k.behind, k.inner, chunk_storer(sizes, k.wide),
    )
    narrow(sizes, k.wide, k.sent_back)
    move2 = Exchange(place, k.sent_back, k.landed2, k.a2_send, k.a2_recv)
    move2.start()
    gathers["down0"].go_on(0)
    gathers["down1"].start(0)
    gathers["up1"].go_on(0)
    gathers["up0"].go_on(2)
    gathers["out0"].go_on(3)
    gathers["down0"].go_on(1)
    gathers["up1"].go_on(1)
    gathers["up0"].go_on(3)
    move2.wait()

    def from_chunk_columns(chunks, col):
        wide = chunks[:, col * channels : (col + 1) * channels, :].astype(F32)
        return wide.reshape(width, LANES).T

    for col in range(sizes.cols):
        k.mixed[col * LANES : (col + 1) * LANES, :] = from_chunk_columns(k.landed2, col)

    def make_inner(at):
        gate = k.gate[at, :]
        inner = (k.mixed[at, :] * (gate * jax.nn.sigmoid(gate))).astype(BF16)
        k.inner_rows[0, at, :] = inner[:, :half]
        k.inner_rows[1, at, :] = inner[:, half:]

    row_tiles(here, make_inner)
    share_rows("inner_rows", 4)
    k.residual[...] = dot_nt(k.inner_rows[0], whole(k.w_out, 0)) + dot_nt(
        k.inner_rows[1], whole(k.w_out, 1)
    )

    def second_norm(at):
        rows = jnp.concatenate([k.x_buf[0, at, :], k.x_buf[1, at, :]], axis=1).astype(F32)
        residual = k.residual[at, :] + rows
        normed, scale = norm(residual)
        k.residual[at, :] = residual
        k.normed2[at, :] = normed
        k.scale2[at, :] = scale
        k.input2[at, :] = (normed * second_gain).astype(BF16)

    row_tiles(here, second_norm)
    share_turned("input2", 1)
    gathers["down1"].go_on(0)
    gathers["down0"].go_on(2)
    gathers["up1"].go_on(2)
    gathers["down1"].go_on(1)
    gathers["down0"].go_on(3)
    gathers["up1"].go_on(3)
    gathers["down1"].go_on(2)
    gathers["down1"].go_on(3)

    k.out_sum[...] = jnp.zeros_like(k.out_sum)
    k.in2_sum[...] = jnp.zeros_like(k.in2_sum)
    per_half = plan.tiles // 2

    def twin_copy(name, tile):
        return remote(
            getattr(k, name).at[tile],
            getattr(k, "twin_" + name).at[tile],
            getattr(k, name + "_send").at[tile],
            getattr(k, name + "_recv").at[tile],
            twin,
        )

    def feed_forward(tile, carry):
        columns = pl.ds(pl.multiple_of(lax.rem(tile, per_half) * plan.tile, LANES), plan.tile)
        up = whole(k.w_up, tile // per_half, columns)
        hidden = dot(k.input2[...], up)
        square = hidden * hidden
        bent = jnp.tanh(GELU_SCALE * hidden * (1.0 + GELU_CUBE * square))
        act = (0.5 * hidden * (1.0 + bent)).astype(BF16)
        slope = 0.5 * (1.0 + bent) + (0.5 * GELU_SCALE) * hidden * (1.0 - bent * bent) * (
            1.0 + 3.0 * GELU_CUBE * square
        )
        down = whole(k.w_down, tile // per_half, columns)
        grad = (dot(k.grad_rows[...], down) * slope).astype(BF16)
        k.act[tile] = act
        k.hid[tile] = grad
        twin_copy("act", tile).start()
        twin_copy("hid", tile).start()
        k.in2_sum[...] += dot_nt(grad, up)
        k.out_sum[...] += dot_nt(act, down)
        return carry

    lax.fori_loop(0, plan.tiles, feed_forward, 0)

    gain_rows = 2 * width // LANES
    k.gain_total[0] = jnp.zeros_like(k.gain_total[0])

    def add_gain(row, sums):
        for at in range(width // LANES):
            base = row * (width // LANES) + at
            k.gain_total[0, base : base + 1, :] += sums[:, at * LANES : (at + 1) * LANES]

    def second_back(at):
        grad = k.in2_sum[at, :]
        normed = k.normed2[at, :]
        add_gain(1, jnp.sum(grad * normed, axis=0, keepdims=True))
        result = k.grad_rows[at, :].astype(F32) + norm_back(grad, normed, k.scale2[at, :], second_gain)
        k.grad_res[at, :] = result
        k.branch_rows[at, :] = result.astype(BF16)

    row_tiles(here, second_back)
    for c in range(2):
        k.in2_sum[:, c * half : (c + 1) * half] = dot(k.branch_rows[...], whole(k.w_out, c))

    def gate_back(at):
        gate = k.gate[at, :]
        grad = k.in2_sum[at, :]
        sig = jax.nn.sigmoid(gate)
        rows = (grad * k.mixed[at, :] * (sig * (1.0 + gate * (1.0 - sig)))).astype(BF16)
        k.gate_rows[0, at, :] = rows[:, :half]
        k.gate_rows[1, at, :] = rows[:, half:]
        k.normed2[at, :] = grad * (gate * sig)

    row_tiles(here, gate_back)
    k.sent[...] = to_chunks(sizes, k.normed2[...])
    move3 = Exchange(place, k.sent, k.landed3, k.a3_send, k.a3_recv)
    move3.start()
    share_rows("gate_rows", 6)
    share_turned("branch_rows", 3)

    reduces = {}
    for name in plan.weight_names:
        pieces = plan.pieces if name in ("up", "down") else 1
        for piece in range(pieces):
            size = plan.columns[name] // pieces
            reduces[name + str(piece)] = Reduce(
                place,
                getattr(k, "g_" + name),
                [getattr(k, f"l_{name}{piece}{phase}") for phase in range(len(plan.reduce_phases[name]))],
                plan.reduce_phases[name],
                getattr(k, f"rs_{name}{piece}"),
                getattr(k, f"rr_{name}{piece}"),
                getattr(k, "v_r_" + name),
                pl.ds(piece * size, size) if pieces > 1 else None,
            )

    def left(name):
        mine = getattr(k, "t_" + name)[:, core]
        rows = width // 2
        return jnp.concatenate(
            [mine.reshape(rows, here), getattr(k, "twin_" + name)[...].reshape(rows, here)], axis=1
        )

    def tile_grads(name, left_name, right_name, piece):
        grads, right = getattr(k, "g_" + name), getattr(k, right_name)
        twin_right = getattr(k, "twin_" + right_name)
        count = plan.per_piece

        def one(turn, carry):
            lead, at = turn // count, lax.rem(turn, count)
            tile = lead * per_half + piece * count + at
            got = dot(left(left_name), jnp.concatenate([right[tile], twin_right[tile]], axis=0))
            columns = pl.ds(pl.multiple_of((piece * count + at) * plan.tile, LANES), plan.tile)
            index = (lead,) + (slice(None),) * (plan.dims - 1) + (columns,)
            grads[index] = got.astype(BF16).reshape((2,) * (plan.dims - 2) + (plan.rows, plan.tile))
            return carry

        lax.fori_loop(0, 2 * count, one, 0)

    def row_grads(name, left_name, right_name):
        grads, right = getattr(k, "g_" + name), getattr(k, right_name)
        twin_right = getattr(k, "twin_" + right_name)
        for c in range(2):
            got = dot(left(left_name), jnp.concatenate([right[c], twin_right[c]], axis=0))
            grads[c] = got.astype(BF16).reshape((2,) * (plan.dims - 2) + (plan.rows, half))

    def wait_tiles(tile, carry):
        twin_copy("act", tile).wait()
        twin_copy("hid", tile).wait()
        return carry

    lax.fori_loop(0, plan.tiles, wait_tiles, 0)
    twins["input2"].wait()
    twins["grad_rows"].wait()
    tile_grads("up", "input2", "hid", 0)
    reduces["up0"].start(0)
    tile_grads("down", "grad_rows", "act", 0)
    reduces["down0"].start(0)
    tile_grads("up", "input2", "hid", 1)
    reduces["up1"].start(0)
    tile_grads("down", "grad_rows", "act", 1)
    reduces["down1"].start(0)

    def make_output(at):
        rows = (k.residual[at, :] + k.out_sum[at, :]).astype(BF16)
        k.out_send[0, at, :] = rows[:, :half]
        k.out_send[1, at, :] = rows[:, half:]

    row_tiles(here, make_output)
    swap_out = remote(
        k.out_send.at[1 - chan], k.v_output.at[chan], k.swap_send.at[3], k.swap_recv.at[3], across
    )
    swap_out.start()
    k.v_output[chan] = k.out_send[chan]
    twins["inner_rows"].wait()
    twins["branch_rows"].wait()
    row_grads("out", "branch_rows", "inner_rows")
    reduces["out0"].start(0)
    twins["gate_rows"].wait()
    twins["input1"].wait()
    row_grads("gate", "input1", "gate_rows")
    reduces["gate0"].start(0)
    move3.wait()

    widen(sizes, k.landed3, k.wide)
    spectrum_into(sizes, chunk_loader(sizes, k.wide), k.into, k.turn, k.ahead, k.inner, k.grad_spec)
    signal_from(
        sizes,
        lambda at: times(k.grad_spec[at, :], k.kernel_spec[at, :], True),
        k.outof, k.turn, k.behind, k.inner, chunk_storer(sizes, k.wide),
    )
    narrow(sizes, k.wide, k.sent_back)
    move4 = Exchange(place, k.sent_back, k.landed4, k.a4_send, k.a4_recv)
    move4.start()

    def store_taps(channel, values):
        k.tap_wide[pl.ds(channel, sizes.tap_rows, stride=channels), :] = values

    reduces["up0"].go_on(0)
    reduces["down0"].go_on(0)
    signal_from(
        sizes,
        lambda at: times(k.grad_spec[at, :], k.value_spec[at, :], True),
        k.taps_outof, k.turn, k.behind, k.inner, store_taps,
    )
    pooled = pooled_taps(k.taps[...])
    bent = jnp.tanh(pooled / THRESH)
    k.tap_grad[...] = pooled_taps(k.tap_wide[...].reshape(pooled.shape) * live * bent * bent)
    tap_back = PlaneExchange(
        place,
        lambda g: k.tap_grad.at[g],
        lambda g: k.v_grad_kernel.at[pl.ds(pl.multiple_of(g * channels, 8), channels)],
        k.t2_send,
        k.t2_recv,
    )
    tap_back.start()
    k.v_grad_kernel[pl.ds(pl.multiple_of(place.freq * channels, 8), channels)] = k.tap_grad[place.freq]
    reduces["up1"].go_on(0)
    reduces["down1"].go_on(0)
    reduces["out0"].go_on(0)
    reduces["gate0"].go_on(0)
    move4.wait()

    for col in range(sizes.cols):
        rows = from_chunk_columns(k.landed4, col).astype(BF16)
        for c in range(2):
            k.signal_rows[c, col * LANES : (col + 1) * LANES, :] = rows[:, c * half : (c + 1) * half]
    share_rows("signal_rows", 5)
    k.out_sum[...] = sum(
        dot_nt(rows[c], whole(weight, c))
        for rows, weight in ((k.signal_rows, k.w_value), (k.gate_rows, k.w_gate))
        for c in range(2)
    )
    twins["signal_rows"].wait()
    row_grads("value", "input1", "signal_rows")
    reduces["value0"].start(0)

    def first_back(at):
        grad = k.out_sum[at, :]
        normed = k.normed1[at, :]
        add_gain(0, jnp.sum(grad * normed, axis=0, keepdims=True))
        result = k.grad_res[at, :] + norm_back(grad, normed, k.scale1[at, :], first_gain)
        k.grad_res[at, :] = result
        k.gin_send[0, at, :] = result[:, :half].astype(BF16)
        k.gin_send[1, at, :] = result[:, half:].astype(BF16)

    row_tiles(here, first_back)
    swap_gin = remote(
        k.gin_send.at[1 - chan], k.gin_land, k.swap_send.at[4], k.swap_recv.at[4], across
    )
    swap_gin.start()
    spread = Spread(place, k.gain_total, k.gain_land, plan.spread_phases, k.gain_send, k.gain_recv)
    spread.start(0)
    k.v_grad_input[chan] = jnp.where(chan == 0, k.grad_res[:, :half], k.grad_res[:, half:])
    for name in ("up0", "down0", "up1", "down1", "out0", "gate0"):
        reduces[name].go_on(1)
    spread.go_on(0)
    reduces["value0"].go_on(0)
    spread.go_on(1)
    swap_out.wait()
    leave("output")
    swap_gin.wait()
    k.v_grad_input[1 - chan] = k.gin_land[...].astype(F32)
    leave("grad_input")
    tap_back.wait()
    leave("grad_kernel")
    for name in ("up0", "down0", "up1", "down1", "out0", "gate0"):
        reduces[name].go_on(2)
    for name in ("up", "down", "out", "gate"):
        leave("r_" + name)
    spread.go_on(2)
    leave("gain_sums")
    reduces["value0"].go_on(1)
    leave("r_value")
    for copy in leaving:
        copy.wait()


def copy_kernel(count, *refs):
    sources, targets, sems = refs[:count], refs[count : 2 * count], refs[-1]
    copies = [pltpu.make_async_copy(sources[n], targets[n], sems.at[n]) for n in range(count)]
    for copy in copies:
        copy.start()
    for copy in copies:
        copy.wait()


def settle(arrays):
    return pl.pallas_call(
        functools.partial(copy_kernel, len(arrays)),
        out_shape=[jax.ShapeDtypeStruct(a.shape, a.dtype) for a in arrays],
        in_specs=[ANY_SPEC] * len(arrays),
        out_specs=[VMEM_SPEC] * len(arrays),
        scratch_shapes=[pltpu.SemaphoreType.DMA((len(arrays),))],
        name="settle",
    )(*arrays)


def one_sequence(
    tokens, cotangent, first_gain, second_gain, w_value, w_gate, w_out, w_up, w_down, raw_kernel, lengths
):
    freq_count = lax.axis_size("freq")
    _, here, half = tokens.shape
    sizes = Sizes(freq_count, here, half, raw_kernel.shape[1] * freq_count)
    plan = Plan(sizes, w_up.shape[1])
    pack = jnp.concatenate(
        [jnp.stack([first_gain, second_gain, lengths.astype(F32)]), jnp.zeros((5, half), F32)]
    )
    shards = (w_value, w_gate, w_out, w_up, w_down)
    tables = conv_tables(sizes)
    out_shape = (
        [jax.ShapeDtypeStruct((2, here, half), BF16), jax.ShapeDtypeStruct((2, here, half), F32)]
        + [jax.ShapeDtypeStruct(w.shape, F32) for w in shards]
        + [
            jax.ShapeDtypeStruct((4 * half // LANES + 4, LANES), F32),
            jax.ShapeDtypeStruct(raw_kernel.shape, F32),
        ]
    )
    results = pl.pallas_call(
        functools.partial(block_kernel, plan),
        out_shape=out_shape,
        in_specs=[ANY_SPEC] * 9 + [VMEM_SPEC] * len(tables),
        out_specs=[ANY_SPEC] * len(out_shape),
        scratch_shapes=plan.scratch,
        compiler_params=pltpu.CompilerParams(
            collective_id=0, has_side_effects=True, vmem_limit_bytes=63 << 20
        ),
        name="block",
    )(tokens, cotangent, pack, raw_kernel, *shards, *tables)
    *arrays, gain_sums, grad_kernel = results
    arrays = settle([*arrays, grad_kernel])
    sums = gain_sums.reshape(-1)[: 4 * half].reshape(2, 2 * half)
    start = lax.axis_index("chan") * half + lax.axis_index("freq") * sizes.channels
    sums = lax.dynamic_slice_in_dim(sums, start, sizes.channels, axis=1)
    return (*arrays[:-1], sums[0][:, None], sums[1][:, None], arrays[-1])


def fits(mesh):
    freq_count = mesh.shape["freq"]
    return lambda tokens, w_value, raw_kernel: (
        mesh.shape["chan"] == 2
        and tokens.shape[0] == 2
        and freq_count >= 8
        and freq_count & (freq_count - 1) == 0
        and w_value.shape[0] % (16 * freq_count) == 0
        and w_value.shape[1] % (16 * freq_count) == 0
        and w_value.shape[1] % 256 == 0
        and tokens.shape[1] % (LANES * freq_count) == 0
        and raw_kernel.shape[1] == LANES * freq_count
        and (tokens.shape[1] + raw_kernel.shape[1]) // LANES % 16 == 0
    )


D = 768
SEQ_MB = 1
MICRO = 2


HIGHEST = lax.Precision.HIGHEST


def circle(height, breadth, period):
    first_index = lax.broadcasted_iota(jnp.int32, (height, breadth), 0)
    second_index = lax.broadcasted_iota(jnp.int32, (height, breadth), 1)
    phase_angle = (first_index * second_index % period).astype(jnp.float32) * (
        2.0 * math.pi / period
    )
    return (jnp.cos(phase_angle), jnp.sin(phase_angle))


def make_tables(padded_size):
    inner_size = 128
    outer_size = padded_size // inner_size
    outer_cos, outer_sin = circle(outer_size, outer_size, outer_size)
    inner_cos, inner_sin = circle(inner_size, inner_size, inner_size)
    twist_cos, twist_sin = circle(outer_size, inner_size, padded_size)
    return (outer_cos, outer_sin, inner_cos, inner_sin, twist_cos, twist_sin)


def spectrum(signal, padded_size, tables):
    outer_cos, outer_sin, inner_cos, inner_sin, twist_cos, twist_sin = tables
    inner_size = inner_cos.shape[0]
    pad_width = [(0, 0)] * (signal.ndim - 1) + [(0, padded_size - signal.shape[-1])]
    grid_values = jnp.pad(signal, pad_width).reshape(
        signal.shape[:-1] + (padded_size // inner_size, inner_size)
    )
    part_real = jnp.einsum("...ab,fa->...fb", grid_values, outer_cos, precision=HIGHEST)
    part_imag = -jnp.einsum("...ab,fa->...fb", grid_values, outer_sin, precision=HIGHEST)
    turned_real = part_real * twist_cos + part_imag * twist_sin
    turned_imag = part_imag * twist_cos - part_real * twist_sin
    spec_real = jnp.einsum(
        "...fb,bg->...fg", turned_real, inner_cos, precision=HIGHEST
    ) + jnp.einsum("...fb,bg->...fg", turned_imag, inner_sin, precision=HIGHEST)
    spec_imag = jnp.einsum(
        "...fb,bg->...fg", turned_imag, inner_cos, precision=HIGHEST
    ) - jnp.einsum("...fb,bg->...fg", turned_real, inner_sin, precision=HIGHEST)
    return (spec_real, spec_imag)


def signal_of(spec_real, spec_imag, keep_count, tables):
    outer_cos, outer_sin, inner_cos, inner_sin, twist_cos, twist_sin = tables
    padded_size = spec_real.shape[-1] * spec_real.shape[-2]
    back_real = jnp.einsum("...fg,bg->...fb", spec_real, inner_cos, precision=HIGHEST) - jnp.einsum(
        "...fg,bg->...fb", spec_imag, inner_sin, precision=HIGHEST
    )
    back_imag = jnp.einsum("...fg,bg->...fb", spec_imag, inner_cos, precision=HIGHEST) + jnp.einsum(
        "...fg,bg->...fb", spec_real, inner_sin, precision=HIGHEST
    )
    turned_real = back_real * twist_cos - back_imag * twist_sin
    turned_imag = back_imag * twist_cos + back_real * twist_sin
    grid_values = (
        jnp.einsum("...fb,af->...ab", turned_real, outer_cos, precision=HIGHEST)
        - jnp.einsum("...fb,af->...ab", turned_imag, outer_sin, precision=HIGHEST)
    ) / padded_size
    flat_values = grid_values.reshape(grid_values.shape[:-2] + (padded_size,))
    return flat_values[..., :keep_count]


def shape_kernel(raw_taps, live_taps):
    padded = jnp.pad(raw_taps, ((0, 0), (1, 1)))
    pooled = (padded[:, :-2] + padded[:, 1:-1] + padded[:, 2:]) / 3.0
    return (pooled - THRESH * jnp.tanh(pooled / THRESH)) * live_taps


def row_norm(values):
    row_width = values.shape[-1] * lax.axis_size("chan")
    row_total, row_square = lax.psum(
        (jnp.sum(values, axis=-1), jnp.sum(values * values, axis=-1)), "chan"
    )
    center = row_total / row_width
    spread = row_square / row_width - center * center
    scale = lax.rsqrt(spread + EPSILON)[..., None]
    return ((values - center[..., None]) * scale, scale)


def row_back(grad_rows, normed, scale, gain_row):
    row_width = grad_rows.shape[-1] * lax.axis_size("chan")
    scaled = grad_rows * gain_row
    sum_plain, sum_cross = lax.psum(
        (jnp.sum(scaled, axis=-1), jnp.sum(scaled * normed, axis=-1)), "chan"
    )
    return scale * (
        scaled - sum_plain[..., None] / row_width - normed * sum_cross[..., None] / row_width
    )


def features(values):
    return lax.all_gather(values, "chan", axis=2, tiled=True)


def partial_sum(values):
    return lax.psum_scatter(
        values.astype(jnp.bfloat16), "chan", scatter_dimension=2, tiled=True
    ).astype(jnp.float32)


def to_channels(values):
    return lax.all_to_all(
        jnp.swapaxes(values, 1, 2), "freq", split_axis=1, concat_axis=2, tiled=True
    )


def to_tokens(values):
    arrived = lax.all_to_all(values, "freq", split_axis=2, concat_axis=1, tiled=True)
    return jnp.swapaxes(arrived, 1, 2)


def by_features(
    tokens,
    cotangent,
    first_gain,
    second_gain,
    w_value,
    w_gate,
    w_out,
    w_up,
    w_down,
    raw_kernel,
    lengths,
):
    full_value, full_gate, full_out, full_up, full_down = (
        lax.all_gather(w_value, "freq", axis=0, tiled=True),
        lax.all_gather(w_gate, "freq", axis=0, tiled=True),
        lax.all_gather(w_out, "freq", axis=0, tiled=True),
        lax.all_gather(w_up, "freq", axis=0, tiled=True),
        lax.all_gather(w_down, "freq", axis=0, tiled=True),
    )
    freq_count = lax.axis_size("freq")
    chan_width = tokens.shape[2]
    channels = chan_width // freq_count
    seq_length = tokens.shape[1] * freq_count
    padded_size = 2 * seq_length
    tables = make_tables(padded_size)
    kernel_rows = lax.all_to_all(raw_kernel, "freq", split_axis=0, concat_axis=1, tiled=True)
    tap_count = kernel_rows.shape[1]
    my_lengths = lax.dynamic_slice_in_dim(lengths, lax.axis_index("freq") * channels, channels)
    tap_index = lax.broadcasted_iota(jnp.int32, (channels, tap_count), 1)
    live_taps = (tap_index < my_lengths[:, None]).astype(jnp.float32)
    kernel, kernel_pull = jax.vjp(functools.partial(shape_kernel, live_taps=live_taps), kernel_rows)
    kernel_real, kernel_imag = spectrum(kernel, padded_size, tables)
    hidden_width = full_up.shape[1]
    shard_factor = 1
    totals = (
        jnp.zeros((D // shard_factor, chan_width), jnp.float32),
        jnp.zeros((D // shard_factor, chan_width), jnp.float32),
        jnp.zeros((D // shard_factor, chan_width), jnp.float32),
        jnp.zeros((D // shard_factor, hidden_width), jnp.float32),
        jnp.zeros((D // shard_factor, hidden_width), jnp.float32),
        jnp.zeros((chan_width // shard_factor, 1), jnp.float32),
        jnp.zeros((chan_width // shard_factor, 1), jnp.float32),
    )
    kernel_grad = jnp.zeros((channels, tap_count), jnp.float32)
    outputs = []
    input_grads = []
    for micro_index in range(MICRO):
        rows_here = tokens[micro_index * SEQ_MB : (micro_index + 1) * SEQ_MB].astype(jnp.float32)
        first_normed, first_scale = row_norm(rows_here)
        input1 = features((first_normed * first_gain).astype(jnp.bfloat16))
        value_low = jnp.einsum(
            "bld,de->ble", input1, full_value, preferred_element_type=jnp.float32
        ).astype(jnp.bfloat16)
        gate_proj = jnp.einsum("bld,de->ble", input1, full_gate, preferred_element_type=jnp.float32)
        signal = to_channels(value_low).astype(jnp.float32)
        signal_real, signal_imag = spectrum(signal, padded_size, tables)
        mixed = signal_of(
            signal_real * kernel_real - signal_imag * kernel_imag,
            signal_real * kernel_imag + signal_imag * kernel_real,
            seq_length,
            tables,
        )
        mixed_rows = to_tokens(mixed.astype(jnp.bfloat16)).astype(jnp.float32)
        gate_act, gate_pull = jax.vjp(jax.nn.silu, gate_proj)
        inner_low = (mixed_rows * gate_act).astype(jnp.bfloat16)
        residual = rows_here + partial_sum(
            jnp.einsum("ble,oe->blo", inner_low, full_out, preferred_element_type=jnp.float32)
        )
        second_normed, second_scale = row_norm(residual)
        input2 = features((second_normed * second_gain).astype(jnp.bfloat16))
        hidden = jnp.einsum("bld,df->blf", input2, full_up, preferred_element_type=jnp.float32)
        activated, act_pull = jax.vjp(jax.nn.gelu, hidden)
        act_low = activated.astype(jnp.bfloat16)
        result = residual + partial_sum(
            jnp.einsum("blf,of->blo", act_low, full_down, preferred_element_type=jnp.float32)
        )
        outputs.append(result.astype(jnp.bfloat16))
        grad_rows_out = cotangent[micro_index * SEQ_MB : (micro_index + 1) * SEQ_MB]
        grad_full = features(grad_rows_out)
        grad_act = jnp.einsum(
            "blo,of->blf", grad_full, full_down, preferred_element_type=jnp.float32
        )
        down_grad = jnp.einsum(
            "blo,blf->of", grad_full, act_low, preferred_element_type=jnp.float32
        )
        grad_hidden = act_pull(grad_act)[0].astype(jnp.bfloat16)
        up_grad = jnp.einsum("bld,blf->df", input2, grad_hidden, preferred_element_type=jnp.float32)
        grad_in2 = partial_sum(
            jnp.einsum("blf,df->bld", grad_hidden, full_up, preferred_element_type=jnp.float32)
        )
        second_grad = jnp.sum(grad_in2 * second_normed, axis=(0, 1))
        grad_residual = grad_rows_out.astype(jnp.float32) + row_back(
            grad_in2, second_normed, second_scale, second_gain
        )
        grad_branch = features(grad_residual.astype(jnp.bfloat16))
        grad_inner = jnp.einsum(
            "blo,oe->ble", grad_branch, full_out, preferred_element_type=jnp.float32
        )
        out_grad = jnp.einsum(
            "blo,ble->oe", grad_branch, inner_low, preferred_element_type=jnp.float32
        )
        grad_mixed = to_channels((grad_inner * gate_act).astype(jnp.bfloat16)).astype(jnp.float32)
        grad_real, grad_imag = spectrum(grad_mixed, padded_size, tables)
        grad_signal = signal_of(
            grad_real * kernel_real + grad_imag * kernel_imag,
            grad_imag * kernel_real - grad_real * kernel_imag,
            seq_length,
            tables,
        )
        kernel_grad = kernel_grad + jnp.sum(
            signal_of(
                grad_real * signal_real + grad_imag * signal_imag,
                grad_imag * signal_real - grad_real * signal_imag,
                tap_count,
                tables,
            ),
            axis=0,
        )
        grad_signal_rows = to_tokens(grad_signal.astype(jnp.bfloat16))
        grad_gate_rows = gate_pull(grad_inner * mixed_rows)[0].astype(jnp.bfloat16)
        value_grad = jnp.einsum(
            "bld,ble->de", input1, grad_signal_rows, preferred_element_type=jnp.float32
        )
        gate_grad = jnp.einsum(
            "bld,ble->de", input1, grad_gate_rows, preferred_element_type=jnp.float32
        )
        grad_in1 = partial_sum(
            jnp.einsum(
                "ble,de->bld", grad_signal_rows, full_value, preferred_element_type=jnp.float32
            )
            + jnp.einsum(
                "ble,de->bld", grad_gate_rows, full_gate, preferred_element_type=jnp.float32
            )
        )
        first_grad = jnp.sum(grad_in1 * first_normed, axis=(0, 1))
        input_grads.append(
            grad_residual + row_back(grad_in1, first_normed, first_scale, first_gain)
        )
        local_terms = (
            value_grad,
            gate_grad,
            out_grad,
            up_grad,
            down_grad,
            first_grad[:, None],
            second_grad[:, None],
        )
        totals = tuple((left + right for left, right in zip(totals, local_terms)))
    totals = lax.psum_scatter(totals, "freq", scatter_dimension=0, tiled=True)
    raw_grad = kernel_pull(kernel_grad)[0]
    grad_kernel = lax.all_to_all(raw_grad, "freq", split_axis=1, concat_axis=0, tiled=True)
    output = jnp.concatenate(outputs, axis=0)
    grad_input = jnp.concatenate(input_grads, axis=0)
    return (
        output,
        grad_input,
        totals[0],
        totals[1],
        totals[2],
        totals[3],
        totals[4],
        totals[5],
        totals[6],
        grad_kernel,
    )


def solution(mesh):
    specs = dict(
        mesh=mesh,
        in_specs=(
            P(None, "freq", "chan"),
            P(None, "freq", "chan"),
            P("chan"),
            P("chan"),
            P("freq", "chan"),
            P("freq", "chan"),
            P("freq", "chan"),
            P("freq", "chan"),
            P("freq", "chan"),
            P("chan", "freq"),
            P("chan"),
        ),
        out_specs=(
            P(None, "freq", "chan"),
            P(None, "freq", "chan"),
            P("freq", "chan"),
            P("freq", "chan"),
            P("freq", "chan"),
            P("freq", "chan"),
            P("freq", "chan"),
            P("freq", "chan"),
            P("freq", "chan"),
            P("chan", "freq"),
        ),
        check_vma=False,
    )

    def step(*args):
        whole = fits(mesh)(args[0], args[4], args[9])
        return jax.shard_map(one_sequence if whole else by_features, **specs)(*args)

    return step
```

```python
import functools
import math
import types

import jax
import jax.numpy as jnp
import numpy as np
from jax import lax
from jax.experimental import pallas as pl
from jax.experimental.pallas import tpu as pltpu
from jax.sharding import PartitionSpec as P

THRESH = 0.003
EPSILON = 1e-05
LANES = 128
MESH = pl.DeviceIdType.MESH
F32 = jnp.float32
BF16 = jnp.bfloat16


def bit_sizes(freq_count):
    return [1 << i for i in reversed(range(freq_count.bit_length() - 1))]


class Place:
    def __init__(self, freq_count):
        self.freq_count = freq_count
        self.freq = lax.axis_index("freq")
        self.chan = lax.axis_index("chan")
        self.bits = bit_sizes(freq_count)
        self.coords = [self.chan] + [lax.rem(self.freq // b, 2) for b in self.bits]
        self.dims = len(self.coords)
        self.core = self.coords[-1]

    def other(self, flipped):
        freq, chan = self.freq, self.chan
        for dim in flipped:
            if dim == 0:
                chan = 1 - chan
            else:
                bit = self.bits[dim - 1]
                freq = freq + bit - 2 * bit * self.coords[dim]
        return (freq, chan)


def flips(dims):
    return [
        tuple(dim for at, dim in enumerate(dims) if mask >> at & 1) for mask in range(1, 1 << len(dims))
    ]


def remote(source, target, send, recv, device):
    return pltpu.make_async_remote_copy(
        src_ref=source,
        dst_ref=target,
        send_sem=send,
        recv_sem=recv,
        device_id=device,
        device_id_type=MESH,
    )


class Line:
    def __init__(self, way, high, low):
        self.way, self.high, self.low = way, high, low

    def ends(self, place):
        middle = place.coords[self.high] + place.coords[self.low] == 1
        end = place.coords[self.high] + place.coords[self.low] != 1
        return {ACROSS: (middle, middle), INWARD: (end, middle), OUTWARD: (middle, end)}[self.way]

    def flipped(self):
        return (self.high, self.low) if self.way == ACROSS else (self.low,)


def when(condition, action):
    if condition is None:
        action()
    else:
        pl.when(condition)(action)


class Leg:
    def __init__(self, copy, ends=(None, None)):
        self.copy, self.ends = copy, ends

    def start(self):
        when(self.ends[0], self.copy.start)

    def wait(self):
        if self.ends[0] is None:
            self.copy.wait()
        else:
            when(self.ends[0], self.copy.wait_send)
            when(self.ends[1], self.copy.wait_recv)


def flips_of(phase):
    return [phase.flipped()] if isinstance(phase, Line) else flips(phase)


def is_outward(phase):
    return isinstance(phase, Line) and phase.way == OUTWARD


def slots(phases):
    return sum(len(flips_of(phase)) for phase in phases if not is_outward(phase))


def first_slot(phases, at):
    return slots(phases[:at]) - is_outward(phases[at])


class Gather:
    def __init__(self, place, buffer, dims, phases, send, recv, prepare):
        self.place, self.buffer, self.dims, self.phases = place, buffer, dims, phases
        self.send, self.recv, self.prepare = send, recv, prepare
        self.turn = 0

    def copies(self, phase):
        done, step = set(), self.phases[phase]
        for before in self.phases[:phase]:
            if not isinstance(before, Line):
                done.update(before)
            elif before.way == OUTWARD:
                done.update((before.high, before.low))
        index = [slice(None) if dim in done else self.place.coords[dim] for dim in self.dims]
        ends = (None, None)
        if isinstance(step, Line):
            ends = step.ends(self.place)
            if step.way == OUTWARD:
                index[self.dims.index(step.high)] = 1 - self.place.coords[step.high]
        region = self.buffer.at[tuple(index)]
        base = first_slot(self.phases, phase)
        return [
            Leg(
                remote(region, region, self.send.at[k], self.recv.at[base + k], self.place.other(flipped)), ends
            )
            for k, flipped in enumerate(flips_of(step))
        ]

    def go(self):
        if self.turn > len(self.phases):
            return
        if self.turn == 0:
            self.prepare()
        else:
            for copy in self.copies(self.turn - 1):
                copy.wait()
        if self.turn < len(self.phases):
            for copy in self.copies(self.turn):
                copy.start()
        self.turn += 1

    def finish(self):
        while self.turn <= len(self.phases):
            self.go()


class Reduce:
    def __init__(self, place, total, landing, dims, phases, send, recv, out, prepare, done):
        self.place, self.total, self.landing, self.dims = place, total, landing, dims
        self.phases, self.send, self.recv, self.out = phases, send, recv, out
        self.prepare, self.done = prepare, done
        self.turn = 0

    def region(self, phase, flipped):
        fixed, step = set(), self.phases[phase]
        for before in self.phases[:phase]:
            if not isinstance(before, Line):
                fixed.update(before)
            elif before.way == ACROSS:
                fixed.add(before.high)
        if not isinstance(step, Line):
            fixed.update(step)
        coords = self.place.coords
        index = [
            (1 - coords[dim] if dim in flipped else coords[dim]) if dim in fixed else slice(None)
            for dim in self.dims
        ]
        if isinstance(step, Line):
            mine = coords[step.high]
            keeps = step.way == ACROSS and not flipped
            index[self.dims.index(step.high)] = mine if keeps else 1 - mine
        return tuple(index)

    def copies(self, phase):
        step = self.phases[phase]
        base = first_slot(self.phases, phase)
        ends = step.ends(self.place) if isinstance(step, Line) else (None, None)
        return [
            Leg(
                remote(
                    self.total.at[self.region(phase, flipped)],
                    self.landing[phase].at[k],
                    self.send.at[k],
                    self.recv.at[base + k],
                    self.place.other(flipped),
                ),
                ends,
            )
            for k, flipped in enumerate(flips_of(step))
        ]

    def add(self, phase):
        kept = self.region(phase, ())
        free = [at for at, part in enumerate(kept) if isinstance(part, slice)]
        landing, step = self.landing[phase], self.phases[phase]

        def one(turn, carry):
            where, there = list(kept), []
            for at, dim in enumerate(free):
                bit = lax.rem(turn // (1 << (len(free) - 1 - at)), 2)
                where[dim] = bit
                there.append(bit)
            where, there = tuple(where), tuple(there)
            total = self.total[where].astype(F32)
            for k in range(len(flips_of(step))):
                total = total + landing[(k,) + there].astype(F32)
            if phase + 1 == len(self.phases):
                self.out[...] = total
            else:
                self.total[where] = total.astype(BF16)
            return carry

        def every():
            if free:
                lax.fori_loop(0, 1 << len(free), one, 0)
            else:
                one(0, 0)

        when(step.ends(self.place)[1] if isinstance(step, Line) else None, every)

    def go(self):
        if self.turn > len(self.phases):
            return
        if self.turn == 0:
            self.prepare()
        else:
            for copy in self.copies(self.turn - 1):
                copy.wait()
            self.add(self.turn - 1)
        if self.turn < len(self.phases):
            for copy in self.copies(self.turn):
                copy.start()
        else:
            self.done()
        self.turn += 1

    def finish(self):
        while self.turn <= len(self.phases):
            self.go()


def landing_shapes(phases, dims, rows, columns):
    shapes, free = [], len(dims)
    for step in phases:
        if isinstance(step, Line):
            free -= 0 if step.way == INWARD else 1
            shapes.append((1,) + (2,) * (free - (step.way == INWARD)) + (rows, columns))
        else:
            free -= len(step)
            shapes.append((len(flips(step)),) + (2,) * free + (rows, columns))
    return shapes


class Spread:
    def __init__(self, place, total, landing, phases, send, recv):
        self.place, self.total, self.landing, self.phases = place, total, landing, phases
        self.send, self.recv = send, recv
        self.turn = 0

    def copies(self, phase):
        base = sum(len(flips(dims)) for dims in self.phases[:phase])
        return base, [
            remote(
                self.total.at[phase],
                self.landing.at[base + k],
                self.send.at[k],
                self.recv.at[base + k],
                self.place.other(flipped),
            )
            for k, flipped in enumerate(flips(self.phases[phase]))
        ]

    def go(self):
        if self.turn > len(self.phases):
            return
        if self.turn:
            base, copies = self.copies(self.turn - 1)
            total = self.total[self.turn - 1]
            for k, copy in enumerate(copies):
                copy.wait()
                total = total + self.landing[base + k]
            self.total[self.turn] = total
        if self.turn < len(self.phases):
            for copy in self.copies(self.turn)[1]:
                copy.start()
        self.turn += 1

    def finish(self):
        while self.turn <= len(self.phases):
            self.go()


class Exchange:
    def __init__(self, count, me, device, source, target, all_sent, all_landed, sems):
        self.count, self.me, self.device = count, me, device
        self.source, self.target = source, target
        self.all_sent, self.all_landed, self.sems = all_sent, all_landed, sems

    def start(self):
        def one(step, carry):
            other = lax.rem(self.me + step, self.count)
            remote(
                self.source(other), self.target(self.me), self.sems.at[0], self.sems.at[1], self.device(other)
            ).start()
            return carry

        lax.fori_loop(1, self.count, one, 0, unroll=True)

    def wait(self):
        for part, sem in ((self.all_sent, self.sems.at[0]), (self.all_landed, self.sems.at[1])):
            pltpu.make_async_copy(part, part, sem).wait()


class Sizes:
    def __init__(self, freq_count, here, half, taps):
        self.freq_count = freq_count
        self.here = here
        self.half = half
        self.cols = here // LANES
        self.channels = half // freq_count
        self.group = 8
        self.groups = self.channels // self.group
        self.chunk = self.cols * self.group
        self.devices = 2 * freq_count
        self.tap_rows = taps // LANES
        self.rows = here * freq_count // LANES + self.tap_rows
        self.size = self.rows * LANES
        self.group_rows = self.group * self.rows


def conv_tables(sizes):
    rows, size = sizes.rows, sizes.size
    f = np.arange(rows)
    a_of, imag = [], []
    for col in range(sizes.cols):
        for seq in range(2):
            for block in range(sizes.freq_count):
                a_of.append(block * sizes.cols + col)
                imag.append(seq)
    a_of, imag = np.array(a_of), np.array(imag)
    angle = 2 * np.pi * np.outer(f, a_of) / rows
    cos, sin = np.cos(angle), np.sin(angle)
    into = np.concatenate([np.where(imag, sin, cos), np.where(imag, cos, -sin)], axis=0)
    outof = into.T / size
    angle = 2 * np.pi * np.outer(f, np.arange(sizes.tap_rows)) / rows
    taps_into = np.concatenate([np.cos(angle), -np.sin(angle)], axis=0)
    taps_outof = taps_into.T / size
    b = np.arange(LANES)
    angle = 2 * np.pi * np.outer(f, b) / size
    turn = np.stack([np.cos(angle), np.sin(angle)])
    angle = 2 * np.pi * np.outer(b, b) / LANES
    cos, sin = np.cos(angle), np.sin(angle)
    ahead = np.block([[cos, -sin], [sin, cos]])
    return (
        jnp.asarray(into, BF16),
        jnp.asarray(outof, BF16),
        jnp.asarray(taps_into, BF16),
        jnp.asarray(taps_outof, BF16),
        jnp.asarray(turn, F32),
        jnp.asarray(ahead, BF16),
        jnp.asarray(ahead.T, BF16),
    )


def dot(left, right):
    return jnp.dot(left, right, preferred_element_type=F32)


def spectrum_into(sizes, load, into, turn, ahead, inner, spectrum):
    rows = sizes.rows
    for pair in range(sizes.group // 2):
        both = jnp.concatenate([load(2 * pair), load(2 * pair + 1)], axis=1).astype(BF16)
        part = dot(into[...], both)
        for side in range(2):
            real = part[:rows, side * LANES : (side + 1) * LANES]
            imag = part[rows:, side * LANES : (side + 1) * LANES]
            start = (2 * pair + side) * rows
            inner[start : start + rows, :] = jnp.concatenate(
                [real * turn[0] + imag * turn[1], imag * turn[0] - real * turn[1]], axis=1
            ).astype(BF16)
    spectrum[...] = dot(inner[...], ahead[...])


def signal_from(sizes, product, outof, turn, behind, inner, store):
    rows = sizes.rows
    inner[...] = dot(product, behind[...])
    for pair in range(sizes.group // 2):
        sides = []
        for side in range(2):
            start = (2 * pair + side) * rows
            real, imag = inner[start : start + rows, :LANES], inner[start : start + rows, LANES:]
            sides.append(
                jnp.concatenate(
                    [real * turn[0] - imag * turn[1], imag * turn[0] + real * turn[1]], axis=0
                ).astype(BF16)
            )
        got = dot(outof[...], jnp.concatenate(sides, axis=1))
        for side in range(2):
            store(2 * pair + side, got[:, side * LANES : (side + 1) * LANES])


def times(left, right, conj):
    a, b = left[:, :LANES], left[:, LANES:]
    c, d = right[:, :LANES], right[:, LANES:]
    if conj:
        return jnp.concatenate([a * c + b * d, b * c - a * d], axis=1).astype(BF16)
    return jnp.concatenate([a * c - b * d, a * d + b * c], axis=1).astype(BF16)


def to_chunks(sizes, rows, target):
    turned = rows.T.reshape(sizes.devices, sizes.channels, sizes.here)
    for group in range(sizes.groups):
        channels = slice(group * sizes.group, (group + 1) * sizes.group)
        pieces = [turned[:, channels, col * LANES : (col + 1) * LANES] for col in range(sizes.cols)]
        target[group] = jnp.concatenate(pieces, axis=1).astype(BF16)


def from_chunks(sizes, chunks):
    wide = [chunks[group].astype(F32) for group in range(sizes.groups)]
    for col in range(sizes.cols):
        pieces = [part[:, col * sizes.group : (col + 1) * sizes.group, :] for part in wide]
        yield col, jnp.concatenate(pieces, axis=1).reshape(2 * sizes.half, LANES).T


def chunk_loader(sizes, ref):
    def load(channel):
        pieces = [
            ref[pl.ds(col * sizes.group + channel, sizes.devices, stride=sizes.chunk), :]
            for col in range(sizes.cols)
        ]
        return jnp.concatenate(pieces, axis=0)

    return load


def chunk_storer(sizes, ref):
    def store(channel, values):
        for col in range(sizes.cols):
            ref[pl.ds(col * sizes.group + channel, sizes.devices, stride=sizes.chunk), :] = values[
                col * sizes.devices : (col + 1) * sizes.devices
            ]

    return store


def pooled_taps(taps):
    lane = lax.broadcasted_iota(jnp.int32, taps.shape, 2)
    zero = jnp.zeros_like(taps[:1])
    after = pltpu.roll(taps, LANES - 1, 2)
    before = pltpu.roll(taps, 1, 2)
    after = jnp.where(lane == LANES - 1, jnp.concatenate([after[1:], zero], axis=0), after)
    before = jnp.where(lane == 0, jnp.concatenate([zero, before[:-1]], axis=0), before)
    return (before + taps + after) / 3.0


def live_mask(shape, lengths):
    tap = lax.broadcasted_iota(jnp.int32, shape, 0) * LANES + lax.broadcasted_iota(
        jnp.int32, shape, 2
    )
    return (tap < lengths[None]).astype(F32)


VALUE, GATE, OUT, UP, DOWN = range(5)
ACT, HID = range(2)
PIECES = 4
ACROSS, INWARD, OUTWARD = range(3)
V, G, O, U0, U1, U2, U3, D0, D1, D2, D3, S = range(12)
TOPS = [lambda n: (1, 2)]
LOW = [lambda n: (2,)]
SPREAD_OUT = LOW + [lambda n: Line(ACROSS, 1, 2), lambda n: Line(OUTWARD, 1, 2)]
BRING_IN = [lambda n: Line(INWARD, 1, 2), lambda n: Line(ACROSS, 1, 2)] + LOW
X, Y, CORE = [lambda n: (0,)], [lambda n: (n - 2,)], [lambda n: (n - 1,)]
PLANE = [lambda n: (0, n - 2)]
GATHER_PHASES = {
    V: TOPS + PLANE + CORE,
    G: SPREAD_OUT + Y + X + CORE,
    O: SPREAD_OUT + Y + X + CORE,
    U0: SPREAD_OUT + Y + CORE,
    D0: SPREAD_OUT + Y + CORE,
    U1: SPREAD_OUT + Y + CORE,
    D1: Y + SPREAD_OUT + CORE,
    U2: Y + SPREAD_OUT + CORE,
    D2: SPREAD_OUT + Y + CORE,
    U3: SPREAD_OUT + Y + CORE,
    D3: SPREAD_OUT + Y + CORE,
}
REDUCE_PHASES = {
    V: PLANE + TOPS,
    G: X + Y + BRING_IN,
    O: PLANE + BRING_IN,
    U0: BRING_IN + Y,
    D0: Y + BRING_IN,
    U1: Y + BRING_IN,
    D1: BRING_IN + Y,
    U2: Y + BRING_IN,
    D2: Y + BRING_IN,
    U3: Y + BRING_IN,
    D3: Y + BRING_IN,
}
SPREAD_PHASES = CORE + PLANE + TOPS


class Order:
    tokens = (D2, G, D0, U2, V, U0, O, D1, U3, D2, G, U2)
    norm = (O, U1, U0, D0, D3, V, D2)
    w_value = (G,)
    value = ()
    sent = (D0, U1, O)
    taps = (D2, G, D0, O, D3)
    kernel = (U3, U1, D1)
    arrive = ((G, U2), (), ())
    conv = ((U0,), (U1,), (D0, D3, D1))
    convolved = ()
    cotangent = ()
    turn = (O, U0)
    w_gate = (U3,)
    gate = (D1, G, D3, V, U1, D2, G, U2, O)
    mixed = (U3, U0)
    inner = ()
    w_out = ()
    residual = ()
    turn_near = ()
    w_tile = ((D1, D3, O), (), (), (D0,))
    near = ((U2,), (U3,), (U1,), ())
    wait_far = ((U2,), (U3,))
    far = ((), ())
    turn_far = ()
    far_back = (D2, D3, D1, U0, U2, U1)
    norm_back = ()
    sent_back = (G, D2, U0, D2)
    output = (D3, U3, U2)
    arrive_back = ((D0,), (U1,), ())
    conv_back = ((), (G,), (U3, D1))
    convolved_back = (G, O, U0)
    taps_back = (U1, U2)
    signal = (G, D0)
    input_back = ()
    first_back = (D1, V, O, D3, U2, U3, D0, U1)
    finish_output = (D2, D1, S, G, O, D3, U3)
    last = (V, U0, S, D3)
    finish_grad = (O, D0, G, S)
    taps_home = ()
    end = (U0, O, V, D2, D1)


VMEM_SPEC = pl.BlockSpec(memory_space=pltpu.VMEM)
ANY_SPEC = pl.BlockSpec(memory_space=pl.ANY)
GELU_SCALE = math.sqrt(2.0 / math.pi)
GELU_CUBE = 0.044715


def dot_nt(left, right):
    return lax.dot_general(left, right, (((1,), (1,)), ((), ())), preferred_element_type=F32)


def norm(values):
    center = jnp.mean(values, axis=-1, keepdims=True)
    shifted = values - center
    scale = lax.rsqrt(jnp.mean(shifted * shifted, axis=-1, keepdims=True) + EPSILON)
    return shifted * scale, scale


def norm_back(grad_rows, normed, scale, gain):
    scaled = grad_rows * gain
    plain = jnp.mean(scaled, axis=-1, keepdims=True)
    cross = jnp.mean(scaled * normed, axis=-1, keepdims=True)
    return scale * (scaled - plain - normed * cross)


class Part:
    def __init__(self, weight, piece, dims, at):
        self.weight, self.piece, self.at = weight, piece, at
        self.dims = tuple(range(dims)) if piece is None else tuple(range(1, dims))
        self.gather = tuple(phase(dims) for phase in GATHER_PHASES[at])
        self.reduce = tuple(phase(dims) for phase in REDUCE_PHASES[at])


def most(phases):
    return max(len(flips_of(step)) for step in phases)


class Plan:
    def __init__(self, sizes):
        self.sizes = sizes
        here, channels, half = sizes.here, sizes.channels, sizes.half
        width = 2 * half
        self.width = width
        dims = 1 + len(bit_sizes(sizes.freq_count))
        self.dims = dims
        self.rows = rows = width // sizes.freq_count
        self.parts = [Part(weight, None, dims, weight) for weight in (VALUE, GATE, OUT)]
        for weight in (UP, DOWN):
            for piece in range(PIECES):
                self.parts.append(Part(weight, piece, dims, len(self.parts)))
        self.spread = tuple(phase(dims) for phase in SPREAD_PHASES)
        groups = [self.spread] + [p.gather for p in self.parts] + [p.reduce for p in self.parts]
        self.partners = sorted(
            {flipped for phases in groups for step in phases for flipped in flips_of(step) if 0 in flipped}
        )

        def vmem(kind, *shape):
            return pltpu.VMEM(shape, kind)

        def sems(*shape):
            return pltpu.SemaphoreType.DMA(shape)

        def weights(shape_of_narrow, shape_of_wide):
            shapes = [shape_of_narrow] * 3 + [(PIECES,) + shape_of_wide] * 2
            return [vmem(BF16, *shape, rows, half) for shape in shapes]

        def rows_of(kind, *lead):
            return vmem(kind, *lead, here, width)

        def turned(tokens):
            return vmem(BF16, width // (2 * rows), 2, rows, tokens)

        def turned_half(tokens):
            return vmem(BF16, width // (2 * rows), rows, tokens)

        def halves():
            return vmem(BF16, 2, here, half)

        def tiles():
            return vmem(BF16, PIECES, 2, 2 * here, half)

        def chunks():
            return vmem(BF16, sizes.groups, sizes.devices, sizes.chunk, LANES)

        def spectra(kind):
            return [vmem(kind, sizes.group_rows, 2 * LANES) for _ in range(sizes.groups)]

        def wide():
            return [vmem(F32, sizes.devices * sizes.chunk, LANES) for _ in range(sizes.groups)]

        taps = (sizes.tap_rows, channels, LANES)
        flat_taps = (sizes.tap_rows * channels, LANES)
        gain_rows = 2 * width // LANES + 4
        scratch = dict(
            x_buf=halves(),
            g_buf=vmem(BF16, 2, 2, here, half),
            gains=[[vmem(F32, half) for _ in range(2)] for _ in range(2)],
            lengths=vmem(jnp.int32, half),
            turned=vmem(F32, half, 8),
            weights=weights((2,) * dims, (2,) * (dims - 1)),
            grads=weights((2,) * (dims - 1), (2,) * (dims - 2)),
            landings=[
                [vmem(BF16, *shape) for shape in landing_shapes(part.reduce, part.dims[:-1], rows, half)]
                for part in self.parts
            ],
            results=[vmem(F32, rows, half) for _ in self.parts],
            part_sems=[
                (sems(max(most(p.gather), most(p.reduce))), sems(slots(p.gather)), sems(slots(p.reduce)))
                for p in self.parts
            ],
            kernel_spec=spectra(F32),
            value_spec=spectra(F32),
            grad_spec=spectra(F32),
            inner_into=spectra(BF16),
            inner_from=spectra(F32),
            inner_taps=spectra(F32),
            wide_in=wide(),
            wide_out=wide(),
            taps=vmem(F32, *taps),
            tap_grad=vmem(F32, *taps),
            tap_wide=vmem(F32, *flat_taps),
            sent=chunks(),
            sent_back=chunks(),
            landed=[chunks() for _ in range(4)],
            move_sems=[[sems(2) for _ in range(sizes.groups)] for _ in range(4)],
            tap_sems=[sems(2) for _ in range(2)],
            normed1=rows_of(F32),
            gate=rows_of(F32),
            mixed=rows_of(F32),
            residual=rows_of(F32),
            normed2=rows_of(F32),
            grad_res=rows_of(F32),
            rows=rows_of(F32),
            out_sum=rows_of(F32, 2),
            in2_sum=rows_of(F32, 2),
            scale1=vmem(F32, here, 1),
            scale2=vmem(F32, here, 1),
            input1=rows_of(BF16),
            branch_rows=rows_of(BF16),
            in2_send=rows_of(BF16),
            in2_land=rows_of(BF16),
            input2=rows_of(BF16, 2),
            grad_rows=rows_of(BF16, 2),
            t_input1=(turned(here), turned_half(here)),
            t_branch=(turned(here), turned_half(here)),
            t_input2=(turned(2 * here), turned_half(2 * here)),
            t_grad=(turned(2 * here), turned_half(2 * here)),
            inner_rows=(halves(), halves()),
            signal_rows=(halves(), halves()),
            gate_rows=(halves(), halves()),
            tiles=(tiles(), tiles()),
            tile_sems=sems(2, 2, PIECES),
            twin_sems=sems(2, 7),
            gain_total=vmem(F32, len(self.spread) + 1, gain_rows, LANES),
            gain_land=vmem(F32, slots(self.spread), gain_rows, LANES),
            gain_sems=(sems(most(self.spread)), sems(slots(self.spread))),
            out_send=halves(),
            out_land=halves(),
            gin_send=vmem(BF16, here, half),
            gin_land=vmem(BF16, here, half),
            swap_sems=sems(2, 10),
            local=sems(6 + len(self.parts)),
            v_output=halves(),
            v_grad_input=vmem(F32, 2, here, half),
            v_grad_kernel=vmem(F32, half, LANES),
        )
        self.scratch, self.tree = jax.tree.flatten(
            scratch, is_leaf=lambda leaf: not isinstance(leaf, (dict, list, tuple))
        )


def row_tiles(count, body, tile=64):
    def one(step, carry):
        body(pl.ds(pl.multiple_of(step * tile, tile), tile))
        return carry

    lax.fori_loop(0, count // tile, one, 0)


def block_kernel(plan, tokens, cotangent, first_gain, second_gain, lengths, raw_kernel, *refs):
    shards, refs = refs[:5], refs[5:]
    into, outof, taps_into, taps_outof, turn, ahead, behind = refs[:7]
    output, grad_input, *weight_grads = refs[7:14]
    gain_sums, grad_kernel = refs[14:16]
    k = types.SimpleNamespace(**jax.tree.unflatten(plan.tree, refs[16:]))
    sizes = plan.sizes
    here, half, width, channels = sizes.here, sizes.half, plan.width, sizes.channels
    place = Place(sizes.freq_count)
    chan, core = place.chan, place.core
    twin = place.other((plan.dims - 1,))
    across = place.other((0,))
    me = chan * sizes.freq_count + place.freq

    def whole(weight, lead):
        return k.weights[weight][lead].reshape(width, half)

    def of_chan(values):
        return jnp.where(chan == 0, values[:, :half], values[:, half:])

    def of_other_chan(values):
        return jnp.where(chan == 0, values[:, half:], values[:, :half])

    leaving = []

    def leave(source, target):
        leaving.append(pltpu.make_async_copy(source, target, k.local.at[len(leaving)]))
        leaving[-1].start()

    own = []
    for part in plan.parts:
        target, source = k.weights[part.weight], shards[part.weight]
        if part.piece is not None:
            target, source = target.at[part.piece], source.at[:, pl.ds(part.piece * half, half)]
        target = target.at[tuple(place.coords[dim] for dim in part.dims)]
        own.append(pltpu.make_async_copy(source, target, k.local.at[part.at]))
    my_channels = pl.ds(pl.multiple_of(place.freq * channels, 8), channels)
    for source, target in (
        (tokens.at[chan], k.x_buf.at[chan]),
        (cotangent, k.g_buf.at[chan]),
        (raw_kernel.at[my_channels], k.taps.at[place.freq]),
        (first_gain, k.gains[0][0]),
        (second_gain, k.gains[0][1]),
        (lengths, k.lengths),
    ):
        own.append(pltpu.make_async_copy(source, target, k.local.at[len(own)]))
    for copy in own:
        copy.start()
    own_tokens, own_cotangent, own_taps, *own_rows = own[len(plan.parts) :]
    barrier = pltpu.get_barrier_semaphore()
    for flipped in plan.partners:
        pl.semaphore_signal(barrier, inc=1, device_id=place.other(flipped), device_id_type=MESH)

    def greet(step, carry):
        peer = (lax.rem(place.freq + step, sizes.freq_count), chan)
        pl.semaphore_signal(barrier, inc=1, device_id=peer, device_id_type=MESH)
        return carry

    lax.fori_loop(1, sizes.freq_count, greet, 0, unroll=True)
    pl.semaphore_wait(barrier, len(plan.partners) + sizes.freq_count - 1)

    def swap(at, source, target):
        copy = remote(source, target, k.swap_sems.at[0, at], k.swap_sems.at[1, at], across)
        copy.start()
        return copy

    moving = {}
    for part in plan.parts:
        buffer = k.weights[part.weight]
        moving[part.at] = Gather(
            place,
            buffer if part.piece is None else buffer.at[part.piece],
            part.dims,
            part.gather,
            k.part_sems[part.at][0],
            k.part_sems[part.at][1],
            own[part.at].wait,
        )

    def ahead_of(names):
        for name in names:
            moving[name].go()

    def all_to_all(move, group, source):
        target = k.landed[move]
        exchange = Exchange(
            sizes.devices,
            me,
            lambda other: (lax.rem(other, sizes.freq_count), other // sizes.freq_count),
            lambda other: source.at[group, other],
            lambda other: target.at[group, other],
            source.at[group, pl.ds(0, sizes.devices - 1)],
            target.at[group, pl.ds(0, sizes.devices - 1)],
            k.move_sems[move][group],
        )
        exchange.start()
        target[group, me] = source[group, me]
        return exchange

    def tap_rows(ref, index):
        return ref.at[pl.ds(pl.multiple_of(index * channels, 8), channels)]

    swap_tokens = swap(0, tokens.at[1 - chan], k.x_buf.at[chan])
    swap_gains = [swap(at, ref, k.gains[1][at - 8]) for at, ref in ((8, first_gain), (9, second_gain))]
    moving[V].go()
    others = sizes.freq_count - 1
    tap_move = Exchange(
        sizes.freq_count,
        place.freq,
        lambda other: (other, chan),
        lambda other: tap_rows(raw_kernel, other),
        lambda other: k.taps.at[other],
        raw_kernel.at[pl.ds(0, others * channels)],
        k.taps.at[pl.ds(0, others)],
        k.tap_sems[0],
    )
    tap_move.start()
    ahead_of(Order.tokens)
    swap_tokens.wait()
    own_tokens.wait()
    for copy in swap_gains + own_rows:
        copy.wait()

    def gain_row(row):
        near, far = k.gains[0][row][...][None], k.gains[1][row][...][None]
        return jnp.concatenate([jnp.where(chan == 0, near, far), jnp.where(chan == 0, far, near)], axis=1)

    first_gain, second_gain = gain_row(0), gain_row(1)

    def first_norm(at):
        rows = jnp.concatenate([k.x_buf[0, at, :], k.x_buf[1, at, :]], axis=1).astype(F32)
        normed, scale = norm(rows)
        k.normed1[at, :] = normed
        k.scale1[at, :] = scale
        k.input1[at, :] = (normed * first_gain).astype(BF16)

    ahead_of(Order.norm)
    row_tiles(here, first_norm)

    def turn_rows(source, target, columns=slice(None)):
        turned = source[...].astype(F32).T.astype(BF16)
        target[:, :, :, columns] = turned.reshape(target.shape[:-1] + (here,))

    arriving = {}

    def share(at, source, target):
        copy = remote(source, target, k.twin_sems.at[0, at], k.twin_sems.at[1, at], twin)
        copy.start()
        arriving[id(target)] = copy

    def share_turned(at, pair):
        share(at, pair[0].at[:, 1 - core], pair[1])

    def need(target):
        if id(target) in arriving:
            arriving.pop(id(target)).wait()

    turn_rows(k.input1, k.t_input1[0])
    share_turned(0, k.t_input1)
    ahead_of(Order.w_value)
    moving[V].finish()

    ahead_of(Order.value)
    for c in range(2):
        k.rows[:, c * half : (c + 1) * half] = dot(k.input1[...], whole(VALUE, c))
    to_chunks(sizes, k.rows[...], k.sent)
    moves = [all_to_all(0, group, k.sent) for group in range(sizes.groups)]
    swap_cotangent = swap(2, cotangent, k.g_buf.at[chan])
    ahead_of(Order.sent)
    ahead_of(Order.taps)
    tap_move.wait()
    own_taps.wait()
    k.turned[...] = jnp.broadcast_to(k.lengths[...].astype(F32)[None], (8, half)).T
    live = live_mask(k.taps.shape, k.turned[my_channels, 0:1])
    pooled = pooled_taps(k.taps[...])
    shrunk = (pooled - THRESH * jnp.tanh(pooled / THRESH)) * live
    k.tap_wide[...] = shrunk.reshape(sizes.tap_rows * channels, LANES)
    ahead_of(Order.kernel)

    def tap_load(group):
        return lambda c: k.tap_wide[pl.ds(group * sizes.group + c, sizes.tap_rows, stride=channels), :]

    for group in range(sizes.groups):
        spectrum_into(
            sizes, tap_load(group), taps_into, turn, ahead, k.inner_into[group], k.kernel_spec[group]
        )

    def spectrum_of(move, group, spectra):
        flat = (sizes.devices * sizes.chunk, LANES)
        k.wide_in[group][...] = k.landed[move][group].astype(F32).reshape(flat)
        spectrum_into(
            sizes, chunk_loader(sizes, k.wide_in[group]), into, turn, ahead, k.inner_into[group], spectra[group]
        )

    def chunks_from(group, product):
        signal_from(
            sizes, product, outof, turn, behind, k.inner_from[group], chunk_storer(sizes, k.wide_out[group])
        )
        k.sent_back[group] = k.wide_out[group][...].reshape(k.sent_back.shape[1:]).astype(BF16)

    moves_back = []
    for group in range(sizes.groups):
        ahead_of(Order.arrive[group])
        moves[group].wait()
        ahead_of(Order.conv[group])
        spectrum_of(0, group, k.value_spec)
        chunks_from(group, times(k.value_spec[group][...], k.kernel_spec[group][...], False))
        moves_back.append(all_to_all(1, group, k.sent_back))
    ahead_of(Order.convolved)
    ahead_of(Order.cotangent)
    swap_cotangent.wait()
    own_cotangent.wait()
    ahead_of(Order.turn)
    for which, seq in ((0, chan), (1, 1 - chan)):
        k.grad_rows[which] = jnp.concatenate([k.g_buf[0, seq], k.g_buf[1, seq]], axis=1)
        turn_rows(k.grad_rows.at[which], k.t_grad[0], slice(which * here, (which + 1) * here))
    share_turned(2, k.t_grad)
    ahead_of(Order.w_gate)
    moving[G].finish()
    ahead_of(Order.gate)
    for c in range(2):
        k.gate[:, c * half : (c + 1) * half] = dot(k.input1[...], whole(GATE, c))
    ahead_of(Order.mixed)
    for move in moves_back:
        move.wait()

    ahead_of(Order.inner)
    for col, rows in from_chunks(sizes, k.landed[1]):
        k.mixed[col * LANES : (col + 1) * LANES, :] = rows

    def make_inner(at):
        gate = k.gate[at, :]
        inner = (k.mixed[at, :] * (gate * jax.nn.sigmoid(gate))).astype(BF16)
        k.inner_rows[0][0, at, :] = inner[:, :half]
        k.inner_rows[0][1, at, :] = inner[:, half:]

    row_tiles(here, make_inner)
    share(4, *k.inner_rows)
    ahead_of(Order.w_out)
    moving[O].finish()
    ahead_of(Order.residual)
    k.residual[...] = dot_nt(k.inner_rows[0][0], whole(OUT, 0)) + dot_nt(k.inner_rows[0][1], whole(OUT, 1))

    def second_norm(at):
        rows = jnp.concatenate([k.x_buf[0, at, :], k.x_buf[1, at, :]], axis=1).astype(F32)
        residual = k.residual[at, :] + rows
        normed, scale = norm(residual)
        k.residual[at, :] = residual
        k.normed2[at, :] = normed
        k.scale2[at, :] = scale
        k.input2[0, at, :] = (normed * second_gain).astype(BF16)

    row_tiles(here, second_norm)
    blocks = [pl.ds(at * (here // 2), here // 2) for at in range(2)]
    swap_input2 = [swap(3 + at, k.input2.at[0, rows], k.input2.at[1, rows]) for at, rows in enumerate(blocks)]
    ahead_of(Order.turn_near)
    turn_rows(k.input2.at[0], k.t_input2[0], slice(0, here))

    k.out_sum[...] = jnp.zeros_like(k.out_sum)
    k.in2_sum[...] = jnp.zeros_like(k.in2_sum)

    def feed_forward(which, piece, first, count):
        rows = pl.ds(first, count)
        stored = pl.ds(which * here + first, count)
        up = whole(UP, piece)
        hidden = dot(k.input2[which, rows, :], up)
        square = hidden * hidden
        bent = jnp.tanh(GELU_SCALE * hidden * (1.0 + GELU_CUBE * square))
        act = (0.5 * hidden * (1.0 + bent)).astype(BF16)
        slope = 0.5 * (1.0 + bent) + (0.5 * GELU_SCALE) * hidden * (1.0 - bent * bent) * (
            1.0 + 3.0 * GELU_CUBE * square
        )
        down = whole(DOWN, piece)
        grad = (dot(k.grad_rows[which, rows, :], down) * slope).astype(BF16)
        k.tiles[0][piece, ACT, stored, :] = act
        k.tiles[0][piece, HID, stored, :] = grad
        k.in2_sum[which, rows, :] += dot_nt(grad, up)
        k.out_sum[which, rows, :] += dot_nt(act, down)

    def tile_copy(which, piece):
        rows = pl.ds(which * here, here)
        return remote(
            k.tiles[0].at[piece, :, rows],
            k.tiles[1].at[piece, :, rows],
            k.tile_sems.at[0, which, piece],
            k.tile_sems.at[1, which, piece],
            twin,
        )

    for piece in range(PIECES):
        ahead_of(Order.w_tile[piece])
        moving[UP + piece].finish()
        moving[UP + PIECES + piece].finish()
        ahead_of(Order.near[piece])
        feed_forward(0, piece, 0, here)
        tile_copy(0, piece).start()
    swap_in2 = []
    for at, rows in enumerate(blocks):
        ahead_of(Order.wait_far[at])
        swap_input2[at].wait()
        ahead_of(Order.far[at])

        for piece in range(PIECES):
            feed_forward(1, piece, at * (here // 2), here // 2)
            if at == 1:
                tile_copy(1, piece).start()
        k.in2_send[rows, :] = k.in2_sum[1, rows, :].astype(BF16)
        swap_in2.append(swap(5 + at, k.in2_send.at[rows], k.in2_land.at[rows]))
    ahead_of(Order.turn_far)
    turn_rows(k.input2.at[1], k.t_input2[0], slice(here, 2 * here))
    share_turned(1, k.t_input2)

    def grads_of(weight, left, right, pick):
        mine, theirs = left[0][:, core], left[1][...]
        shape = (width // 2, mine.shape[-1])
        got = dot(
            jnp.concatenate([mine.reshape(shape), theirs.reshape(shape)], axis=1),
            jnp.concatenate([right[0][pick], right[1][pick]], axis=0),
        )
        pick = pick[0] if isinstance(pick, tuple) else pick
        k.grads[weight][pick] = got.astype(BF16).reshape((2,) * (plan.dims - 2) + (plan.rows, half))

    factors = {
        VALUE: (k.t_input1, k.signal_rows),
        GATE: (k.t_input1, k.gate_rows),
        OUT: (k.t_branch, k.inner_rows),
        UP: (k.t_input2, k.tiles),
        DOWN: (k.t_grad, k.tiles),
    }

    tiles_here = set()

    def prepare(part):
        left, right = factors[part.weight]
        need(left[1])
        if part.piece is None:
            need(right[1])
            for c in range(2):
                grads_of(part.weight, left, right, c)
        else:
            if part.piece not in tiles_here:
                tiles_here.add(part.piece)
                tile_copy(0, part.piece).wait()
                tile_copy(1, part.piece).wait()
            grads_of(part.weight, left, right, (part.piece, HID if part.weight == UP else ACT))

    def depart(part):
        target = weight_grads[part.weight]
        if part.piece is not None:
            target = target.at[:, pl.ds(part.piece * half, half)]
        leave(k.results[part.at], target)

    for part in plan.parts:
        total = k.grads[part.weight]
        moving[part.at] = Reduce(
            place,
            total if part.piece is None else total.at[part.piece],
            k.landings[part.at],
            part.dims[:-1],
            part.reduce,
            k.part_sems[part.at][0],
            k.part_sems[part.at][2],
            k.results[part.at],
            functools.partial(prepare, part),
            functools.partial(depart, part),
        )
    ahead_of(Order.far_back)
    for copy in swap_in2:
        copy.wait()

    k.gain_total[0] = jnp.zeros_like(k.gain_total[0])

    def add_gain(row, sums):
        for at in range(width // LANES):
            base = row * (width // LANES) + at
            k.gain_total[0, base : base + 1, :] += sums[:, at * LANES : (at + 1) * LANES]

    def second_back(at):
        grad = k.in2_sum[0, at, :] + k.in2_land[at, :].astype(F32)
        normed = k.normed2[at, :]
        add_gain(1, jnp.sum(grad * normed, axis=0, keepdims=True))
        result = k.grad_rows[0, at, :].astype(F32) + norm_back(
            grad, normed, k.scale2[at, :], second_gain
        )
        k.grad_res[at, :] = result
        k.branch_rows[at, :] = result.astype(BF16)

    ahead_of(Order.norm_back)
    row_tiles(here, second_back)
    for c in range(2):
        k.rows[:, c * half : (c + 1) * half] = dot(k.branch_rows[...], whole(OUT, c))

    def gate_back(at):
        gate = k.gate[at, :]
        grad = k.rows[at, :]
        sig = jax.nn.sigmoid(gate)
        rows = (grad * k.mixed[at, :] * (sig * (1.0 + gate * (1.0 - sig)))).astype(BF16)
        k.gate_rows[0][0, at, :] = rows[:, :half]
        k.gate_rows[0][1, at, :] = rows[:, half:]
        k.normed2[at, :] = grad * (gate * sig)

    row_tiles(here, gate_back)
    to_chunks(sizes, k.normed2[...], k.sent)
    moves = [all_to_all(2, group, k.sent) for group in range(sizes.groups)]
    share(6, *k.gate_rows)
    ahead_of(Order.sent_back)
    turn_rows(k.branch_rows, k.t_branch[0])
    share_turned(3, k.t_branch)
    ahead_of(Order.output)

    def make_output(at):
        near = k.residual[at, :] + k.out_sum[0, at, :]
        far = k.out_sum[1, at, :]
        k.out_send[0, at, :] = of_other_chan(near).astype(BF16)
        k.out_send[1, at, :] = of_other_chan(far).astype(BF16)

    row_tiles(here, make_output)
    swap_out = swap(7, k.out_send, k.out_land)

    moves_back = []
    for group in range(sizes.groups):
        ahead_of(Order.arrive_back[group])
        moves[group].wait()
        ahead_of(Order.conv_back[group])
        spectrum_of(2, group, k.grad_spec)
        chunks_from(group, times(k.grad_spec[group][...], k.kernel_spec[group][...], True))
        moves_back.append(all_to_all(3, group, k.sent_back))
    ahead_of(Order.convolved_back)

    def tap_store(group):
        def store(channel, values):
            k.tap_wide[pl.ds(group * sizes.group + channel, sizes.tap_rows, stride=channels), :] = values

        return store

    ahead_of(Order.taps_back)
    for group in range(sizes.groups):
        signal_from(
            sizes,
            times(k.grad_spec[group][...], k.value_spec[group][...], True),
            taps_outof, turn, behind, k.inner_taps[group], tap_store(group),
        )
    pooled = pooled_taps(k.taps[...])
    bent = jnp.tanh(pooled / THRESH)
    k.tap_grad[...] = pooled_taps(k.tap_wide[...].reshape(pooled.shape) * live * bent * bent)
    tap_back = Exchange(
        sizes.freq_count,
        place.freq,
        lambda other: (other, chan),
        lambda other: k.tap_grad.at[other],
        lambda other: tap_rows(k.v_grad_kernel, other),
        k.tap_grad.at[pl.ds(0, others)],
        k.v_grad_kernel.at[pl.ds(0, others * channels)],
        k.tap_sems[1],
    )
    tap_back.start()
    k.v_grad_kernel[my_channels] = k.tap_grad[place.freq]
    ahead_of(Order.signal)
    for move in moves_back:
        move.wait()

    ahead_of(Order.input_back)
    for col, rows in from_chunks(sizes, k.landed[3]):
        rows = rows.astype(BF16)
        for c in range(2):
            k.signal_rows[0][c, col * LANES : (col + 1) * LANES, :] = rows[:, c * half : (c + 1) * half]
    share(5, *k.signal_rows)
    k.rows[...] = sum(
        dot_nt(rows[0][c], whole(weight, c))
        for rows, weight in ((k.signal_rows, VALUE), (k.gate_rows, GATE))
        for c in range(2)
    )
    ahead_of(Order.first_back)

    def first_back(at):
        grad = k.rows[at, :]
        normed = k.normed1[at, :]
        add_gain(0, jnp.sum(grad * normed, axis=0, keepdims=True))
        result = k.grad_res[at, :] + norm_back(grad, normed, k.scale1[at, :], first_gain)
        k.gin_send[at, :] = of_other_chan(result).astype(BF16)
        k.v_grad_input[chan, at, :] = of_chan(result)

    row_tiles(here, first_back)
    swap_gin = swap(1, k.gin_send, k.gin_land)
    spread = Spread(place, k.gain_total, k.gain_land, plan.spread, *k.gain_sems)
    moving[S] = spread
    spread.go()
    ahead_of(Order.finish_output)
    swap_out.wait()

    def finish_output(at):
        near = of_chan(k.residual[at, :] + k.out_sum[0, at, :]) + k.out_land[1, at, :].astype(F32)
        far = of_chan(k.out_sum[1, at, :]) + k.out_land[0, at, :].astype(F32)
        k.v_output[chan, at, :] = near.astype(BF16)
        k.v_output[1 - chan, at, :] = far.astype(BF16)

    row_tiles(here, finish_output)
    leave(k.v_output, output)
    ahead_of(Order.last)
    swap_gin.wait()
    ahead_of(Order.finish_grad)
    k.v_grad_input[1 - chan] = k.gin_land[...].astype(F32)
    leave(k.v_grad_input, grad_input)
    ahead_of(Order.taps_home)
    tap_back.wait()
    leave(k.v_grad_kernel, grad_kernel)
    ahead_of(Order.end)
    for mover in moving.values():
        mover.finish()
    leave(k.gain_total.at[len(plan.spread)], gain_sums)
    for copy in leaving:
        copy.wait()


def settle_kernel(count, channels, freq_count, *refs):
    sources, sums, refs = refs[:count], refs[count], refs[count + 1 :]
    targets, gains, refs = refs[:count], refs[count : count + 2], refs[count + 2 :]
    held, sems = refs[:count], refs[-1]
    coming = [pltpu.make_async_copy(sources[n], held[n], sems.at[0, n]) for n in range(count)]
    going = [pltpu.make_async_copy(held[n], targets[n], sems.at[1, n]) for n in range(count)]
    for copy in coming:
        copy.start()
    tiles = 2 * channels * freq_count // LANES
    mine = (lax.axis_index("chan") * freq_count + lax.axis_index("freq")) * channels
    lane = lax.broadcasted_iota(jnp.int32, (channels, LANES), 1)
    feature = mine + lax.broadcasted_iota(jnp.int32, (channels, LANES), 0)
    for row, gain in enumerate(gains):
        total = jnp.zeros((channels, LANES), F32)
        for tile in range(tiles):
            at = row * tiles + tile
            total = total + jnp.where(lane + tile * LANES == feature, sums[at : at + 1, :], 0.0)
        gain[...] = jnp.sum(total.T, axis=0, keepdims=True)
    for arrive, depart in zip(coming, going):
        arrive.wait()
        depart.start()
    for copy in going:
        copy.wait()


def settle(arrays, sums, sizes):
    out = [jax.ShapeDtypeStruct(a.shape, a.dtype) for a in arrays]
    out += [jax.ShapeDtypeStruct((1, sizes.channels), F32)] * 2
    return pl.pallas_call(
        functools.partial(settle_kernel, len(arrays), sizes.channels, sizes.freq_count),
        out_shape=out,
        in_specs=[ANY_SPEC] * len(arrays) + [VMEM_SPEC],
        out_specs=[ANY_SPEC] * len(arrays) + [VMEM_SPEC] * 2,
        scratch_shapes=[pltpu.VMEM(a.shape, a.dtype) for a in arrays]
        + [pltpu.SemaphoreType.DMA((2, len(arrays)))],
        name="settle",
    )(*arrays, sums)


def one_sequence(
    tokens, cotangent, first_gain, second_gain, w_value, w_gate, w_out, w_up, w_down, raw_kernel, lengths
):
    freq_count = lax.axis_size("freq")
    _, here, half = tokens.shape
    sizes = Sizes(freq_count, here, half, raw_kernel.shape[1] * freq_count)
    plan = Plan(sizes)
    shards = (w_value, w_gate, w_out, w_up, w_down)
    tables = conv_tables(sizes)
    out_shape = (
        [jax.ShapeDtypeStruct((2, here, half), BF16), jax.ShapeDtypeStruct((2, here, half), F32)]
        + [jax.ShapeDtypeStruct(w.shape, F32) for w in shards]
        + [
            jax.ShapeDtypeStruct((4 * half // LANES + 4, LANES), F32),
            jax.ShapeDtypeStruct(raw_kernel.shape, F32),
        ]
    )
    results = pl.pallas_call(
        functools.partial(block_kernel, plan),
        out_shape=out_shape,
        in_specs=[ANY_SPEC] * 11 + [VMEM_SPEC] * len(tables),
        out_specs=[ANY_SPEC] * len(out_shape),
        scratch_shapes=plan.scratch,
        compiler_params=pltpu.CompilerParams(
            collective_id=0, has_side_effects=True, vmem_limit_bytes=60 << 20
        ),
        name="block",
    )(tokens, cotangent, first_gain, second_gain, lengths, raw_kernel, *shards, *tables)
    *arrays, gain_sums, grad_kernel = results
    *arrays, grad_kernel, first_grad, second_grad = settle([*arrays, grad_kernel], gain_sums, sizes)
    return (*arrays, first_grad.T, second_grad.T, grad_kernel)


def fits(mesh):
    freq_count = mesh.shape["freq"]
    return lambda tokens, w_value, w_up, raw_kernel: (
        mesh.shape["chan"] == 2
        and tokens.shape[0] == 2
        and freq_count == 16
        and w_value.shape[0] % (16 * freq_count) == 0
        and w_value.shape[1] % (16 * freq_count) == 0
        and w_value.shape[1] % 256 == 0
        and w_up.shape[1] == PIECES * w_value.shape[1]
        and tokens.shape[1] % (2 * LANES * freq_count) == 0
        and raw_kernel.shape[1] == LANES * freq_count
        and (tokens.shape[1] + raw_kernel.shape[1]) // LANES % 16 == 0
    )


D = 768
SEQ_MB = 1
MICRO = 2


HIGHEST = lax.Precision.HIGHEST


def circle(height, breadth, period):
    first_index = lax.broadcasted_iota(jnp.int32, (height, breadth), 0)
    second_index = lax.broadcasted_iota(jnp.int32, (height, breadth), 1)
    phase_angle = (first_index * second_index % period).astype(jnp.float32) * (
        2.0 * math.pi / period
    )
    return (jnp.cos(phase_angle), jnp.sin(phase_angle))


def make_tables(padded_size):
    inner_size = 128
    outer_size = padded_size // inner_size
    outer_cos, outer_sin = circle(outer_size, outer_size, outer_size)
    inner_cos, inner_sin = circle(inner_size, inner_size, inner_size)
    twist_cos, twist_sin = circle(outer_size, inner_size, padded_size)
    return (outer_cos, outer_sin, inner_cos, inner_sin, twist_cos, twist_sin)


def spectrum(signal, padded_size, tables):
    outer_cos, outer_sin, inner_cos, inner_sin, twist_cos, twist_sin = tables
    inner_size = inner_cos.shape[0]
    pad_width = [(0, 0)] * (signal.ndim - 1) + [(0, padded_size - signal.shape[-1])]
    grid_values = jnp.pad(signal, pad_width).reshape(
        signal.shape[:-1] + (padded_size // inner_size, inner_size)
    )
    part_real = jnp.einsum("...ab,fa->...fb", grid_values, outer_cos, precision=HIGHEST)
    part_imag = -jnp.einsum("...ab,fa->...fb", grid_values, outer_sin, precision=HIGHEST)
    turned_real = part_real * twist_cos + part_imag * twist_sin
    turned_imag = part_imag * twist_cos - part_real * twist_sin
    spec_real = jnp.einsum(
        "...fb,bg->...fg", turned_real, inner_cos, precision=HIGHEST
    ) + jnp.einsum("...fb,bg->...fg", turned_imag, inner_sin, precision=HIGHEST)
    spec_imag = jnp.einsum(
        "...fb,bg->...fg", turned_imag, inner_cos, precision=HIGHEST
    ) - jnp.einsum("...fb,bg->...fg", turned_real, inner_sin, precision=HIGHEST)
    return (spec_real, spec_imag)


def signal_of(spec_real, spec_imag, keep_count, tables):
    outer_cos, outer_sin, inner_cos, inner_sin, twist_cos, twist_sin = tables
    padded_size = spec_real.shape[-1] * spec_real.shape[-2]
    back_real = jnp.einsum("...fg,bg->...fb", spec_real, inner_cos, precision=HIGHEST) - jnp.einsum(
        "...fg,bg->...fb", spec_imag, inner_sin, precision=HIGHEST
    )
    back_imag = jnp.einsum("...fg,bg->...fb", spec_imag, inner_cos, precision=HIGHEST) + jnp.einsum(
        "...fg,bg->...fb", spec_real, inner_sin, precision=HIGHEST
    )
    turned_real = back_real * twist_cos - back_imag * twist_sin
    turned_imag = back_imag * twist_cos + back_real * twist_sin
    grid_values = (
        jnp.einsum("...fb,af->...ab", turned_real, outer_cos, precision=HIGHEST)
        - jnp.einsum("...fb,af->...ab", turned_imag, outer_sin, precision=HIGHEST)
    ) / padded_size
    flat_values = grid_values.reshape(grid_values.shape[:-2] + (padded_size,))
    return flat_values[..., :keep_count]


def shape_kernel(raw_taps, live_taps):
    padded = jnp.pad(raw_taps, ((0, 0), (1, 1)))
    pooled = (padded[:, :-2] + padded[:, 1:-1] + padded[:, 2:]) / 3.0
    return (pooled - THRESH * jnp.tanh(pooled / THRESH)) * live_taps


def row_norm(values):
    row_width = values.shape[-1] * lax.axis_size("chan")
    row_total, row_square = lax.psum(
        (jnp.sum(values, axis=-1), jnp.sum(values * values, axis=-1)), "chan"
    )
    center = row_total / row_width
    spread = row_square / row_width - center * center
    scale = lax.rsqrt(spread + EPSILON)[..., None]
    return ((values - center[..., None]) * scale, scale)


def row_back(grad_rows, normed, scale, gain_row):
    row_width = grad_rows.shape[-1] * lax.axis_size("chan")
    scaled = grad_rows * gain_row
    sum_plain, sum_cross = lax.psum(
        (jnp.sum(scaled, axis=-1), jnp.sum(scaled * normed, axis=-1)), "chan"
    )
    return scale * (
        scaled - sum_plain[..., None] / row_width - normed * sum_cross[..., None] / row_width
    )


def features(values):
    return lax.all_gather(values, "chan", axis=2, tiled=True)


def partial_sum(values):
    return lax.psum_scatter(
        values.astype(jnp.bfloat16), "chan", scatter_dimension=2, tiled=True
    ).astype(jnp.float32)


def to_channels(values):
    return lax.all_to_all(
        jnp.swapaxes(values, 1, 2), "freq", split_axis=1, concat_axis=2, tiled=True
    )


def to_tokens(values):
    arrived = lax.all_to_all(values, "freq", split_axis=2, concat_axis=1, tiled=True)
    return jnp.swapaxes(arrived, 1, 2)


def by_features(
    tokens,
    cotangent,
    first_gain,
    second_gain,
    w_value,
    w_gate,
    w_out,
    w_up,
    w_down,
    raw_kernel,
    lengths,
):
    full_value, full_gate, full_out, full_up, full_down = (
        lax.all_gather(w_value, "freq", axis=0, tiled=True),
        lax.all_gather(w_gate, "freq", axis=0, tiled=True),
        lax.all_gather(w_out, "freq", axis=0, tiled=True),
        lax.all_gather(w_up, "freq", axis=0, tiled=True),
        lax.all_gather(w_down, "freq", axis=0, tiled=True),
    )
    freq_count = lax.axis_size("freq")
    chan_width = tokens.shape[2]
    channels = chan_width // freq_count
    seq_length = tokens.shape[1] * freq_count
    padded_size = 2 * seq_length
    tables = make_tables(padded_size)
    kernel_rows = lax.all_to_all(raw_kernel, "freq", split_axis=0, concat_axis=1, tiled=True)
    tap_count = kernel_rows.shape[1]
    my_lengths = lax.dynamic_slice_in_dim(lengths, lax.axis_index("freq") * channels, channels)
    tap_index = lax.broadcasted_iota(jnp.int32, (channels, tap_count), 1)
    live_taps = (tap_index < my_lengths[:, None]).astype(jnp.float32)
    kernel, kernel_pull = jax.vjp(functools.partial(shape_kernel, live_taps=live_taps), kernel_rows)
    kernel_real, kernel_imag = spectrum(kernel, padded_size, tables)
    hidden_width = full_up.shape[1]
    shard_factor = 1
    totals = (
        jnp.zeros((D // shard_factor, chan_width), jnp.float32),
        jnp.zeros((D // shard_factor, chan_width), jnp.float32),
        jnp.zeros((D // shard_factor, chan_width), jnp.float32),
        jnp.zeros((D // shard_factor, hidden_width), jnp.float32),
        jnp.zeros((D // shard_factor, hidden_width), jnp.float32),
        jnp.zeros((chan_width // shard_factor, 1), jnp.float32),
        jnp.zeros((chan_width // shard_factor, 1), jnp.float32),
    )
    kernel_grad = jnp.zeros((channels, tap_count), jnp.float32)
    outputs = []
    input_grads = []
    for micro_index in range(MICRO):
        rows_here = tokens[micro_index * SEQ_MB : (micro_index + 1) * SEQ_MB].astype(jnp.float32)
        first_normed, first_scale = row_norm(rows_here)
        input1 = features((first_normed * first_gain).astype(jnp.bfloat16))
        value_low = jnp.einsum(
            "bld,de->ble", input1, full_value, preferred_element_type=jnp.float32
        ).astype(jnp.bfloat16)
        gate_proj = jnp.einsum("bld,de->ble", input1, full_gate, preferred_element_type=jnp.float32)
        signal = to_channels(value_low).astype(jnp.float32)
        signal_real, signal_imag = spectrum(signal, padded_size, tables)
        mixed = signal_of(
            signal_real * kernel_real - signal_imag * kernel_imag,
            signal_real * kernel_imag + signal_imag * kernel_real,
            seq_length,
            tables,
        )
        mixed_rows = to_tokens(mixed.astype(jnp.bfloat16)).astype(jnp.float32)
        gate_act, gate_pull = jax.vjp(jax.nn.silu, gate_proj)
        inner_low = (mixed_rows * gate_act).astype(jnp.bfloat16)
        residual = rows_here + partial_sum(
            jnp.einsum("ble,oe->blo", inner_low, full_out, preferred_element_type=jnp.float32)
        )
        second_normed, second_scale = row_norm(residual)
        input2 = features((second_normed * second_gain).astype(jnp.bfloat16))
        hidden = jnp.einsum("bld,df->blf", input2, full_up, preferred_element_type=jnp.float32)
        activated, act_pull = jax.vjp(jax.nn.gelu, hidden)
        act_low = activated.astype(jnp.bfloat16)
        result = residual + partial_sum(
            jnp.einsum("blf,of->blo", act_low, full_down, preferred_element_type=jnp.float32)
        )
        outputs.append(result.astype(jnp.bfloat16))
        grad_rows_out = cotangent[micro_index * SEQ_MB : (micro_index + 1) * SEQ_MB]
        grad_full = features(grad_rows_out)
        grad_act = jnp.einsum(
            "blo,of->blf", grad_full, full_down, preferred_element_type=jnp.float32
        )
        down_grad = jnp.einsum(
            "blo,blf->of", grad_full, act_low, preferred_element_type=jnp.float32
        )
        grad_hidden = act_pull(grad_act)[0].astype(jnp.bfloat16)
        up_grad = jnp.einsum("bld,blf->df", input2, grad_hidden, preferred_element_type=jnp.float32)
        grad_in2 = partial_sum(
            jnp.einsum("blf,df->bld", grad_hidden, full_up, preferred_element_type=jnp.float32)
        )
        second_grad = jnp.sum(grad_in2 * second_normed, axis=(0, 1))
        grad_residual = grad_rows_out.astype(jnp.float32) + row_back(
            grad_in2, second_normed, second_scale, second_gain
        )
        grad_branch = features(grad_residual.astype(jnp.bfloat16))
        grad_inner = jnp.einsum(
            "blo,oe->ble", grad_branch, full_out, preferred_element_type=jnp.float32
        )
        out_grad = jnp.einsum(
            "blo,ble->oe", grad_branch, inner_low, preferred_element_type=jnp.float32
        )
        grad_mixed = to_channels((grad_inner * gate_act).astype(jnp.bfloat16)).astype(jnp.float32)
        grad_real, grad_imag = spectrum(grad_mixed, padded_size, tables)
        grad_signal = signal_of(
            grad_real * kernel_real + grad_imag * kernel_imag,
            grad_imag * kernel_real - grad_real * kernel_imag,
            seq_length,
            tables,
        )
        kernel_grad = kernel_grad + jnp.sum(
            signal_of(
                grad_real * signal_real + grad_imag * signal_imag,
                grad_imag * signal_real - grad_real * signal_imag,
                tap_count,
                tables,
            ),
            axis=0,
        )
        grad_signal_rows = to_tokens(grad_signal.astype(jnp.bfloat16))
        grad_gate_rows = gate_pull(grad_inner * mixed_rows)[0].astype(jnp.bfloat16)
        value_grad = jnp.einsum(
            "bld,ble->de", input1, grad_signal_rows, preferred_element_type=jnp.float32
        )
        gate_grad = jnp.einsum(
            "bld,ble->de", input1, grad_gate_rows, preferred_element_type=jnp.float32
        )
        grad_in1 = partial_sum(
            jnp.einsum(
                "ble,de->bld", grad_signal_rows, full_value, preferred_element_type=jnp.float32
            )
            + jnp.einsum(
                "ble,de->bld", grad_gate_rows, full_gate, preferred_element_type=jnp.float32
            )
        )
        first_grad = jnp.sum(grad_in1 * first_normed, axis=(0, 1))
        input_grads.append(
            grad_residual + row_back(grad_in1, first_normed, first_scale, first_gain)
        )
        local_terms = (
            value_grad,
            gate_grad,
            out_grad,
            up_grad,
            down_grad,
            first_grad[:, None],
            second_grad[:, None],
        )
        totals = tuple((left + right for left, right in zip(totals, local_terms)))
    totals = lax.psum_scatter(totals, "freq", scatter_dimension=0, tiled=True)
    raw_grad = kernel_pull(kernel_grad)[0]
    grad_kernel = lax.all_to_all(raw_grad, "freq", split_axis=1, concat_axis=0, tiled=True)
    output = jnp.concatenate(outputs, axis=0)
    grad_input = jnp.concatenate(input_grads, axis=0)
    return (
        output,
        grad_input,
        totals[0],
        totals[1],
        totals[2],
        totals[3],
        totals[4],
        totals[5],
        totals[6],
        grad_kernel,
    )


def solution(mesh):
    specs = dict(
        mesh=mesh,
        in_specs=(
            P(None, "freq", "chan"),
            P(None, "freq", "chan"),
            P("chan"),
            P("chan"),
            P("freq", "chan"),
            P("freq", "chan"),
            P("freq", "chan"),
            P("freq", "chan"),
            P("freq", "chan"),
            P("chan", "freq"),
            P("chan"),
        ),
        out_specs=(
            P(None, "freq", "chan"),
            P(None, "freq", "chan"),
            P("freq", "chan"),
            P("freq", "chan"),
            P("freq", "chan"),
            P("freq", "chan"),
            P("freq", "chan"),
            P("freq", "chan"),
            P("freq", "chan"),
            P("chan", "freq"),
        ),
        check_vma=False,
    )

    def step(*args):
        whole = fits(mesh)(args[0], args[4], args[7], args[9])
        return jax.shard_map(one_sequence if whole else by_features, **specs)(*args)

    return step
```

```python
import functools
import math
import types

import jax
import jax.numpy as jnp
import numpy as np
from jax import lax
from jax.experimental import pallas as pl
from jax.experimental.pallas import tpu as pltpu
from jax.sharding import PartitionSpec as P

THRESH = 0.003
EPSILON = 1e-05
LANES = 128
MESH = pl.DeviceIdType.MESH
F32 = jnp.float32
BF16 = jnp.bfloat16


def bit_sizes(freq_count):
    return [1 << i for i in reversed(range(freq_count.bit_length() - 1))]


class Place:
    def __init__(self, freq_count):
        self.freq_count = freq_count
        self.freq = lax.axis_index("freq")
        self.chan = lax.axis_index("chan")
        self.bits = bit_sizes(freq_count)
        self.coords = [self.chan] + [lax.rem(self.freq // b, 2) for b in self.bits]
        self.dims = len(self.coords)
        self.core = self.coords[-1]

    def other(self, flipped):
        freq, chan = self.freq, self.chan
        for dim in flipped:
            if dim == 0:
                chan = 1 - chan
            else:
                bit = self.bits[dim - 1]
                freq = freq + bit - 2 * bit * self.coords[dim]
        return (freq, chan)


def flips(dims):
    return [
        tuple(dim for at, dim in enumerate(dims) if mask >> at & 1) for mask in range(1, 1 << len(dims))
    ]


def remote(source, target, send, recv, device):
    return pltpu.make_async_remote_copy(
        src_ref=source,
        dst_ref=target,
        send_sem=send,
        recv_sem=recv,
        device_id=device,
        device_id_type=MESH,
    )


class Line:
    def __init__(self, way, high, low):
        self.way, self.high, self.low = way, high, low

    def ends(self, place):
        middle = place.coords[self.high] + place.coords[self.low] == 1
        end = place.coords[self.high] + place.coords[self.low] != 1
        return {ACROSS: (middle, middle), INWARD: (end, middle), OUTWARD: (middle, end)}[self.way]

    def flipped(self):
        return (self.high, self.low) if self.way == ACROSS else (self.low,)


def when(condition, action):
    if condition is None:
        action()
    else:
        pl.when(condition)(action)


class Leg:
    def __init__(self, copy, ends=(None, None)):
        self.copy, self.ends = copy, ends

    def start(self):
        when(self.ends[0], self.copy.start)

    def wait(self):
        if self.ends[0] is None:
            self.copy.wait()
        else:
            when(self.ends[0], self.copy.wait_send)
            when(self.ends[1], self.copy.wait_recv)


def flips_of(phase):
    return [phase.flipped()] if isinstance(phase, Line) else flips(phase)


def is_outward(phase):
    return isinstance(phase, Line) and phase.way == OUTWARD


def slots(phases):
    return sum(len(flips_of(phase)) for phase in phases if not is_outward(phase))


def first_slot(phases, at):
    return slots(phases[:at]) - is_outward(phases[at])


class Gather:
    def __init__(self, place, buffer, dims, phases, send, recv, prepare):
        self.place, self.buffer, self.dims, self.phases = place, buffer, dims, phases
        self.send, self.recv, self.prepare = send, recv, prepare
        self.turn = 0

    def copies(self, phase):
        done, step = set(), self.phases[phase]
        for before in self.phases[:phase]:
            if not isinstance(before, Line):
                done.update(before)
            elif before.way == OUTWARD:
                done.update((before.high, before.low))
        index = [slice(None) if dim in done else self.place.coords[dim] for dim in self.dims]
        ends = (None, None)
        if isinstance(step, Line):
            ends = step.ends(self.place)
            if step.way == OUTWARD:
                index[self.dims.index(step.high)] = 1 - self.place.coords[step.high]
        region = self.buffer.at[tuple(index)]
        base = first_slot(self.phases, phase)
        return [
            Leg(
                remote(region, region, self.send.at[k], self.recv.at[base + k], self.place.other(flipped)), ends
            )
            for k, flipped in enumerate(flips_of(step))
        ]

    def go(self):
        if self.turn > len(self.phases):
            return
        if self.turn == 0:
            self.prepare()
        else:
            for copy in self.copies(self.turn - 1):
                copy.wait()
        if self.turn < len(self.phases):
            for copy in self.copies(self.turn):
                copy.start()
        self.turn += 1

    def finish(self):
        while self.turn <= len(self.phases):
            self.go()


class Once:
    def __init__(self, begin):
        self.begin, self.copy = begin, None

    def go(self):
        if self.copy is None:
            self.copy = self.begin()

    def finish(self):
        self.go()
        self.copy.wait()


class Reduce:
    def __init__(self, place, total, landing, dims, phases, send, recv, out, prepare, done):
        self.place, self.total, self.landing, self.dims = place, total, landing, dims
        self.phases, self.send, self.recv, self.out = phases, send, recv, out
        self.prepare, self.done = prepare, done
        self.turn = 0

    def region(self, phase, flipped):
        fixed, step = set(), self.phases[phase]
        for before in self.phases[:phase]:
            if not isinstance(before, Line):
                fixed.update(before)
            elif before.way == ACROSS:
                fixed.add(before.high)
        if not isinstance(step, Line):
            fixed.update(step)
        coords = self.place.coords
        index = [
            (1 - coords[dim] if dim in flipped else coords[dim]) if dim in fixed else slice(None)
            for dim in self.dims
        ]
        if isinstance(step, Line):
            mine = coords[step.high]
            keeps = step.way == ACROSS and not flipped
            index[self.dims.index(step.high)] = mine if keeps else 1 - mine
        return tuple(index)

    def copies(self, phase):
        step = self.phases[phase]
        base = first_slot(self.phases, phase)
        ends = step.ends(self.place) if isinstance(step, Line) else (None, None)
        return [
            Leg(
                remote(
                    self.total.at[self.region(phase, flipped)],
                    self.landing[phase].at[k],
                    self.send.at[k],
                    self.recv.at[base + k],
                    self.place.other(flipped),
                ),
                ends,
            )
            for k, flipped in enumerate(flips_of(step))
        ]

    def add(self, phase):
        kept = self.region(phase, ())
        free = [at for at, part in enumerate(kept) if isinstance(part, slice)]
        landing, step = self.landing[phase], self.phases[phase]

        def one(turn, carry):
            where, there = list(kept), []
            for at, dim in enumerate(free):
                bit = lax.rem(turn // (1 << (len(free) - 1 - at)), 2)
                where[dim] = bit
                there.append(bit)
            where, there = tuple(where), tuple(there)
            total = self.total[where].astype(F32)
            for k in range(len(flips_of(step))):
                total = total + landing[(k,) + there].astype(F32)
            if phase + 1 == len(self.phases):
                self.out[...] = total
            else:
                self.total[where] = total.astype(BF16)
            return carry

        def every():
            if free:
                lax.fori_loop(0, 1 << len(free), one, 0)
            else:
                one(0, 0)

        when(step.ends(self.place)[1] if isinstance(step, Line) else None, every)

    def go(self):
        if self.turn > len(self.phases):
            return
        if self.turn == 0:
            self.prepare()
        else:
            for copy in self.copies(self.turn - 1):
                copy.wait()
            self.add(self.turn - 1)
        if self.turn < len(self.phases):
            for copy in self.copies(self.turn):
                copy.start()
        else:
            self.done()
        self.turn += 1

    def finish(self):
        while self.turn <= len(self.phases):
            self.go()


def landing_shapes(phases, dims, rows, columns):
    shapes, free = [], len(dims)
    for step in phases:
        if isinstance(step, Line):
            free -= 0 if step.way == INWARD else 1
            shapes.append((1,) + (2,) * (free - (step.way == INWARD)) + (rows, columns))
        else:
            free -= len(step)
            shapes.append((len(flips(step)),) + (2,) * free + (rows, columns))
    return shapes


class Spread:
    def __init__(self, place, total, landing, phases, send, recv):
        self.place, self.total, self.landing, self.phases = place, total, landing, phases
        self.send, self.recv = send, recv
        self.turn = 0

    def copies(self, phase):
        base = sum(len(flips(dims)) for dims in self.phases[:phase])
        return base, [
            remote(
                self.total.at[phase],
                self.landing.at[base + k],
                self.send.at[k],
                self.recv.at[base + k],
                self.place.other(flipped),
            )
            for k, flipped in enumerate(flips(self.phases[phase]))
        ]

    def go(self):
        if self.turn > len(self.phases):
            return
        if self.turn:
            base, copies = self.copies(self.turn - 1)
            total = self.total[self.turn - 1]
            for k, copy in enumerate(copies):
                copy.wait()
                total = total + self.landing[base + k]
            self.total[self.turn] = total
        if self.turn < len(self.phases):
            for copy in self.copies(self.turn)[1]:
                copy.start()
        self.turn += 1

    def finish(self):
        while self.turn <= len(self.phases):
            self.go()


class Exchange:
    def __init__(self, count, me, device, source, target, all_sent, all_landed, sems):
        self.count, self.me, self.device = count, me, device
        self.source, self.target = source, target
        self.all_sent, self.all_landed, self.sems = all_sent, all_landed, sems

    def start(self):
        def one(step, carry):
            other = lax.rem(self.me + step, self.count)
            remote(
                self.source(other), self.target(self.me), self.sems.at[0], self.sems.at[1], self.device(other)
            ).start()
            return carry

        lax.fori_loop(1, self.count, one, 0, unroll=True)

    def wait(self):
        for part, sem in ((self.all_sent, self.sems.at[0]), (self.all_landed, self.sems.at[1])):
            pltpu.make_async_copy(part, part, sem).wait()


class Sizes:
    def __init__(self, freq_count, here, half, taps):
        self.freq_count = freq_count
        self.here = here
        self.half = half
        self.cols = here // LANES
        self.channels = half // freq_count
        self.group = LANES // freq_count
        self.groups = self.channels // self.group
        self.chunk = self.cols * self.group
        self.devices = 2 * freq_count
        self.tap_rows = taps // LANES
        self.rows = here * freq_count // LANES + self.tap_rows
        self.size = self.rows * LANES
        self.group_rows = self.group * self.rows


def conv_tables(sizes):
    rows, size = sizes.rows, sizes.size
    f = np.arange(rows)
    a_of, imag = [], []
    for col in range(sizes.cols):
        for seq in range(2):
            for block in range(sizes.freq_count):
                a_of.append(block * sizes.cols + col)
                imag.append(seq)
    a_of, imag = np.array(a_of), np.array(imag)
    angle = 2 * np.pi * np.outer(f, a_of) / rows
    cos, sin = np.cos(angle), np.sin(angle)
    into = np.concatenate([np.where(imag, sin, cos), np.where(imag, cos, -sin)], axis=0)
    outof = into.T / size
    angle = 2 * np.pi * np.outer(f, np.arange(sizes.tap_rows)) / rows
    taps_into = np.concatenate([np.cos(angle), -np.sin(angle)], axis=0)
    taps_outof = taps_into.T / size
    b = np.arange(LANES)
    angle = 2 * np.pi * np.outer(f, b) / size
    turn = np.stack([np.cos(angle), np.sin(angle)])
    angle = 2 * np.pi * np.outer(b, b) / LANES
    cos, sin = np.cos(angle), np.sin(angle)
    ahead = np.block([[cos, -sin], [sin, cos]])
    return (
        jnp.asarray(into, BF16),
        jnp.asarray(outof, BF16),
        jnp.asarray(taps_into, BF16),
        jnp.asarray(taps_outof, BF16),
        jnp.asarray(turn, F32),
        jnp.asarray(ahead, BF16),
        jnp.asarray(ahead.T, BF16),
    )


def dot(left, right):
    return jnp.dot(left, right, preferred_element_type=F32)


def spectrum_into(sizes, load, into, turn, ahead, inner, spectrum):
    rows = sizes.rows
    for pair in range(sizes.group // 2):
        both = jnp.concatenate([load(2 * pair), load(2 * pair + 1)], axis=1).astype(BF16)
        part = dot(into[...], both)
        for side in range(2):
            real = part[:rows, side * LANES : (side + 1) * LANES]
            imag = part[rows:, side * LANES : (side + 1) * LANES]
            start = (2 * pair + side) * rows
            inner[start : start + rows, :] = jnp.concatenate(
                [real * turn[0] + imag * turn[1], imag * turn[0] - real * turn[1]], axis=1
            ).astype(BF16)
    spectrum[...] = dot(inner[...], ahead[...])


def signal_from(sizes, product, outof, turn, behind, inner, store):
    rows = sizes.rows
    inner[...] = dot(product, behind[...])
    for pair in range(sizes.group // 2):
        sides = []
        for side in range(2):
            start = (2 * pair + side) * rows
            real, imag = inner[start : start + rows, :LANES], inner[start : start + rows, LANES:]
            sides.append(
                jnp.concatenate(
                    [real * turn[0] - imag * turn[1], imag * turn[0] + real * turn[1]], axis=0
                ).astype(BF16)
            )
        got = dot(outof[...], jnp.concatenate(sides, axis=1))
        for side in range(2):
            store(2 * pair + side, got[:, side * LANES : (side + 1) * LANES])


def times(left, right, conj):
    a, b = left[:, :LANES], left[:, LANES:]
    c, d = right[:, :LANES], right[:, LANES:]
    if conj:
        return jnp.concatenate([a * c + b * d, b * c - a * d], axis=1).astype(BF16)
    return jnp.concatenate([a * c - b * d, a * d + b * c], axis=1).astype(BF16)


def to_chunks(sizes, rows, target):
    turned = rows.T.reshape(sizes.freq_count, sizes.group, sizes.here)
    pieces = [turned[:, :, col * LANES : (col + 1) * LANES] for col in range(sizes.cols)]
    target[...] = jnp.concatenate(pieces, axis=1).astype(BF16)


def from_chunks(sizes, chunks):
    wide = chunks[...].astype(F32)
    for c in range(2):
        for col in range(sizes.cols):
            piece = wide[
                c * sizes.freq_count : (c + 1) * sizes.freq_count, col * sizes.group : (col + 1) * sizes.group
            ]
            yield c, slice(col * LANES, (col + 1) * LANES), piece.reshape(LANES, LANES).T


def chunk_loader(sizes, ref):
    def load(channel):
        pieces = [
            ref[pl.ds(col * sizes.group + channel, sizes.devices, stride=sizes.chunk), :]
            for col in range(sizes.cols)
        ]
        return jnp.concatenate(pieces, axis=0)

    return load


def chunk_storer(sizes, ref):
    def store(channel, values):
        for col in range(sizes.cols):
            ref[pl.ds(col * sizes.group + channel, sizes.devices, stride=sizes.chunk), :] = values[
                col * sizes.devices : (col + 1) * sizes.devices
            ]

    return store


def pooled_taps(taps):
    lane = lax.broadcasted_iota(jnp.int32, taps.shape, 2)
    zero = jnp.zeros_like(taps[:1])
    after = pltpu.roll(taps, LANES - 1, 2)
    before = pltpu.roll(taps, 1, 2)
    after = jnp.where(lane == LANES - 1, jnp.concatenate([after[1:], zero], axis=0), after)
    before = jnp.where(lane == 0, jnp.concatenate([zero, before[:-1]], axis=0), before)
    return (before + taps + after) / 3.0


def live_mask(shape, lengths):
    tap = lax.broadcasted_iota(jnp.int32, shape, 0) * LANES + lax.broadcasted_iota(
        jnp.int32, shape, 2
    )
    return (tap < lengths[None]).astype(F32)


VALUE, GATE, OUT, UP, DOWN = range(5)
ACT, HID = range(2)
PIECES = 4
ACROSS, INWARD, OUTWARD = range(3)
V0, V1, V2, G, O, U0, U1, U2, U3, D0, D1, D2, D3, S, T, C, W = range(17)
TOPS = [lambda n: (1, 2)]
LOW = [lambda n: (2,)]
SPREAD_OUT = LOW + [lambda n: Line(ACROSS, 1, 2), lambda n: Line(OUTWARD, 1, 2)]
BRING_IN = [lambda n: Line(INWARD, 1, 2), lambda n: Line(ACROSS, 1, 2)] + LOW
X, Y, CORE = [lambda n: (0,)], [lambda n: (n - 2,)], [lambda n: (n - 1,)]
PLANE = [lambda n: (0, n - 2)]
GATHER_PHASES = {
    G: SPREAD_OUT + Y + X + CORE,
    O: SPREAD_OUT + Y + X + CORE,
    U0: SPREAD_OUT + Y + CORE,
    D0: SPREAD_OUT + Y + CORE,
    U1: SPREAD_OUT + Y + CORE,
    D1: Y + SPREAD_OUT + CORE,
    U2: Y + SPREAD_OUT + CORE,
    D2: SPREAD_OUT + Y + CORE,
    U3: SPREAD_OUT + Y + CORE,
    D3: SPREAD_OUT + Y + CORE,
    V0: TOPS + PLANE + CORE,
    V1: TOPS + PLANE + CORE,
    V2: TOPS + X + Y + CORE,
}
REDUCE_PHASES = {
    G: X + Y + BRING_IN,
    O: Y + X + BRING_IN,
    U0: Y + BRING_IN,
    D0: Y + BRING_IN,
    U1: Y + BRING_IN,
    D1: BRING_IN + Y,
    U2: BRING_IN + Y,
    D2: BRING_IN + Y,
    U3: Y + BRING_IN,
    D3: Y + BRING_IN,
    V0: PLANE + TOPS,
    V1: PLANE + TOPS,
    V2: PLANE + TOPS,
}
SPREAD_PHASES = CORE + PLANE + TOPS


class Order:
    tokens = (O, D0, U2, O, G, U1, D2, T, V0)
    norm = ()
    w_value = ((V1, O, U0, V2, D0, C, G, D3), (U3, D0, V0, V2, D1, U1, G, U0, D3, O), (D2,))
    value = ((), (U2,), (U3,))
    sent = (U1,)
    taps = (D0, G, U2, O)
    kernel = (U0, D0)
    arrive = ((), (U1, U0, G), (U3,))
    conv = ((), (D1,), ())
    convolved = ()
    cotangent = (G, O)
    turn = ()
    w_gate = (D2, U3, D3, U2, D1)
    gate = ()
    mixed = ((), (), ())
    inner = ()
    w_out = (U1,)
    residual = (U0, D2)
    turn_near = ()
    w_up = ((D1,), (), (U3, U0), (D1,))
    near_up = ((D3,), (), (D2,), ())
    wait_far = ((), ())
    far_up = ((D3,), ())
    down_a = ((D2, V0), (), (), ())
    far_a = ((), (G,), (), (V1,))
    far_b = ()
    near_down = (D2, D3, D0, D1)
    far_back = (D3,)
    norm_back = ()
    sent_back = (D1,)
    output = (U1, G, O)
    arrive_back = ((U2,), (D3, D1), ())
    conv_back = ((), (), (G, D0, U0, D2, U1, O))
    convolved_back = (W, U3, G, O, U2)
    taps_back = ()
    signal = ((), (), (U0, D2))
    input_back = ((), (V1, O, U3, D3, V0, G), (V2, D0))
    first_back = ()
    finish_output = (U2, U1, U0, D1)
    last = (O, V0, V1, D2, U3, S, V2, D0, G, U1, U0)
    finish_grad = (U2,)
    taps_home = (U3,)
    end = (S,)


VMEM_SPEC = pl.BlockSpec(memory_space=pltpu.VMEM)
ANY_SPEC = pl.BlockSpec(memory_space=pl.ANY)
GELU_SCALE = math.sqrt(2.0 / math.pi)
GELU_CUBE = 0.044715


def dot_nt(left, right):
    return lax.dot_general(left, right, (((1,), (1,)), ((), ())), preferred_element_type=F32)


def norm(values):
    center = jnp.mean(values, axis=-1, keepdims=True)
    shifted = values - center
    scale = lax.rsqrt(jnp.mean(shifted * shifted, axis=-1, keepdims=True) + EPSILON)
    return shifted * scale, scale


def norm_back(grad_rows, normed, scale, gain):
    scaled = grad_rows * gain
    plain = jnp.mean(scaled, axis=-1, keepdims=True)
    cross = jnp.mean(scaled * normed, axis=-1, keepdims=True)
    return scale * (scaled - plain - normed * cross)


class Part:
    def __init__(self, weight, piece, columns, dims, at):
        self.weight, self.piece, self.columns, self.at = weight, piece, columns, at
        self.dims = tuple(range(1 if weight in (UP, DOWN) else 0, dims))
        self.gather = tuple(phase(dims) for phase in GATHER_PHASES[at])
        self.reduce = tuple(phase(dims) for phase in REDUCE_PHASES[at])


def most(phases):
    return max(len(flips_of(step)) for step in phases)


class Plan:
    def __init__(self, sizes, tables):
        self.sizes = sizes
        here, channels, half = sizes.here, sizes.channels, sizes.half
        width = 2 * half
        self.width = width
        dims = 1 + len(bit_sizes(sizes.freq_count))
        self.dims = dims
        self.rows = rows = width // sizes.freq_count
        pieces = ((VALUE, sizes.groups, LANES), (GATE, 1, half), (OUT, 1, half), (UP, PIECES, half), (DOWN, PIECES, half))
        self.parts = []
        for weight, count, columns in pieces:
            for piece in range(count):
                self.parts.append(Part(weight, piece, columns, dims, len(self.parts)))
        self.spread = tuple(phase(dims) for phase in SPREAD_PHASES)
        groups = [self.spread] + [p.gather for p in self.parts] + [p.reduce for p in self.parts]
        self.partners = sorted(
            {flipped for phases in groups for step in phases for flipped in flips_of(step) if 0 in flipped}
        )

        def vmem(kind, *shape):
            return pltpu.VMEM(shape, kind)

        def sems(*shape):
            return pltpu.SemaphoreType.DMA(shape)

        def weights(bits):
            return [
                vmem(BF16, count, *(2,) * (bits + (weight not in (UP, DOWN))), rows, columns)
                for weight, count, columns in pieces
            ]

        def rows_of(kind, *lead):
            return vmem(kind, *lead, here, width)

        def turned(tokens):
            return vmem(BF16, width // (2 * rows), 2, rows, tokens)

        def turned_half(tokens):
            return vmem(BF16, width // (2 * rows), rows, tokens)

        def halves():
            return vmem(BF16, 2, here, half)

        def tiles():
            return vmem(BF16, PIECES, 2, 2 * here, half)

        def chunks():
            return vmem(BF16, sizes.groups, sizes.devices, sizes.chunk, LANES)

        def spectra(kind):
            return [vmem(kind, sizes.group_rows, 2 * LANES) for _ in range(sizes.groups)]

        def wide():
            return [vmem(F32, sizes.devices * sizes.chunk, LANES) for _ in range(sizes.groups)]

        taps = (sizes.tap_rows, sizes.groups, sizes.group, LANES)
        flat_taps = (sizes.tap_rows * channels, LANES)
        gain_rows = 2 * width // LANES + 4
        scratch = dict(
            x_buf=halves(),
            g_buf=vmem(BF16, 2, 2, here, half),
            gains=[[vmem(F32, half) for _ in range(2)] for _ in range(2)],
            lengths=vmem(jnp.int32, half),
            turned=vmem(F32, half, 8),
            weights=weights(dims - 1),
            grads=weights(dims - 2),
            landings=[
                [vmem(BF16, *shape) for shape in landing_shapes(part.reduce, part.dims[:-1], rows, part.columns)]
                for part in self.parts
            ],
            results=[vmem(F32, rows, part.columns) for part in self.parts],
            part_sems=[
                (sems(max(most(p.gather), most(p.reduce))), sems(slots(p.gather)), sems(slots(p.reduce)))
                for p in self.parts
            ],
            kernel_spec=spectra(F32),
            value_spec=spectra(F32),
            grad_spec=spectra(F32),
            inner_into=spectra(BF16),
            inner_from=spectra(F32),
            inner_taps=spectra(F32),
            wide_in=wide(),
            wide_out=wide(),
            taps=vmem(F32, *taps),
            tap_grad=vmem(F32, *taps),
            tap_wide=vmem(F32, *flat_taps),
            sent=chunks(),
            sent_back=chunks(),
            landed=[chunks() for _ in range(4)],
            move_sems=[[sems(2) for _ in range(sizes.groups)] for _ in range(4)],
            tap_sems=[sems(2) for _ in range(2)],
            normed1=rows_of(F32),
            gate=rows_of(F32),
            mixed=rows_of(F32),
            residual=rows_of(F32),
            normed2=rows_of(F32),
            grad_res=rows_of(F32),
            rows=rows_of(F32),
            out_sum=rows_of(F32, 2),
            in2_sum=rows_of(F32, 2),
            scale1=vmem(F32, here, 1),
            scale2=vmem(F32, here, 1),
            input1=rows_of(BF16),
            branch_rows=rows_of(BF16),
            in2_send=rows_of(BF16),
            in2_land=rows_of(BF16),
            input2=rows_of(BF16, 2),
            grad_rows=rows_of(BF16, 2),
            t_input1=(turned(here), turned_half(here)),
            t_branch=(turned(here), turned_half(here)),
            t_input2=(turned(2 * here), turned_half(2 * here)),
            t_grad=(turned(2 * here), turned_half(2 * here)),
            inner_rows=(halves(), halves()),
            signal_rows=[vmem(BF16, sizes.groups, here, 2 * LANES) for _ in range(2)],
            gate_rows=(halves(), halves()),
            tiles=(tiles(), tiles()),
            slopes=vmem(F32, PIECES, 2 * here, half),
            tile_sems=sems(2, 2, PIECES),
            twin_sems=sems(2, 6 + sizes.groups),
            gain_total=vmem(F32, len(self.spread) + 1, gain_rows, LANES),
            gain_land=vmem(F32, slots(self.spread), gain_rows, LANES),
            gain_sems=(sems(most(self.spread)), sems(slots(self.spread))),
            out_send=halves(),
            out_land=halves(),
            gin_send=vmem(BF16, here, half),
            gin_land=vmem(BF16, here, half),
            swap_sems=sems(2, 10),
            local=sems(13 + len(self.parts)),
            tables=[vmem(table.dtype, *table.shape) for table in tables],
            v_output=halves(),
            v_grad_input=vmem(F32, 2, here, half),
            v_grad_kernel=vmem(F32, sizes.groups, sizes.freq_count, sizes.group, LANES),
        )
        self.scratch, self.tree = jax.tree.flatten(
            scratch, is_leaf=lambda leaf: not isinstance(leaf, (dict, list, tuple))
        )


def row_tiles(count, body, tile=64):
    def one(step, carry):
        body(pl.ds(pl.multiple_of(step * tile, tile), tile))
        return carry

    lax.fori_loop(0, count // tile, one, 0)


def block_kernel(plan, tokens, cotangent, first_gain, second_gain, lengths, raw_kernel, *refs):
    shards, refs = refs[:5], refs[5:]
    tables = refs[:7]
    output, grad_input, *weight_grads = refs[7:14]
    gain_sums, grad_kernel = refs[14:16]
    k = types.SimpleNamespace(**jax.tree.unflatten(plan.tree, refs[16:]))
    into, outof, taps_into, taps_outof, turn, ahead, behind = k.tables
    sizes = plan.sizes
    here, half, width, channels = sizes.here, sizes.half, plan.width, sizes.channels
    place = Place(sizes.freq_count)
    chan, core = place.chan, place.core
    twin = place.other((plan.dims - 1,))
    across = place.other((0,))
    me = chan * sizes.freq_count + place.freq

    def whole(weight, *lead, lanes=slice(None)):
        value = k.weights[weight][lead + (slice(None),) * plan.dims + (lanes,)]
        return value.reshape(width, value.shape[-1])

    def of_group(group):
        return slice(group * LANES, (group + 1) * LANES)

    def both_halves(weight, *lead, lanes=slice(None)):
        return jnp.concatenate([whole(weight, *lead, c, lanes=lanes) for c in range(2)], axis=1)

    def of_chan(values):
        return jnp.where(chan == 0, values[:, :half], values[:, half:])

    def of_other_chan(values):
        return jnp.where(chan == 0, values[:, half:], values[:, :half])

    leaving = []

    def leave(source, target):
        leaving.append(pltpu.make_async_copy(source, target, k.local.at[len(leaving)]))
        leaving[-1].start()

    own = []
    for part in plan.parts:
        source = shards[part.weight].at[:, pl.ds(part.piece * part.columns, part.columns)]
        target = k.weights[part.weight].at[(part.piece,) + tuple(place.coords[dim] for dim in part.dims)]
        own.append(pltpu.make_async_copy(source, target, k.local.at[part.at]))
    for source, target in (
        (tokens.at[chan], k.x_buf.at[chan]),
        (cotangent, k.g_buf.at[chan]),
        (raw_kernel.at[:, place.freq], k.taps.at[place.freq]),
        (first_gain, k.gains[0][0]),
        (second_gain, k.gains[0][1]),
        (lengths, k.lengths),
    ):
        own.append(pltpu.make_async_copy(source, target, k.local.at[len(own)]))
    for source, target in zip(tables, k.tables):
        own.append(pltpu.make_async_copy(source, target, k.local.at[len(own)]))
    for copy in own:
        copy.start()
    own_tokens, own_cotangent, own_taps, *own_rows = own[len(plan.parts) :]
    own_tables, own_rows = own_rows[3:], own_rows[:3]
    barrier = pltpu.get_barrier_semaphore()
    for flipped in plan.partners:
        pl.semaphore_signal(barrier, inc=1, device_id=place.other(flipped), device_id_type=MESH)

    def greet(step, carry):
        peer = (lax.rem(place.freq + step, sizes.freq_count), chan)
        pl.semaphore_signal(barrier, inc=1, device_id=peer, device_id_type=MESH)
        return carry

    lax.fori_loop(1, sizes.freq_count, greet, 0, unroll=True)
    pl.semaphore_wait(barrier, len(plan.partners) + sizes.freq_count - 1)

    def swap(at, source, target):
        copy = remote(source, target, k.swap_sems.at[0, at], k.swap_sems.at[1, at], across)
        copy.start()
        return copy

    moving = {}
    for part in plan.parts:
        moving[part.at] = Gather(
            place,
            k.weights[part.weight].at[part.piece],
            part.dims,
            part.gather,
            k.part_sems[part.at][0],
            k.part_sems[part.at][1],
            own[part.at].wait,
        )

    def ahead_of(names):
        for name in names:
            moving[name].go()

    def all_to_all(move, group, source):
        target = k.landed[move]
        exchange = Exchange(
            sizes.devices,
            me,
            lambda other: (lax.rem(other, sizes.freq_count), other // sizes.freq_count),
            lambda other: source.at[group, other],
            lambda other: target.at[group, other],
            source.at[group, pl.ds(0, sizes.devices - 1)],
            target.at[group, pl.ds(0, sizes.devices - 1)],
            k.move_sems[move][group],
        )
        exchange.start()
        target[group, me] = source[group, me]
        return exchange

    swap_tokens = swap(0, tokens.at[1 - chan], k.x_buf.at[chan])
    swap_gains = [swap(at, ref, k.gains[1][at - 8]) for at, ref in ((8, first_gain), (9, second_gain))]
    for group in range(sizes.groups):
        moving[V0 + group].go()
    others = sizes.freq_count - 1

    def begin(exchange):
        exchange.start()
        return exchange

    tap_move = Exchange(
        sizes.freq_count,
        place.freq,
        lambda other: (other, chan),
        lambda other: raw_kernel.at[:, other],
        lambda other: k.taps.at[other],
        raw_kernel.at[:, pl.ds(0, others)],
        k.taps.at[pl.ds(0, others)],
        k.tap_sems[0],
    )
    moving[T] = Once(lambda: begin(tap_move))
    moving[C] = Once(lambda: swap(2, cotangent, k.g_buf.at[chan]))
    ahead_of(Order.tokens)
    swap_tokens.wait()
    own_tokens.wait()
    for copy in swap_gains + own_rows:
        copy.wait()

    def gain_row(row):
        near, far = k.gains[0][row][...][None], k.gains[1][row][...][None]
        return jnp.concatenate([jnp.where(chan == 0, near, far), jnp.where(chan == 0, far, near)], axis=1)

    first_gain, second_gain = gain_row(0), gain_row(1)

    def first_norm(at):
        rows = jnp.concatenate([k.x_buf[0, at, :], k.x_buf[1, at, :]], axis=1).astype(F32)
        normed, scale = norm(rows)
        k.normed1[at, :] = normed
        k.scale1[at, :] = scale
        k.input1[at, :] = (normed * first_gain).astype(BF16)

    ahead_of(Order.norm)
    row_tiles(here, first_norm)

    def turn_rows(source, target, columns=slice(None)):
        turned = source[...].astype(F32).T.astype(BF16)
        target[:, :, :, columns] = turned.reshape(target.shape[:-1] + (here,))

    arriving = {}

    def share(at, source, target):
        copy = remote(source, target, k.twin_sems.at[0, at], k.twin_sems.at[1, at], twin)
        copy.start()
        arriving[at] = copy

    def share_turned(at, pair):
        share(at, pair[0].at[:, 1 - core], pair[1])

    def need(at):
        if at in arriving:
            arriving.pop(at).wait()

    turn_rows(k.input1, k.t_input1[0])
    share_turned(0, k.t_input1)

    def send_chunks(move, group, source, halves):
        for c in range(2):
            devices = pl.ds(c * sizes.freq_count, sizes.freq_count)
            to_chunks(sizes, halves[c], source.at[group, devices])
        return all_to_all(move, group, source)

    moves = []
    for group in range(sizes.groups):
        ahead_of(Order.w_value[group])
        moving[V0 + group].finish()
        ahead_of(Order.value[group])
        got = dot(k.input1[...], both_halves(VALUE, group))
        moves.append(send_chunks(0, group, k.sent, (got[:, :LANES], got[:, LANES:])))
    ahead_of(Order.sent)
    ahead_of(Order.taps)
    moving[T].finish()
    for copy in own_tables:
        copy.wait()
    own_taps.wait()
    k.turned[...] = jnp.broadcast_to(k.lengths[...].astype(F32)[None], (8, half)).T
    lives = [
        k.turned[pl.ds(pl.multiple_of(group * LANES + place.freq * sizes.group, 8), sizes.group), 0:1]
        for group in range(sizes.groups)
    ]
    flat_taps = (sizes.tap_rows, channels, LANES)
    live = live_mask(flat_taps, jnp.concatenate(lives, axis=0))
    pooled = pooled_taps(k.taps[...].reshape(flat_taps))
    shrunk = (pooled - THRESH * jnp.tanh(pooled / THRESH)) * live
    k.tap_wide[...] = shrunk.reshape(sizes.tap_rows * channels, LANES)
    ahead_of(Order.kernel)

    def tap_load(group):
        return lambda c: k.tap_wide[pl.ds(group * sizes.group + c, sizes.tap_rows, stride=channels), :]

    for group in range(sizes.groups):
        spectrum_into(
            sizes, tap_load(group), taps_into, turn, ahead, k.inner_into[group], k.kernel_spec[group]
        )

    def spectrum_of(move, group, spectra):
        flat = (sizes.devices * sizes.chunk, LANES)
        k.wide_in[group][...] = k.landed[move][group].astype(F32).reshape(flat)
        spectrum_into(
            sizes, chunk_loader(sizes, k.wide_in[group]), into, turn, ahead, k.inner_into[group], spectra[group]
        )

    def chunks_from(group, product):
        signal_from(
            sizes, product, outof, turn, behind, k.inner_from[group], chunk_storer(sizes, k.wide_out[group])
        )
        k.sent_back[group] = k.wide_out[group][...].reshape(k.sent_back.shape[1:]).astype(BF16)

    moves_back = []
    for group in range(sizes.groups):
        ahead_of(Order.arrive[group])
        moves[group].wait()
        ahead_of(Order.conv[group])
        spectrum_of(0, group, k.value_spec)
        chunks_from(group, times(k.value_spec[group][...], k.kernel_spec[group][...], False))
        moves_back.append(all_to_all(1, group, k.sent_back))
    ahead_of(Order.convolved)
    ahead_of(Order.cotangent)
    moving[C].finish()
    own_cotangent.wait()
    ahead_of(Order.turn)
    for which, seq in ((0, chan), (1, 1 - chan)):
        k.grad_rows[which] = jnp.concatenate([k.g_buf[0, seq], k.g_buf[1, seq]], axis=1)
        turn_rows(k.grad_rows.at[which], k.t_grad[0], slice(which * here, (which + 1) * here))
    share_turned(2, k.t_grad)
    ahead_of(Order.w_gate)
    moving[G].finish()
    ahead_of(Order.gate)
    for c in range(2):
        k.gate[:, c * half : (c + 1) * half] = dot(k.input1[...], whole(GATE, 0, c))
    for group in range(sizes.groups):
        ahead_of(Order.mixed[group])
        moves_back[group].wait()
        for c, tokens_at, rows in from_chunks(sizes, k.landed[1].at[group]):
            k.mixed[tokens_at, c * half + group * LANES : c * half + (group + 1) * LANES] = rows
    ahead_of(Order.inner)

    def make_inner(at):
        gate = k.gate[at, :]
        inner = (k.mixed[at, :] * (gate * jax.nn.sigmoid(gate))).astype(BF16)
        k.inner_rows[0][0, at, :] = inner[:, :half]
        k.inner_rows[0][1, at, :] = inner[:, half:]

    row_tiles(here, make_inner)
    share(4, *k.inner_rows)
    ahead_of(Order.w_out)
    moving[O].finish()
    ahead_of(Order.residual)
    k.residual[...] = dot_nt(k.inner_rows[0][0], whole(OUT, 0, 0)) + dot_nt(
        k.inner_rows[0][1], whole(OUT, 0, 1)
    )

    def second_norm(at):
        rows = jnp.concatenate([k.x_buf[0, at, :], k.x_buf[1, at, :]], axis=1).astype(F32)
        residual = k.residual[at, :] + rows
        normed, scale = norm(residual)
        k.residual[at, :] = residual
        k.normed2[at, :] = normed
        k.scale2[at, :] = scale
        k.input2[0, at, :] = (normed * second_gain).astype(BF16)

    row_tiles(here, second_norm)
    blocks = [pl.ds(at * (here // 2), here // 2) for at in range(2)]
    swap_input2 = [swap(3 + at, k.input2.at[0, rows], k.input2.at[1, rows]) for at, rows in enumerate(blocks)]
    ahead_of(Order.turn_near)
    turn_rows(k.input2.at[0], k.t_input2[0], slice(0, here))

    def product(left, right, pick):
        mine, theirs = left[0][:, core], left[1][...]
        shape = (width // 2, mine.shape[-1])
        got = dot(
            jnp.concatenate([mine.reshape(shape), theirs.reshape(shape)], axis=1),
            jnp.concatenate([right[0][pick], right[1][pick]], axis=0),
        ).astype(BF16)
        return got.reshape((2,) * (plan.dims - 2) + (plan.rows, got.shape[-1]))

    factors = {
        VALUE: (k.t_input1, 0, k.signal_rows, 6),
        GATE: (k.t_input1, 0, k.gate_rows, 5),
        OUT: (k.t_branch, 3, k.inner_rows, 4),
        UP: (k.t_input2, 1, k.tiles, None),
        DOWN: (k.t_grad, 2, k.tiles, None),
    }

    def prepare(part):
        left, left_share, right, right_share = factors[part.weight]
        need(left_share)
        total = k.grads[part.weight]
        if part.weight == VALUE:
            need(right_share + part.piece)
            got = product(left, right, part.piece)
            for c in range(2):
                total[part.piece, c] = got[..., of_group(c)]
        elif part.weight in (GATE, OUT):
            need(right_share)
            for c in range(2):
                total[part.piece, c] = product(left, right, c)
        else:
            kind = HID if part.weight == UP else ACT
            tile_copy(kind, part.piece).wait()
            total[part.piece] = product(left, right, (part.piece, kind))

    def depart(part):
        columns = pl.ds(part.piece * part.columns, part.columns)
        leave(k.results[part.at], weight_grads[part.weight].at[:, columns])

    def begin_reducing(part):
        moving[part.at] = Reduce(
            place,
            k.grads[part.weight].at[part.piece],
            k.landings[part.at],
            part.dims[:-1],
            part.reduce,
            k.part_sems[part.at][0],
            k.part_sems[part.at][2],
            k.results[part.at],
            functools.partial(prepare, part),
            functools.partial(depart, part),
        )
    def start_reducing():
        for name, mover in list(moving.items()):
            if isinstance(mover, Gather):
                mover.finish()
        for part in plan.parts:
            begin_reducing(part)

    def up_part(which, piece, first, count):
        rows = pl.ds(first, count)
        stored = pl.ds(which * here + first, count)
        hidden = dot(k.input2[which, rows, :], whole(UP, piece))
        square = hidden * hidden
        bent = jnp.tanh(GELU_SCALE * hidden * (1.0 + GELU_CUBE * square))
        k.tiles[0][piece, ACT, stored, :] = (0.5 * hidden * (1.0 + bent)).astype(BF16)
        k.slopes[piece, stored, :] = 0.5 * (1.0 + bent) + (0.5 * GELU_SCALE) * hidden * (1.0 - bent * bent) * (
            1.0 + 3.0 * GELU_CUBE * square
        )

    def down_part(which, piece, first, count):
        rows = pl.ds(first, count)
        stored = pl.ds(which * here + first, count)
        down = whole(DOWN, piece)
        grad = (dot(k.grad_rows[which, rows, :], down) * k.slopes[piece, stored, :]).astype(BF16)
        k.tiles[0][piece, HID, stored, :] = grad
        into_in2, into_out = dot_nt(grad, whole(UP, piece)), dot_nt(k.tiles[0][piece, ACT, stored, :], down)
        if piece:
            into_in2, into_out = k.in2_sum[which, rows, :] + into_in2, k.out_sum[which, rows, :] + into_out
        k.in2_sum[which, rows, :] = into_in2
        k.out_sum[which, rows, :] = into_out

    def tile_copy(kind, piece):
        return remote(
            k.tiles[0].at[piece, kind],
            k.tiles[1].at[piece, kind],
            k.tile_sems.at[0, kind, piece],
            k.tile_sems.at[1, kind, piece],
            twin,
        )

    for piece in range(PIECES):
        ahead_of(Order.w_up[piece])
        moving[U0 + piece].finish()
        ahead_of(Order.near_up[piece])
        up_part(0, piece, 0, here)
    swap_in2 = []

    def return_far(at):
        rows = blocks[at]
        k.in2_send[rows, :] = k.in2_sum[1, rows, :].astype(BF16)
        swap_in2.append(swap(5 + at, k.in2_send.at[rows], k.in2_land.at[rows]))

    for at in range(2):
        ahead_of(Order.wait_far[at])
        swap_input2[at].wait()
        ahead_of(Order.far_up[at])
        for piece in range(PIECES):
            up_part(1, piece, at * (here // 2), here // 2)
            if at:
                tile_copy(ACT, piece).start()
        if at:
            start_reducing()
            ahead_of(Order.far_b)
        for piece in range(PIECES):
            if not at:
                ahead_of(Order.down_a[piece])
                moving[D0 + piece].finish()
                ahead_of(Order.far_a[piece])
            down_part(1, piece, at * (here // 2), here // 2)
        return_far(at)
    ahead_of(Order.near_down)
    for piece in range(PIECES):
        down_part(0, piece, 0, here)
        tile_copy(HID, piece).start()
    turn_rows(k.input2.at[1], k.t_input2[0], slice(here, 2 * here))
    share_turned(1, k.t_input2)

    ahead_of(Order.far_back)
    for copy in swap_in2:
        copy.wait()

    k.gain_total[0] = jnp.zeros_like(k.gain_total[0])

    def add_gain(row, sums):
        for at in range(width // LANES):
            base = row * (width // LANES) + at
            k.gain_total[0, base : base + 1, :] += sums[:, at * LANES : (at + 1) * LANES]

    def second_back(at):
        grad = k.in2_sum[0, at, :] + k.in2_land[at, :].astype(F32)
        normed = k.normed2[at, :]
        add_gain(1, jnp.sum(grad * normed, axis=0, keepdims=True))
        result = k.grad_rows[0, at, :].astype(F32) + norm_back(
            grad, normed, k.scale2[at, :], second_gain
        )
        k.grad_res[at, :] = result
        k.branch_rows[at, :] = result.astype(BF16)

    ahead_of(Order.norm_back)
    row_tiles(here, second_back)
    moves = []
    for group in range(sizes.groups):
        got = dot(k.branch_rows[...], both_halves(OUT, 0, lanes=of_group(group)))
        grad_mixed = []
        for c in range(2):
            columns = slice(c * half + group * LANES, c * half + (group + 1) * LANES)
            gate, grad = k.gate[:, columns], got[:, of_group(c)]
            sig = jax.nn.sigmoid(gate)
            k.gate_rows[0][c, :, of_group(group)] = (
                grad * k.mixed[:, columns] * (sig * (1.0 + gate * (1.0 - sig)))
            ).astype(BF16)
            grad_mixed.append(grad * (gate * sig))
        moves.append(send_chunks(2, group, k.sent, grad_mixed))
    share(5, *k.gate_rows)
    ahead_of(Order.sent_back)
    turn_rows(k.branch_rows, k.t_branch[0])
    share_turned(3, k.t_branch)
    ahead_of(Order.output)

    def make_output(at):
        near = k.residual[at, :] + k.out_sum[0, at, :]
        far = k.out_sum[1, at, :]
        k.out_send[0, at, :] = of_other_chan(near).astype(BF16)
        k.out_send[1, at, :] = of_other_chan(far).astype(BF16)

    row_tiles(here, make_output)
    moving[W] = Once(lambda: swap(7, k.out_send, k.out_land))

    moves_back = []
    for group in range(sizes.groups):
        ahead_of(Order.arrive_back[group])
        moves[group].wait()
        ahead_of(Order.conv_back[group])
        spectrum_of(2, group, k.grad_spec)
        chunks_from(group, times(k.grad_spec[group][...], k.kernel_spec[group][...], True))
        moves_back.append(all_to_all(3, group, k.sent_back))
    ahead_of(Order.convolved_back)

    def tap_store(group):
        def store(channel, values):
            k.tap_wide[pl.ds(group * sizes.group + channel, sizes.tap_rows, stride=channels), :] = values

        return store

    ahead_of(Order.taps_back)
    for group in range(sizes.groups):
        signal_from(
            sizes,
            times(k.grad_spec[group][...], k.value_spec[group][...], True),
            taps_outof, turn, behind, k.inner_taps[group], tap_store(group),
        )
    pooled = pooled_taps(k.taps[...].reshape(flat_taps))
    bent = jnp.tanh(pooled / THRESH)
    tap_grads = pooled_taps(k.tap_wide[...].reshape(pooled.shape) * live * bent * bent)
    k.tap_grad[...] = tap_grads.reshape(k.tap_grad.shape)
    tap_back = Exchange(
        sizes.freq_count,
        place.freq,
        lambda other: (other, chan),
        lambda other: k.tap_grad.at[other],
        lambda other: k.v_grad_kernel.at[:, other],
        k.tap_grad.at[pl.ds(0, others)],
        k.v_grad_kernel.at[:, pl.ds(0, others)],
        k.tap_sems[1],
    )
    tap_back.start()
    k.v_grad_kernel[:, place.freq] = k.tap_grad[place.freq]

    k.rows[...] = dot_nt(k.gate_rows[0][0], whole(GATE, 0, 0)) + dot_nt(k.gate_rows[0][1], whole(GATE, 0, 1))
    for group in range(sizes.groups):
        ahead_of(Order.signal[group])
        moves_back[group].wait()
        for c, tokens_at, rows in from_chunks(sizes, k.landed[3].at[group]):
            k.signal_rows[0][group, tokens_at, of_group(c)] = rows.astype(BF16)
        share(6 + group, k.signal_rows[0].at[group], k.signal_rows[1].at[group])
        ahead_of(Order.input_back[group])
        k.rows[...] += dot_nt(k.signal_rows[0][group], both_halves(VALUE, group))
    ahead_of(Order.first_back)

    def first_back(at):
        grad = k.rows[at, :]
        normed = k.normed1[at, :]
        add_gain(0, jnp.sum(grad * normed, axis=0, keepdims=True))
        result = k.grad_res[at, :] + norm_back(grad, normed, k.scale1[at, :], first_gain)
        k.gin_send[at, :] = of_other_chan(result).astype(BF16)
        k.v_grad_input[chan, at, :] = of_chan(result)

    row_tiles(here, first_back)
    swap_gin = swap(1, k.gin_send, k.gin_land)
    spread = Spread(place, k.gain_total, k.gain_land, plan.spread, *k.gain_sems)
    moving[S] = spread
    spread.go()
    ahead_of(Order.finish_output)
    moving[W].finish()

    def finish_output(at):
        near = of_chan(k.residual[at, :] + k.out_sum[0, at, :]) + k.out_land[1, at, :].astype(F32)
        far = of_chan(k.out_sum[1, at, :]) + k.out_land[0, at, :].astype(F32)
        k.v_output[chan, at, :] = near.astype(BF16)
        k.v_output[1 - chan, at, :] = far.astype(BF16)

    row_tiles(here, finish_output)
    leave(k.v_output, output)
    ahead_of(Order.last)
    swap_gin.wait()
    ahead_of(Order.finish_grad)
    k.v_grad_input[1 - chan] = k.gin_land[...].astype(F32)
    leave(k.v_grad_input, grad_input)
    ahead_of(Order.taps_home)
    tap_back.wait()
    leave(k.v_grad_kernel, grad_kernel)
    ahead_of(Order.end)
    for mover in moving.values():
        if not isinstance(mover, Once):
            mover.finish()
    leave(k.gain_total.at[len(plan.spread)], gain_sums)
    for copy in leaving:
        copy.wait()


def settle_kernel(count, channels, freq_count, *refs):
    sources, refs = refs[: count + 1], refs[count + 1 :]
    targets, refs = refs[: count + 2], refs[count + 2 :]
    held, sems = refs[: count + 3], refs[-1]
    gains, sums = held[count : count + 2], held[-1]
    coming = [pltpu.make_async_copy(sources[n], held[n], sems.at[0, n]) for n in range(count)]
    going = [pltpu.make_async_copy(held[n], targets[n], sems.at[1, n]) for n in range(count + 2)]
    sums_in = pltpu.make_async_copy(sources[-1], sums, sems.at[0, count])
    sums_in.start()
    for copy in coming:
        copy.start()
    for arrive, depart in zip(coming, going):
        arrive.wait()
        depart.start()
    sums_in.wait()
    tiles = 2 * channels * freq_count // LANES
    mine = (lax.axis_index("chan") * freq_count + lax.axis_index("freq")) * channels
    lane = lax.broadcasted_iota(jnp.int32, (channels, LANES), 1)
    feature = mine + lax.broadcasted_iota(jnp.int32, (channels, LANES), 0)
    for row, gain in enumerate(gains):
        total = jnp.zeros((channels, LANES), F32)
        for tile in range(tiles):
            at = row * tiles + tile
            total = total + jnp.where(lane + tile * LANES == feature, sums[at : at + 1, :], 0.0)
        gain[...] = jnp.sum(total.T, axis=0, keepdims=True)
        going[count + row].start()
    for copy in going:
        copy.wait()


def settle(arrays, sums, sizes):
    out = [jax.ShapeDtypeStruct(a.shape, a.dtype) for a in arrays]
    out += [jax.ShapeDtypeStruct((1, sizes.channels), F32)] * 2
    return pl.pallas_call(
        functools.partial(settle_kernel, len(arrays), sizes.channels, sizes.freq_count),
        out_shape=out,
        in_specs=[ANY_SPEC] * (len(arrays) + 1),
        out_specs=[ANY_SPEC] * len(out),
        scratch_shapes=[pltpu.VMEM(a.shape, a.dtype) for a in out + [sums]]
        + [pltpu.SemaphoreType.DMA((2, len(out)))],
        name="settle",
    )(*arrays, sums)


def one_sequence(
    tokens, cotangent, first_gain, second_gain, w_value, w_gate, w_out, w_up, w_down, raw_kernel, lengths
):
    freq_count = lax.axis_size("freq")
    _, here, half = tokens.shape
    sizes = Sizes(freq_count, here, half, raw_kernel.shape[1] * freq_count)
    tables = conv_tables(sizes)
    plan = Plan(sizes, tables)
    shards = (w_value, w_gate, w_out, w_up, w_down)
    out_shape = (
        [jax.ShapeDtypeStruct((2, here, half), BF16), jax.ShapeDtypeStruct((2, here, half), F32)]
        + [jax.ShapeDtypeStruct(w.shape, F32) for w in shards]
        + [
            jax.ShapeDtypeStruct((4 * half // LANES + 4, LANES), F32),
            jax.ShapeDtypeStruct((sizes.groups, freq_count, sizes.group, LANES), F32),
        ]
    )
    results = pl.pallas_call(
        functools.partial(block_kernel, plan),
        out_shape=out_shape,
        in_specs=[ANY_SPEC] * (11 + len(tables)),
        out_specs=[ANY_SPEC] * len(out_shape),
        scratch_shapes=plan.scratch,
        compiler_params=pltpu.CompilerParams(
            collective_id=0, has_side_effects=True, vmem_limit_bytes=60 << 20
        ),
        name="block",
    )(
        tokens,
        cotangent,
        first_gain,
        second_gain,
        lengths,
        raw_kernel.reshape(sizes.groups, freq_count, sizes.group, LANES),
        *shards,
        *tables,
    )
    *arrays, gain_sums, grad_kernel = results
    *arrays, grad_kernel, first_grad, second_grad = settle([*arrays, grad_kernel], gain_sums, sizes)
    return (*arrays, first_grad.T, second_grad.T, grad_kernel.reshape(raw_kernel.shape))


def fits(mesh):
    freq_count = mesh.shape["freq"]
    return lambda tokens, w_value, w_up, raw_kernel: (
        mesh.shape["chan"] == 2
        and tokens.shape[0] == 2
        and freq_count == 16
        and w_value.shape[1] == 6 * LANES
        and w_value.shape[0] % (16 * freq_count) == 0
        and w_value.shape[1] % (16 * freq_count) == 0
        and w_value.shape[1] % 256 == 0
        and w_up.shape[1] == PIECES * w_value.shape[1]
        and tokens.shape[1] % (2 * LANES * freq_count) == 0
        and raw_kernel.shape[1] == LANES * freq_count
        and (tokens.shape[1] + raw_kernel.shape[1]) // LANES % 16 == 0
    )


D = 768
SEQ_MB = 1
MICRO = 2


HIGHEST = lax.Precision.HIGHEST


def circle(height, breadth, period):
    first_index = lax.broadcasted_iota(jnp.int32, (height, breadth), 0)
    second_index = lax.broadcasted_iota(jnp.int32, (height, breadth), 1)
    phase_angle = (first_index * second_index % period).astype(jnp.float32) * (
        2.0 * math.pi / period
    )
    return (jnp.cos(phase_angle), jnp.sin(phase_angle))


def make_tables(padded_size):
    inner_size = 128
    outer_size = padded_size // inner_size
    outer_cos, outer_sin = circle(outer_size, outer_size, outer_size)
    inner_cos, inner_sin = circle(inner_size, inner_size, inner_size)
    twist_cos, twist_sin = circle(outer_size, inner_size, padded_size)
    return (outer_cos, outer_sin, inner_cos, inner_sin, twist_cos, twist_sin)


def spectrum(signal, padded_size, tables):
    outer_cos, outer_sin, inner_cos, inner_sin, twist_cos, twist_sin = tables
    inner_size = inner_cos.shape[0]
    pad_width = [(0, 0)] * (signal.ndim - 1) + [(0, padded_size - signal.shape[-1])]
    grid_values = jnp.pad(signal, pad_width).reshape(
        signal.shape[:-1] + (padded_size // inner_size, inner_size)
    )
    part_real = jnp.einsum("...ab,fa->...fb", grid_values, outer_cos, precision=HIGHEST)
    part_imag = -jnp.einsum("...ab,fa->...fb", grid_values, outer_sin, precision=HIGHEST)
    turned_real = part_real * twist_cos + part_imag * twist_sin
    turned_imag = part_imag * twist_cos - part_real * twist_sin
    spec_real = jnp.einsum(
        "...fb,bg->...fg", turned_real, inner_cos, precision=HIGHEST
    ) + jnp.einsum("...fb,bg->...fg", turned_imag, inner_sin, precision=HIGHEST)
    spec_imag = jnp.einsum(
        "...fb,bg->...fg", turned_imag, inner_cos, precision=HIGHEST
    ) - jnp.einsum("...fb,bg->...fg", turned_real, inner_sin, precision=HIGHEST)
    return (spec_real, spec_imag)


def signal_of(spec_real, spec_imag, keep_count, tables):
    outer_cos, outer_sin, inner_cos, inner_sin, twist_cos, twist_sin = tables
    padded_size = spec_real.shape[-1] * spec_real.shape[-2]
    back_real = jnp.einsum("...fg,bg->...fb", spec_real, inner_cos, precision=HIGHEST) - jnp.einsum(
        "...fg,bg->...fb", spec_imag, inner_sin, precision=HIGHEST
    )
    back_imag = jnp.einsum("...fg,bg->...fb", spec_imag, inner_cos, precision=HIGHEST) + jnp.einsum(
        "...fg,bg->...fb", spec_real, inner_sin, precision=HIGHEST
    )
    turned_real = back_real * twist_cos - back_imag * twist_sin
    turned_imag = back_imag * twist_cos + back_real * twist_sin
    grid_values = (
        jnp.einsum("...fb,af->...ab", turned_real, outer_cos, precision=HIGHEST)
        - jnp.einsum("...fb,af->...ab", turned_imag, outer_sin, precision=HIGHEST)
    ) / padded_size
    flat_values = grid_values.reshape(grid_values.shape[:-2] + (padded_size,))
    return flat_values[..., :keep_count]


def shape_kernel(raw_taps, live_taps):
    padded = jnp.pad(raw_taps, ((0, 0), (1, 1)))
    pooled = (padded[:, :-2] + padded[:, 1:-1] + padded[:, 2:]) / 3.0
    return (pooled - THRESH * jnp.tanh(pooled / THRESH)) * live_taps


def row_norm(values):
    row_width = values.shape[-1] * lax.axis_size("chan")
    row_total, row_square = lax.psum(
        (jnp.sum(values, axis=-1), jnp.sum(values * values, axis=-1)), "chan"
    )
    center = row_total / row_width
    spread = row_square / row_width - center * center
    scale = lax.rsqrt(spread + EPSILON)[..., None]
    return ((values - center[..., None]) * scale, scale)


def row_back(grad_rows, normed, scale, gain_row):
    row_width = grad_rows.shape[-1] * lax.axis_size("chan")
    scaled = grad_rows * gain_row
    sum_plain, sum_cross = lax.psum(
        (jnp.sum(scaled, axis=-1), jnp.sum(scaled * normed, axis=-1)), "chan"
    )
    return scale * (
        scaled - sum_plain[..., None] / row_width - normed * sum_cross[..., None] / row_width
    )


def features(values):
    return lax.all_gather(values, "chan", axis=2, tiled=True)


def partial_sum(values):
    return lax.psum_scatter(
        values.astype(jnp.bfloat16), "chan", scatter_dimension=2, tiled=True
    ).astype(jnp.float32)


def to_channels(values):
    return lax.all_to_all(
        jnp.swapaxes(values, 1, 2), "freq", split_axis=1, concat_axis=2, tiled=True
    )


def to_tokens(values):
    arrived = lax.all_to_all(values, "freq", split_axis=2, concat_axis=1, tiled=True)
    return jnp.swapaxes(arrived, 1, 2)


def by_features(
    tokens,
    cotangent,
    first_gain,
    second_gain,
    w_value,
    w_gate,
    w_out,
    w_up,
    w_down,
    raw_kernel,
    lengths,
):
    full_value, full_gate, full_out, full_up, full_down = (
        lax.all_gather(w_value, "freq", axis=0, tiled=True),
        lax.all_gather(w_gate, "freq", axis=0, tiled=True),
        lax.all_gather(w_out, "freq", axis=0, tiled=True),
        lax.all_gather(w_up, "freq", axis=0, tiled=True),
        lax.all_gather(w_down, "freq", axis=0, tiled=True),
    )
    freq_count = lax.axis_size("freq")
    chan_width = tokens.shape[2]
    channels = chan_width // freq_count
    seq_length = tokens.shape[1] * freq_count
    padded_size = 2 * seq_length
    tables = make_tables(padded_size)
    kernel_rows = lax.all_to_all(raw_kernel, "freq", split_axis=0, concat_axis=1, tiled=True)
    tap_count = kernel_rows.shape[1]
    my_lengths = lax.dynamic_slice_in_dim(lengths, lax.axis_index("freq") * channels, channels)
    tap_index = lax.broadcasted_iota(jnp.int32, (channels, tap_count), 1)
    live_taps = (tap_index < my_lengths[:, None]).astype(jnp.float32)
    kernel, kernel_pull = jax.vjp(functools.partial(shape_kernel, live_taps=live_taps), kernel_rows)
    kernel_real, kernel_imag = spectrum(kernel, padded_size, tables)
    hidden_width = full_up.shape[1]
    shard_factor = 1
    totals = (
        jnp.zeros((D // shard_factor, chan_width), jnp.float32),
        jnp.zeros((D // shard_factor, chan_width), jnp.float32),
        jnp.zeros((D // shard_factor, chan_width), jnp.float32),
        jnp.zeros((D // shard_factor, hidden_width), jnp.float32),
        jnp.zeros((D // shard_factor, hidden_width), jnp.float32),
        jnp.zeros((chan_width // shard_factor, 1), jnp.float32),
        jnp.zeros((chan_width // shard_factor, 1), jnp.float32),
    )
    kernel_grad = jnp.zeros((channels, tap_count), jnp.float32)
    outputs = []
    input_grads = []
    for micro_index in range(MICRO):
        rows_here = tokens[micro_index * SEQ_MB : (micro_index + 1) * SEQ_MB].astype(jnp.float32)
        first_normed, first_scale = row_norm(rows_here)
        input1 = features((first_normed * first_gain).astype(jnp.bfloat16))
        value_low = jnp.einsum(
            "bld,de->ble", input1, full_value, preferred_element_type=jnp.float32
        ).astype(jnp.bfloat16)
        gate_proj = jnp.einsum("bld,de->ble", input1, full_gate, preferred_element_type=jnp.float32)
        signal = to_channels(value_low).astype(jnp.float32)
        signal_real, signal_imag = spectrum(signal, padded_size, tables)
        mixed = signal_of(
            signal_real * kernel_real - signal_imag * kernel_imag,
            signal_real * kernel_imag + signal_imag * kernel_real,
            seq_length,
            tables,
        )
        mixed_rows = to_tokens(mixed.astype(jnp.bfloat16)).astype(jnp.float32)
        gate_act, gate_pull = jax.vjp(jax.nn.silu, gate_proj)
        inner_low = (mixed_rows * gate_act).astype(jnp.bfloat16)
        residual = rows_here + partial_sum(
            jnp.einsum("ble,oe->blo", inner_low, full_out, preferred_element_type=jnp.float32)
        )
        second_normed, second_scale = row_norm(residual)
        input2 = features((second_normed * second_gain).astype(jnp.bfloat16))
        hidden = jnp.einsum("bld,df->blf", input2, full_up, preferred_element_type=jnp.float32)
        activated, act_pull = jax.vjp(jax.nn.gelu, hidden)
        act_low = activated.astype(jnp.bfloat16)
        result = residual + partial_sum(
            jnp.einsum("blf,of->blo", act_low, full_down, preferred_element_type=jnp.float32)
        )
        outputs.append(result.astype(jnp.bfloat16))
        grad_rows_out = cotangent[micro_index * SEQ_MB : (micro_index + 1) * SEQ_MB]
        grad_full = features(grad_rows_out)
        grad_act = jnp.einsum(
            "blo,of->blf", grad_full, full_down, preferred_element_type=jnp.float32
        )
        down_grad = jnp.einsum(
            "blo,blf->of", grad_full, act_low, preferred_element_type=jnp.float32
        )
        grad_hidden = act_pull(grad_act)[0].astype(jnp.bfloat16)
        up_grad = jnp.einsum("bld,blf->df", input2, grad_hidden, preferred_element_type=jnp.float32)
        grad_in2 = partial_sum(
            jnp.einsum("blf,df->bld", grad_hidden, full_up, preferred_element_type=jnp.float32)
        )
        second_grad = jnp.sum(grad_in2 * second_normed, axis=(0, 1))
        grad_residual = grad_rows_out.astype(jnp.float32) + row_back(
            grad_in2, second_normed, second_scale, second_gain
        )
        grad_branch = features(grad_residual.astype(jnp.bfloat16))
        grad_inner = jnp.einsum(
            "blo,oe->ble", grad_branch, full_out, preferred_element_type=jnp.float32
        )
        out_grad = jnp.einsum(
            "blo,ble->oe", grad_branch, inner_low, preferred_element_type=jnp.float32
        )
        grad_mixed = to_channels((grad_inner * gate_act).astype(jnp.bfloat16)).astype(jnp.float32)
        grad_real, grad_imag = spectrum(grad_mixed, padded_size, tables)
        grad_signal = signal_of(
            grad_real * kernel_real + grad_imag * kernel_imag,
            grad_imag * kernel_real - grad_real * kernel_imag,
            seq_length,
            tables,
        )
        kernel_grad = kernel_grad + jnp.sum(
            signal_of(
                grad_real * signal_real + grad_imag * signal_imag,
                grad_imag * signal_real - grad_real * signal_imag,
                tap_count,
                tables,
            ),
            axis=0,
        )
        grad_signal_rows = to_tokens(grad_signal.astype(jnp.bfloat16))
        grad_gate_rows = gate_pull(grad_inner * mixed_rows)[0].astype(jnp.bfloat16)
        value_grad = jnp.einsum(
            "bld,ble->de", input1, grad_signal_rows, preferred_element_type=jnp.float32
        )
        gate_grad = jnp.einsum(
            "bld,ble->de", input1, grad_gate_rows, preferred_element_type=jnp.float32
        )
        grad_in1 = partial_sum(
            jnp.einsum(
                "ble,de->bld", grad_signal_rows, full_value, preferred_element_type=jnp.float32
            )
            + jnp.einsum(
                "ble,de->bld", grad_gate_rows, full_gate, preferred_element_type=jnp.float32
            )
        )
        first_grad = jnp.sum(grad_in1 * first_normed, axis=(0, 1))
        input_grads.append(
            grad_residual + row_back(grad_in1, first_normed, first_scale, first_gain)
        )
        local_terms = (
            value_grad,
            gate_grad,
            out_grad,
            up_grad,
            down_grad,
            first_grad[:, None],
            second_grad[:, None],
        )
        totals = tuple((left + right for left, right in zip(totals, local_terms)))
    totals = lax.psum_scatter(totals, "freq", scatter_dimension=0, tiled=True)
    raw_grad = kernel_pull(kernel_grad)[0]
    grad_kernel = lax.all_to_all(raw_grad, "freq", split_axis=1, concat_axis=0, tiled=True)
    output = jnp.concatenate(outputs, axis=0)
    grad_input = jnp.concatenate(input_grads, axis=0)
    return (
        output,
        grad_input,
        totals[0],
        totals[1],
        totals[2],
        totals[3],
        totals[4],
        totals[5],
        totals[6],
        grad_kernel,
    )


def solution(mesh):
    specs = dict(
        mesh=mesh,
        in_specs=(
            P(None, "freq", "chan"),
            P(None, "freq", "chan"),
            P("chan"),
            P("chan"),
            P("freq", "chan"),
            P("freq", "chan"),
            P("freq", "chan"),
            P("freq", "chan"),
            P("freq", "chan"),
            P("chan", "freq"),
            P("chan"),
        ),
        out_specs=(
            P(None, "freq", "chan"),
            P(None, "freq", "chan"),
            P("freq", "chan"),
            P("freq", "chan"),
            P("freq", "chan"),
            P("freq", "chan"),
            P("freq", "chan"),
            P("freq", "chan"),
            P("freq", "chan"),
            P("chan", "freq"),
        ),
        check_vma=False,
    )

    def step(*args):
        whole = fits(mesh)(args[0], args[4], args[7], args[9])
        return jax.shard_map(one_sequence if whole else by_features, **specs)(*args)

    return step
```

```python
import functools
import math
import types

import jax
import jax.numpy as jnp
import numpy as np
from jax import lax
from jax.experimental import pallas as pl
from jax.experimental.pallas import tpu as pltpu
from jax.sharding import PartitionSpec as P

THRESH = 0.003
EPSILON = 1e-05
LANES = 128
MESH = pl.DeviceIdType.MESH
F32 = jnp.float32
BF16 = jnp.bfloat16


def bit_sizes(freq_count):
    return [1 << i for i in reversed(range(freq_count.bit_length() - 1))]


class Place:
    def __init__(self, freq_count):
        self.freq_count = freq_count
        self.freq = lax.axis_index("freq")
        self.chan = lax.axis_index("chan")
        self.bits = bit_sizes(freq_count)
        self.coords = [self.chan] + [lax.rem(self.freq // b, 2) for b in self.bits]
        self.dims = len(self.coords)
        self.core = self.coords[-1]

    def other(self, flipped):
        freq, chan = self.freq, self.chan
        for dim in flipped:
            if dim == 0:
                chan = 1 - chan
            else:
                bit = self.bits[dim - 1]
                freq = freq + bit - 2 * bit * self.coords[dim]
        return (freq, chan)


def flips(dims):
    return [
        tuple(dim for at, dim in enumerate(dims) if mask >> at & 1) for mask in range(1, 1 << len(dims))
    ]


def remote(source, target, send, recv, device):
    return pltpu.make_async_remote_copy(
        src_ref=source,
        dst_ref=target,
        send_sem=send,
        recv_sem=recv,
        device_id=device,
        device_id_type=MESH,
    )


class Line:
    def __init__(self, way, high, low):
        self.way, self.high, self.low = way, high, low

    def ends(self, place):
        middle = place.coords[self.high] + place.coords[self.low] == 1
        end = place.coords[self.high] + place.coords[self.low] != 1
        return {ACROSS: (middle, middle), INWARD: (end, middle), OUTWARD: (middle, end)}[self.way]

    def flipped(self):
        return (self.high, self.low) if self.way == ACROSS else (self.low,)


def when(condition, action):
    if condition is None:
        action()
    else:
        pl.when(condition)(action)


class Leg:
    def __init__(self, copy, ends=(None, None)):
        self.copy, self.ends = copy, ends

    def start(self):
        when(self.ends[0], self.copy.start)

    def wait(self):
        if self.ends[0] is None:
            self.copy.wait()
        else:
            when(self.ends[0], self.copy.wait_send)
            when(self.ends[1], self.copy.wait_recv)


def flips_of(phase):
    return [phase.flipped()] if isinstance(phase, Line) else flips(phase)


def is_outward(phase):
    return isinstance(phase, Line) and phase.way == OUTWARD


def slots(phases):
    return sum(len(flips_of(phase)) for phase in phases if not is_outward(phase))


def first_slot(phases, at):
    return slots(phases[:at]) - is_outward(phases[at])


class Gather:
    def __init__(self, place, buffer, dims, phases, send, recv, prepare):
        self.place, self.buffer, self.dims, self.phases = place, buffer, dims, phases
        self.send, self.recv, self.prepare = send, recv, prepare
        self.turn = 0

    def copies(self, phase):
        done, step = set(), self.phases[phase]
        for before in self.phases[:phase]:
            if not isinstance(before, Line):
                done.update(before)
            elif before.way == OUTWARD:
                done.update((before.high, before.low))
        index = [slice(None) if dim in done else self.place.coords[dim] for dim in self.dims]
        ends = (None, None)
        if isinstance(step, Line):
            ends = step.ends(self.place)
            if step.way == OUTWARD:
                index[self.dims.index(step.high)] = 1 - self.place.coords[step.high]
        region = self.buffer.at[tuple(index)]
        base = first_slot(self.phases, phase)
        return [
            Leg(
                remote(region, region, self.send.at[k], self.recv.at[base + k], self.place.other(flipped)), ends
            )
            for k, flipped in enumerate(flips_of(step))
        ]

    def go(self):
        if self.turn > len(self.phases):
            return
        if self.turn == 0:
            self.prepare()
        else:
            for copy in self.copies(self.turn - 1):
                copy.wait()
        if self.turn < len(self.phases):
            for copy in self.copies(self.turn):
                copy.start()
        self.turn += 1

    def finish(self):
        while self.turn <= len(self.phases):
            self.go()


class Once:
    def __init__(self, begin):
        self.begin, self.copy = begin, None

    def go(self):
        if self.copy is None:
            self.copy = self.begin()

    def finish(self):
        self.go()
        self.copy.wait()


class Reduce:
    def __init__(self, place, total, landing, dims, phases, send, recv, out, prepare):
        self.place, self.total, self.landing, self.dims = place, total, landing, dims
        self.phases, self.send, self.recv, self.out = phases, send, recv, out
        self.prepare = prepare
        self.turn = 0

    def region(self, phase, flipped):
        fixed, step = set(), self.phases[phase]
        for before in self.phases[:phase]:
            if not isinstance(before, Line):
                fixed.update(before)
            elif before.way == ACROSS:
                fixed.add(before.high)
        if not isinstance(step, Line):
            fixed.update(step)
        coords = self.place.coords
        index = [
            (1 - coords[dim] if dim in flipped else coords[dim]) if dim in fixed else slice(None)
            for dim in self.dims
        ]
        if isinstance(step, Line):
            mine = coords[step.high]
            keeps = step.way == ACROSS and not flipped
            index[self.dims.index(step.high)] = mine if keeps else 1 - mine
        return tuple(index)

    def copies(self, phase):
        step = self.phases[phase]
        base = first_slot(self.phases, phase)
        ends = step.ends(self.place) if isinstance(step, Line) else (None, None)
        return [
            Leg(
                remote(
                    self.total.at[self.region(phase, flipped)],
                    self.landing[phase].at[k],
                    self.send.at[k],
                    self.recv.at[base + k],
                    self.place.other(flipped),
                ),
                ends,
            )
            for k, flipped in enumerate(flips_of(step))
        ]

    def add(self, phase):
        kept = self.region(phase, ())
        free = [at for at, part in enumerate(kept) if isinstance(part, slice)]
        landing, step = self.landing[phase], self.phases[phase]

        def one(turn, carry):
            where, there = list(kept), []
            for at, dim in enumerate(free):
                bit = lax.rem(turn // (1 << (len(free) - 1 - at)), 2)
                where[dim] = bit
                there.append(bit)
            where, there = tuple(where), tuple(there)
            total = self.total[where].astype(F32)
            for k in range(len(flips_of(step))):
                total = total + landing[(k,) + there].astype(F32)
            if phase + 1 == len(self.phases):
                self.out[...] = total
            else:
                self.total[where] = total.astype(BF16)
            return carry

        def every():
            if free:
                lax.fori_loop(0, 1 << len(free), one, 0)
            else:
                one(0, 0)

        when(step.ends(self.place)[1] if isinstance(step, Line) else None, every)

    def go(self):
        if self.turn > len(self.phases):
            return
        if self.turn == 0:
            self.prepare()
        else:
            for copy in self.copies(self.turn - 1):
                copy.wait()
            self.add(self.turn - 1)
        if self.turn < len(self.phases):
            for copy in self.copies(self.turn):
                copy.start()
        self.turn += 1

    def finish(self):
        while self.turn <= len(self.phases):
            self.go()


def landing_shapes(phases, dims, rows, columns):
    shapes, free = [], len(dims)
    for step in phases:
        if isinstance(step, Line):
            free -= 0 if step.way == INWARD else 1
            shapes.append((1,) + (2,) * (free - (step.way == INWARD)) + (rows, columns))
        else:
            free -= len(step)
            shapes.append((len(flips(step)),) + (2,) * free + (rows, columns))
    return shapes


class Spread:
    def __init__(self, place, total, landing, phases, send, recv):
        self.place, self.total, self.landing, self.phases = place, total, landing, phases
        self.send, self.recv = send, recv
        self.turn = 0

    def copies(self, phase):
        base = sum(len(flips(dims)) for dims in self.phases[:phase])
        return base, [
            remote(
                self.total.at[phase],
                self.landing.at[base + k],
                self.send.at[k],
                self.recv.at[base + k],
                self.place.other(flipped),
            )
            for k, flipped in enumerate(flips(self.phases[phase]))
        ]

    def go(self):
        if self.turn > len(self.phases):
            return
        if self.turn:
            base, copies = self.copies(self.turn - 1)
            total = self.total[self.turn - 1]
            for k, copy in enumerate(copies):
                copy.wait()
                total = total + self.landing[base + k]
            self.total[self.turn] = total
        if self.turn < len(self.phases):
            for copy in self.copies(self.turn)[1]:
                copy.start()
        self.turn += 1

    def finish(self):
        while self.turn <= len(self.phases):
            self.go()


class Exchange:
    def __init__(self, count, me, device, source, target, all_sent, all_landed, sems):
        self.count, self.me, self.device = count, me, device
        self.source, self.target = source, target
        self.all_sent, self.all_landed, self.sems = all_sent, all_landed, sems

    def start(self):
        def one(step, carry):
            other = lax.rem(self.me + step, self.count)
            remote(
                self.source(other), self.target(self.me), self.sems.at[0], self.sems.at[1], self.device(other)
            ).start()
            return carry

        lax.fori_loop(1, self.count, one, 0, unroll=True)

    def wait(self):
        for part, sem in ((self.all_sent, self.sems.at[0]), (self.all_landed, self.sems.at[1])):
            pltpu.make_async_copy(part, part, sem).wait()


class Sizes:
    def __init__(self, freq_count, here, half, taps):
        self.freq_count = freq_count
        self.here = here
        self.half = half
        self.cols = here // LANES
        self.channels = half // freq_count
        self.group = LANES // freq_count
        self.groups = self.channels // self.group
        self.chunk = self.cols * self.group
        self.devices = 2 * freq_count
        self.tap_rows = taps // LANES
        self.rows = here * freq_count // LANES + self.tap_rows
        self.size = self.rows * LANES
        self.group_rows = self.group * self.rows


def conv_tables(sizes):
    rows, size = sizes.rows, sizes.size
    f = np.arange(rows)
    a_of, imag = [], []
    for col in range(sizes.cols):
        for seq in range(2):
            for block in range(sizes.freq_count):
                a_of.append(block * sizes.cols + col)
                imag.append(seq)
    a_of, imag = np.array(a_of), np.array(imag)
    angle = 2 * np.pi * np.outer(f, a_of) / rows
    cos, sin = np.cos(angle), np.sin(angle)
    into = np.concatenate([np.where(imag, sin, cos), np.where(imag, cos, -sin)], axis=0)
    outof = into.T / size
    angle = 2 * np.pi * np.outer(f, np.arange(sizes.tap_rows)) / rows
    taps_into = np.concatenate([np.cos(angle), -np.sin(angle)], axis=0)
    taps_outof = taps_into.T / size
    b = np.arange(LANES)
    angle = 2 * np.pi * np.outer(f, b) / size
    turn = np.stack([np.cos(angle), np.sin(angle)])
    angle = 2 * np.pi * np.outer(b, b) / LANES
    cos, sin = np.cos(angle), np.sin(angle)
    ahead = np.block([[cos, -sin], [sin, cos]])
    return (
        jnp.asarray(into, BF16),
        jnp.asarray(outof, BF16),
        jnp.asarray(taps_into, BF16),
        jnp.asarray(taps_outof, BF16),
        jnp.asarray(turn, F32),
        jnp.asarray(ahead, BF16),
        jnp.asarray(ahead.T, BF16),
    )


def dot(left, right):
    return jnp.dot(left, right, preferred_element_type=F32)


def spectrum_into(sizes, load, into, turn, ahead, inner, spectrum):
    rows = sizes.rows
    for pair in range(sizes.group // 2):
        both = jnp.concatenate([load(2 * pair), load(2 * pair + 1)], axis=1).astype(BF16)
        part = dot(into[...], both)
        for side in range(2):
            real = part[:rows, side * LANES : (side + 1) * LANES]
            imag = part[rows:, side * LANES : (side + 1) * LANES]
            start = (2 * pair + side) * rows
            inner[start : start + rows, :] = jnp.concatenate(
                [real * turn[0] + imag * turn[1], imag * turn[0] - real * turn[1]], axis=1
            ).astype(BF16)
    spectrum[...] = dot(inner[...], ahead[...])


def signal_from(sizes, product, outof, turn, behind, inner, store):
    rows = sizes.rows
    inner[...] = dot(product, behind[...])
    for pair in range(sizes.group // 2):
        sides = []
        for side in range(2):
            start = (2 * pair + side) * rows
            real, imag = inner[start : start + rows, :LANES], inner[start : start + rows, LANES:]
            sides.append(
                jnp.concatenate(
                    [real * turn[0] - imag * turn[1], imag * turn[0] + real * turn[1]], axis=0
                ).astype(BF16)
            )
        got = dot(outof[...], jnp.concatenate(sides, axis=1))
        for side in range(2):
            store(2 * pair + side, got[:, side * LANES : (side + 1) * LANES])


def times(left, right, conj):
    a, b = left[:, :LANES], left[:, LANES:]
    c, d = right[:, :LANES], right[:, LANES:]
    if conj:
        return jnp.concatenate([a * c + b * d, b * c - a * d], axis=1).astype(BF16)
    return jnp.concatenate([a * c - b * d, a * d + b * c], axis=1).astype(BF16)


def to_chunks(sizes, rows, target):
    turned = rows.T.reshape(sizes.freq_count, sizes.group, sizes.here)
    pieces = [turned[:, :, col * LANES : (col + 1) * LANES] for col in range(sizes.cols)]
    target[...] = jnp.concatenate(pieces, axis=1).astype(BF16)


def from_chunks(sizes, chunks):
    wide = chunks[...].astype(F32)
    for c in range(2):
        for col in range(sizes.cols):
            piece = wide[
                c * sizes.freq_count : (c + 1) * sizes.freq_count, col * sizes.group : (col + 1) * sizes.group
            ]
            yield c, slice(col * LANES, (col + 1) * LANES), piece.reshape(LANES, LANES).T


def chunk_loader(sizes, ref):
    def load(channel):
        pieces = [
            ref[pl.ds(col * sizes.group + channel, sizes.devices, stride=sizes.chunk), :]
            for col in range(sizes.cols)
        ]
        return jnp.concatenate(pieces, axis=0)

    return load


def chunk_storer(sizes, ref):
    def store(channel, values):
        for col in range(sizes.cols):
            ref[pl.ds(col * sizes.group + channel, sizes.devices, stride=sizes.chunk), :] = values[
                col * sizes.devices : (col + 1) * sizes.devices
            ]

    return store


def pooled_taps(taps):
    lane = lax.broadcasted_iota(jnp.int32, taps.shape, 2)
    zero = jnp.zeros_like(taps[:1])
    after = pltpu.roll(taps, LANES - 1, 2)
    before = pltpu.roll(taps, 1, 2)
    after = jnp.where(lane == LANES - 1, jnp.concatenate([after[1:], zero], axis=0), after)
    before = jnp.where(lane == 0, jnp.concatenate([zero, before[:-1]], axis=0), before)
    return (before + taps + after) / 3.0


def live_mask(shape, lengths):
    tap = lax.broadcasted_iota(jnp.int32, shape, 0) * LANES + lax.broadcasted_iota(
        jnp.int32, shape, 2
    )
    return (tap < lengths[None]).astype(F32)


VALUE, GATE, OUT, UP, DOWN = range(5)
ACT, HID = range(2)
PIECES = 4
ACROSS, INWARD, OUTWARD = range(3)
V0, V1, V2, G, O, U0, U1, U2, U3, D0, D1, D2, D3, S, T, C, W = range(17)
TOPS = [lambda n: (1, 2)]
LOW = [lambda n: (2,)]
SPREAD_OUT = LOW + [lambda n: Line(ACROSS, 1, 2), lambda n: Line(OUTWARD, 1, 2)]
BRING_IN = [lambda n: Line(INWARD, 1, 2), lambda n: Line(ACROSS, 1, 2)] + LOW
X, Y, CORE = [lambda n: (0,)], [lambda n: (n - 2,)], [lambda n: (n - 1,)]
PLANE = [lambda n: (0, n - 2)]
GATHER_PHASES = {
    G: SPREAD_OUT + Y + X + CORE,
    O: SPREAD_OUT + Y + X + CORE,
    U0: SPREAD_OUT + Y + CORE,
    D0: SPREAD_OUT + Y + CORE,
    U1: SPREAD_OUT + Y + CORE,
    D1: Y + SPREAD_OUT + CORE,
    U2: Y + SPREAD_OUT + CORE,
    D2: SPREAD_OUT + Y + CORE,
    U3: SPREAD_OUT + Y + CORE,
    D3: SPREAD_OUT + Y + CORE,
    V0: TOPS + PLANE + CORE,
    V1: TOPS + PLANE + CORE,
    V2: TOPS + PLANE + CORE,
}
REDUCE_PHASES = {
    G: X + Y + BRING_IN,
    O: X + Y + BRING_IN,
    U0: Y + BRING_IN,
    D0: Y + BRING_IN,
    U1: Y + BRING_IN,
    D1: BRING_IN + Y,
    U2: Y + BRING_IN,
    D2: BRING_IN + Y,
    U3: Y + BRING_IN,
    D3: Y + BRING_IN,
    V0: PLANE + TOPS,
    V1: PLANE + TOPS,
    V2: PLANE + TOPS,
}
SPREAD_PHASES = CORE + PLANE + TOPS


class Order:
    tokens = (D1, G, U2, O, G, U3, D3, O, U0, V0, D2, V2, V1, U1, T)
    norm = ()
    w_value = ((C, D0, U3, U0), (D0, V0, U1, O, U0, U2, G), (D2,))
    value = ((G,), (), ())
    sent = ()
    taps = (O, D0, G, U3)
    kernel = ()
    arrive = ((), (O, U2, D1, D3), ())
    conv = ((D2, U0, U1), (U3,), ())
    convolved = ()
    cotangent = ()
    turn = (U1, U0)
    w_gate = (U3,)
    gate = (D3, D1, U2, D0, O)
    mixed = ((), (), ())
    inner = ()
    w_out = ()
    residual = (D2,)
    turn_near = ()
    w_up = ((), (V0,), (), (D1,))
    near_up = ((D1, U1, D0, D3), (), (D2,), ())
    wait_far = ((), ())
    far_up = ((D3,), ())
    down_a = ((), (), (V1,), (V2,))
    far_a = ((), (), (), ())
    far_b = ()
    near_down = (D2, D0)
    far_back = ((D1,), (D3,))
    norm_back = ()
    sent_back = ()
    output = (G, U0, U3, D2, U1, O, D3)
    arrive_back = ((D1, D0), (), (D2,))
    conv_back = ((U0,), (), (G, U3))
    convolved_back = (U2, U1)
    taps_back = (D0, D1, O, U0, W)
    signal = ((), (G, U3, V0), ())
    input_back = ((), (), (O,))
    first_back = (V1, U2, U1, D0, D1, V2, U0)
    finish_output = (D3, U3, G, S, V0)
    last = (O, U1, D3, U2, V2, G, V1, O)
    finish_grad = ()
    taps_home = (U2,)
    end = (D2, S)


VMEM_SPEC = pl.BlockSpec(memory_space=pltpu.VMEM)
ANY_SPEC = pl.BlockSpec(memory_space=pl.ANY)
GELU_SCALE = math.sqrt(2.0 / math.pi)
GELU_CUBE = 0.044715


def dot_nt(left, right):
    return lax.dot_general(left, right, (((1,), (1,)), ((), ())), preferred_element_type=F32)


def norm(values):
    center = jnp.mean(values, axis=-1, keepdims=True)
    shifted = values - center
    scale = lax.rsqrt(jnp.mean(shifted * shifted, axis=-1, keepdims=True) + EPSILON)
    return shifted * scale, scale


def norm_back(grad_rows, normed, scale, gain):
    scaled = grad_rows * gain
    plain = jnp.mean(scaled, axis=-1, keepdims=True)
    cross = jnp.mean(scaled * normed, axis=-1, keepdims=True)
    return scale * (scaled - plain - normed * cross)


class Part:
    def __init__(self, weight, piece, columns, dims, at):
        self.weight, self.piece, self.columns, self.at = weight, piece, columns, at
        self.dims = tuple(range(1 if weight in (UP, DOWN) else 0, dims))
        self.gather = tuple(phase(dims) for phase in GATHER_PHASES[at])
        self.reduce = tuple(phase(dims) for phase in REDUCE_PHASES[at])


def most(phases):
    return max(len(flips_of(step)) for step in phases)


class Plan:
    def __init__(self, sizes, tables):
        self.sizes = sizes
        here, channels, half = sizes.here, sizes.channels, sizes.half
        width = 2 * half
        self.width = width
        dims = 1 + len(bit_sizes(sizes.freq_count))
        self.dims = dims
        self.rows = rows = width // sizes.freq_count
        pieces = ((VALUE, sizes.groups, LANES), (GATE, 1, half), (OUT, 1, half), (UP, PIECES, half), (DOWN, PIECES, half))
        self.parts = []
        for weight, count, columns in pieces:
            for piece in range(count):
                self.parts.append(Part(weight, piece, columns, dims, len(self.parts)))
        self.spread = tuple(phase(dims) for phase in SPREAD_PHASES)
        groups = [self.spread] + [p.gather for p in self.parts] + [p.reduce for p in self.parts]
        self.partners = sorted(
            {flipped for phases in groups for step in phases for flipped in flips_of(step) if 0 in flipped}
        )

        def vmem(kind, *shape):
            return pltpu.VMEM(shape, kind)

        def sems(*shape):
            return pltpu.SemaphoreType.DMA(shape)

        def weights(bits):
            return [
                vmem(BF16, count, *(2,) * (bits + (weight not in (UP, DOWN))), rows, columns)
                for weight, count, columns in pieces
            ]

        def rows_of(kind, *lead):
            return vmem(kind, *lead, here, width)

        def turned(tokens):
            return vmem(BF16, width // (2 * rows), 2, rows, tokens)

        def turned_half(tokens):
            return vmem(BF16, width // (2 * rows), rows, tokens)

        def halves():
            return vmem(BF16, 2, here, half)

        def tiles():
            return vmem(BF16, PIECES, 2, 2 * here, half)

        def chunks():
            return vmem(BF16, sizes.groups, sizes.devices, sizes.chunk, LANES)

        def spectra(kind):
            return [vmem(kind, sizes.group_rows, 2 * LANES) for _ in range(sizes.groups)]

        def wide():
            return [vmem(F32, sizes.devices * sizes.chunk, LANES) for _ in range(sizes.groups)]

        taps = (sizes.tap_rows, sizes.groups, sizes.group, LANES)
        flat_taps = (sizes.tap_rows * channels, LANES)
        gain_rows = 2 * width // LANES + 4
        scratch = dict(
            x_buf=halves(),
            g_buf=vmem(BF16, 2, 2, here, half),
            gains=[[vmem(F32, half) for _ in range(2)] for _ in range(2)],
            lengths=vmem(jnp.int32, half),
            turned=vmem(F32, half, 8),
            weights=weights(dims - 1),
            grads=weights(dims - 2),
            landings=[
                [vmem(BF16, *shape) for shape in landing_shapes(part.reduce, part.dims[:-1], rows, part.columns)]
                for part in self.parts
            ],
            part_sems=[
                (sems(max(most(p.gather), most(p.reduce))), sems(slots(p.gather)), sems(slots(p.reduce)))
                for p in self.parts
            ],
            kernel_spec=spectra(F32),
            value_spec=spectra(F32),
            grad_spec=spectra(F32),
            inner_into=spectra(BF16),
            inner_from=spectra(F32),
            inner_taps=spectra(F32),
            wide_in=wide(),
            wide_out=wide(),
            taps=vmem(F32, *taps),
            tap_grad=vmem(F32, *taps),
            tap_wide=vmem(F32, *flat_taps),
            sent=chunks(),
            sent_back=chunks(),
            landed=[chunks() for _ in range(4)],
            move_sems=[[sems(2) for _ in range(sizes.groups)] for _ in range(4)],
            tap_sems=[sems(2) for _ in range(2)],
            normed1=rows_of(F32),
            gate=rows_of(F32),
            mixed=rows_of(F32),
            residual=rows_of(F32),
            normed2=rows_of(F32),
            grad_res=rows_of(F32),
            rows=rows_of(F32),
            out_sum=rows_of(F32, 2),
            in2_sum=rows_of(F32),
            scale1=vmem(F32, here, 1),
            scale2=vmem(F32, here, 1),
            input1=rows_of(BF16),
            branch_rows=rows_of(BF16),
            in2_send=rows_of(BF16),
            in2_land=rows_of(BF16),
            input2=rows_of(BF16, 2),
            grad_rows=rows_of(BF16, 2),
            t_input1=(turned(here), turned_half(here)),
            t_branch=(turned(here), turned_half(here)),
            t_input2=(turned(2 * here), turned_half(2 * here)),
            t_grad=(turned(2 * here), turned_half(2 * here)),
            inner_rows=(halves(), halves()),
            signal_rows=[vmem(BF16, sizes.groups, here, 2 * LANES) for _ in range(2)],
            gate_rows=(halves(), halves()),
            tiles=(tiles(), tiles()),
            slopes=vmem(F32, PIECES, 2 * here, half),
            tile_sems=sems(2, 2, PIECES),
            twin_sems=sems(2, 6 + sizes.groups),
            gain_total=vmem(F32, len(self.spread) + 1, gain_rows, LANES),
            gain_land=vmem(F32, slots(self.spread), gain_rows, LANES),
            gain_sems=(sems(most(self.spread)), sems(slots(self.spread))),
            out_send=halves(),
            out_land=halves(),
            gin_send=vmem(BF16, here, half),
            gin_land=vmem(BF16, here, half),
            swap_sems=sems(2, 12),
            local=sems(13 + len(self.parts)),
            tables=[vmem(table.dtype, *table.shape) for table in tables],
        )
        self.scratch, self.tree = jax.tree.flatten(
            scratch, is_leaf=lambda leaf: not isinstance(leaf, (dict, list, tuple))
        )


def row_tiles(count, body, first=0, tile=64):
    def one(step, carry):
        body(pl.ds(pl.multiple_of(first + step * tile, tile), tile))
        return carry

    lax.fori_loop(0, count // tile, one, 0)


def block_kernel(plan, tokens, cotangent, first_gain, second_gain, lengths, raw_kernel, *refs):
    shards, refs = refs[:5], refs[5:]
    tables = refs[:7]
    output, grad_input, *weight_grads = refs[7:14]
    gain_sums, grad_kernel = refs[14:16]
    k = types.SimpleNamespace(**jax.tree.unflatten(plan.tree, refs[16:]))
    into, outof, taps_into, taps_outof, turn, ahead, behind = k.tables
    sizes = plan.sizes
    here, half, width, channels = sizes.here, sizes.half, plan.width, sizes.channels
    place = Place(sizes.freq_count)
    chan, core = place.chan, place.core
    twin = place.other((plan.dims - 1,))
    across = place.other((0,))
    me = chan * sizes.freq_count + place.freq

    def whole(weight, *lead, lanes=slice(None)):
        value = k.weights[weight][lead + (slice(None),) * plan.dims + (lanes,)]
        return value.reshape(width, value.shape[-1])

    def of_group(group):
        return slice(group * LANES, (group + 1) * LANES)

    def both_halves(weight, *lead, lanes=slice(None)):
        return jnp.concatenate([whole(weight, *lead, c, lanes=lanes) for c in range(2)], axis=1)

    def of_chan(values):
        return jnp.where(chan == 0, values[:, :half], values[:, half:])

    def of_other_chan(values):
        return jnp.where(chan == 0, values[:, half:], values[:, :half])

    own = []
    for part in plan.parts:
        source = shards[part.weight].at[:, pl.ds(part.piece * part.columns, part.columns)]
        target = k.weights[part.weight].at[(part.piece,) + tuple(place.coords[dim] for dim in part.dims)]
        own.append(pltpu.make_async_copy(source, target, k.local.at[part.at]))
    for source, target in (
        (tokens.at[chan], k.x_buf.at[chan]),
        (cotangent, k.g_buf.at[chan]),
        (raw_kernel.at[:, place.freq], k.taps.at[place.freq]),
        (first_gain, k.gains[0][0]),
        (second_gain, k.gains[0][1]),
        (lengths, k.lengths),
    ):
        own.append(pltpu.make_async_copy(source, target, k.local.at[len(own)]))
    for source, target in zip(tables, k.tables):
        own.append(pltpu.make_async_copy(source, target, k.local.at[len(own)]))
    for copy in own:
        copy.start()
    own_tokens, own_cotangent, own_taps, *own_rows = own[len(plan.parts) :]
    own_tables, own_rows = own_rows[3:], own_rows[:3]
    barrier = pltpu.get_barrier_semaphore()
    for flipped in plan.partners:
        pl.semaphore_signal(barrier, inc=1, device_id=place.other(flipped), device_id_type=MESH)

    def greet(step, carry):
        peer = (lax.rem(place.freq + step, sizes.freq_count), chan)
        pl.semaphore_signal(barrier, inc=1, device_id=peer, device_id_type=MESH)
        return carry

    lax.fori_loop(1, sizes.freq_count, greet, 0, unroll=True)
    pl.semaphore_wait(barrier, len(plan.partners) + sizes.freq_count - 1)

    def swap(at, source, target):
        copy = remote(source, target, k.swap_sems.at[0, at], k.swap_sems.at[1, at], across)
        copy.start()
        return copy

    moving = {}
    for part in plan.parts:
        moving[part.at] = Gather(
            place,
            k.weights[part.weight].at[part.piece],
            part.dims,
            part.gather,
            k.part_sems[part.at][0],
            k.part_sems[part.at][1],
            own[part.at].wait,
        )

    def ahead_of(names):
        for name in names:
            moving[name].go()

    def all_to_all(move, group, source):
        target = k.landed[move]
        exchange = Exchange(
            sizes.devices,
            me,
            lambda other: (lax.rem(other, sizes.freq_count), other // sizes.freq_count),
            lambda other: source.at[group, other],
            lambda other: target.at[group, other],
            source.at[group, pl.ds(0, sizes.devices - 1)],
            target.at[group, pl.ds(0, sizes.devices - 1)],
            k.move_sems[move][group],
        )
        exchange.start()
        target[group, me] = source[group, me]
        return exchange

    swap_tokens = swap(0, tokens.at[1 - chan], k.x_buf.at[chan])
    swap_gains = [swap(at, ref, k.gains[1][at - 9]) for at, ref in ((9, first_gain), (10, second_gain))]
    for group in range(sizes.groups):
        moving[V0 + group].go()
    others = sizes.freq_count - 1

    def begin(exchange):
        exchange.start()
        return exchange

    tap_move = Exchange(
        sizes.freq_count,
        place.freq,
        lambda other: (other, chan),
        lambda other: raw_kernel.at[:, other],
        lambda other: k.taps.at[other],
        raw_kernel.at[:, pl.ds(0, others)],
        k.taps.at[pl.ds(0, others)],
        k.tap_sems[0],
    )
    moving[T] = Once(lambda: begin(tap_move))
    moving[C] = Once(lambda: swap(2, cotangent, k.g_buf.at[chan]))
    ahead_of(Order.tokens)
    swap_tokens.wait()
    own_tokens.wait()
    for copy in swap_gains + own_rows:
        copy.wait()

    def gain_row(row):
        near, far = k.gains[0][row][...][None], k.gains[1][row][...][None]
        return jnp.concatenate([jnp.where(chan == 0, near, far), jnp.where(chan == 0, far, near)], axis=1)

    first_gain, second_gain = gain_row(0), gain_row(1)

    def first_norm(at):
        rows = jnp.concatenate([k.x_buf[0, at, :], k.x_buf[1, at, :]], axis=1).astype(F32)
        normed, scale = norm(rows)
        k.normed1[at, :] = normed
        k.scale1[at, :] = scale
        k.input1[at, :] = (normed * first_gain).astype(BF16)

    ahead_of(Order.norm)
    row_tiles(here, first_norm)

    def turn_rows(source, target, columns=slice(None)):
        turned = source[...].astype(F32).T.astype(BF16)
        target[:, :, :, columns] = turned.reshape(target.shape[:-1] + (here,))

    arriving = {}

    def share(at, source, target):
        copy = remote(source, target, k.twin_sems.at[0, at], k.twin_sems.at[1, at], twin)
        copy.start()
        arriving[at] = copy

    def share_turned(at, pair):
        share(at, pair[0].at[:, 1 - core], pair[1])

    def need(at):
        if arriving[at] is not None:
            arriving[at].wait()
            arriving[at] = None

    turn_rows(k.input1, k.t_input1[0])
    share_turned(0, k.t_input1)

    def send_chunks(move, group, source, halves):
        for c in range(2):
            devices = pl.ds(c * sizes.freq_count, sizes.freq_count)
            to_chunks(sizes, halves[c], source.at[group, devices])
        return all_to_all(move, group, source)

    moves = []
    for group in range(sizes.groups):
        ahead_of(Order.w_value[group])
        moving[V0 + group].finish()
        ahead_of(Order.value[group])
        got = dot(k.input1[...], both_halves(VALUE, group))
        moves.append(send_chunks(0, group, k.sent, (got[:, :LANES], got[:, LANES:])))
    ahead_of(Order.sent)
    ahead_of(Order.taps)
    moving[T].finish()
    for copy in own_tables:
        copy.wait()
    own_taps.wait()
    k.turned[...] = jnp.broadcast_to(k.lengths[...].astype(F32)[None], (8, half)).T
    lives = [
        k.turned[pl.ds(pl.multiple_of(group * LANES + place.freq * sizes.group, 8), sizes.group), 0:1]
        for group in range(sizes.groups)
    ]
    flat_taps = (sizes.tap_rows, channels, LANES)
    live = live_mask(flat_taps, jnp.concatenate(lives, axis=0))
    pooled = pooled_taps(k.taps[...].reshape(flat_taps))
    shrunk = (pooled - THRESH * jnp.tanh(pooled / THRESH)) * live
    k.tap_wide[...] = shrunk.reshape(sizes.tap_rows * channels, LANES)
    ahead_of(Order.kernel)

    def tap_load(group):
        return lambda c: k.tap_wide[pl.ds(group * sizes.group + c, sizes.tap_rows, stride=channels), :]

    for group in range(sizes.groups):
        spectrum_into(
            sizes, tap_load(group), taps_into, turn, ahead, k.inner_into[group], k.kernel_spec[group]
        )

    def spectrum_of(move, group, spectra):
        flat = (sizes.devices * sizes.chunk, LANES)
        k.wide_in[group][...] = k.landed[move][group].astype(F32).reshape(flat)
        spectrum_into(
            sizes, chunk_loader(sizes, k.wide_in[group]), into, turn, ahead, k.inner_into[group], spectra[group]
        )

    def chunks_from(group, product):
        signal_from(
            sizes, product, outof, turn, behind, k.inner_from[group], chunk_storer(sizes, k.wide_out[group])
        )
        k.sent_back[group] = k.wide_out[group][...].reshape(k.sent_back.shape[1:]).astype(BF16)

    moves_back = []
    for group in range(sizes.groups):
        ahead_of(Order.arrive[group])
        moves[group].wait()
        ahead_of(Order.conv[group])
        spectrum_of(0, group, k.value_spec)
        chunks_from(group, times(k.value_spec[group][...], k.kernel_spec[group][...], False))
        moves_back.append(all_to_all(1, group, k.sent_back))
    ahead_of(Order.convolved)
    ahead_of(Order.cotangent)
    moving[C].finish()
    own_cotangent.wait()
    ahead_of(Order.turn)
    for which, seq in ((0, chan), (1, 1 - chan)):
        k.grad_rows[which] = jnp.concatenate([k.g_buf[0, seq], k.g_buf[1, seq]], axis=1)
        turn_rows(k.grad_rows.at[which], k.t_grad[0], slice(which * here, (which + 1) * here))
    share_turned(2, k.t_grad)
    ahead_of(Order.w_gate)
    moving[G].finish()
    ahead_of(Order.gate)
    for c in range(2):
        k.gate[:, c * half : (c + 1) * half] = dot(k.input1[...], whole(GATE, 0, c))
    for group in range(sizes.groups):
        ahead_of(Order.mixed[group])
        moves_back[group].wait()
        for c, tokens_at, rows in from_chunks(sizes, k.landed[1].at[group]):
            k.mixed[tokens_at, c * half + group * LANES : c * half + (group + 1) * LANES] = rows
    ahead_of(Order.inner)

    def make_inner(at):
        gate = k.gate[at, :]
        inner = (k.mixed[at, :] * (gate * jax.nn.sigmoid(gate))).astype(BF16)
        k.inner_rows[0][0, at, :] = inner[:, :half]
        k.inner_rows[0][1, at, :] = inner[:, half:]

    row_tiles(here, make_inner)
    share(4, *k.inner_rows)
    ahead_of(Order.w_out)
    moving[O].finish()
    ahead_of(Order.residual)
    k.residual[...] = dot_nt(k.inner_rows[0][0], whole(OUT, 0, 0)) + dot_nt(
        k.inner_rows[0][1], whole(OUT, 0, 1)
    )

    def second_norm(at):
        rows = jnp.concatenate([k.x_buf[0, at, :], k.x_buf[1, at, :]], axis=1).astype(F32)
        residual = k.residual[at, :] + rows
        normed, scale = norm(residual)
        k.residual[at, :] = residual
        k.normed2[at, :] = normed
        k.scale2[at, :] = scale
        k.input2[0, at, :] = (normed * second_gain).astype(BF16)

    row_tiles(here, second_norm)
    blocks = [pl.ds(at * (here // 2), here // 2) for at in range(2)]
    swap_input2 = [swap(3 + at, k.input2.at[0, rows], k.input2.at[1, rows]) for at, rows in enumerate(blocks)]
    ahead_of(Order.turn_near)
    turn_rows(k.input2.at[0], k.t_input2[0], slice(0, here))

    def product(left, right, pick):
        mine, theirs = left[0][:, core], left[1][...]
        shape = (width // 2, mine.shape[-1])
        got = dot(
            jnp.concatenate([mine.reshape(shape), theirs.reshape(shape)], axis=1),
            jnp.concatenate([right[0][pick], right[1][pick]], axis=0),
        ).astype(BF16)
        return got.reshape((2,) * (plan.dims - 2) + (plan.rows, got.shape[-1]))

    factors = {
        VALUE: (k.t_input1, 0, k.signal_rows, 6),
        GATE: (k.t_input1, 0, k.gate_rows, 5),
        OUT: (k.t_branch, 3, k.inner_rows, 4),
        UP: (k.t_input2, 1, k.tiles, None),
        DOWN: (k.t_grad, 2, k.tiles, None),
    }

    def prepare(part):
        left, left_share, right, right_share = factors[part.weight]
        need(left_share)
        total = k.grads[part.weight]
        if part.weight == VALUE:
            need(right_share + part.piece)
            got = product(left, right, part.piece)
            for c in range(2):
                total[part.piece, c] = got[..., of_group(c)]
        elif part.weight in (GATE, OUT):
            need(right_share)
            for c in range(2):
                total[part.piece, c] = product(left, right, c)
        else:
            kind = HID if part.weight == UP else ACT
            tile_copy(kind, part.piece).wait()
            total[part.piece] = product(left, right, (part.piece, kind))

    def begin_reducing(part):
        moving[part.at] = Reduce(
            place,
            k.grads[part.weight].at[part.piece],
            k.landings[part.at],
            part.dims[:-1],
            part.reduce,
            k.part_sems[part.at][0],
            k.part_sems[part.at][2],
            weight_grads[part.weight].at[:, pl.ds(part.piece * part.columns, part.columns)],
            functools.partial(prepare, part),
        )
    def start_reducing():
        for name, mover in list(moving.items()):
            if isinstance(mover, Gather):
                mover.finish()
        for part in plan.parts:
            begin_reducing(part)

    def up_part(which, piece, first, count):
        rows = pl.ds(first, count)
        stored = pl.ds(which * here + first, count)
        hidden = dot(k.input2[which, rows, :], whole(UP, piece))
        square = hidden * hidden
        bent = jnp.tanh(GELU_SCALE * hidden * (1.0 + GELU_CUBE * square))
        k.tiles[0][piece, ACT, stored, :] = (0.5 * hidden * (1.0 + bent)).astype(BF16)
        k.slopes[piece, stored, :] = 0.5 * (1.0 + bent) + (0.5 * GELU_SCALE) * hidden * (1.0 - bent * bent) * (
            1.0 + 3.0 * GELU_CUBE * square
        )

    def grad_part(which, piece, first, count):
        stored = pl.ds(which * here + first, count)
        grad = dot(k.grad_rows[which, pl.ds(first, count), :], whole(DOWN, piece)) * k.slopes[piece, stored, :]
        k.tiles[0][piece, HID, stored, :] = grad.astype(BF16)

    def in2_part(which, first, count, side):
        rows = pl.ds(which * here + first, count)
        return sum(
            dot_nt(k.tiles[0][piece, HID, rows, :], k.weights[UP][piece, side].reshape(half, half))
            for piece in range(PIECES)
        )

    def out_part(which, side):
        rows = pl.ds(which * here, here)
        return sum(
            dot_nt(k.tiles[0][piece, ACT, rows, :], k.weights[DOWN][piece, side].reshape(half, half))
            for piece in range(PIECES)
        )

    def tile_copy(kind, piece):
        return remote(
            k.tiles[0].at[piece, kind],
            k.tiles[1].at[piece, kind],
            k.tile_sems.at[0, kind, piece],
            k.tile_sems.at[1, kind, piece],
            twin,
        )

    for piece in range(PIECES):
        ahead_of(Order.w_up[piece])
        moving[U0 + piece].finish()
        ahead_of(Order.near_up[piece])
        up_part(0, piece, 0, here)
    swap_in2 = []

    def return_far(at):
        back = []
        for side in range(2):
            index = (blocks[at], pl.ds(side * half, half))
            k.in2_send[index] = in2_part(1, at * (here // 2), here // 2, side).astype(BF16)
            back.append(swap(5 + 2 * at + side, k.in2_send.at[index], k.in2_land.at[index]))
        swap_in2.append(back)

    for at in range(2):
        ahead_of(Order.wait_far[at])
        swap_input2[at].wait()
        ahead_of(Order.far_up[at])
        for piece in range(PIECES):
            up_part(1, piece, at * (here // 2), here // 2)
            if at:
                tile_copy(ACT, piece).start()
        if at:
            start_reducing()
            ahead_of(Order.far_b)
        for piece in range(PIECES):
            if not at:
                ahead_of(Order.down_a[piece])
                moving[D0 + piece].finish()
                ahead_of(Order.far_a[piece])
            grad_part(1, piece, at * (here // 2), here // 2)
        return_far(at)
    ahead_of(Order.near_down)
    for piece in range(PIECES):
        grad_part(0, piece, 0, here)
        tile_copy(HID, piece).start()
    for side in range(2):
        k.in2_sum[:, side * half : (side + 1) * half] = in2_part(0, 0, here, side)
    turn_rows(k.input2.at[1], k.t_input2[0], slice(here, 2 * here))
    share_turned(1, k.t_input2)

    k.gain_total[0] = jnp.zeros_like(k.gain_total[0])

    def add_gain(row, sums):
        for at in range(width // LANES):
            base = row * (width // LANES) + at
            k.gain_total[0, base : base + 1, :] += sums[:, at * LANES : (at + 1) * LANES]

    def second_back(at):
        grad = k.in2_sum[at, :] + k.in2_land[at, :].astype(F32)
        normed = k.normed2[at, :]
        add_gain(1, jnp.sum(grad * normed, axis=0, keepdims=True))
        result = k.grad_rows[0, at, :].astype(F32) + norm_back(
            grad, normed, k.scale2[at, :], second_gain
        )
        k.grad_res[at, :] = result
        k.branch_rows[at, :] = result.astype(BF16)

    for at in range(2):
        ahead_of(Order.far_back[at])
        for copy in swap_in2[at]:
            copy.wait()
        row_tiles(here // 2, second_back, at * (here // 2))
    ahead_of(Order.norm_back)
    moves = []
    for group in range(sizes.groups):
        got = dot(k.branch_rows[...], both_halves(OUT, 0, lanes=of_group(group)))
        grad_mixed = []
        for c in range(2):
            columns = slice(c * half + group * LANES, c * half + (group + 1) * LANES)
            gate, grad = k.gate[:, columns], got[:, of_group(c)]
            sig = jax.nn.sigmoid(gate)
            k.gate_rows[0][c, :, of_group(group)] = (
                grad * k.mixed[:, columns] * (sig * (1.0 + gate * (1.0 - sig)))
            ).astype(BF16)
            grad_mixed.append(grad * (gate * sig))
        moves.append(send_chunks(2, group, k.sent, grad_mixed))
    share(5, *k.gate_rows)
    turn_rows(k.branch_rows, k.t_branch[0])
    share_turned(3, k.t_branch)
    ahead_of(Order.sent_back)
    ahead_of(Order.output)
    for which in range(2):
        for side in range(2):
            k.out_sum[which, :, side * half : (side + 1) * half] = out_part(which, side)

    def make_output(at):
        near = k.residual[at, :] + k.out_sum[0, at, :]
        far = k.out_sum[1, at, :]
        k.out_send[0, at, :] = of_other_chan(near).astype(BF16)
        k.out_send[1, at, :] = of_other_chan(far).astype(BF16)

    row_tiles(here, make_output)
    moving[W] = Once(lambda: swap(1, k.out_send, k.out_land))

    moves_back = []
    for group in range(sizes.groups):
        ahead_of(Order.arrive_back[group])
        moves[group].wait()
        ahead_of(Order.conv_back[group])
        spectrum_of(2, group, k.grad_spec)
        chunks_from(group, times(k.grad_spec[group][...], k.kernel_spec[group][...], True))
        moves_back.append(all_to_all(3, group, k.sent_back))
    ahead_of(Order.convolved_back)

    def tap_store(group):
        def store(channel, values):
            k.tap_wide[pl.ds(group * sizes.group + channel, sizes.tap_rows, stride=channels), :] = values

        return store

    ahead_of(Order.taps_back)
    for group in range(sizes.groups):
        signal_from(
            sizes,
            times(k.grad_spec[group][...], k.value_spec[group][...], True),
            taps_outof, turn, behind, k.inner_taps[group], tap_store(group),
        )
    pooled = pooled_taps(k.taps[...].reshape(flat_taps))
    bent = jnp.tanh(pooled / THRESH)
    tap_grads = pooled_taps(k.tap_wide[...].reshape(pooled.shape) * live * bent * bent)
    k.tap_grad[...] = tap_grads.reshape(k.tap_grad.shape)
    tap_back = Exchange(
        sizes.freq_count,
        place.freq,
        lambda other: (other, chan),
        lambda other: k.tap_grad.at[other],
        lambda other: grad_kernel.at[:, other],
        k.tap_grad.at[pl.ds(0, others)],
        grad_kernel.at[:, pl.ds(0, others)],
        k.tap_sems[1],
    )
    tap_back.start()
    grad_kernel[:, place.freq] = k.tap_grad[place.freq]

    k.rows[...] = dot_nt(k.gate_rows[0][0], whole(GATE, 0, 0)) + dot_nt(k.gate_rows[0][1], whole(GATE, 0, 1))
    for group in range(sizes.groups):
        ahead_of(Order.signal[group])
        moves_back[group].wait()
        for c, tokens_at, rows in from_chunks(sizes, k.landed[3].at[group]):
            k.signal_rows[0][group, tokens_at, of_group(c)] = rows.astype(BF16)
        share(6 + group, k.signal_rows[0].at[group], k.signal_rows[1].at[group])
        ahead_of(Order.input_back[group])
        k.rows[...] += dot_nt(k.signal_rows[0][group], both_halves(VALUE, group))
    ahead_of(Order.first_back)

    def first_back(at):
        grad = k.rows[at, :]
        normed = k.normed1[at, :]
        add_gain(0, jnp.sum(grad * normed, axis=0, keepdims=True))
        result = k.grad_res[at, :] + norm_back(grad, normed, k.scale1[at, :], first_gain)
        k.gin_send[at, :] = of_other_chan(result).astype(BF16)
        grad_input[chan, at, :] = of_chan(result)

    row_tiles(here, first_back)
    swap_gin = swap(11, k.gin_send, k.gin_land)
    spread = Spread(place, k.gain_total, k.gain_land, plan.spread, *k.gain_sems)
    moving[S] = spread
    spread.go()
    ahead_of(Order.finish_output)
    moving[W].finish()

    def finish_output(at):
        near = of_chan(k.residual[at, :] + k.out_sum[0, at, :]) + k.out_land[1, at, :].astype(F32)
        far = of_chan(k.out_sum[1, at, :]) + k.out_land[0, at, :].astype(F32)
        output[chan, at, :] = near.astype(BF16)
        output[1 - chan, at, :] = far.astype(BF16)

    row_tiles(here, finish_output)
    ahead_of(Order.last)
    swap_gin.wait()
    ahead_of(Order.finish_grad)
    grad_input[1 - chan] = k.gin_land[...].astype(F32)
    ahead_of(Order.taps_home)
    tap_back.wait()
    ahead_of(Order.end)
    for mover in moving.values():
        if not isinstance(mover, Once):
            mover.finish()
    gain_sums[...] = k.gain_total[len(plan.spread)]


def settle_kernel(count, channels, freq_count, *refs):
    sources, sums, refs = refs[:count], refs[count], refs[count + 1 :]
    targets, gains, sems = refs[: count + 2], refs[count + 2 : count + 4], refs[-1]
    going = [pltpu.make_async_copy(sources[n], targets[n], sems.at[n]) for n in range(count)]
    for copy in going:
        copy.start()
    tiles = 2 * channels * freq_count // LANES
    mine = (lax.axis_index("chan") * freq_count + lax.axis_index("freq")) * channels
    lane = lax.broadcasted_iota(jnp.int32, (channels, LANES), 1)
    feature = mine + lax.broadcasted_iota(jnp.int32, (channels, LANES), 0)
    for row, gain in enumerate(gains):
        total = jnp.zeros((channels, LANES), F32)
        for tile in range(tiles):
            at = row * tiles + tile
            total = total + jnp.where(lane + tile * LANES == feature, sums[at : at + 1, :], 0.0)
        gain[...] = jnp.sum(total.T, axis=0, keepdims=True)
        going.append(pltpu.make_async_copy(gain, targets[count + row], sems.at[count + row]))
        going[-1].start()
    for copy in going:
        copy.wait()


def settle(arrays, sums, sizes):
    gain = (1, sizes.channels)
    out = [jax.ShapeDtypeStruct(a.shape, a.dtype) for a in arrays] + [jax.ShapeDtypeStruct(gain, F32)] * 2
    return pl.pallas_call(
        functools.partial(settle_kernel, len(arrays), sizes.channels, sizes.freq_count),
        out_shape=out,
        in_specs=[VMEM_SPEC] * (len(arrays) + 1),
        out_specs=[ANY_SPEC] * len(out),
        scratch_shapes=[pltpu.VMEM(gain, F32)] * 2 + [pltpu.SemaphoreType.DMA((len(out),))],
        name="settle",
    )(*arrays, sums)


def one_sequence(
    tokens, cotangent, first_gain, second_gain, w_value, w_gate, w_out, w_up, w_down, raw_kernel, lengths
):
    freq_count = lax.axis_size("freq")
    _, here, half = tokens.shape
    sizes = Sizes(freq_count, here, half, raw_kernel.shape[1] * freq_count)
    tables = conv_tables(sizes)
    plan = Plan(sizes, tables)
    shards = (w_value, w_gate, w_out, w_up, w_down)
    out_shape = (
        [pltpu.VMEM((2, here, half), BF16), pltpu.VMEM((2, here, half), F32)]
        + [pltpu.VMEM(w.shape, F32) for w in shards]
        + [
            pltpu.VMEM((4 * half // LANES + 4, LANES), F32),
            pltpu.VMEM((sizes.groups, freq_count, sizes.group, LANES), F32),
        ]
    )
    results = pl.pallas_call(
        functools.partial(block_kernel, plan),
        out_shape=out_shape,
        in_specs=[ANY_SPEC] * (11 + len(tables)),
        out_specs=[VMEM_SPEC] * len(out_shape),
        scratch_shapes=plan.scratch,
        compiler_params=pltpu.CompilerParams(
            collective_id=0, has_side_effects=True, vmem_limit_bytes=60 << 20
        ),
        name="block",
    )(
        tokens,
        cotangent,
        first_gain,
        second_gain,
        lengths,
        raw_kernel.reshape(sizes.groups, freq_count, sizes.group, LANES),
        *shards,
        *tables,
    )
    results = [pltpu.with_memory_space_constraint(result, pltpu.VMEM) for result in results]
    *arrays, gain_sums, grad_kernel = results
    *arrays, grad_kernel, first_grad, second_grad = settle([*arrays, grad_kernel], gain_sums, sizes)
    return (*arrays, first_grad.T, second_grad.T, grad_kernel.reshape(raw_kernel.shape))


def fits(mesh):
    freq_count = mesh.shape["freq"]
    return lambda tokens, w_value, w_up, raw_kernel: (
        mesh.shape["chan"] == 2
        and tokens.shape[0] == 2
        and freq_count == 16
        and w_value.shape[1] == 6 * LANES
        and w_value.shape[0] % (16 * freq_count) == 0
        and w_value.shape[1] % (16 * freq_count) == 0
        and w_value.shape[1] % 256 == 0
        and w_up.shape[1] == PIECES * w_value.shape[1]
        and tokens.shape[1] % (2 * LANES * freq_count) == 0
        and raw_kernel.shape[1] == LANES * freq_count
        and (tokens.shape[1] + raw_kernel.shape[1]) // LANES % 16 == 0
    )


D = 768
SEQ_MB = 1
MICRO = 2


HIGHEST = lax.Precision.HIGHEST


def circle(height, breadth, period):
    first_index = lax.broadcasted_iota(jnp.int32, (height, breadth), 0)
    second_index = lax.broadcasted_iota(jnp.int32, (height, breadth), 1)
    phase_angle = (first_index * second_index % period).astype(jnp.float32) * (
        2.0 * math.pi / period
    )
    return (jnp.cos(phase_angle), jnp.sin(phase_angle))


def make_tables(padded_size):
    inner_size = 128
    outer_size = padded_size // inner_size
    outer_cos, outer_sin = circle(outer_size, outer_size, outer_size)
    inner_cos, inner_sin = circle(inner_size, inner_size, inner_size)
    twist_cos, twist_sin = circle(outer_size, inner_size, padded_size)
    return (outer_cos, outer_sin, inner_cos, inner_sin, twist_cos, twist_sin)


def spectrum(signal, padded_size, tables):
    outer_cos, outer_sin, inner_cos, inner_sin, twist_cos, twist_sin = tables
    inner_size = inner_cos.shape[0]
    pad_width = [(0, 0)] * (signal.ndim - 1) + [(0, padded_size - signal.shape[-1])]
    grid_values = jnp.pad(signal, pad_width).reshape(
        signal.shape[:-1] + (padded_size // inner_size, inner_size)
    )
    part_real = jnp.einsum("...ab,fa->...fb", grid_values, outer_cos, precision=HIGHEST)
    part_imag = -jnp.einsum("...ab,fa->...fb", grid_values, outer_sin, precision=HIGHEST)
    turned_real = part_real * twist_cos + part_imag * twist_sin
    turned_imag = part_imag * twist_cos - part_real * twist_sin
    spec_real = jnp.einsum(
        "...fb,bg->...fg", turned_real, inner_cos, precision=HIGHEST
    ) + jnp.einsum("...fb,bg->...fg", turned_imag, inner_sin, precision=HIGHEST)
    spec_imag = jnp.einsum(
        "...fb,bg->...fg", turned_imag, inner_cos, precision=HIGHEST
    ) - jnp.einsum("...fb,bg->...fg", turned_real, inner_sin, precision=HIGHEST)
    return (spec_real, spec_imag)


def signal_of(spec_real, spec_imag, keep_count, tables):
    outer_cos, outer_sin, inner_cos, inner_sin, twist_cos, twist_sin = tables
    padded_size = spec_real.shape[-1] * spec_real.shape[-2]
    back_real = jnp.einsum("...fg,bg->...fb", spec_real, inner_cos, precision=HIGHEST) - jnp.einsum(
        "...fg,bg->...fb", spec_imag, inner_sin, precision=HIGHEST
    )
    back_imag = jnp.einsum("...fg,bg->...fb", spec_imag, inner_cos, precision=HIGHEST) + jnp.einsum(
        "...fg,bg->...fb", spec_real, inner_sin, precision=HIGHEST
    )
    turned_real = back_real * twist_cos - back_imag * twist_sin
    turned_imag = back_imag * twist_cos + back_real * twist_sin
    grid_values = (
        jnp.einsum("...fb,af->...ab", turned_real, outer_cos, precision=HIGHEST)
        - jnp.einsum("...fb,af->...ab", turned_imag, outer_sin, precision=HIGHEST)
    ) / padded_size
    flat_values = grid_values.reshape(grid_values.shape[:-2] + (padded_size,))
    return flat_values[..., :keep_count]


def shape_kernel(raw_taps, live_taps):
    padded = jnp.pad(raw_taps, ((0, 0), (1, 1)))
    pooled = (padded[:, :-2] + padded[:, 1:-1] + padded[:, 2:]) / 3.0
    return (pooled - THRESH * jnp.tanh(pooled / THRESH)) * live_taps


def row_norm(values):
    row_width = values.shape[-1] * lax.axis_size("chan")
    row_total, row_square = lax.psum(
        (jnp.sum(values, axis=-1), jnp.sum(values * values, axis=-1)), "chan"
    )
    center = row_total / row_width
    spread = row_square / row_width - center * center
    scale = lax.rsqrt(spread + EPSILON)[..., None]
    return ((values - center[..., None]) * scale, scale)


def row_back(grad_rows, normed, scale, gain_row):
    row_width = grad_rows.shape[-1] * lax.axis_size("chan")
    scaled = grad_rows * gain_row
    sum_plain, sum_cross = lax.psum(
        (jnp.sum(scaled, axis=-1), jnp.sum(scaled * normed, axis=-1)), "chan"
    )
    return scale * (
        scaled - sum_plain[..., None] / row_width - normed * sum_cross[..., None] / row_width
    )


def features(values):
    return lax.all_gather(values, "chan", axis=2, tiled=True)


def partial_sum(values):
    return lax.psum_scatter(
        values.astype(jnp.bfloat16), "chan", scatter_dimension=2, tiled=True
    ).astype(jnp.float32)


def to_channels(values):
    return lax.all_to_all(
        jnp.swapaxes(values, 1, 2), "freq", split_axis=1, concat_axis=2, tiled=True
    )


def to_tokens(values):
    arrived = lax.all_to_all(values, "freq", split_axis=2, concat_axis=1, tiled=True)
    return jnp.swapaxes(arrived, 1, 2)


def by_features(
    tokens,
    cotangent,
    first_gain,
    second_gain,
    w_value,
    w_gate,
    w_out,
    w_up,
    w_down,
    raw_kernel,
    lengths,
):
    full_value, full_gate, full_out, full_up, full_down = (
        lax.all_gather(w_value, "freq", axis=0, tiled=True),
        lax.all_gather(w_gate, "freq", axis=0, tiled=True),
        lax.all_gather(w_out, "freq", axis=0, tiled=True),
        lax.all_gather(w_up, "freq", axis=0, tiled=True),
        lax.all_gather(w_down, "freq", axis=0, tiled=True),
    )
    freq_count = lax.axis_size("freq")
    chan_width = tokens.shape[2]
    channels = chan_width // freq_count
    seq_length = tokens.shape[1] * freq_count
    padded_size = 2 * seq_length
    tables = make_tables(padded_size)
    kernel_rows = lax.all_to_all(raw_kernel, "freq", split_axis=0, concat_axis=1, tiled=True)
    tap_count = kernel_rows.shape[1]
    my_lengths = lax.dynamic_slice_in_dim(lengths, lax.axis_index("freq") * channels, channels)
    tap_index = lax.broadcasted_iota(jnp.int32, (channels, tap_count), 1)
    live_taps = (tap_index < my_lengths[:, None]).astype(jnp.float32)
    kernel, kernel_pull = jax.vjp(functools.partial(shape_kernel, live_taps=live_taps), kernel_rows)
    kernel_real, kernel_imag = spectrum(kernel, padded_size, tables)
    hidden_width = full_up.shape[1]
    shard_factor = 1
    totals = (
        jnp.zeros((D // shard_factor, chan_width), jnp.float32),
        jnp.zeros((D // shard_factor, chan_width), jnp.float32),
        jnp.zeros((D // shard_factor, chan_width), jnp.float32),
        jnp.zeros((D // shard_factor, hidden_width), jnp.float32),
        jnp.zeros((D // shard_factor, hidden_width), jnp.float32),
        jnp.zeros((chan_width // shard_factor, 1), jnp.float32),
        jnp.zeros((chan_width // shard_factor, 1), jnp.float32),
    )
    kernel_grad = jnp.zeros((channels, tap_count), jnp.float32)
    outputs = []
    input_grads = []
    for micro_index in range(MICRO):
        rows_here = tokens[micro_index * SEQ_MB : (micro_index + 1) * SEQ_MB].astype(jnp.float32)
        first_normed, first_scale = row_norm(rows_here)
        input1 = features((first_normed * first_gain).astype(jnp.bfloat16))
        value_low = jnp.einsum(
            "bld,de->ble", input1, full_value, preferred_element_type=jnp.float32
        ).astype(jnp.bfloat16)
        gate_proj = jnp.einsum("bld,de->ble", input1, full_gate, preferred_element_type=jnp.float32)
        signal = to_channels(value_low).astype(jnp.float32)
        signal_real, signal_imag = spectrum(signal, padded_size, tables)
        mixed = signal_of(
            signal_real * kernel_real - signal_imag * kernel_imag,
            signal_real * kernel_imag + signal_imag * kernel_real,
            seq_length,
            tables,
        )
        mixed_rows = to_tokens(mixed.astype(jnp.bfloat16)).astype(jnp.float32)
        gate_act, gate_pull = jax.vjp(jax.nn.silu, gate_proj)
        inner_low = (mixed_rows * gate_act).astype(jnp.bfloat16)
        residual = rows_here + partial_sum(
            jnp.einsum("ble,oe->blo", inner_low, full_out, preferred_element_type=jnp.float32)
        )
        second_normed, second_scale = row_norm(residual)
        input2 = features((second_normed * second_gain).astype(jnp.bfloat16))
        hidden = jnp.einsum("bld,df->blf", input2, full_up, preferred_element_type=jnp.float32)
        activated, act_pull = jax.vjp(jax.nn.gelu, hidden)
        act_low = activated.astype(jnp.bfloat16)
        result = residual + partial_sum(
            jnp.einsum("blf,of->blo", act_low, full_down, preferred_element_type=jnp.float32)
        )
        outputs.append(result.astype(jnp.bfloat16))
        grad_rows_out = cotangent[micro_index * SEQ_MB : (micro_index + 1) * SEQ_MB]
        grad_full = features(grad_rows_out)
        grad_act = jnp.einsum(
            "blo,of->blf", grad_full, full_down, preferred_element_type=jnp.float32
        )
        down_grad = jnp.einsum(
            "blo,blf->of", grad_full, act_low, preferred_element_type=jnp.float32
        )
        grad_hidden = act_pull(grad_act)[0].astype(jnp.bfloat16)
        up_grad = jnp.einsum("bld,blf->df", input2, grad_hidden, preferred_element_type=jnp.float32)
        grad_in2 = partial_sum(
            jnp.einsum("blf,df->bld", grad_hidden, full_up, preferred_element_type=jnp.float32)
        )
        second_grad = jnp.sum(grad_in2 * second_normed, axis=(0, 1))
        grad_residual = grad_rows_out.astype(jnp.float32) + row_back(
            grad_in2, second_normed, second_scale, second_gain
        )
        grad_branch = features(grad_residual.astype(jnp.bfloat16))
        grad_inner = jnp.einsum(
            "blo,oe->ble", grad_branch, full_out, preferred_element_type=jnp.float32
        )
        out_grad = jnp.einsum(
            "blo,ble->oe", grad_branch, inner_low, preferred_element_type=jnp.float32
        )
        grad_mixed = to_channels((grad_inner * gate_act).astype(jnp.bfloat16)).astype(jnp.float32)
        grad_real, grad_imag = spectrum(grad_mixed, padded_size, tables)
        grad_signal = signal_of(
            grad_real * kernel_real + grad_imag * kernel_imag,
            grad_imag * kernel_real - grad_real * kernel_imag,
            seq_length,
            tables,
        )
        kernel_grad = kernel_grad + jnp.sum(
            signal_of(
                grad_real * signal_real + grad_imag * signal_imag,
                grad_imag * signal_real - grad_real * signal_imag,
                tap_count,
                tables,
            ),
            axis=0,
        )
        grad_signal_rows = to_tokens(grad_signal.astype(jnp.bfloat16))
        grad_gate_rows = gate_pull(grad_inner * mixed_rows)[0].astype(jnp.bfloat16)
        value_grad = jnp.einsum(
            "bld,ble->de", input1, grad_signal_rows, preferred_element_type=jnp.float32
        )
        gate_grad = jnp.einsum(
            "bld,ble->de", input1, grad_gate_rows, preferred_element_type=jnp.float32
        )
        grad_in1 = partial_sum(
            jnp.einsum(
                "ble,de->bld", grad_signal_rows, full_value, preferred_element_type=jnp.float32
            )
            + jnp.einsum(
                "ble,de->bld", grad_gate_rows, full_gate, preferred_element_type=jnp.float32
            )
        )
        first_grad = jnp.sum(grad_in1 * first_normed, axis=(0, 1))
        input_grads.append(
            grad_residual + row_back(grad_in1, first_normed, first_scale, first_gain)
        )
        local_terms = (
            value_grad,
            gate_grad,
            out_grad,
            up_grad,
            down_grad,
            first_grad[:, None],
            second_grad[:, None],
        )
        totals = tuple((left + right for left, right in zip(totals, local_terms)))
    totals = lax.psum_scatter(totals, "freq", scatter_dimension=0, tiled=True)
    raw_grad = kernel_pull(kernel_grad)[0]
    grad_kernel = lax.all_to_all(raw_grad, "freq", split_axis=1, concat_axis=0, tiled=True)
    output = jnp.concatenate(outputs, axis=0)
    grad_input = jnp.concatenate(input_grads, axis=0)
    return (
        output,
        grad_input,
        totals[0],
        totals[1],
        totals[2],
        totals[3],
        totals[4],
        totals[5],
        totals[6],
        grad_kernel,
    )


def solution(mesh):
    specs = dict(
        mesh=mesh,
        in_specs=(
            P(None, "freq", "chan"),
            P(None, "freq", "chan"),
            P("chan"),
            P("chan"),
            P("freq", "chan"),
            P("freq", "chan"),
            P("freq", "chan"),
            P("freq", "chan"),
            P("freq", "chan"),
            P("chan", "freq"),
            P("chan"),
        ),
        out_specs=(
            P(None, "freq", "chan"),
            P(None, "freq", "chan"),
            P("freq", "chan"),
            P("freq", "chan"),
            P("freq", "chan"),
            P("freq", "chan"),
            P("freq", "chan"),
            P("freq", "chan"),
            P("freq", "chan"),
            P("chan", "freq"),
        ),
        check_vma=False,
    )

    def step(*args):
        whole = fits(mesh)(args[0], args[4], args[7], args[9])
        return jax.shard_map(one_sequence if whole else by_features, **specs)(*args)

    return step
```

```python
import functools
import math
import types

import jax
import jax.numpy as jnp
import numpy as np
from jax import lax
from jax.experimental import pallas as pl
from jax.experimental.pallas import tpu as pltpu
from jax.sharding import PartitionSpec as P

THRESH = 0.003
EPSILON = 1e-05
LANES = 128
MESH = pl.DeviceIdType.MESH
F32 = jnp.float32
BF16 = jnp.bfloat16


def bit_sizes(freq_count):
    return [1 << i for i in reversed(range(freq_count.bit_length() - 1))]


class Place:
    def __init__(self, freq_count):
        self.freq_count = freq_count
        self.freq = lax.axis_index("freq")
        self.chan = lax.axis_index("chan")
        self.bits = bit_sizes(freq_count)
        self.coords = [self.chan] + [lax.rem(self.freq // b, 2) for b in self.bits]
        self.dims = len(self.coords)
        self.core = self.coords[-1]

    def other(self, flipped):
        freq, chan = self.freq, self.chan
        for dim in flipped:
            if dim == 0:
                chan = 1 - chan
            else:
                bit = self.bits[dim - 1]
                freq = freq + bit - 2 * bit * self.coords[dim]
        return (freq, chan)


def flips(dims):
    return [
        tuple(dim for at, dim in enumerate(dims) if mask >> at & 1) for mask in range(1, 1 << len(dims))
    ]


def remote(source, target, send, recv, device):
    return pltpu.make_async_remote_copy(
        src_ref=source,
        dst_ref=target,
        send_sem=send,
        recv_sem=recv,
        device_id=device,
        device_id_type=MESH,
    )


class Line:
    def __init__(self, way, high, low):
        self.way, self.high, self.low = way, high, low

    def ends(self, place):
        middle = place.coords[self.high] + place.coords[self.low] == 1
        end = place.coords[self.high] + place.coords[self.low] != 1
        return {ACROSS: (middle, middle), INWARD: (end, middle), OUTWARD: (middle, end)}[self.way]

    def flipped(self):
        return (self.high, self.low) if self.way == ACROSS else (self.low,)


def when(condition, action):
    if condition is None:
        action()
    else:
        pl.when(condition)(action)


class Leg:
    def __init__(self, copy, ends=(None, None)):
        self.copy, self.ends = copy, ends

    def start(self):
        when(self.ends[0], self.copy.start)

    def wait(self):
        if self.ends[0] is None:
            self.copy.wait()
        else:
            when(self.ends[0], self.copy.wait_send)
            when(self.ends[1], self.copy.wait_recv)


def flips_of(phase):
    return [phase.flipped()] if isinstance(phase, Line) else flips(phase)


def is_outward(phase):
    return isinstance(phase, Line) and phase.way == OUTWARD


def slots(phases):
    return sum(len(flips_of(phase)) for phase in phases if not is_outward(phase))


def first_slot(phases, at):
    return slots(phases[:at]) - is_outward(phases[at])


class Gather:
    def __init__(self, place, buffer, dims, phases, send, recv, prepare):
        self.place, self.buffer, self.dims, self.phases = place, buffer, dims, phases
        self.send, self.recv, self.prepare = send, recv, prepare
        self.turn = 0

    def copies(self, phase):
        done, step = set(), self.phases[phase]
        for before in self.phases[:phase]:
            if not isinstance(before, Line):
                done.update(before)
            elif before.way == OUTWARD:
                done.update((before.high, before.low))
        index = [slice(None) if dim in done else self.place.coords[dim] for dim in self.dims]
        ends = (None, None)
        if isinstance(step, Line):
            ends = step.ends(self.place)
            if step.way == OUTWARD:
                index[self.dims.index(step.high)] = 1 - self.place.coords[step.high]
        region = self.buffer.at[tuple(index)]
        base = first_slot(self.phases, phase)
        return [
            Leg(
                remote(region, region, self.send.at[k], self.recv.at[base + k], self.place.other(flipped)), ends
            )
            for k, flipped in enumerate(flips_of(step))
        ]

    def go(self):
        if self.turn > len(self.phases):
            return
        if self.turn == 0:
            self.prepare()
        else:
            for copy in self.copies(self.turn - 1):
                copy.wait()
        if self.turn < len(self.phases):
            for copy in self.copies(self.turn):
                copy.start()
        self.turn += 1

    def finish(self):
        while self.turn <= len(self.phases):
            self.go()


class Once:
    def __init__(self, begin):
        self.begin, self.copy = begin, None

    def go(self):
        if self.copy is None:
            self.copy = self.begin()

    def finish(self):
        self.go()
        self.copy.wait()


class Reduce:
    def __init__(self, place, total, landing, dims, phases, send, recv, out, prepare):
        self.place, self.total, self.landing, self.dims = place, total, landing, dims
        self.phases, self.send, self.recv, self.out = phases, send, recv, out
        self.prepare = prepare
        self.turn = 0

    def region(self, phase, flipped):
        fixed, step = set(), self.phases[phase]
        for before in self.phases[:phase]:
            if not isinstance(before, Line):
                fixed.update(before)
            elif before.way == ACROSS:
                fixed.add(before.high)
        if not isinstance(step, Line):
            fixed.update(step)
        coords = self.place.coords
        index = [
            (1 - coords[dim] if dim in flipped else coords[dim]) if dim in fixed else slice(None)
            for dim in self.dims
        ]
        if isinstance(step, Line):
            mine = coords[step.high]
            keeps = step.way == ACROSS and not flipped
            index[self.dims.index(step.high)] = mine if keeps else 1 - mine
        return tuple(index)

    def copies(self, phase):
        step = self.phases[phase]
        base = first_slot(self.phases, phase)
        ends = step.ends(self.place) if isinstance(step, Line) else (None, None)
        return [
            Leg(
                remote(
                    self.total.at[self.region(phase, flipped)],
                    self.landing[phase].at[k],
                    self.send.at[k],
                    self.recv.at[base + k],
                    self.place.other(flipped),
                ),
                ends,
            )
            for k, flipped in enumerate(flips_of(step))
        ]

    def add(self, phase):
        kept = self.region(phase, ())
        free = [at for at, part in enumerate(kept) if isinstance(part, slice)]
        landing, step = self.landing[phase], self.phases[phase]

        def one(turn, carry):
            where, there = list(kept), []
            for at, dim in enumerate(free):
                bit = lax.rem(turn // (1 << (len(free) - 1 - at)), 2)
                where[dim] = bit
                there.append(bit)
            where, there = tuple(where), tuple(there)
            total = self.total[where].astype(F32)
            for k in range(len(flips_of(step))):
                total = total + landing[(k,) + there].astype(F32)
            if phase + 1 == len(self.phases):
                self.out[...] = total
            else:
                self.total[where] = total.astype(BF16)
            return carry

        def every():
            if free:
                lax.fori_loop(0, 1 << len(free), one, 0)
            else:
                one(0, 0)

        when(step.ends(self.place)[1] if isinstance(step, Line) else None, every)

    def go(self):
        if self.turn > len(self.phases):
            return
        if self.turn == 0:
            self.prepare()
        else:
            for copy in self.copies(self.turn - 1):
                copy.wait()
            self.add(self.turn - 1)
        if self.turn < len(self.phases):
            for copy in self.copies(self.turn):
                copy.start()
        self.turn += 1

    def finish(self):
        while self.turn <= len(self.phases):
            self.go()


def landing_shapes(phases, dims, rows, columns):
    shapes, free = [], len(dims)
    for step in phases:
        if isinstance(step, Line):
            free -= 0 if step.way == INWARD else 1
            shapes.append((1,) + (2,) * (free - (step.way == INWARD)) + (rows, columns))
        else:
            free -= len(step)
            shapes.append((len(flips(step)),) + (2,) * free + (rows, columns))
    return shapes


class Spread:
    def __init__(self, place, total, landing, phases, send, recv):
        self.place, self.total, self.landing, self.phases = place, total, landing, phases
        self.send, self.recv = send, recv
        self.turn = 0

    def copies(self, phase):
        base = sum(len(flips(dims)) for dims in self.phases[:phase])
        return base, [
            remote(
                self.total.at[phase],
                self.landing.at[base + k],
                self.send.at[k],
                self.recv.at[base + k],
                self.place.other(flipped),
            )
            for k, flipped in enumerate(flips(self.phases[phase]))
        ]

    def go(self):
        if self.turn > len(self.phases):
            return
        if self.turn:
            base, copies = self.copies(self.turn - 1)
            total = self.total[self.turn - 1]
            for k, copy in enumerate(copies):
                copy.wait()
                total = total + self.landing[base + k]
            self.total[self.turn] = total
        if self.turn < len(self.phases):
            for copy in self.copies(self.turn)[1]:
                copy.start()
        self.turn += 1

    def finish(self):
        while self.turn <= len(self.phases):
            self.go()


class Exchange:
    def __init__(self, count, me, device, source, target, all_sent, all_landed, sems):
        self.count, self.me, self.device = count, me, device
        self.source, self.target = source, target
        self.all_sent, self.all_landed, self.sems = all_sent, all_landed, sems

    def start(self):
        def one(step, carry):
            other = lax.rem(self.me + step, self.count)
            remote(
                self.source(other), self.target(self.me), self.sems.at[0], self.sems.at[1], self.device(other)
            ).start()
            return carry

        lax.fori_loop(1, self.count, one, 0, unroll=True)

    def wait(self):
        for part, sem in ((self.all_sent, self.sems.at[0]), (self.all_landed, self.sems.at[1])):
            pltpu.make_async_copy(part, part, sem).wait()


class Sizes:
    def __init__(self, freq_count, here, half, taps):
        self.freq_count = freq_count
        self.here = here
        self.half = half
        self.cols = here // LANES
        self.channels = half // freq_count
        self.group = LANES // freq_count
        self.groups = self.channels // self.group
        self.chunk = self.cols * self.group
        self.devices = 2 * freq_count
        self.tap_rows = taps // LANES
        self.rows = here * freq_count // LANES + self.tap_rows
        self.size = self.rows * LANES
        self.group_rows = self.group * self.rows


def conv_tables(sizes):
    rows, size = sizes.rows, sizes.size
    f = np.arange(rows)
    a_of, imag = [], []
    for col in range(sizes.cols):
        for seq in range(2):
            for block in range(sizes.freq_count):
                a_of.append(block * sizes.cols + col)
                imag.append(seq)
    a_of, imag = np.array(a_of), np.array(imag)
    angle = 2 * np.pi * np.outer(f, a_of) / rows
    cos, sin = np.cos(angle), np.sin(angle)
    into = np.concatenate([np.where(imag, sin, cos), np.where(imag, cos, -sin)], axis=0)
    outof = into.T / size
    angle = 2 * np.pi * np.outer(f, np.arange(sizes.tap_rows)) / rows
    taps_into = np.concatenate([np.cos(angle), -np.sin(angle)], axis=0)
    taps_outof = taps_into.T / size
    b = np.arange(LANES)
    angle = 2 * np.pi * np.outer(f, b) / size
    turn = np.stack([np.cos(angle), np.sin(angle)])
    angle = 2 * np.pi * np.outer(b, b) / LANES
    cos, sin = np.cos(angle), np.sin(angle)
    ahead = np.block([[cos, -sin], [sin, cos]])
    return (
        jnp.asarray(into, BF16),
        jnp.asarray(outof, BF16),
        jnp.asarray(taps_into, BF16),
        jnp.asarray(taps_outof, BF16),
        jnp.asarray(turn, F32),
        jnp.asarray(ahead, BF16),
        jnp.asarray(ahead.T, BF16),
    )


def dot(left, right):
    return jnp.dot(left, right, preferred_element_type=F32)


def spectrum_into(sizes, load, into, turn, ahead, inner, spectrum):
    rows = sizes.rows
    for pair in range(sizes.group // 2):
        both = jnp.concatenate([load(2 * pair), load(2 * pair + 1)], axis=1).astype(BF16)
        part = dot(into[...], both)
        for side in range(2):
            real = part[:rows, side * LANES : (side + 1) * LANES]
            imag = part[rows:, side * LANES : (side + 1) * LANES]
            start = (2 * pair + side) * rows
            inner[start : start + rows, :] = jnp.concatenate(
                [real * turn[0] + imag * turn[1], imag * turn[0] - real * turn[1]], axis=1
            ).astype(BF16)
    spectrum[...] = dot(inner[...], ahead[...])


def signal_from(sizes, product, outof, turn, behind, inner, store):
    rows = sizes.rows
    inner[...] = dot(product, behind[...])
    for pair in range(sizes.group // 2):
        sides = []
        for side in range(2):
            start = (2 * pair + side) * rows
            real, imag = inner[start : start + rows, :LANES], inner[start : start + rows, LANES:]
            sides.append(
                jnp.concatenate(
                    [real * turn[0] - imag * turn[1], imag * turn[0] + real * turn[1]], axis=0
                ).astype(BF16)
            )
        got = dot(outof[...], jnp.concatenate(sides, axis=1))
        for side in range(2):
            store(2 * pair + side, got[:, side * LANES : (side + 1) * LANES])


def times(left, right, conj):
    a, b = left[:, :LANES], left[:, LANES:]
    c, d = right[:, :LANES], right[:, LANES:]
    if conj:
        return jnp.concatenate([a * c + b * d, b * c - a * d], axis=1).astype(BF16)
    return jnp.concatenate([a * c - b * d, a * d + b * c], axis=1).astype(BF16)


def to_chunks(sizes, rows, target):
    turned = rows.T.reshape(sizes.freq_count, sizes.group, sizes.here)
    pieces = [turned[:, :, col * LANES : (col + 1) * LANES] for col in range(sizes.cols)]
    target[...] = jnp.concatenate(pieces, axis=1).astype(BF16)


def from_chunks(sizes, chunks):
    wide = chunks[...].astype(F32)
    for c in range(2):
        for col in range(sizes.cols):
            piece = wide[
                c * sizes.freq_count : (c + 1) * sizes.freq_count, col * sizes.group : (col + 1) * sizes.group
            ]
            yield c, slice(col * LANES, (col + 1) * LANES), piece.reshape(LANES, LANES).T


def chunk_loader(sizes, ref):
    def load(channel):
        pieces = [
            ref[pl.ds(col * sizes.group + channel, sizes.devices, stride=sizes.chunk), :]
            for col in range(sizes.cols)
        ]
        return jnp.concatenate(pieces, axis=0)

    return load


def chunk_storer(sizes, ref):
    def store(channel, values):
        for col in range(sizes.cols):
            ref[pl.ds(col * sizes.group + channel, sizes.devices, stride=sizes.chunk), :] = values[
                col * sizes.devices : (col + 1) * sizes.devices
            ]

    return store


def pooled_taps(taps):
    lane = lax.broadcasted_iota(jnp.int32, taps.shape, 2)
    zero = jnp.zeros_like(taps[:1])
    after = pltpu.roll(taps, LANES - 1, 2)
    before = pltpu.roll(taps, 1, 2)
    after = jnp.where(lane == LANES - 1, jnp.concatenate([after[1:], zero], axis=0), after)
    before = jnp.where(lane == 0, jnp.concatenate([zero, before[:-1]], axis=0), before)
    return (before + taps + after) / 3.0


def live_mask(shape, lengths):
    tap = lax.broadcasted_iota(jnp.int32, shape, 0) * LANES + lax.broadcasted_iota(
        jnp.int32, shape, 2
    )
    return (tap < lengths[None]).astype(F32)


VALUE, GATE, OUT, UP, DOWN = range(5)
ACT, HID = range(2)
PIECES = 4
ACROSS, INWARD, OUTWARD = range(3)
V0, V1, V2, G, O, U0, U1, U2, U3, D0, D1, D2, D3, S, T, C, W = range(17)
TOPS = [lambda n: (1, 2)]
LOW = [lambda n: (2,)]
SPREAD_OUT = LOW + [lambda n: Line(ACROSS, 1, 2), lambda n: Line(OUTWARD, 1, 2)]
BRING_IN = [lambda n: Line(INWARD, 1, 2), lambda n: Line(ACROSS, 1, 2)] + LOW
X, Y, CORE = [lambda n: (0,)], [lambda n: (n - 2,)], [lambda n: (n - 1,)]
PLANE = [lambda n: (0, n - 2)]
GATHER_PHASES = {
    G: SPREAD_OUT + Y + X + CORE,
    O: SPREAD_OUT + Y + X + CORE,
    U0: SPREAD_OUT + Y + CORE,
    D0: SPREAD_OUT + Y + CORE,
    U1: SPREAD_OUT + Y + CORE,
    D1: Y + SPREAD_OUT + CORE,
    U2: Y + SPREAD_OUT + CORE,
    D2: SPREAD_OUT + Y + CORE,
    U3: SPREAD_OUT + Y + CORE,
    D3: SPREAD_OUT + Y + CORE,
    V0: TOPS + PLANE + CORE,
    V1: TOPS + PLANE + CORE,
    V2: TOPS + PLANE + CORE,
}
REDUCE_PHASES = {
    G: X + Y + BRING_IN,
    O: X + Y + BRING_IN,
    U0: Y + BRING_IN,
    D0: Y + BRING_IN,
    U1: Y + BRING_IN,
    D1: BRING_IN + Y,
    U2: Y + BRING_IN,
    D2: BRING_IN + Y,
    U3: Y + BRING_IN,
    D3: Y + BRING_IN,
    V0: PLANE + TOPS,
    V1: PLANE + TOPS,
    V2: PLANE + TOPS,
}
SPREAD_PHASES = CORE + PLANE + TOPS


class Order:
    tokens = (G, U0, G, D2, U0, O, D3, T, V0, G, V1, O, U2, D2, U3)
    norm = (U1,)
    w_value = ((D0, V2, V0, C, U0, D3, U3, G, O), (), (O, D1, U2))
    value = ((), (U1,), ())
    sent = (G,)
    taps = (V1,)
    kernel = (U1,)
    arrive = ((U0,), (), (U2, D2))
    conv = ((U3, D0), (U1, O), (D1, U3, D0))
    convolved = ()
    cotangent = ()
    turn = ()
    w_gate = ()
    gate = ()
    mixed = ((U1, D0, D3, U0, U2, D1, D2), (O, U3), ())
    inner = ()
    w_out = ()
    residual = ()
    turn_near = (D1, D3, D0)
    w_up = ((), (), (), ())
    near_up = ((), (), (D2,), (D1, G))
    wait_far = ((D3,), ())
    far_up = ((), ())
    down_a = ((), (), (), ())
    far_a = ((), (), (), ())
    far_b = ()
    near_down = (D2, D0, D1)
    far_back = ((), (D3,))
    norm_back = ()
    sent_back = (D0, O, U2, D2, D3, U0, D1)
    output = ()
    arrive_back = ((), (O, U0), ())
    conv_back = ((G, U2, U1), (), ())
    convolved_back = ()
    taps_back = (G, D1, U2, W, D0, U1)
    signal = ((D3,), (), (U3, G, V1, V0, U1))
    input_back = ((O, U0), (), (D2, V2))
    first_back = (U3,)
    finish_output = (U2, O, G)
    last = (D3, D0, U0, V0, U3, U1, S, D2, V1, V2, O, G, D1, U3)
    finish_grad = (S,)
    taps_home = ()
    end = ()


VMEM_SPEC = pl.BlockSpec(memory_space=pltpu.VMEM)
ANY_SPEC = pl.BlockSpec(memory_space=pl.ANY)
GELU_SCALE = math.sqrt(2.0 / math.pi)
GELU_CUBE = 0.044715


def dot_nt(left, right):
    return lax.dot_general(left, right, (((1,), (1,)), ((), ())), preferred_element_type=F32)


def norm(values):
    center = jnp.mean(values, axis=-1, keepdims=True)
    shifted = values - center
    scale = lax.rsqrt(jnp.mean(shifted * shifted, axis=-1, keepdims=True) + EPSILON)
    return shifted * scale, scale


def norm_back(grad_rows, normed, scale, gain):
    scaled = grad_rows * gain
    plain = jnp.mean(scaled, axis=-1, keepdims=True)
    cross = jnp.mean(scaled * normed, axis=-1, keepdims=True)
    return scale * (scaled - plain - normed * cross)


class Part:
    def __init__(self, weight, piece, columns, dims, at):
        self.weight, self.piece, self.columns, self.at = weight, piece, columns, at
        self.dims = tuple(range(1 if weight in (UP, DOWN) else 0, dims))
        self.gather = tuple(phase(dims) for phase in GATHER_PHASES[at])
        self.reduce = tuple(phase(dims) for phase in REDUCE_PHASES[at])


def most(phases):
    return max(len(flips_of(step)) for step in phases)


class Plan:
    def __init__(self, sizes, tables):
        self.sizes = sizes
        here, channels, half = sizes.here, sizes.channels, sizes.half
        width = 2 * half
        self.width = width
        dims = 1 + len(bit_sizes(sizes.freq_count))
        self.dims = dims
        self.rows = rows = width // sizes.freq_count
        pieces = ((VALUE, sizes.groups, LANES), (GATE, 1, half), (OUT, 1, half), (UP, PIECES, half), (DOWN, PIECES, half))
        self.parts = []
        for weight, count, columns in pieces:
            for piece in range(count):
                self.parts.append(Part(weight, piece, columns, dims, len(self.parts)))
        self.spread = tuple(phase(dims) for phase in SPREAD_PHASES)
        groups = [self.spread] + [p.gather for p in self.parts] + [p.reduce for p in self.parts]
        self.partners = sorted(
            {flipped for phases in groups for step in phases for flipped in flips_of(step) if 0 in flipped}
        )

        def vmem(kind, *shape):
            return pltpu.VMEM(shape, kind)

        def sems(*shape):
            return pltpu.SemaphoreType.DMA(shape)

        def weights(bits):
            return [
                vmem(BF16, count, *(2,) * (bits + (weight not in (UP, DOWN))), rows, columns)
                for weight, count, columns in pieces
            ]

        def rows_of(kind, *lead):
            return vmem(kind, *lead, here, width)

        def turned(tokens):
            return vmem(BF16, width // (2 * rows), 2, rows, tokens)

        def turned_half(tokens):
            return vmem(BF16, width // (2 * rows), rows, tokens)

        def halves():
            return vmem(BF16, 2, here, half)

        def tiles():
            return vmem(BF16, PIECES, 2, 2 * here, half)

        def chunks():
            return vmem(BF16, sizes.groups, sizes.devices, sizes.chunk, LANES)

        def spectra(kind):
            return [vmem(kind, sizes.group_rows, 2 * LANES) for _ in range(sizes.groups)]

        def wide():
            return [vmem(F32, sizes.devices * sizes.chunk, LANES) for _ in range(sizes.groups)]

        taps = (sizes.tap_rows, sizes.groups, sizes.group, LANES)
        flat_taps = (sizes.tap_rows * channels, LANES)
        gain_rows = 2 * width // LANES + 4
        scratch = dict(
            x_buf=halves(),
            g_buf=vmem(BF16, 2, 2, here, half),
            gains=[[vmem(F32, half) for _ in range(2)] for _ in range(2)],
            lengths=vmem(jnp.int32, half),
            turned=vmem(F32, half, 8),
            weights=weights(dims - 1),
            grads=weights(dims - 2),
            landings=[
                [vmem(BF16, *shape) for shape in landing_shapes(part.reduce, part.dims[:-1], rows, part.columns)]
                for part in self.parts
            ],
            part_sems=[
                (sems(max(most(p.gather), most(p.reduce))), sems(slots(p.gather)), sems(slots(p.reduce)))
                for p in self.parts
            ],
            kernel_spec=spectra(F32),
            value_spec=spectra(F32),
            grad_spec=spectra(F32),
            inner_into=spectra(BF16),
            inner_from=spectra(F32),
            inner_taps=spectra(F32),
            wide_in=wide(),
            wide_out=wide(),
            taps=vmem(F32, *taps),
            tap_grad=vmem(BF16, sizes.tap_rows, -(-channels // 16) * 16, LANES),
            tap_land=vmem(BF16, sizes.freq_count, -(-channels // 16) * 16, LANES),
            tap_wide=vmem(F32, *flat_taps),
            sent=chunks(),
            sent_back=chunks(),
            landed=[chunks() for _ in range(4)],
            move_sems=[[sems(2) for _ in range(sizes.groups)] for _ in range(4)],
            tap_sems=[sems(2) for _ in range(2)],
            normed1=rows_of(F32),
            gate=rows_of(F32),
            mixed=rows_of(F32),
            residual=rows_of(F32),
            normed2=rows_of(F32),
            grad_res=rows_of(F32),
            rows=rows_of(F32),
            out_sum=rows_of(F32, 2),
            in2_sum=rows_of(F32),
            scale1=vmem(F32, here, 1),
            scale2=vmem(F32, here, 1),
            input1=rows_of(BF16),
            branch_rows=rows_of(BF16),
            in2_send=rows_of(BF16),
            in2_land=rows_of(BF16),
            input2=rows_of(BF16, 2),
            grad_rows=rows_of(BF16, 2),
            t_input1=(turned(here), turned_half(here)),
            t_branch=(turned(here), turned_half(here)),
            t_input2=(turned(2 * here), turned_half(2 * here)),
            t_grad=(turned(2 * here), turned_half(2 * here)),
            inner_rows=(halves(), halves()),
            signal_rows=[vmem(BF16, sizes.groups, here, 2 * LANES) for _ in range(2)],
            gate_rows=(halves(), halves()),
            tiles=(tiles(), tiles()),
            slopes=vmem(F32, PIECES, 2 * here, half),
            tile_sems=sems(2, 2, PIECES),
            twin_sems=sems(2, 6 + sizes.groups),
            gain_total=vmem(F32, len(self.spread) + 1, gain_rows, LANES),
            gain_land=vmem(F32, slots(self.spread), gain_rows, LANES),
            gain_sems=(sems(most(self.spread)), sems(slots(self.spread))),
            out_send=halves(),
            out_land=halves(),
            gin_send=vmem(BF16, here, half),
            gin_land=vmem(BF16, here, half),
            swap_sems=sems(2, 12),
            local=sems(13 + len(self.parts)),
            tables=[vmem(table.dtype, *table.shape) for table in tables],
        )
        self.scratch, self.tree = jax.tree.flatten(
            scratch, is_leaf=lambda leaf: not isinstance(leaf, (dict, list, tuple))
        )


def row_tiles(count, body, first=0, tile=64):
    def one(step, carry):
        body(pl.ds(pl.multiple_of(first + step * tile, tile), tile))
        return carry

    lax.fori_loop(0, count // tile, one, 0)


def block_kernel(plan, tokens, cotangent, first_gain, second_gain, lengths, raw_kernel, *refs):
    shards, refs = refs[:5], refs[5:]
    tables = refs[:7]
    output, grad_input, *weight_grads = refs[7:14]
    gain_sums, grad_kernel = refs[14:16]
    k = types.SimpleNamespace(**jax.tree.unflatten(plan.tree, refs[16:]))
    into, outof, taps_into, taps_outof, turn, ahead, behind = k.tables
    sizes = plan.sizes
    here, half, width, channels = sizes.here, sizes.half, plan.width, sizes.channels
    place = Place(sizes.freq_count)
    chan, core = place.chan, place.core
    twin = place.other((plan.dims - 1,))
    across = place.other((0,))
    me = chan * sizes.freq_count + place.freq

    def whole(weight, *lead, lanes=slice(None)):
        value = k.weights[weight][lead + (slice(None),) * plan.dims + (lanes,)]
        return value.reshape(width, value.shape[-1])

    def of_group(group):
        return slice(group * LANES, (group + 1) * LANES)

    def both_halves(weight, *lead, lanes=slice(None)):
        return jnp.concatenate([whole(weight, *lead, c, lanes=lanes) for c in range(2)], axis=1)

    def of_chan(values):
        return jnp.where(chan == 0, values[:, :half], values[:, half:])

    def of_other_chan(values):
        return jnp.where(chan == 0, values[:, half:], values[:, :half])

    own = []
    for part in plan.parts:
        source = shards[part.weight].at[:, pl.ds(part.piece * part.columns, part.columns)]
        target = k.weights[part.weight].at[(part.piece,) + tuple(place.coords[dim] for dim in part.dims)]
        own.append(pltpu.make_async_copy(source, target, k.local.at[part.at]))
    for source, target in (
        (tokens.at[chan], k.x_buf.at[chan]),
        (cotangent, k.g_buf.at[chan]),
        (raw_kernel.at[:, place.freq], k.taps.at[place.freq]),
        (first_gain, k.gains[0][0]),
        (second_gain, k.gains[0][1]),
        (lengths, k.lengths),
    ):
        own.append(pltpu.make_async_copy(source, target, k.local.at[len(own)]))
    for source, target in zip(tables, k.tables):
        own.append(pltpu.make_async_copy(source, target, k.local.at[len(own)]))
    for copy in own:
        copy.start()
    own_tokens, own_cotangent, own_taps, *own_rows = own[len(plan.parts) :]
    own_tables, own_rows = own_rows[3:], own_rows[:3]
    barrier = pltpu.get_barrier_semaphore()
    for flipped in plan.partners:
        pl.semaphore_signal(barrier, inc=1, device_id=place.other(flipped), device_id_type=MESH)

    def greet(step, carry):
        peer = (lax.rem(place.freq + step, sizes.freq_count), chan)
        pl.semaphore_signal(barrier, inc=1, device_id=peer, device_id_type=MESH)
        return carry

    lax.fori_loop(1, sizes.freq_count, greet, 0, unroll=True)
    pl.semaphore_wait(barrier, len(plan.partners) + sizes.freq_count - 1)

    def swap(at, source, target):
        copy = remote(source, target, k.swap_sems.at[0, at], k.swap_sems.at[1, at], across)
        copy.start()
        return copy

    moving = {}
    for part in plan.parts:
        moving[part.at] = Gather(
            place,
            k.weights[part.weight].at[part.piece],
            part.dims,
            part.gather,
            k.part_sems[part.at][0],
            k.part_sems[part.at][1],
            own[part.at].wait,
        )

    def ahead_of(names):
        for name in names:
            moving[name].go()

    def all_to_all(move, group, source):
        target = k.landed[move]
        exchange = Exchange(
            sizes.devices,
            me,
            lambda other: (lax.rem(other, sizes.freq_count), other // sizes.freq_count),
            lambda other: source.at[group, other],
            lambda other: target.at[group, other],
            source.at[group, pl.ds(0, sizes.devices - 1)],
            target.at[group, pl.ds(0, sizes.devices - 1)],
            k.move_sems[move][group],
        )
        exchange.start()
        target[group, me] = source[group, me]
        return exchange

    swap_tokens = swap(0, tokens.at[1 - chan], k.x_buf.at[chan])
    swap_gains = [swap(at, ref, k.gains[1][at - 9]) for at, ref in ((9, first_gain), (10, second_gain))]
    for group in range(sizes.groups):
        moving[V0 + group].go()
    others = sizes.freq_count - 1

    def begin(exchange):
        exchange.start()
        return exchange

    tap_move = Exchange(
        sizes.freq_count,
        place.freq,
        lambda other: (other, chan),
        lambda other: raw_kernel.at[:, other],
        lambda other: k.taps.at[other],
        raw_kernel.at[:, pl.ds(0, others)],
        k.taps.at[pl.ds(0, others)],
        k.tap_sems[0],
    )
    moving[T] = Once(lambda: begin(tap_move))
    moving[C] = Once(lambda: swap(2, cotangent, k.g_buf.at[chan]))
    ahead_of(Order.tokens)
    swap_tokens.wait()
    own_tokens.wait()
    for copy in swap_gains + own_rows:
        copy.wait()

    def gain_row(row):
        near, far = k.gains[0][row][...][None], k.gains[1][row][...][None]
        return jnp.concatenate([jnp.where(chan == 0, near, far), jnp.where(chan == 0, far, near)], axis=1)

    first_gain, second_gain = gain_row(0), gain_row(1)

    def first_norm(at):
        rows = jnp.concatenate([k.x_buf[0, at, :], k.x_buf[1, at, :]], axis=1).astype(F32)
        normed, scale = norm(rows)
        k.normed1[at, :] = normed
        k.scale1[at, :] = scale
        k.input1[at, :] = (normed * first_gain).astype(BF16)

    ahead_of(Order.norm)
    row_tiles(here, first_norm)

    def turn_rows(source, target, columns=slice(None)):
        turned = source[...].astype(F32).T.astype(BF16)
        target[:, :, :, columns] = turned.reshape(target.shape[:-1] + (here,))

    arriving = {}

    def share(at, source, target):
        copy = remote(source, target, k.twin_sems.at[0, at], k.twin_sems.at[1, at], twin)
        copy.start()
        arriving[at] = copy

    def share_turned(at, pair):
        share(at, pair[0].at[:, 1 - core], pair[1])

    def need(at):
        if arriving[at] is not None:
            arriving[at].wait()
            arriving[at] = None

    turn_rows(k.input1, k.t_input1[0])
    share_turned(0, k.t_input1)

    def send_chunks(move, group, source, halves):
        for c in range(2):
            devices = pl.ds(c * sizes.freq_count, sizes.freq_count)
            to_chunks(sizes, halves[c], source.at[group, devices])
        return all_to_all(move, group, source)

    moves = []
    for group in range(sizes.groups):
        ahead_of(Order.w_value[group])
        moving[V0 + group].finish()
        ahead_of(Order.value[group])
        got = dot(k.input1[...], both_halves(VALUE, group))
        moves.append(send_chunks(0, group, k.sent, (got[:, :LANES], got[:, LANES:])))
    ahead_of(Order.sent)
    ahead_of(Order.taps)
    moving[T].finish()
    for copy in own_tables:
        copy.wait()
    own_taps.wait()
    k.turned[...] = jnp.broadcast_to(k.lengths[...].astype(F32)[None], (8, half)).T
    lives = [
        k.turned[pl.ds(pl.multiple_of(group * LANES + place.freq * sizes.group, 8), sizes.group), 0:1]
        for group in range(sizes.groups)
    ]
    flat_taps = (sizes.tap_rows, channels, LANES)
    live = live_mask(flat_taps, jnp.concatenate(lives, axis=0))
    pooled = pooled_taps(k.taps[...].reshape(flat_taps))
    shrunk = (pooled - THRESH * jnp.tanh(pooled / THRESH)) * live
    k.tap_wide[...] = shrunk.reshape(sizes.tap_rows * channels, LANES)
    ahead_of(Order.kernel)

    def tap_load(group):
        return lambda c: k.tap_wide[pl.ds(group * sizes.group + c, sizes.tap_rows, stride=channels), :]

    for group in range(sizes.groups):
        spectrum_into(
            sizes, tap_load(group), taps_into, turn, ahead, k.inner_into[group], k.kernel_spec[group]
        )

    def spectrum_of(move, group, spectra):
        flat = (sizes.devices * sizes.chunk, LANES)
        k.wide_in[group][...] = k.landed[move][group].astype(F32).reshape(flat)
        spectrum_into(
            sizes, chunk_loader(sizes, k.wide_in[group]), into, turn, ahead, k.inner_into[group], spectra[group]
        )

    def chunks_from(group, product):
        signal_from(
            sizes, product, outof, turn, behind, k.inner_from[group], chunk_storer(sizes, k.wide_out[group])
        )
        k.sent_back[group] = k.wide_out[group][...].reshape(k.sent_back.shape[1:]).astype(BF16)

    moves_back = []
    for group in range(sizes.groups):
        ahead_of(Order.arrive[group])
        moves[group].wait()
        ahead_of(Order.conv[group])
        spectrum_of(0, group, k.value_spec)
        chunks_from(group, times(k.value_spec[group][...], k.kernel_spec[group][...], False))
        moves_back.append(all_to_all(1, group, k.sent_back))
    ahead_of(Order.convolved)
    ahead_of(Order.cotangent)
    moving[C].finish()
    own_cotangent.wait()
    ahead_of(Order.turn)
    for which, seq in ((0, chan), (1, 1 - chan)):
        k.grad_rows[which] = jnp.concatenate([k.g_buf[0, seq], k.g_buf[1, seq]], axis=1)
        turn_rows(k.grad_rows.at[which], k.t_grad[0], slice(which * here, (which + 1) * here))
    share_turned(2, k.t_grad)
    ahead_of(Order.w_gate)
    moving[G].finish()
    ahead_of(Order.gate)
    for c in range(2):
        k.gate[:, c * half : (c + 1) * half] = dot(k.input1[...], whole(GATE, 0, c))
    for group in range(sizes.groups):
        ahead_of(Order.mixed[group])
        moves_back[group].wait()
        for c, tokens_at, rows in from_chunks(sizes, k.landed[1].at[group]):
            k.mixed[tokens_at, c * half + group * LANES : c * half + (group + 1) * LANES] = rows
    ahead_of(Order.inner)

    def make_inner(at):
        gate = k.gate[at, :]
        inner = (k.mixed[at, :] * (gate * jax.nn.sigmoid(gate))).astype(BF16)
        k.inner_rows[0][0, at, :] = inner[:, :half]
        k.inner_rows[0][1, at, :] = inner[:, half:]

    row_tiles(here, make_inner)
    share(4, *k.inner_rows)
    ahead_of(Order.w_out)
    moving[O].finish()
    ahead_of(Order.residual)
    k.residual[...] = dot_nt(k.inner_rows[0][0], whole(OUT, 0, 0)) + dot_nt(
        k.inner_rows[0][1], whole(OUT, 0, 1)
    )

    def second_norm(at):
        rows = jnp.concatenate([k.x_buf[0, at, :], k.x_buf[1, at, :]], axis=1).astype(F32)
        residual = k.residual[at, :] + rows
        normed, scale = norm(residual)
        k.residual[at, :] = residual
        k.normed2[at, :] = normed
        k.scale2[at, :] = scale
        k.input2[0, at, :] = (normed * second_gain).astype(BF16)

    row_tiles(here, second_norm)
    blocks = [pl.ds(at * (here // 2), here // 2) for at in range(2)]
    swap_input2 = [swap(3 + at, k.input2.at[0, rows], k.input2.at[1, rows]) for at, rows in enumerate(blocks)]
    ahead_of(Order.turn_near)
    turn_rows(k.input2.at[0], k.t_input2[0], slice(0, here))

    def product(left, right, pick):
        mine, theirs = left[0][:, core], left[1][...]
        shape = (width // 2, mine.shape[-1])
        got = dot(
            jnp.concatenate([mine.reshape(shape), theirs.reshape(shape)], axis=1),
            jnp.concatenate([right[0][pick], right[1][pick]], axis=0),
        ).astype(BF16)
        return got.reshape((2,) * (plan.dims - 2) + (plan.rows, got.shape[-1]))

    factors = {
        VALUE: (k.t_input1, 0, k.signal_rows, 6),
        GATE: (k.t_input1, 0, k.gate_rows, 5),
        OUT: (k.t_branch, 3, k.inner_rows, 4),
        UP: (k.t_input2, 1, k.tiles, None),
        DOWN: (k.t_grad, 2, k.tiles, None),
    }

    def prepare(part):
        left, left_share, right, right_share = factors[part.weight]
        need(left_share)
        total = k.grads[part.weight]
        if part.weight == VALUE:
            need(right_share + part.piece)
            got = product(left, right, part.piece)
            for c in range(2):
                total[part.piece, c] = got[..., of_group(c)]
        elif part.weight in (GATE, OUT):
            need(right_share)
            for c in range(2):
                total[part.piece, c] = product(left, right, c)
        else:
            kind = HID if part.weight == UP else ACT
            tile_copy(kind, part.piece).wait()
            total[part.piece] = product(left, right, (part.piece, kind))

    def begin_reducing(part):
        moving[part.at] = Reduce(
            place,
            k.grads[part.weight].at[part.piece],
            k.landings[part.at],
            part.dims[:-1],
            part.reduce,
            k.part_sems[part.at][0],
            k.part_sems[part.at][2],
            weight_grads[part.weight].at[:, pl.ds(part.piece * part.columns, part.columns)],
            functools.partial(prepare, part),
        )
    def start_reducing():
        for name, mover in list(moving.items()):
            if isinstance(mover, Gather):
                mover.finish()
        for part in plan.parts:
            begin_reducing(part)

    def up_part(which, piece, first, count):
        rows = pl.ds(first, count)
        stored = pl.ds(which * here + first, count)
        hidden = dot(k.input2[which, rows, :], whole(UP, piece))
        square = hidden * hidden
        bent = jnp.tanh(GELU_SCALE * hidden * (1.0 + GELU_CUBE * square))
        k.tiles[0][piece, ACT, stored, :] = (0.5 * hidden * (1.0 + bent)).astype(BF16)
        k.slopes[piece, stored, :] = 0.5 * (1.0 + bent) + (0.5 * GELU_SCALE) * hidden * (1.0 - bent * bent) * (
            1.0 + 3.0 * GELU_CUBE * square
        )

    def grad_part(which, piece, first, count):
        stored = pl.ds(which * here + first, count)
        grad = dot(k.grad_rows[which, pl.ds(first, count), :], whole(DOWN, piece)) * k.slopes[piece, stored, :]
        k.tiles[0][piece, HID, stored, :] = grad.astype(BF16)

    def in2_part(which, first, count, side):
        rows = pl.ds(which * here + first, count)
        return sum(
            dot_nt(k.tiles[0][piece, HID, rows, :], k.weights[UP][piece, side].reshape(half, half))
            for piece in range(PIECES)
        )

    def out_part(which, side):
        rows = pl.ds(which * here, here)
        return sum(
            dot_nt(k.tiles[0][piece, ACT, rows, :], k.weights[DOWN][piece, side].reshape(half, half))
            for piece in range(PIECES)
        )

    def tile_copy(kind, piece):
        return remote(
            k.tiles[0].at[piece, kind],
            k.tiles[1].at[piece, kind],
            k.tile_sems.at[0, kind, piece],
            k.tile_sems.at[1, kind, piece],
            twin,
        )

    for piece in range(PIECES):
        ahead_of(Order.w_up[piece])
        moving[U0 + piece].finish()
        ahead_of(Order.near_up[piece])
        up_part(0, piece, 0, here)
    swap_in2 = []

    def return_far(at):
        back = []
        for side in range(2):
            index = (blocks[at], pl.ds(side * half, half))
            k.in2_send[index] = in2_part(1, at * (here // 2), here // 2, side).astype(BF16)
            back.append(swap(5 + 2 * at + side, k.in2_send.at[index], k.in2_land.at[index]))
        swap_in2.append(back)

    for at in range(2):
        ahead_of(Order.wait_far[at])
        swap_input2[at].wait()
        ahead_of(Order.far_up[at])
        for piece in range(PIECES):
            up_part(1, piece, at * (here // 2), here // 2)
            if at:
                tile_copy(ACT, piece).start()
        if at:
            start_reducing()
            ahead_of(Order.far_b)
        for piece in range(PIECES):
            if not at:
                ahead_of(Order.down_a[piece])
                moving[D0 + piece].finish()
                ahead_of(Order.far_a[piece])
            grad_part(1, piece, at * (here // 2), here // 2)
        return_far(at)
    ahead_of(Order.near_down)
    for piece in range(PIECES):
        grad_part(0, piece, 0, here)
        tile_copy(HID, piece).start()
    for side in range(2):
        k.in2_sum[:, side * half : (side + 1) * half] = in2_part(0, 0, here, side)
    turn_rows(k.input2.at[1], k.t_input2[0], slice(here, 2 * here))
    share_turned(1, k.t_input2)

    k.gain_total[0] = jnp.zeros_like(k.gain_total[0])

    def add_gain(row, sums):
        for at in range(width // LANES):
            base = row * (width // LANES) + at
            k.gain_total[0, base : base + 1, :] += sums[:, at * LANES : (at + 1) * LANES]

    def second_back(at):
        grad = k.in2_sum[at, :] + k.in2_land[at, :].astype(F32)
        normed = k.normed2[at, :]
        add_gain(1, jnp.sum(grad * normed, axis=0, keepdims=True))
        result = k.grad_rows[0, at, :].astype(F32) + norm_back(
            grad, normed, k.scale2[at, :], second_gain
        )
        k.grad_res[at, :] = result
        k.branch_rows[at, :] = result.astype(BF16)

    for at in range(2):
        ahead_of(Order.far_back[at])
        for copy in swap_in2[at]:
            copy.wait()
        row_tiles(here // 2, second_back, at * (here // 2))
    ahead_of(Order.norm_back)
    moves = []
    for group in range(sizes.groups):
        got = dot(k.branch_rows[...], both_halves(OUT, 0, lanes=of_group(group)))
        grad_mixed = []
        for c in range(2):
            columns = slice(c * half + group * LANES, c * half + (group + 1) * LANES)
            gate, grad = k.gate[:, columns], got[:, of_group(c)]
            sig = jax.nn.sigmoid(gate)
            k.gate_rows[0][c, :, of_group(group)] = (
                grad * k.mixed[:, columns] * (sig * (1.0 + gate * (1.0 - sig)))
            ).astype(BF16)
            grad_mixed.append(grad * (gate * sig))
        moves.append(send_chunks(2, group, k.sent, grad_mixed))
    share(5, *k.gate_rows)
    turn_rows(k.branch_rows, k.t_branch[0])
    share_turned(3, k.t_branch)
    ahead_of(Order.sent_back)
    ahead_of(Order.output)
    for which in range(2):
        for side in range(2):
            k.out_sum[which, :, side * half : (side + 1) * half] = out_part(which, side)

    def make_output(at):
        near = k.residual[at, :] + k.out_sum[0, at, :]
        far = k.out_sum[1, at, :]
        k.out_send[0, at, :] = of_other_chan(near).astype(BF16)
        k.out_send[1, at, :] = of_other_chan(far).astype(BF16)

    row_tiles(here, make_output)
    moving[W] = Once(lambda: swap(1, k.out_send, k.out_land))

    moves_back = []
    for group in range(sizes.groups):
        ahead_of(Order.arrive_back[group])
        moves[group].wait()
        ahead_of(Order.conv_back[group])
        spectrum_of(2, group, k.grad_spec)
        chunks_from(group, times(k.grad_spec[group][...], k.kernel_spec[group][...], True))
        moves_back.append(all_to_all(3, group, k.sent_back))
    ahead_of(Order.convolved_back)

    def tap_store(group):
        def store(channel, values):
            k.tap_wide[pl.ds(group * sizes.group + channel, sizes.tap_rows, stride=channels), :] = values

        return store

    ahead_of(Order.taps_back)
    for group in range(sizes.groups):
        signal_from(
            sizes,
            times(k.grad_spec[group][...], k.value_spec[group][...], True),
            taps_outof, turn, behind, k.inner_taps[group], tap_store(group),
        )
    pooled = pooled_taps(k.taps[...].reshape(flat_taps))
    bent = jnp.tanh(pooled / THRESH)
    tap_grads = pooled_taps(k.tap_wide[...].reshape(pooled.shape) * live * bent * bent)
    filling = jnp.zeros((sizes.tap_rows, k.tap_grad.shape[1] - channels, LANES), F32)
    k.tap_grad[...] = jnp.concatenate([tap_grads, filling], axis=1).astype(BF16)
    tap_back = Exchange(
        sizes.freq_count,
        place.freq,
        lambda other: (other, chan),
        lambda other: k.tap_grad.at[other],
        lambda other: k.tap_land.at[other],
        k.tap_grad.at[pl.ds(0, others)],
        k.tap_land.at[pl.ds(0, others)],
        k.tap_sems[1],
    )
    tap_back.start()
    k.tap_land[place.freq] = k.tap_grad[place.freq]

    k.rows[...] = dot_nt(k.gate_rows[0][0], whole(GATE, 0, 0)) + dot_nt(k.gate_rows[0][1], whole(GATE, 0, 1))
    for group in range(sizes.groups):
        ahead_of(Order.signal[group])
        moves_back[group].wait()
        for c, tokens_at, rows in from_chunks(sizes, k.landed[3].at[group]):
            k.signal_rows[0][group, tokens_at, of_group(c)] = rows.astype(BF16)
        share(6 + group, k.signal_rows[0].at[group], k.signal_rows[1].at[group])
        ahead_of(Order.input_back[group])
        k.rows[...] += dot_nt(k.signal_rows[0][group], both_halves(VALUE, group))
    ahead_of(Order.first_back)

    def first_back(at):
        grad = k.rows[at, :]
        normed = k.normed1[at, :]
        add_gain(0, jnp.sum(grad * normed, axis=0, keepdims=True))
        result = k.grad_res[at, :] + norm_back(grad, normed, k.scale1[at, :], first_gain)
        k.gin_send[at, :] = of_other_chan(result).astype(BF16)
        grad_input[chan, at, :] = of_chan(result)

    row_tiles(here, first_back)
    swap_gin = swap(11, k.gin_send, k.gin_land)
    spread = Spread(place, k.gain_total, k.gain_land, plan.spread, *k.gain_sems)
    moving[S] = spread
    spread.go()
    ahead_of(Order.finish_output)
    moving[W].finish()

    def finish_output(at):
        near = of_chan(k.residual[at, :] + k.out_sum[0, at, :]) + k.out_land[1, at, :].astype(F32)
        far = of_chan(k.out_sum[1, at, :]) + k.out_land[0, at, :].astype(F32)
        output[chan, at, :] = near.astype(BF16)
        output[1 - chan, at, :] = far.astype(BF16)

    row_tiles(here, finish_output)
    ahead_of(Order.last)
    swap_gin.wait()
    ahead_of(Order.finish_grad)
    grad_input[1 - chan] = k.gin_land[...].astype(F32)
    ahead_of(Order.taps_home)
    tap_back.wait()
    for group in range(sizes.groups):
        rows = slice(group * sizes.group, (group + 1) * sizes.group)
        grad_kernel[group] = k.tap_land[...].astype(F32)[:, rows]
    ahead_of(Order.end)
    for mover in moving.values():
        if not isinstance(mover, Once):
            mover.finish()
    gain_sums[...] = k.gain_total[len(plan.spread)]


def settle_kernel(count, channels, freq_count, *refs):
    sources, sums, refs = refs[:count], refs[count], refs[count + 1 :]
    targets, gains, sems = refs[: count + 2], refs[count + 2 : count + 4], refs[-1]
    going = [pltpu.make_async_copy(sources[n], targets[n], sems.at[n]) for n in range(count)]
    for copy in going:
        copy.start()
    tiles = 2 * channels * freq_count // LANES
    mine = (lax.axis_index("chan") * freq_count + lax.axis_index("freq")) * channels
    lane = lax.broadcasted_iota(jnp.int32, (channels, LANES), 1)
    feature = mine + lax.broadcasted_iota(jnp.int32, (channels, LANES), 0)
    for row, gain in enumerate(gains):
        total = jnp.zeros((channels, LANES), F32)
        for tile in range(tiles):
            at = row * tiles + tile
            total = total + jnp.where(lane + tile * LANES == feature, sums[at : at + 1, :], 0.0)
        gain[...] = jnp.sum(total.T, axis=0, keepdims=True)
        going.append(pltpu.make_async_copy(gain, targets[count + row], sems.at[count + row]))
        going[-1].start()
    for copy in going:
        copy.wait()


def settle(arrays, sums, sizes):
    gain = (1, sizes.channels)
    out = [jax.ShapeDtypeStruct(a.shape, a.dtype) for a in arrays] + [jax.ShapeDtypeStruct(gain, F32)] * 2
    return pl.pallas_call(
        functools.partial(settle_kernel, len(arrays), sizes.channels, sizes.freq_count),
        out_shape=out,
        in_specs=[VMEM_SPEC] * (len(arrays) + 1),
        out_specs=[ANY_SPEC] * len(out),
        scratch_shapes=[pltpu.VMEM(gain, F32)] * 2 + [pltpu.SemaphoreType.DMA((len(out),))],
        name="settle",
    )(*arrays, sums)


def one_sequence(
    tokens, cotangent, first_gain, second_gain, w_value, w_gate, w_out, w_up, w_down, raw_kernel, lengths
):
    freq_count = lax.axis_size("freq")
    _, here, half = tokens.shape
    sizes = Sizes(freq_count, here, half, raw_kernel.shape[1] * freq_count)
    tables = conv_tables(sizes)
    plan = Plan(sizes, tables)
    shards = (w_value, w_gate, w_out, w_up, w_down)
    out_shape = (
        [pltpu.VMEM((2, here, half), BF16), pltpu.VMEM((2, here, half), F32)]
        + [pltpu.VMEM(w.shape, F32) for w in shards]
        + [
            pltpu.VMEM((4 * half // LANES + 4, LANES), F32),
            pltpu.VMEM((sizes.groups, freq_count, sizes.group, LANES), F32),
        ]
    )
    results = pl.pallas_call(
        functools.partial(block_kernel, plan),
        out_shape=out_shape,
        in_specs=[ANY_SPEC] * (11 + len(tables)),
        out_specs=[VMEM_SPEC] * len(out_shape),
        scratch_shapes=plan.scratch,
        compiler_params=pltpu.CompilerParams(
            collective_id=0, has_side_effects=True, vmem_limit_bytes=60 << 20
        ),
        name="block",
    )(
        tokens,
        cotangent,
        first_gain,
        second_gain,
        lengths,
        raw_kernel.reshape(sizes.groups, freq_count, sizes.group, LANES),
        *shards,
        *tables,
    )
    results = [pltpu.with_memory_space_constraint(result, pltpu.VMEM) for result in results]
    *arrays, gain_sums, grad_kernel = results
    *arrays, grad_kernel, first_grad, second_grad = settle([*arrays, grad_kernel], gain_sums, sizes)
    return (*arrays, first_grad.T, second_grad.T, grad_kernel.reshape(raw_kernel.shape))


def fits(mesh):
    freq_count = mesh.shape["freq"]
    return lambda tokens, w_value, w_up, raw_kernel: (
        mesh.shape["chan"] == 2
        and tokens.shape[0] == 2
        and freq_count == 16
        and w_value.shape[1] == 6 * LANES
        and w_value.shape[0] % (16 * freq_count) == 0
        and w_value.shape[1] % (16 * freq_count) == 0
        and w_value.shape[1] % 256 == 0
        and w_up.shape[1] == PIECES * w_value.shape[1]
        and tokens.shape[1] % (2 * LANES * freq_count) == 0
        and raw_kernel.shape[1] == LANES * freq_count
        and (tokens.shape[1] + raw_kernel.shape[1]) // LANES % 16 == 0
    )


D = 768
SEQ_MB = 1
MICRO = 2


HIGHEST = lax.Precision.HIGHEST


def circle(height, breadth, period):
    first_index = lax.broadcasted_iota(jnp.int32, (height, breadth), 0)
    second_index = lax.broadcasted_iota(jnp.int32, (height, breadth), 1)
    phase_angle = (first_index * second_index % period).astype(jnp.float32) * (
        2.0 * math.pi / period
    )
    return (jnp.cos(phase_angle), jnp.sin(phase_angle))


def make_tables(padded_size):
    inner_size = 128
    outer_size = padded_size // inner_size
    outer_cos, outer_sin = circle(outer_size, outer_size, outer_size)
    inner_cos, inner_sin = circle(inner_size, inner_size, inner_size)
    twist_cos, twist_sin = circle(outer_size, inner_size, padded_size)
    return (outer_cos, outer_sin, inner_cos, inner_sin, twist_cos, twist_sin)


def spectrum(signal, padded_size, tables):
    outer_cos, outer_sin, inner_cos, inner_sin, twist_cos, twist_sin = tables
    inner_size = inner_cos.shape[0]
    pad_width = [(0, 0)] * (signal.ndim - 1) + [(0, padded_size - signal.shape[-1])]
    grid_values = jnp.pad(signal, pad_width).reshape(
        signal.shape[:-1] + (padded_size // inner_size, inner_size)
    )
    part_real = jnp.einsum("...ab,fa->...fb", grid_values, outer_cos, precision=HIGHEST)
    part_imag = -jnp.einsum("...ab,fa->...fb", grid_values, outer_sin, precision=HIGHEST)
    turned_real = part_real * twist_cos + part_imag * twist_sin
    turned_imag = part_imag * twist_cos - part_real * twist_sin
    spec_real = jnp.einsum(
        "...fb,bg->...fg", turned_real, inner_cos, precision=HIGHEST
    ) + jnp.einsum("...fb,bg->...fg", turned_imag, inner_sin, precision=HIGHEST)
    spec_imag = jnp.einsum(
        "...fb,bg->...fg", turned_imag, inner_cos, precision=HIGHEST
    ) - jnp.einsum("...fb,bg->...fg", turned_real, inner_sin, precision=HIGHEST)
    return (spec_real, spec_imag)


def signal_of(spec_real, spec_imag, keep_count, tables):
    outer_cos, outer_sin, inner_cos, inner_sin, twist_cos, twist_sin = tables
    padded_size = spec_real.shape[-1] * spec_real.shape[-2]
    back_real = jnp.einsum("...fg,bg->...fb", spec_real, inner_cos, precision=HIGHEST) - jnp.einsum(
        "...fg,bg->...fb", spec_imag, inner_sin, precision=HIGHEST
    )
    back_imag = jnp.einsum("...fg,bg->...fb", spec_imag, inner_cos, precision=HIGHEST) + jnp.einsum(
        "...fg,bg->...fb", spec_real, inner_sin, precision=HIGHEST
    )
    turned_real = back_real * twist_cos - back_imag * twist_sin
    turned_imag = back_imag * twist_cos + back_real * twist_sin
    grid_values = (
        jnp.einsum("...fb,af->...ab", turned_real, outer_cos, precision=HIGHEST)
        - jnp.einsum("...fb,af->...ab", turned_imag, outer_sin, precision=HIGHEST)
    ) / padded_size
    flat_values = grid_values.reshape(grid_values.shape[:-2] + (padded_size,))
    return flat_values[..., :keep_count]


def shape_kernel(raw_taps, live_taps):
    padded = jnp.pad(raw_taps, ((0, 0), (1, 1)))
    pooled = (padded[:, :-2] + padded[:, 1:-1] + padded[:, 2:]) / 3.0
    return (pooled - THRESH * jnp.tanh(pooled / THRESH)) * live_taps


def row_norm(values):
    row_width = values.shape[-1] * lax.axis_size("chan")
    row_total, row_square = lax.psum(
        (jnp.sum(values, axis=-1), jnp.sum(values * values, axis=-1)), "chan"
    )
    center = row_total / row_width
    spread = row_square / row_width - center * center
    scale = lax.rsqrt(spread + EPSILON)[..., None]
    return ((values - center[..., None]) * scale, scale)


def row_back(grad_rows, normed, scale, gain_row):
    row_width = grad_rows.shape[-1] * lax.axis_size("chan")
    scaled = grad_rows * gain_row
    sum_plain, sum_cross = lax.psum(
        (jnp.sum(scaled, axis=-1), jnp.sum(scaled * normed, axis=-1)), "chan"
    )
    return scale * (
        scaled - sum_plain[..., None] / row_width - normed * sum_cross[..., None] / row_width
    )


def features(values):
    return lax.all_gather(values, "chan", axis=2, tiled=True)


def partial_sum(values):
    return lax.psum_scatter(
        values.astype(jnp.bfloat16), "chan", scatter_dimension=2, tiled=True
    ).astype(jnp.float32)


def to_channels(values):
    return lax.all_to_all(
        jnp.swapaxes(values, 1, 2), "freq", split_axis=1, concat_axis=2, tiled=True
    )


def to_tokens(values):
    arrived = lax.all_to_all(values, "freq", split_axis=2, concat_axis=1, tiled=True)
    return jnp.swapaxes(arrived, 1, 2)


def by_features(
    tokens,
    cotangent,
    first_gain,
    second_gain,
    w_value,
    w_gate,
    w_out,
    w_up,
    w_down,
    raw_kernel,
    lengths,
):
    full_value, full_gate, full_out, full_up, full_down = (
        lax.all_gather(w_value, "freq", axis=0, tiled=True),
        lax.all_gather(w_gate, "freq", axis=0, tiled=True),
        lax.all_gather(w_out, "freq", axis=0, tiled=True),
        lax.all_gather(w_up, "freq", axis=0, tiled=True),
        lax.all_gather(w_down, "freq", axis=0, tiled=True),
    )
    freq_count = lax.axis_size("freq")
    chan_width = tokens.shape[2]
    channels = chan_width // freq_count
    seq_length = tokens.shape[1] * freq_count
    padded_size = 2 * seq_length
    tables = make_tables(padded_size)
    kernel_rows = lax.all_to_all(raw_kernel, "freq", split_axis=0, concat_axis=1, tiled=True)
    tap_count = kernel_rows.shape[1]
    my_lengths = lax.dynamic_slice_in_dim(lengths, lax.axis_index("freq") * channels, channels)
    tap_index = lax.broadcasted_iota(jnp.int32, (channels, tap_count), 1)
    live_taps = (tap_index < my_lengths[:, None]).astype(jnp.float32)
    kernel, kernel_pull = jax.vjp(functools.partial(shape_kernel, live_taps=live_taps), kernel_rows)
    kernel_real, kernel_imag = spectrum(kernel, padded_size, tables)
    hidden_width = full_up.shape[1]
    shard_factor = 1
    totals = (
        jnp.zeros((D // shard_factor, chan_width), jnp.float32),
        jnp.zeros((D // shard_factor, chan_width), jnp.float32),
        jnp.zeros((D // shard_factor, chan_width), jnp.float32),
        jnp.zeros((D // shard_factor, hidden_width), jnp.float32),
        jnp.zeros((D // shard_factor, hidden_width), jnp.float32),
        jnp.zeros((chan_width // shard_factor, 1), jnp.float32),
        jnp.zeros((chan_width // shard_factor, 1), jnp.float32),
    )
    kernel_grad = jnp.zeros((channels, tap_count), jnp.float32)
    outputs = []
    input_grads = []
    for micro_index in range(MICRO):
        rows_here = tokens[micro_index * SEQ_MB : (micro_index + 1) * SEQ_MB].astype(jnp.float32)
        first_normed, first_scale = row_norm(rows_here)
        input1 = features((first_normed * first_gain).astype(jnp.bfloat16))
        value_low = jnp.einsum(
            "bld,de->ble", input1, full_value, preferred_element_type=jnp.float32
        ).astype(jnp.bfloat16)
        gate_proj = jnp.einsum("bld,de->ble", input1, full_gate, preferred_element_type=jnp.float32)
        signal = to_channels(value_low).astype(jnp.float32)
        signal_real, signal_imag = spectrum(signal, padded_size, tables)
        mixed = signal_of(
            signal_real * kernel_real - signal_imag * kernel_imag,
            signal_real * kernel_imag + signal_imag * kernel_real,
            seq_length,
            tables,
        )
        mixed_rows = to_tokens(mixed.astype(jnp.bfloat16)).astype(jnp.float32)
        gate_act, gate_pull = jax.vjp(jax.nn.silu, gate_proj)
        inner_low = (mixed_rows * gate_act).astype(jnp.bfloat16)
        residual = rows_here + partial_sum(
            jnp.einsum("ble,oe->blo", inner_low, full_out, preferred_element_type=jnp.float32)
        )
        second_normed, second_scale = row_norm(residual)
        input2 = features((second_normed * second_gain).astype(jnp.bfloat16))
        hidden = jnp.einsum("bld,df->blf", input2, full_up, preferred_element_type=jnp.float32)
        activated, act_pull = jax.vjp(jax.nn.gelu, hidden)
        act_low = activated.astype(jnp.bfloat16)
        result = residual + partial_sum(
            jnp.einsum("blf,of->blo", act_low, full_down, preferred_element_type=jnp.float32)
        )
        outputs.append(result.astype(jnp.bfloat16))
        grad_rows_out = cotangent[micro_index * SEQ_MB : (micro_index + 1) * SEQ_MB]
        grad_full = features(grad_rows_out)
        grad_act = jnp.einsum(
            "blo,of->blf", grad_full, full_down, preferred_element_type=jnp.float32
        )
        down_grad = jnp.einsum(
            "blo,blf->of", grad_full, act_low, preferred_element_type=jnp.float32
        )
        grad_hidden = act_pull(grad_act)[0].astype(jnp.bfloat16)
        up_grad = jnp.einsum("bld,blf->df", input2, grad_hidden, preferred_element_type=jnp.float32)
        grad_in2 = partial_sum(
            jnp.einsum("blf,df->bld", grad_hidden, full_up, preferred_element_type=jnp.float32)
        )
        second_grad = jnp.sum(grad_in2 * second_normed, axis=(0, 1))
        grad_residual = grad_rows_out.astype(jnp.float32) + row_back(
            grad_in2, second_normed, second_scale, second_gain
        )
        grad_branch = features(grad_residual.astype(jnp.bfloat16))
        grad_inner = jnp.einsum(
            "blo,oe->ble", grad_branch, full_out, preferred_element_type=jnp.float32
        )
        out_grad = jnp.einsum(
            "blo,ble->oe", grad_branch, inner_low, preferred_element_type=jnp.float32
        )
        grad_mixed = to_channels((grad_inner * gate_act).astype(jnp.bfloat16)).astype(jnp.float32)
        grad_real, grad_imag = spectrum(grad_mixed, padded_size, tables)
        grad_signal = signal_of(
            grad_real * kernel_real + grad_imag * kernel_imag,
            grad_imag * kernel_real - grad_real * kernel_imag,
            seq_length,
            tables,
        )
        kernel_grad = kernel_grad + jnp.sum(
            signal_of(
                grad_real * signal_real + grad_imag * signal_imag,
                grad_imag * signal_real - grad_real * signal_imag,
                tap_count,
                tables,
            ),
            axis=0,
        )
        grad_signal_rows = to_tokens(grad_signal.astype(jnp.bfloat16))
        grad_gate_rows = gate_pull(grad_inner * mixed_rows)[0].astype(jnp.bfloat16)
        value_grad = jnp.einsum(
            "bld,ble->de", input1, grad_signal_rows, preferred_element_type=jnp.float32
        )
        gate_grad = jnp.einsum(
            "bld,ble->de", input1, grad_gate_rows, preferred_element_type=jnp.float32
        )
        grad_in1 = partial_sum(
            jnp.einsum(
                "ble,de->bld", grad_signal_rows, full_value, preferred_element_type=jnp.float32
            )
            + jnp.einsum(
                "ble,de->bld", grad_gate_rows, full_gate, preferred_element_type=jnp.float32
            )
        )
        first_grad = jnp.sum(grad_in1 * first_normed, axis=(0, 1))
        input_grads.append(
            grad_residual + row_back(grad_in1, first_normed, first_scale, first_gain)
        )
        local_terms = (
            value_grad,
            gate_grad,
            out_grad,
            up_grad,
            down_grad,
            first_grad[:, None],
            second_grad[:, None],
        )
        totals = tuple((left + right for left, right in zip(totals, local_terms)))
    totals = lax.psum_scatter(totals, "freq", scatter_dimension=0, tiled=True)
    raw_grad = kernel_pull(kernel_grad)[0]
    grad_kernel = lax.all_to_all(raw_grad, "freq", split_axis=1, concat_axis=0, tiled=True)
    output = jnp.concatenate(outputs, axis=0)
    grad_input = jnp.concatenate(input_grads, axis=0)
    return (
        output,
        grad_input,
        totals[0],
        totals[1],
        totals[2],
        totals[3],
        totals[4],
        totals[5],
        totals[6],
        grad_kernel,
    )


def solution(mesh):
    specs = dict(
        mesh=mesh,
        in_specs=(
            P(None, "freq", "chan"),
            P(None, "freq", "chan"),
            P("chan"),
            P("chan"),
            P("freq", "chan"),
            P("freq", "chan"),
            P("freq", "chan"),
            P("freq", "chan"),
            P("freq", "chan"),
            P("chan", "freq"),
            P("chan"),
        ),
        out_specs=(
            P(None, "freq", "chan"),
            P(None, "freq", "chan"),
            P("freq", "chan"),
            P("freq", "chan"),
            P("freq", "chan"),
            P("freq", "chan"),
            P("freq", "chan"),
            P("freq", "chan"),
            P("freq", "chan"),
            P("chan", "freq"),
        ),
        check_vma=False,
    )

    def step(*args):
        whole = fits(mesh)(args[0], args[4], args[7], args[9])
        return jax.shard_map(one_sequence if whole else by_features, **specs)(*args)

    return step
```

```python
import functools
import math
import types

import jax
import jax.numpy as jnp
import numpy as np
from jax import lax
from jax.experimental import pallas as pl
from jax.experimental.pallas import tpu as pltpu
from jax.sharding import PartitionSpec as P

THRESH = 0.003
EPSILON = 1e-05
LANES = 128
MESH = pl.DeviceIdType.MESH
F32 = jnp.float32
BF16 = jnp.bfloat16


def bit_sizes(freq_count):
    return [1 << i for i in reversed(range(freq_count.bit_length() - 1))]


class Place:
    def __init__(self, freq_count):
        self.freq_count = freq_count
        self.freq = lax.axis_index("freq")
        self.chan = lax.axis_index("chan")
        self.bits = bit_sizes(freq_count)
        self.coords = [self.chan] + [lax.rem(self.freq // b, 2) for b in self.bits]
        self.dims = len(self.coords)
        self.core = self.coords[-1]

    def other(self, flipped):
        freq, chan = self.freq, self.chan
        for dim in flipped:
            if dim == 0:
                chan = 1 - chan
            else:
                bit = self.bits[dim - 1]
                freq = freq + bit - 2 * bit * self.coords[dim]
        return (freq, chan)


def flips(dims):
    return [
        tuple(dim for at, dim in enumerate(dims) if mask >> at & 1) for mask in range(1, 1 << len(dims))
    ]


def remote(source, target, send, recv, device):
    return pltpu.make_async_remote_copy(
        src_ref=source,
        dst_ref=target,
        send_sem=send,
        recv_sem=recv,
        device_id=device,
        device_id_type=MESH,
    )


class Line:
    def __init__(self, way, high, low):
        self.way, self.high, self.low = way, high, low

    def ends(self, place):
        middle = place.coords[self.high] + place.coords[self.low] == 1
        end = place.coords[self.high] + place.coords[self.low] != 1
        return {ACROSS: (middle, middle), INWARD: (end, middle), OUTWARD: (middle, end)}[self.way]

    def flipped(self):
        return (self.high, self.low) if self.way == ACROSS else (self.low,)


def when(condition, action):
    if condition is None:
        action()
    else:
        pl.when(condition)(action)


class Leg:
    def __init__(self, copy, ends=(None, None)):
        self.copy, self.ends = copy, ends

    def start(self):
        when(self.ends[0], self.copy.start)

    def wait(self):
        if self.ends[0] is None:
            self.copy.wait()
        else:
            when(self.ends[0], self.copy.wait_send)
            when(self.ends[1], self.copy.wait_recv)


def flips_of(phase):
    return [phase.flipped()] if isinstance(phase, Line) else flips(phase)


def is_outward(phase):
    return isinstance(phase, Line) and phase.way == OUTWARD


def slots(phases):
    return sum(len(flips_of(phase)) for phase in phases if not is_outward(phase))


def first_slot(phases, at):
    return slots(phases[:at]) - is_outward(phases[at])


class Gather:
    def __init__(self, place, buffer, dims, phases, send, recv, prepare):
        self.place, self.buffer, self.dims, self.phases = place, buffer, dims, phases
        self.send, self.recv, self.prepare = send, recv, prepare
        self.turn = 0

    def copies(self, phase):
        done, step = set(), self.phases[phase]
        for before in self.phases[:phase]:
            if not isinstance(before, Line):
                done.update(before)
            elif before.way == OUTWARD:
                done.update((before.high, before.low))
        index = [slice(None) if dim in done else self.place.coords[dim] for dim in self.dims]
        ends = (None, None)
        if isinstance(step, Line):
            ends = step.ends(self.place)
            if step.way == OUTWARD:
                index[self.dims.index(step.high)] = 1 - self.place.coords[step.high]
        region = self.buffer.at[tuple(index)]
        base = first_slot(self.phases, phase)
        return [
            Leg(
                remote(region, region, self.send.at[k], self.recv.at[base + k], self.place.other(flipped)), ends
            )
            for k, flipped in enumerate(flips_of(step))
        ]

    def go(self):
        if self.turn > len(self.phases):
            return
        if self.turn == 0:
            self.prepare()
        else:
            for copy in self.copies(self.turn - 1):
                copy.wait()
        if self.turn < len(self.phases):
            for copy in self.copies(self.turn):
                copy.start()
        self.turn += 1

    def finish(self):
        while self.turn <= len(self.phases):
            self.go()


class Once:
    def __init__(self, begin):
        self.begin, self.copy = begin, None

    def go(self):
        if self.copy is None:
            self.copy = self.begin()

    def finish(self):
        self.go()
        self.copy.wait()


class Reduce:
    def __init__(self, place, total, landing, dims, phases, send, recv, out, prepare):
        self.place, self.total, self.landing, self.dims = place, total, landing, dims
        self.phases, self.send, self.recv, self.out = phases, send, recv, out
        self.prepare = prepare
        self.turn = 0

    def region(self, phase, flipped):
        fixed, step = set(), self.phases[phase]
        for before in self.phases[:phase]:
            if not isinstance(before, Line):
                fixed.update(before)
            elif before.way == ACROSS:
                fixed.add(before.high)
        if not isinstance(step, Line):
            fixed.update(step)
        coords = self.place.coords
        index = [
            (1 - coords[dim] if dim in flipped else coords[dim]) if dim in fixed else slice(None)
            for dim in self.dims
        ]
        if isinstance(step, Line):
            mine = coords[step.high]
            keeps = step.way == ACROSS and not flipped
            index[self.dims.index(step.high)] = mine if keeps else 1 - mine
        return tuple(index)

    def copies(self, phase):
        step = self.phases[phase]
        base = first_slot(self.phases, phase)
        ends = step.ends(self.place) if isinstance(step, Line) else (None, None)
        return [
            Leg(
                remote(
                    self.total.at[self.region(phase, flipped)],
                    self.landing[phase].at[k],
                    self.send.at[k],
                    self.recv.at[base + k],
                    self.place.other(flipped),
                ),
                ends,
            )
            for k, flipped in enumerate(flips_of(step))
        ]

    def add(self, phase):
        kept = self.region(phase, ())
        free = [at for at, part in enumerate(kept) if isinstance(part, slice)]
        landing, step = self.landing[phase], self.phases[phase]

        def one(turn, carry):
            where, there = list(kept), []
            for at, dim in enumerate(free):
                bit = lax.rem(turn // (1 << (len(free) - 1 - at)), 2)
                where[dim] = bit
                there.append(bit)
            where, there = tuple(where), tuple(there)
            total = self.total[where].astype(F32)
            for k in range(len(flips_of(step))):
                total = total + landing[(k,) + there].astype(F32)
            if phase + 1 == len(self.phases):
                self.out[...] = total
            else:
                self.total[where] = total.astype(BF16)
            return carry

        def every():
            if free:
                lax.fori_loop(0, 1 << len(free), one, 0)
            else:
                one(0, 0)

        when(step.ends(self.place)[1] if isinstance(step, Line) else None, every)

    def go(self):
        if self.turn > len(self.phases):
            return
        if self.turn == 0:
            self.prepare()
        else:
            for copy in self.copies(self.turn - 1):
                copy.wait()
            self.add(self.turn - 1)
        if self.turn < len(self.phases):
            for copy in self.copies(self.turn):
                copy.start()
        self.turn += 1

    def finish(self):
        while self.turn <= len(self.phases):
            self.go()


def landing_shapes(phases, dims, rows, columns):
    shapes, free = [], len(dims)
    for step in phases:
        if isinstance(step, Line):
            free -= 0 if step.way == INWARD else 1
            shapes.append((1,) + (2,) * (free - (step.way == INWARD)) + (rows, columns))
        else:
            free -= len(step)
            shapes.append((len(flips(step)),) + (2,) * free + (rows, columns))
    return shapes


class Spread:
    def __init__(self, place, total, landing, phases, send, recv):
        self.place, self.total, self.landing, self.phases = place, total, landing, phases
        self.send, self.recv = send, recv
        self.turn = 0

    def copies(self, phase):
        base = sum(len(flips(dims)) for dims in self.phases[:phase])
        return base, [
            remote(
                self.total.at[phase],
                self.landing.at[base + k],
                self.send.at[k],
                self.recv.at[base + k],
                self.place.other(flipped),
            )
            for k, flipped in enumerate(flips(self.phases[phase]))
        ]

    def go(self):
        if self.turn > len(self.phases):
            return
        if self.turn:
            base, copies = self.copies(self.turn - 1)
            total = self.total[self.turn - 1]
            for k, copy in enumerate(copies):
                copy.wait()
                total = total + self.landing[base + k]
            self.total[self.turn] = total
        if self.turn < len(self.phases):
            for copy in self.copies(self.turn)[1]:
                copy.start()
        self.turn += 1

    def finish(self):
        while self.turn <= len(self.phases):
            self.go()


class Exchange:
    def __init__(self, count, me, device, source, target, all_sent, all_landed, sems):
        self.count, self.me, self.device = count, me, device
        self.source, self.target = source, target
        self.all_sent, self.all_landed, self.sems = all_sent, all_landed, sems

    def start(self):
        def one(step, carry):
            other = lax.rem(self.me + step, self.count)
            remote(
                self.source(other), self.target(self.me), self.sems.at[0], self.sems.at[1], self.device(other)
            ).start()
            return carry

        lax.fori_loop(1, self.count, one, 0, unroll=True)

    def wait(self):
        for part, sem in ((self.all_sent, self.sems.at[0]), (self.all_landed, self.sems.at[1])):
            pltpu.make_async_copy(part, part, sem).wait()


class Sizes:
    def __init__(self, freq_count, here, half, taps):
        self.freq_count = freq_count
        self.here = here
        self.half = half
        self.cols = here // LANES
        self.channels = half // freq_count
        self.group = LANES // freq_count
        self.groups = self.channels // self.group
        self.chunk = self.cols * self.group
        self.devices = 2 * freq_count
        self.tap_rows = taps // LANES
        self.rows = here * freq_count // LANES + self.tap_rows
        self.size = self.rows * LANES
        self.group_rows = self.group * self.rows


def conv_tables(sizes):
    rows, size = sizes.rows, sizes.size
    f = np.arange(rows)
    a_of, imag = [], []
    for col in range(sizes.cols):
        for seq in range(2):
            for block in range(sizes.freq_count):
                a_of.append(block * sizes.cols + col)
                imag.append(seq)
    a_of, imag = np.array(a_of), np.array(imag)
    angle = 2 * np.pi * np.outer(f, a_of) / rows
    cos, sin = np.cos(angle), np.sin(angle)
    into = np.concatenate([np.where(imag, sin, cos), np.where(imag, cos, -sin)], axis=0)
    outof = into.T / size
    angle = 2 * np.pi * np.outer(f, np.arange(sizes.tap_rows)) / rows
    taps_into = np.concatenate([np.cos(angle), -np.sin(angle)], axis=0)
    taps_outof = taps_into.T / size
    b = np.arange(LANES)
    angle = 2 * np.pi * np.outer(f, b) / size
    turn = np.stack([np.cos(angle), np.sin(angle)])
    angle = 2 * np.pi * np.outer(b, b) / LANES
    cos, sin = np.cos(angle), np.sin(angle)
    ahead = np.block([[cos, -sin], [sin, cos]])
    return (
        jnp.asarray(into, BF16),
        jnp.asarray(outof, BF16),
        jnp.asarray(taps_into, BF16),
        jnp.asarray(taps_outof, BF16),
        jnp.asarray(turn, F32),
        jnp.asarray(ahead, BF16),
        jnp.asarray(ahead.T, BF16),
    )


def dot(left, right):
    return jnp.dot(left, right, preferred_element_type=F32)


def spectrum_into(sizes, load, into, turn, ahead, inner, spectrum):
    rows = sizes.rows
    for pair in range(sizes.group // 2):
        both = jnp.concatenate([load(2 * pair), load(2 * pair + 1)], axis=1).astype(BF16)
        part = dot(into[...], both)
        for side in range(2):
            real = part[:rows, side * LANES : (side + 1) * LANES]
            imag = part[rows:, side * LANES : (side + 1) * LANES]
            start = (2 * pair + side) * rows
            inner[start : start + rows, :] = jnp.concatenate(
                [real * turn[0] + imag * turn[1], imag * turn[0] - real * turn[1]], axis=1
            ).astype(BF16)
    spectrum[...] = dot(inner[...], ahead[...])


def signal_from(sizes, product, outof, turn, behind, inner, store):
    rows = sizes.rows
    inner[...] = dot(product, behind[...])
    for pair in range(sizes.group // 2):
        sides = []
        for side in range(2):
            start = (2 * pair + side) * rows
            real, imag = inner[start : start + rows, :LANES], inner[start : start + rows, LANES:]
            sides.append(
                jnp.concatenate(
                    [real * turn[0] - imag * turn[1], imag * turn[0] + real * turn[1]], axis=0
                ).astype(BF16)
            )
        got = dot(outof[...], jnp.concatenate(sides, axis=1))
        for side in range(2):
            store(2 * pair + side, got[:, side * LANES : (side + 1) * LANES])


def times(left, right, conj):
    a, b = left[:, :LANES], left[:, LANES:]
    c, d = right[:, :LANES], right[:, LANES:]
    if conj:
        return jnp.concatenate([a * c + b * d, b * c - a * d], axis=1).astype(BF16)
    return jnp.concatenate([a * c - b * d, a * d + b * c], axis=1).astype(BF16)


def to_chunks(sizes, rows, target):
    turned = rows.T.reshape(sizes.freq_count, sizes.group, sizes.here)
    pieces = [turned[:, :, col * LANES : (col + 1) * LANES] for col in range(sizes.cols)]
    target[...] = jnp.concatenate(pieces, axis=1).astype(BF16)


def from_chunks(sizes, chunks):
    wide = chunks[...].astype(F32)
    for c in range(2):
        for col in range(sizes.cols):
            piece = wide[
                c * sizes.freq_count : (c + 1) * sizes.freq_count, col * sizes.group : (col + 1) * sizes.group
            ]
            yield c, slice(col * LANES, (col + 1) * LANES), piece.reshape(LANES, LANES).T


def chunk_loader(sizes, ref):
    def load(channel):
        pieces = [
            ref[pl.ds(col * sizes.group + channel, sizes.devices, stride=sizes.chunk), :]
            for col in range(sizes.cols)
        ]
        return jnp.concatenate(pieces, axis=0)

    return load


def chunk_storer(sizes, ref):
    def store(channel, values):
        for col in range(sizes.cols):
            ref[pl.ds(col * sizes.group + channel, sizes.devices, stride=sizes.chunk), :] = values[
                col * sizes.devices : (col + 1) * sizes.devices
            ]

    return store


def pooled_taps(taps):
    lane = lax.broadcasted_iota(jnp.int32, taps.shape, 2)
    zero = jnp.zeros_like(taps[:1])
    after = pltpu.roll(taps, LANES - 1, 2)
    before = pltpu.roll(taps, 1, 2)
    after = jnp.where(lane == LANES - 1, jnp.concatenate([after[1:], zero], axis=0), after)
    before = jnp.where(lane == 0, jnp.concatenate([zero, before[:-1]], axis=0), before)
    return (before + taps + after) / 3.0


def live_mask(shape, lengths):
    tap = lax.broadcasted_iota(jnp.int32, shape, 0) * LANES + lax.broadcasted_iota(
        jnp.int32, shape, 2
    )
    return (tap < lengths[None]).astype(F32)


VALUE, GATE, OUT, UP, DOWN = range(5)
ACT, HID = range(2)
PIECES = 4
ACROSS, INWARD, OUTWARD = range(3)
V0, V1, V2, G, O, U0, U1, U2, U3, D0, D1, D2, D3, S, T, C, W = range(17)
TOPS = [lambda n: (1, 2)]
LOW = [lambda n: (2,)]
SPREAD_OUT = LOW + [lambda n: Line(ACROSS, 1, 2), lambda n: Line(OUTWARD, 1, 2)]
BRING_IN = [lambda n: Line(INWARD, 1, 2), lambda n: Line(ACROSS, 1, 2)] + LOW
X, Y, CORE = [lambda n: (0,)], [lambda n: (n - 2,)], [lambda n: (n - 1,)]
PLANE = [lambda n: (0, n - 2)]
GATHER_PHASES = {
    G: SPREAD_OUT + Y + X + CORE,
    O: SPREAD_OUT + Y + X + CORE,
    U0: SPREAD_OUT + Y + CORE,
    D0: SPREAD_OUT + Y + CORE,
    U1: SPREAD_OUT + Y + CORE,
    D1: Y + SPREAD_OUT + CORE,
    U2: Y + SPREAD_OUT + CORE,
    D2: SPREAD_OUT + Y + CORE,
    U3: SPREAD_OUT + Y + CORE,
    D3: SPREAD_OUT + Y + CORE,
    V0: TOPS + PLANE + CORE,
    V1: TOPS + PLANE + CORE,
    V2: TOPS + PLANE + CORE,
}
REDUCE_PHASES = {
    G: X + Y + BRING_IN,
    O: X + Y + BRING_IN,
    U0: Y + BRING_IN,
    D0: Y + BRING_IN,
    U1: Y + BRING_IN,
    D1: BRING_IN + Y,
    U2: Y + BRING_IN,
    D2: BRING_IN + Y,
    U3: Y + BRING_IN,
    D3: Y + BRING_IN,
    V0: PLANE + TOPS,
    V1: PLANE + TOPS,
    V2: PLANE + TOPS,
}
SPREAD_PHASES = CORE + PLANE + TOPS


class Order:
    tokens = (G, U1, U2, D1, G, O, D3, U1, U3, V0)
    norm = (D2, U0, V2, V1, T, G, C, O, U2, U3)
    w_value = ((D2,), (), (D0, G, U3, U0))
    value = ((), (D3, U1, O), ())
    sent = (G, O, D2, U1, D1)
    taps = (D0,)
    kernel = ()
    arrive = ((), (U0,), ())
    conv = ((), (U3, U2, O), (D0,))
    convolved = (U0,)
    cotangent = ()
    turn = ()
    w_gate = ()
    gate = (O, V1, U3, D3)
    mixed = ((D0, D1, V0, D2, U0), (U2,), (U1,))
    inner = ()
    w_out = ()
    residual = ()
    turn_near = (D1, G)
    w_up = ((D3,), (), (), ())
    near_up = ((D0,), (), (D2,), ())
    wait_far = ((D1,), ())
    far_up = ((D2, D3), ())
    down_a = ((), (), (), ())
    far_a = ((), (), (), ())
    far_b = ()
    near_down = (D1, D0, D2)
    far_back = ((D3,), ())
    norm_back = ()
    sent_back = (U0, G)
    output = (U2, D3)
    arrive_back = ((D2, D1, U1, O, U0), (D0,), ())
    conv_back = ((), (U2, G), ())
    convolved_back = (U1, G, W, O, U3, D3)
    taps_back = (U0,)
    signal = ((D0,), (V0,), (O,))
    input_back = ((), (), (U2, U1, D2, V2, V1))
    first_back = ()
    finish_output = (D1, G, U3, U0, D3, D0)
    last = (U2, O, V0, U3, V2, U1, G, S, D1, V1, O, U3)
    finish_grad = (D2,)
    taps_home = ()
    end = (S,)


VMEM_SPEC = pl.BlockSpec(memory_space=pltpu.VMEM)
ANY_SPEC = pl.BlockSpec(memory_space=pl.ANY)
GELU_SCALE = math.sqrt(2.0 / math.pi)
GELU_CUBE = 0.044715


def dot_nt(left, right):
    return lax.dot_general(left, right, (((1,), (1,)), ((), ())), preferred_element_type=F32)


def norm(values):
    center = jnp.mean(values, axis=-1, keepdims=True)
    shifted = values - center
    scale = lax.rsqrt(jnp.mean(shifted * shifted, axis=-1, keepdims=True) + EPSILON)
    return shifted * scale, scale


def norm_back(grad_rows, normed, scale, gain):
    scaled = grad_rows * gain
    plain = jnp.mean(scaled, axis=-1, keepdims=True)
    cross = jnp.mean(scaled * normed, axis=-1, keepdims=True)
    return scale * (scaled - plain - normed * cross)


class Part:
    def __init__(self, weight, piece, columns, dims, at):
        self.weight, self.piece, self.columns, self.at = weight, piece, columns, at
        self.dims = tuple(range(1 if weight in (UP, DOWN) else 0, dims))
        self.gather = tuple(phase(dims) for phase in GATHER_PHASES[at])
        self.reduce = tuple(phase(dims) for phase in REDUCE_PHASES[at])


def most(phases):
    return max(len(flips_of(step)) for step in phases)


class Plan:
    def __init__(self, sizes, tables):
        self.sizes = sizes
        here, channels, half = sizes.here, sizes.channels, sizes.half
        width = 2 * half
        self.width = width
        dims = 1 + len(bit_sizes(sizes.freq_count))
        self.dims = dims
        self.rows = rows = width // sizes.freq_count
        pieces = ((VALUE, sizes.groups, LANES), (GATE, 1, half), (OUT, 1, half), (UP, PIECES, half), (DOWN, PIECES, half))
        self.parts = []
        for weight, count, columns in pieces:
            for piece in range(count):
                self.parts.append(Part(weight, piece, columns, dims, len(self.parts)))
        self.spread = tuple(phase(dims) for phase in SPREAD_PHASES)
        groups = [self.spread] + [p.gather for p in self.parts] + [p.reduce for p in self.parts]
        self.partners = sorted(
            {flipped for phases in groups for step in phases for flipped in flips_of(step) if 0 in flipped}
        )

        def vmem(kind, *shape):
            return pltpu.VMEM(shape, kind)

        def sems(*shape):
            return pltpu.SemaphoreType.DMA(shape)

        def weights(bits):
            return [
                vmem(BF16, count, *(2,) * (bits + (weight not in (UP, DOWN))), rows, columns)
                for weight, count, columns in pieces
            ]

        def rows_of(kind, *lead):
            return vmem(kind, *lead, here, width)

        def turned(tokens):
            return vmem(BF16, width // (2 * rows), 2, rows, tokens)

        def turned_half(tokens):
            return vmem(BF16, width // (2 * rows), rows, tokens)

        def halves():
            return vmem(BF16, 2, here, half)

        def tiles():
            return vmem(BF16, PIECES, 2, 2 * here, half)

        def chunks():
            return vmem(BF16, sizes.groups, sizes.devices, sizes.chunk, LANES)

        def spectra(kind):
            return [vmem(kind, sizes.group_rows, 2 * LANES) for _ in range(sizes.groups)]

        def wide():
            return [vmem(F32, sizes.devices * sizes.chunk, LANES) for _ in range(sizes.groups)]

        taps = (sizes.tap_rows, sizes.groups, sizes.group, LANES)
        flat_taps = (sizes.tap_rows * channels, LANES)
        gain_rows = 2 * width // LANES + 4
        scratch = dict(
            x_buf=halves(),
            g_buf=vmem(BF16, 2, 2, here, half),
            gains=[[vmem(F32, half) for _ in range(2)] for _ in range(2)],
            lengths=vmem(jnp.int32, half),
            turned=vmem(F32, half, 8),
            weights=weights(dims - 1),
            grads=weights(dims - 2),
            landings=[
                [vmem(BF16, *shape) for shape in landing_shapes(part.reduce, part.dims[:-1], rows, part.columns)]
                for part in self.parts
            ],
            part_sems=[
                (sems(max(most(p.gather), most(p.reduce))), sems(slots(p.gather)), sems(slots(p.reduce)))
                for p in self.parts
            ],
            kernel_spec=spectra(F32),
            value_spec=spectra(F32),
            grad_spec=spectra(F32),
            inner_into=spectra(BF16),
            inner_from=spectra(F32),
            inner_taps=spectra(F32),
            wide_in=wide(),
            wide_out=wide(),
            taps=vmem(F32, *taps),
            tap_grad=vmem(BF16, sizes.tap_rows, -(-channels // 16) * 16, LANES),
            tap_land=vmem(BF16, sizes.freq_count, -(-channels // 16) * 16, LANES),
            tap_wide=vmem(F32, *flat_taps),
            sent=chunks(),
            sent_back=chunks(),
            landed=[chunks() for _ in range(4)],
            move_sems=[[sems(2) for _ in range(sizes.groups)] for _ in range(4)],
            tap_sems=[sems(2) for _ in range(2)],
            normed1=rows_of(F32),
            gate=rows_of(F32),
            mixed=rows_of(F32),
            residual=rows_of(F32),
            normed2=rows_of(F32),
            grad_res=rows_of(F32),
            rows=rows_of(F32),
            out_sum=rows_of(F32, 2),
            in2_sum=rows_of(F32),
            scale1=vmem(F32, here, 1),
            scale2=vmem(F32, here, 1),
            input1=rows_of(BF16),
            branch_rows=rows_of(BF16),
            in2_send=rows_of(BF16),
            in2_land=rows_of(BF16),
            input2=rows_of(BF16, 2),
            grad_rows=rows_of(BF16, 2),
            t_input1=(turned(here), turned_half(here)),
            t_branch=(turned(here), turned_half(here)),
            t_input2=(turned(2 * here), turned_half(2 * here)),
            t_grad=(turned(2 * here), turned_half(2 * here)),
            inner_rows=(halves(), halves()),
            signal_rows=[vmem(BF16, sizes.groups, here, 2 * LANES) for _ in range(2)],
            gate_rows=(halves(), halves()),
            tiles=(tiles(), tiles()),
            slopes=vmem(F32, PIECES, 2 * here, half),
            tile_sems=sems(2, 2, PIECES),
            twin_sems=sems(2, 6 + sizes.groups),
            gain_total=vmem(F32, len(self.spread) + 1, gain_rows, LANES),
            gain_land=vmem(F32, slots(self.spread), gain_rows, LANES),
            gain_sems=(sems(most(self.spread)), sems(slots(self.spread))),
            out_send=halves(),
            out_land=halves(),
            gin_send=vmem(BF16, here, half),
            gin_land=vmem(BF16, here, half),
            swap_sems=sems(2, 12),
            local=sems(13 + len(self.parts)),
            tables=[vmem(table.dtype, *table.shape) for table in tables],
        )
        self.scratch, self.tree = jax.tree.flatten(
            scratch, is_leaf=lambda leaf: not isinstance(leaf, (dict, list, tuple))
        )


def row_tiles(count, body, first=0, tile=64):
    def one(step, carry):
        body(pl.ds(pl.multiple_of(first + step * tile, tile), tile))
        return carry

    lax.fori_loop(0, count // tile, one, 0)


def block_kernel(plan, tokens, cotangent, first_gain, second_gain, lengths, raw_kernel, *refs):
    shards, refs = refs[:5], refs[5:]
    tables = refs[:7]
    output, grad_input, *weight_grads = refs[7:14]
    gain_sums, grad_kernel = refs[14:16]
    k = types.SimpleNamespace(**jax.tree.unflatten(plan.tree, refs[16:]))
    into, outof, taps_into, taps_outof, turn, ahead, behind = k.tables
    sizes = plan.sizes
    here, half, width, channels = sizes.here, sizes.half, plan.width, sizes.channels
    place = Place(sizes.freq_count)
    chan, core = place.chan, place.core
    twin = place.other((plan.dims - 1,))
    across = place.other((0,))
    me = chan * sizes.freq_count + place.freq

    def whole(weight, *lead, lanes=slice(None)):
        value = k.weights[weight][lead + (slice(None),) * plan.dims + (lanes,)]
        return value.reshape(width, value.shape[-1])

    def of_group(group):
        return slice(group * LANES, (group + 1) * LANES)

    def both_halves(weight, *lead, lanes=slice(None)):
        return jnp.concatenate([whole(weight, *lead, c, lanes=lanes) for c in range(2)], axis=1)

    def of_chan(values):
        return jnp.where(chan == 0, values[:, :half], values[:, half:])

    def of_other_chan(values):
        return jnp.where(chan == 0, values[:, half:], values[:, :half])

    own = []
    for part in plan.parts:
        source = shards[part.weight].at[:, pl.ds(part.piece * part.columns, part.columns)]
        target = k.weights[part.weight].at[(part.piece,) + tuple(place.coords[dim] for dim in part.dims)]
        own.append(pltpu.make_async_copy(source, target, k.local.at[part.at]))
    for source, target in (
        (tokens.at[chan], k.x_buf.at[chan]),
        (cotangent, k.g_buf.at[chan]),
        (raw_kernel.at[:, place.freq], k.taps.at[place.freq]),
        (first_gain, k.gains[0][0]),
        (second_gain, k.gains[0][1]),
        (lengths, k.lengths),
    ):
        own.append(pltpu.make_async_copy(source, target, k.local.at[len(own)]))
    for source, target in zip(tables, k.tables):
        own.append(pltpu.make_async_copy(source, target, k.local.at[len(own)]))
    for copy in own:
        copy.start()
    own_tokens, own_cotangent, own_taps, *own_rows = own[len(plan.parts) :]
    own_tables, own_rows = own_rows[3:], own_rows[:3]
    barrier = pltpu.get_barrier_semaphore()
    for flipped in plan.partners:
        pl.semaphore_signal(barrier, inc=1, device_id=place.other(flipped), device_id_type=MESH)

    def greet(step, carry):
        peer = (lax.rem(place.freq + step, sizes.freq_count), chan)
        pl.semaphore_signal(barrier, inc=1, device_id=peer, device_id_type=MESH)
        return carry

    lax.fori_loop(1, sizes.freq_count, greet, 0, unroll=True)
    pl.semaphore_wait(barrier, len(plan.partners) + sizes.freq_count - 1)

    def swap(at, source, target):
        copy = remote(source, target, k.swap_sems.at[0, at], k.swap_sems.at[1, at], across)
        copy.start()
        return copy

    moving = {}
    for part in plan.parts:
        moving[part.at] = Gather(
            place,
            k.weights[part.weight].at[part.piece],
            part.dims,
            part.gather,
            k.part_sems[part.at][0],
            k.part_sems[part.at][1],
            own[part.at].wait,
        )

    def ahead_of(names):
        for name in names:
            moving[name].go()

    def all_to_all(move, group, source):
        target = k.landed[move]
        exchange = Exchange(
            sizes.devices,
            me,
            lambda other: (lax.rem(other, sizes.freq_count), other // sizes.freq_count),
            lambda other: source.at[group, other],
            lambda other: target.at[group, other],
            source.at[group, pl.ds(0, sizes.devices - 1)],
            target.at[group, pl.ds(0, sizes.devices - 1)],
            k.move_sems[move][group],
        )
        exchange.start()
        target[group, me] = source[group, me]
        return exchange

    swap_tokens = swap(0, tokens.at[1 - chan], k.x_buf.at[chan])
    swap_gains = [swap(at, ref, k.gains[1][at - 9]) for at, ref in ((9, first_gain), (10, second_gain))]
    for group in range(sizes.groups):
        moving[V0 + group].go()
    others = sizes.freq_count - 1

    def begin(exchange):
        exchange.start()
        return exchange

    tap_move = Exchange(
        sizes.freq_count,
        place.freq,
        lambda other: (other, chan),
        lambda other: raw_kernel.at[:, other],
        lambda other: k.taps.at[other],
        raw_kernel.at[:, pl.ds(0, others)],
        k.taps.at[pl.ds(0, others)],
        k.tap_sems[0],
    )
    moving[T] = Once(lambda: begin(tap_move))
    moving[C] = Once(lambda: swap(2, cotangent, k.g_buf.at[chan]))
    ahead_of(Order.tokens)
    swap_tokens.wait()
    own_tokens.wait()
    for copy in swap_gains + own_rows:
        copy.wait()

    def gain_row(row):
        near, far = k.gains[0][row][...][None], k.gains[1][row][...][None]
        return jnp.concatenate([jnp.where(chan == 0, near, far), jnp.where(chan == 0, far, near)], axis=1)

    first_gain, second_gain = gain_row(0), gain_row(1)

    def first_norm(at):
        rows = jnp.concatenate([k.x_buf[0, at, :], k.x_buf[1, at, :]], axis=1).astype(F32)
        normed, scale = norm(rows)
        k.normed1[at, :] = normed
        k.scale1[at, :] = scale
        k.input1[at, :] = (normed * first_gain).astype(BF16)

    ahead_of(Order.norm)
    row_tiles(here, first_norm)

    def turn_rows(source, target, columns=slice(None)):
        turned = source[...].astype(F32).T.astype(BF16)
        target[:, :, :, columns] = turned.reshape(target.shape[:-1] + (here,))

    arriving = {}

    def share(at, source, target):
        copy = remote(source, target, k.twin_sems.at[0, at], k.twin_sems.at[1, at], twin)
        copy.start()
        arriving[at] = copy

    def share_turned(at, pair):
        share(at, pair[0].at[:, 1 - core], pair[1])

    def need(at):
        if arriving[at] is not None:
            arriving[at].wait()
            arriving[at] = None

    turn_rows(k.input1, k.t_input1[0])
    share_turned(0, k.t_input1)

    def send_chunks(move, group, source, halves):
        for c in range(2):
            devices = pl.ds(c * sizes.freq_count, sizes.freq_count)
            to_chunks(sizes, halves[c], source.at[group, devices])
        return all_to_all(move, group, source)

    moves = []
    for group in range(sizes.groups):
        ahead_of(Order.w_value[group])
        moving[V0 + group].finish()
        ahead_of(Order.value[group])
        got = dot(k.input1[...], both_halves(VALUE, group))
        moves.append(send_chunks(0, group, k.sent, (got[:, :LANES], got[:, LANES:])))
    ahead_of(Order.sent)
    ahead_of(Order.taps)
    moving[T].finish()
    for copy in own_tables:
        copy.wait()
    own_taps.wait()
    k.turned[...] = jnp.broadcast_to(k.lengths[...].astype(F32)[None], (8, half)).T
    lives = [
        k.turned[pl.ds(pl.multiple_of(group * LANES + place.freq * sizes.group, 8), sizes.group), 0:1]
        for group in range(sizes.groups)
    ]
    flat_taps = (sizes.tap_rows, channels, LANES)
    live = live_mask(flat_taps, jnp.concatenate(lives, axis=0))
    pooled = pooled_taps(k.taps[...].reshape(flat_taps))
    shrunk = (pooled - THRESH * jnp.tanh(pooled / THRESH)) * live
    k.tap_wide[...] = shrunk.reshape(sizes.tap_rows * channels, LANES)
    ahead_of(Order.kernel)

    def tap_load(group):
        return lambda c: k.tap_wide[pl.ds(group * sizes.group + c, sizes.tap_rows, stride=channels), :]

    for group in range(sizes.groups):
        spectrum_into(
            sizes, tap_load(group), taps_into, turn, ahead, k.inner_into[group], k.kernel_spec[group]
        )

    def spectrum_of(move, group, spectra):
        flat = (sizes.devices * sizes.chunk, LANES)
        k.wide_in[group][...] = k.landed[move][group].astype(F32).reshape(flat)
        spectrum_into(
            sizes, chunk_loader(sizes, k.wide_in[group]), into, turn, ahead, k.inner_into[group], spectra[group]
        )

    def chunks_from(group, product):
        signal_from(
            sizes, product, outof, turn, behind, k.inner_from[group], chunk_storer(sizes, k.wide_out[group])
        )
        k.sent_back[group] = k.wide_out[group][...].reshape(k.sent_back.shape[1:]).astype(BF16)

    moves_back = []
    for group in range(sizes.groups):
        ahead_of(Order.arrive[group])
        moves[group].wait()
        ahead_of(Order.conv[group])
        spectrum_of(0, group, k.value_spec)
        chunks_from(group, times(k.value_spec[group][...], k.kernel_spec[group][...], False))
        moves_back.append(all_to_all(1, group, k.sent_back))
    ahead_of(Order.convolved)
    ahead_of(Order.cotangent)
    moving[C].finish()
    own_cotangent.wait()
    ahead_of(Order.turn)
    for which, seq in ((0, chan), (1, 1 - chan)):
        k.grad_rows[which] = jnp.concatenate([k.g_buf[0, seq], k.g_buf[1, seq]], axis=1)
        turn_rows(k.grad_rows.at[which], k.t_grad[0], slice(which * here, (which + 1) * here))
    share_turned(2, k.t_grad)
    ahead_of(Order.w_gate)
    moving[G].finish()
    ahead_of(Order.gate)
    for c in range(2):
        k.gate[:, c * half : (c + 1) * half] = dot(k.input1[...], whole(GATE, 0, c))
    for group in range(sizes.groups):
        ahead_of(Order.mixed[group])
        moves_back[group].wait()
        for c, tokens_at, rows in from_chunks(sizes, k.landed[1].at[group]):
            k.mixed[tokens_at, c * half + group * LANES : c * half + (group + 1) * LANES] = rows
    ahead_of(Order.inner)

    def make_inner(at):
        gate = k.gate[at, :]
        inner = (k.mixed[at, :] * (gate * jax.nn.sigmoid(gate))).astype(BF16)
        k.inner_rows[0][0, at, :] = inner[:, :half]
        k.inner_rows[0][1, at, :] = inner[:, half:]

    row_tiles(here, make_inner)
    share(4, *k.inner_rows)
    ahead_of(Order.w_out)
    moving[O].finish()
    ahead_of(Order.residual)
    k.residual[...] = dot_nt(k.inner_rows[0][0], whole(OUT, 0, 0)) + dot_nt(
        k.inner_rows[0][1], whole(OUT, 0, 1)
    )

    def second_norm(at):
        rows = jnp.concatenate([k.x_buf[0, at, :], k.x_buf[1, at, :]], axis=1).astype(F32)
        residual = k.residual[at, :] + rows
        normed, scale = norm(residual)
        k.residual[at, :] = residual
        k.normed2[at, :] = normed
        k.scale2[at, :] = scale
        k.input2[0, at, :] = (normed * second_gain).astype(BF16)

    row_tiles(here, second_norm)
    blocks = [pl.ds(at * (here // 2), here // 2) for at in range(2)]
    swap_input2 = [swap(3 + at, k.input2.at[0, rows], k.input2.at[1, rows]) for at, rows in enumerate(blocks)]
    ahead_of(Order.turn_near)
    turn_rows(k.input2.at[0], k.t_input2[0], slice(0, here))

    def product(left, right, pick):
        mine, theirs = left[0][:, core], left[1][...]
        shape = (width // 2, mine.shape[-1])
        got = dot(
            jnp.concatenate([mine.reshape(shape), theirs.reshape(shape)], axis=1),
            jnp.concatenate([right[0][pick], right[1][pick]], axis=0),
        ).astype(BF16)
        return got.reshape((2,) * (plan.dims - 2) + (plan.rows, got.shape[-1]))

    factors = {
        VALUE: (k.t_input1, 0, k.signal_rows, 6),
        GATE: (k.t_input1, 0, k.gate_rows, 5),
        OUT: (k.t_branch, 3, k.inner_rows, 4),
        UP: (k.t_input2, 1, k.tiles, None),
        DOWN: (k.t_grad, 2, k.tiles, None),
    }

    def prepare(part):
        left, left_share, right, right_share = factors[part.weight]
        need(left_share)
        total = k.grads[part.weight]
        if part.weight == VALUE:
            need(right_share + part.piece)
            got = product(left, right, part.piece)
            for c in range(2):
                total[part.piece, c] = got[..., of_group(c)]
        elif part.weight in (GATE, OUT):
            need(right_share)
            for c in range(2):
                total[part.piece, c] = product(left, right, c)
        else:
            kind = HID if part.weight == UP else ACT
            tile_copy(kind, part.piece).wait()
            total[part.piece] = product(left, right, (part.piece, kind))

    def begin_reducing(part):
        moving[part.at] = Reduce(
            place,
            k.grads[part.weight].at[part.piece],
            k.landings[part.at],
            part.dims[:-1],
            part.reduce,
            k.part_sems[part.at][0],
            k.part_sems[part.at][2],
            weight_grads[part.weight].at[:, pl.ds(part.piece * part.columns, part.columns)],
            functools.partial(prepare, part),
        )
    def start_reducing():
        for name, mover in list(moving.items()):
            if isinstance(mover, Gather):
                mover.finish()
        for part in plan.parts:
            begin_reducing(part)

    def up_part(which, piece, first, count):
        rows = pl.ds(first, count)
        stored = pl.ds(which * here + first, count)
        hidden = dot(k.input2[which, rows, :], whole(UP, piece))
        square = hidden * hidden
        bent = jnp.tanh(GELU_SCALE * hidden * (1.0 + GELU_CUBE * square))
        k.tiles[0][piece, ACT, stored, :] = (0.5 * hidden * (1.0 + bent)).astype(BF16)
        k.slopes[piece, stored, :] = 0.5 * (1.0 + bent) + (0.5 * GELU_SCALE) * hidden * (1.0 - bent * bent) * (
            1.0 + 3.0 * GELU_CUBE * square
        )

    def grad_part(which, piece, first, count):
        stored = pl.ds(which * here + first, count)
        grad = dot(k.grad_rows[which, pl.ds(first, count), :], whole(DOWN, piece)) * k.slopes[piece, stored, :]
        k.tiles[0][piece, HID, stored, :] = grad.astype(BF16)

    def in2_part(which, first, count, side):
        rows = pl.ds(which * here + first, count)
        return sum(
            dot_nt(k.tiles[0][piece, HID, rows, :], k.weights[UP][piece, side].reshape(half, half))
            for piece in range(PIECES)
        )

    def out_part(which, side):
        rows = pl.ds(which * here, here)
        return sum(
            dot_nt(k.tiles[0][piece, ACT, rows, :], k.weights[DOWN][piece, side].reshape(half, half))
            for piece in range(PIECES)
        )

    def tile_copy(kind, piece):
        return remote(
            k.tiles[0].at[piece, kind],
            k.tiles[1].at[piece, kind],
            k.tile_sems.at[0, kind, piece],
            k.tile_sems.at[1, kind, piece],
            twin,
        )

    for piece in range(PIECES):
        ahead_of(Order.w_up[piece])
        moving[U0 + piece].finish()
        ahead_of(Order.near_up[piece])
        up_part(0, piece, 0, here)
    swap_in2 = []

    def return_far(at):
        back = []
        for side in range(2):
            index = (blocks[at], pl.ds(side * half, half))
            k.in2_send[index] = in2_part(1, at * (here // 2), here // 2, side).astype(BF16)
            back.append(swap(5 + 2 * at + side, k.in2_send.at[index], k.in2_land.at[index]))
        swap_in2.append(back)

    for at in range(2):
        ahead_of(Order.wait_far[at])
        swap_input2[at].wait()
        ahead_of(Order.far_up[at])
        for piece in range(PIECES):
            up_part(1, piece, at * (here // 2), here // 2)
            if at:
                tile_copy(ACT, piece).start()
        if at:
            start_reducing()
            ahead_of(Order.far_b)
        for piece in range(PIECES):
            if not at:
                ahead_of(Order.down_a[piece])
                moving[D0 + piece].finish()
                ahead_of(Order.far_a[piece])
            grad_part(1, piece, at * (here // 2), here // 2)
        return_far(at)
    ahead_of(Order.near_down)
    for piece in range(PIECES):
        grad_part(0, piece, 0, here)
        tile_copy(HID, piece).start()
    for side in range(2):
        k.in2_sum[:, side * half : (side + 1) * half] = in2_part(0, 0, here, side)
    turn_rows(k.input2.at[1], k.t_input2[0], slice(here, 2 * here))
    share_turned(1, k.t_input2)

    k.gain_total[0] = jnp.zeros_like(k.gain_total[0])

    def add_gain(row, sums):
        for at in range(width // LANES):
            base = row * (width // LANES) + at
            k.gain_total[0, base : base + 1, :] += sums[:, at * LANES : (at + 1) * LANES]

    def second_back(at):
        grad = k.in2_sum[at, :] + k.in2_land[at, :].astype(F32)
        normed = k.normed2[at, :]
        add_gain(1, jnp.sum(grad * normed, axis=0, keepdims=True))
        result = k.grad_rows[0, at, :].astype(F32) + norm_back(
            grad, normed, k.scale2[at, :], second_gain
        )
        k.grad_res[at, :] = result
        k.branch_rows[at, :] = result.astype(BF16)

    for at in range(2):
        ahead_of(Order.far_back[at])
        for copy in swap_in2[at]:
            copy.wait()
        row_tiles(here // 2, second_back, at * (here // 2))
    ahead_of(Order.norm_back)
    moves = []
    for group in range(sizes.groups):
        got = dot(k.branch_rows[...], both_halves(OUT, 0, lanes=of_group(group)))
        grad_mixed = []
        for c in range(2):
            columns = slice(c * half + group * LANES, c * half + (group + 1) * LANES)
            gate, grad = k.gate[:, columns], got[:, of_group(c)]
            sig = jax.nn.sigmoid(gate)
            k.gate_rows[0][c, :, of_group(group)] = (
                grad * k.mixed[:, columns] * (sig * (1.0 + gate * (1.0 - sig)))
            ).astype(BF16)
            grad_mixed.append(grad * (gate * sig))
        moves.append(send_chunks(2, group, k.sent, grad_mixed))
    share(5, *k.gate_rows)
    turn_rows(k.branch_rows, k.t_branch[0])
    share_turned(3, k.t_branch)
    ahead_of(Order.sent_back)
    ahead_of(Order.output)
    for which in range(2):
        for side in range(2):
            k.out_sum[which, :, side * half : (side + 1) * half] = out_part(which, side)

    def make_output(at):
        near = k.residual[at, :] + k.out_sum[0, at, :]
        far = k.out_sum[1, at, :]
        k.out_send[0, at, :] = of_other_chan(near).astype(BF16)
        k.out_send[1, at, :] = of_other_chan(far).astype(BF16)

    row_tiles(here, make_output)
    moving[W] = Once(lambda: swap(1, k.out_send, k.out_land))

    moves_back = []
    for group in range(sizes.groups):
        ahead_of(Order.arrive_back[group])
        moves[group].wait()
        ahead_of(Order.conv_back[group])
        spectrum_of(2, group, k.grad_spec)
        chunks_from(group, times(k.grad_spec[group][...], k.kernel_spec[group][...], True))
        moves_back.append(all_to_all(3, group, k.sent_back))
    ahead_of(Order.convolved_back)

    def tap_store(group):
        def store(channel, values):
            k.tap_wide[pl.ds(group * sizes.group + channel, sizes.tap_rows, stride=channels), :] = values

        return store

    ahead_of(Order.taps_back)
    for group in range(sizes.groups):
        signal_from(
            sizes,
            times(k.grad_spec[group][...], k.value_spec[group][...], True),
            taps_outof, turn, behind, k.inner_taps[group], tap_store(group),
        )
    pooled = pooled_taps(k.taps[...].reshape(flat_taps))
    bent = jnp.tanh(pooled / THRESH)
    tap_grads = pooled_taps(k.tap_wide[...].reshape(pooled.shape) * live * bent * bent)
    filling = jnp.zeros((sizes.tap_rows, k.tap_grad.shape[1] - channels, LANES), F32)
    k.tap_grad[...] = jnp.concatenate([tap_grads, filling], axis=1).astype(BF16)
    tap_back = Exchange(
        sizes.freq_count,
        place.freq,
        lambda other: (other, chan),
        lambda other: k.tap_grad.at[other],
        lambda other: k.tap_land.at[other],
        k.tap_grad.at[pl.ds(0, others)],
        k.tap_land.at[pl.ds(0, others)],
        k.tap_sems[1],
    )
    tap_back.start()
    k.tap_land[place.freq] = k.tap_grad[place.freq]

    k.rows[...] = dot_nt(k.gate_rows[0][0], whole(GATE, 0, 0)) + dot_nt(k.gate_rows[0][1], whole(GATE, 0, 1))
    for group in range(sizes.groups):
        ahead_of(Order.signal[group])
        moves_back[group].wait()
        for c, tokens_at, rows in from_chunks(sizes, k.landed[3].at[group]):
            k.signal_rows[0][group, tokens_at, of_group(c)] = rows.astype(BF16)
        share(6 + group, k.signal_rows[0].at[group], k.signal_rows[1].at[group])
        ahead_of(Order.input_back[group])
        k.rows[...] += dot_nt(k.signal_rows[0][group], both_halves(VALUE, group))
    ahead_of(Order.first_back)

    def first_back(at):
        grad = k.rows[at, :]
        normed = k.normed1[at, :]
        add_gain(0, jnp.sum(grad * normed, axis=0, keepdims=True))
        result = k.grad_res[at, :] + norm_back(grad, normed, k.scale1[at, :], first_gain)
        k.gin_send[at, :] = of_other_chan(result).astype(BF16)
        grad_input[chan, at, :] = of_chan(result)

    row_tiles(here, first_back)
    swap_gin = swap(11, k.gin_send, k.gin_land)
    spread = Spread(place, k.gain_total, k.gain_land, plan.spread, *k.gain_sems)
    moving[S] = spread
    spread.go()
    ahead_of(Order.finish_output)
    moving[W].finish()

    def finish_output(at):
        near = of_chan(k.residual[at, :] + k.out_sum[0, at, :]) + k.out_land[1, at, :].astype(F32)
        far = of_chan(k.out_sum[1, at, :]) + k.out_land[0, at, :].astype(F32)
        output[chan, at, :] = near.astype(BF16)
        output[1 - chan, at, :] = far.astype(BF16)

    row_tiles(here, finish_output)
    ahead_of(Order.last)
    swap_gin.wait()
    ahead_of(Order.finish_grad)
    grad_input[1 - chan] = k.gin_land[...].astype(F32)
    ahead_of(Order.taps_home)
    tap_back.wait()
    for group in range(sizes.groups):
        rows = slice(group * sizes.group, (group + 1) * sizes.group)
        grad_kernel[group] = k.tap_land[...].astype(F32)[:, rows]
    ahead_of(Order.end)
    for mover in moving.values():
        if not isinstance(mover, Once):
            mover.finish()
    gain_sums[...] = k.gain_total[len(plan.spread)]


def settle_kernel(count, channels, freq_count, *refs):
    sources, sums, refs = refs[:count], refs[count], refs[count + 1 :]
    targets, gains, sems = refs[: count + 2], refs[count + 2 : count + 4], refs[-1]
    going = [pltpu.make_async_copy(sources[n], targets[n], sems.at[n]) for n in range(count)]
    for copy in going:
        copy.start()
    tiles = 2 * channels * freq_count // LANES
    mine = (lax.axis_index("chan") * freq_count + lax.axis_index("freq")) * channels
    lane = lax.broadcasted_iota(jnp.int32, (channels, LANES), 1)
    feature = mine + lax.broadcasted_iota(jnp.int32, (channels, LANES), 0)
    for row, gain in enumerate(gains):
        total = jnp.zeros((channels, LANES), F32)
        for tile in range(tiles):
            at = row * tiles + tile
            total = total + jnp.where(lane + tile * LANES == feature, sums[at : at + 1, :], 0.0)
        gain[...] = jnp.sum(total.T, axis=0, keepdims=True)
        going.append(pltpu.make_async_copy(gain, targets[count + row], sems.at[count + row]))
        going[-1].start()
    for copy in going:
        copy.wait()


def settle(arrays, sums, sizes):
    gain = (1, sizes.channels)
    out = [jax.ShapeDtypeStruct(a.shape, a.dtype) for a in arrays] + [jax.ShapeDtypeStruct(gain, F32)] * 2
    return pl.pallas_call(
        functools.partial(settle_kernel, len(arrays), sizes.channels, sizes.freq_count),
        out_shape=out,
        in_specs=[VMEM_SPEC] * (len(arrays) + 1),
        out_specs=[ANY_SPEC] * len(out),
        scratch_shapes=[pltpu.VMEM(gain, F32)] * 2 + [pltpu.SemaphoreType.DMA((len(out),))],
        name="settle",
    )(*arrays, sums)


def one_sequence(
    tokens, cotangent, first_gain, second_gain, w_value, w_gate, w_out, w_up, w_down, raw_kernel, lengths
):
    freq_count = lax.axis_size("freq")
    _, here, half = tokens.shape
    sizes = Sizes(freq_count, here, half, raw_kernel.shape[1] * freq_count)
    tables = conv_tables(sizes)
    plan = Plan(sizes, tables)
    shards = (w_value, w_gate, w_out, w_up, w_down)
    out_shape = (
        [pltpu.VMEM((2, here, half), BF16), pltpu.VMEM((2, here, half), F32)]
        + [pltpu.VMEM(w.shape, F32) for w in shards]
        + [
            pltpu.VMEM((4 * half // LANES + 4, LANES), F32),
            pltpu.VMEM((sizes.groups, freq_count, sizes.group, LANES), F32),
        ]
    )
    results = pl.pallas_call(
        functools.partial(block_kernel, plan),
        out_shape=out_shape,
        in_specs=[ANY_SPEC] * (11 + len(tables)),
        out_specs=[VMEM_SPEC] * len(out_shape),
        scratch_shapes=plan.scratch,
        compiler_params=pltpu.CompilerParams(
            collective_id=0, has_side_effects=True, vmem_limit_bytes=60 << 20
        ),
        name="block",
    )(
        tokens,
        cotangent,
        first_gain,
        second_gain,
        lengths,
        raw_kernel.reshape(sizes.groups, freq_count, sizes.group, LANES),
        *shards,
        *tables,
    )
    results = [pltpu.with_memory_space_constraint(result, pltpu.VMEM) for result in results]
    *arrays, gain_sums, grad_kernel = results
    *arrays, grad_kernel, first_grad, second_grad = settle([*arrays, grad_kernel], gain_sums, sizes)
    return (*arrays, first_grad.T, second_grad.T, grad_kernel.reshape(raw_kernel.shape))


def fits(mesh):
    freq_count = mesh.shape["freq"]
    return lambda tokens, w_value, w_up, raw_kernel: (
        mesh.shape["chan"] == 2
        and tokens.shape[0] == 2
        and freq_count == 16
        and w_value.shape[1] == 6 * LANES
        and w_value.shape[0] % (16 * freq_count) == 0
        and w_value.shape[1] % (16 * freq_count) == 0
        and w_value.shape[1] % 256 == 0
        and w_up.shape[1] == PIECES * w_value.shape[1]
        and tokens.shape[1] % (2 * LANES * freq_count) == 0
        and raw_kernel.shape[1] == LANES * freq_count
        and (tokens.shape[1] + raw_kernel.shape[1]) // LANES % 16 == 0
    )


D = 768
SEQ_MB = 1
MICRO = 2


HIGHEST = lax.Precision.HIGHEST


def circle(height, breadth, period):
    first_index = lax.broadcasted_iota(jnp.int32, (height, breadth), 0)
    second_index = lax.broadcasted_iota(jnp.int32, (height, breadth), 1)
    phase_angle = (first_index * second_index % period).astype(jnp.float32) * (
        2.0 * math.pi / period
    )
    return (jnp.cos(phase_angle), jnp.sin(phase_angle))


def make_tables(padded_size):
    inner_size = 128
    outer_size = padded_size // inner_size
    outer_cos, outer_sin = circle(outer_size, outer_size, outer_size)
    inner_cos, inner_sin = circle(inner_size, inner_size, inner_size)
    twist_cos, twist_sin = circle(outer_size, inner_size, padded_size)
    return (outer_cos, outer_sin, inner_cos, inner_sin, twist_cos, twist_sin)


def spectrum(signal, padded_size, tables):
    outer_cos, outer_sin, inner_cos, inner_sin, twist_cos, twist_sin = tables
    inner_size = inner_cos.shape[0]
    pad_width = [(0, 0)] * (signal.ndim - 1) + [(0, padded_size - signal.shape[-1])]
    grid_values = jnp.pad(signal, pad_width).reshape(
        signal.shape[:-1] + (padded_size // inner_size, inner_size)
    )
    part_real = jnp.einsum("...ab,fa->...fb", grid_values, outer_cos, precision=HIGHEST)
    part_imag = -jnp.einsum("...ab,fa->...fb", grid_values, outer_sin, precision=HIGHEST)
    turned_real = part_real * twist_cos + part_imag * twist_sin
    turned_imag = part_imag * twist_cos - part_real * twist_sin
    spec_real = jnp.einsum(
        "...fb,bg->...fg", turned_real, inner_cos, precision=HIGHEST
    ) + jnp.einsum("...fb,bg->...fg", turned_imag, inner_sin, precision=HIGHEST)
    spec_imag = jnp.einsum(
        "...fb,bg->...fg", turned_imag, inner_cos, precision=HIGHEST
    ) - jnp.einsum("...fb,bg->...fg", turned_real, inner_sin, precision=HIGHEST)
    return (spec_real, spec_imag)


def signal_of(spec_real, spec_imag, keep_count, tables):
    outer_cos, outer_sin, inner_cos, inner_sin, twist_cos, twist_sin = tables
    padded_size = spec_real.shape[-1] * spec_real.shape[-2]
    back_real = jnp.einsum("...fg,bg->...fb", spec_real, inner_cos, precision=HIGHEST) - jnp.einsum(
        "...fg,bg->...fb", spec_imag, inner_sin, precision=HIGHEST
    )
    back_imag = jnp.einsum("...fg,bg->...fb", spec_imag, inner_cos, precision=HIGHEST) + jnp.einsum(
        "...fg,bg->...fb", spec_real, inner_sin, precision=HIGHEST
    )
    turned_real = back_real * twist_cos - back_imag * twist_sin
    turned_imag = back_imag * twist_cos + back_real * twist_sin
    grid_values = (
        jnp.einsum("...fb,af->...ab", turned_real, outer_cos, precision=HIGHEST)
        - jnp.einsum("...fb,af->...ab", turned_imag, outer_sin, precision=HIGHEST)
    ) / padded_size
    flat_values = grid_values.reshape(grid_values.shape[:-2] + (padded_size,))
    return flat_values[..., :keep_count]


def shape_kernel(raw_taps, live_taps):
    padded = jnp.pad(raw_taps, ((0, 0), (1, 1)))
    pooled = (padded[:, :-2] + padded[:, 1:-1] + padded[:, 2:]) / 3.0
    return (pooled - THRESH * jnp.tanh(pooled / THRESH)) * live_taps


def row_norm(values):
    row_width = values.shape[-1] * lax.axis_size("chan")
    row_total, row_square = lax.psum(
        (jnp.sum(values, axis=-1), jnp.sum(values * values, axis=-1)), "chan"
    )
    center = row_total / row_width
    spread = row_square / row_width - center * center
    scale = lax.rsqrt(spread + EPSILON)[..., None]
    return ((values - center[..., None]) * scale, scale)


def row_back(grad_rows, normed, scale, gain_row):
    row_width = grad_rows.shape[-1] * lax.axis_size("chan")
    scaled = grad_rows * gain_row
    sum_plain, sum_cross = lax.psum(
        (jnp.sum(scaled, axis=-1), jnp.sum(scaled * normed, axis=-1)), "chan"
    )
    return scale * (
        scaled - sum_plain[..., None] / row_width - normed * sum_cross[..., None] / row_width
    )


def features(values):
    return lax.all_gather(values, "chan", axis=2, tiled=True)


def partial_sum(values):
    return lax.psum_scatter(
        values.astype(jnp.bfloat16), "chan", scatter_dimension=2, tiled=True
    ).astype(jnp.float32)


def to_channels(values):
    return lax.all_to_all(
        jnp.swapaxes(values, 1, 2), "freq", split_axis=1, concat_axis=2, tiled=True
    )


def to_tokens(values):
    arrived = lax.all_to_all(values, "freq", split_axis=2, concat_axis=1, tiled=True)
    return jnp.swapaxes(arrived, 1, 2)


def by_features(
    tokens,
    cotangent,
    first_gain,
    second_gain,
    w_value,
    w_gate,
    w_out,
    w_up,
    w_down,
    raw_kernel,
    lengths,
):
    full_value, full_gate, full_out, full_up, full_down = (
        lax.all_gather(w_value, "freq", axis=0, tiled=True),
        lax.all_gather(w_gate, "freq", axis=0, tiled=True),
        lax.all_gather(w_out, "freq", axis=0, tiled=True),
        lax.all_gather(w_up, "freq", axis=0, tiled=True),
        lax.all_gather(w_down, "freq", axis=0, tiled=True),
    )
    freq_count = lax.axis_size("freq")
    chan_width = tokens.shape[2]
    channels = chan_width // freq_count
    seq_length = tokens.shape[1] * freq_count
    padded_size = 2 * seq_length
    tables = make_tables(padded_size)
    kernel_rows = lax.all_to_all(raw_kernel, "freq", split_axis=0, concat_axis=1, tiled=True)
    tap_count = kernel_rows.shape[1]
    my_lengths = lax.dynamic_slice_in_dim(lengths, lax.axis_index("freq") * channels, channels)
    tap_index = lax.broadcasted_iota(jnp.int32, (channels, tap_count), 1)
    live_taps = (tap_index < my_lengths[:, None]).astype(jnp.float32)
    kernel, kernel_pull = jax.vjp(functools.partial(shape_kernel, live_taps=live_taps), kernel_rows)
    kernel_real, kernel_imag = spectrum(kernel, padded_size, tables)
    hidden_width = full_up.shape[1]
    shard_factor = 1
    totals = (
        jnp.zeros((D // shard_factor, chan_width), jnp.float32),
        jnp.zeros((D // shard_factor, chan_width), jnp.float32),
        jnp.zeros((D // shard_factor, chan_width), jnp.float32),
        jnp.zeros((D // shard_factor, hidden_width), jnp.float32),
        jnp.zeros((D // shard_factor, hidden_width), jnp.float32),
        jnp.zeros((chan_width // shard_factor, 1), jnp.float32),
        jnp.zeros((chan_width // shard_factor, 1), jnp.float32),
    )
    kernel_grad = jnp.zeros((channels, tap_count), jnp.float32)
    outputs = []
    input_grads = []
    for micro_index in range(MICRO):
        rows_here = tokens[micro_index * SEQ_MB : (micro_index + 1) * SEQ_MB].astype(jnp.float32)
        first_normed, first_scale = row_norm(rows_here)
        input1 = features((first_normed * first_gain).astype(jnp.bfloat16))
        value_low = jnp.einsum(
            "bld,de->ble", input1, full_value, preferred_element_type=jnp.float32
        ).astype(jnp.bfloat16)
        gate_proj = jnp.einsum("bld,de->ble", input1, full_gate, preferred_element_type=jnp.float32)
        signal = to_channels(value_low).astype(jnp.float32)
        signal_real, signal_imag = spectrum(signal, padded_size, tables)
        mixed = signal_of(
            signal_real * kernel_real - signal_imag * kernel_imag,
            signal_real * kernel_imag + signal_imag * kernel_real,
            seq_length,
            tables,
        )
        mixed_rows = to_tokens(mixed.astype(jnp.bfloat16)).astype(jnp.float32)
        gate_act, gate_pull = jax.vjp(jax.nn.silu, gate_proj)
        inner_low = (mixed_rows * gate_act).astype(jnp.bfloat16)
        residual = rows_here + partial_sum(
            jnp.einsum("ble,oe->blo", inner_low, full_out, preferred_element_type=jnp.float32)
        )
        second_normed, second_scale = row_norm(residual)
        input2 = features((second_normed * second_gain).astype(jnp.bfloat16))
        hidden = jnp.einsum("bld,df->blf", input2, full_up, preferred_element_type=jnp.float32)
        activated, act_pull = jax.vjp(jax.nn.gelu, hidden)
        act_low = activated.astype(jnp.bfloat16)
        result = residual + partial_sum(
            jnp.einsum("blf,of->blo", act_low, full_down, preferred_element_type=jnp.float32)
        )
        outputs.append(result.astype(jnp.bfloat16))
        grad_rows_out = cotangent[micro_index * SEQ_MB : (micro_index + 1) * SEQ_MB]
        grad_full = features(grad_rows_out)
        grad_act = jnp.einsum(
            "blo,of->blf", grad_full, full_down, preferred_element_type=jnp.float32
        )
        down_grad = jnp.einsum(
            "blo,blf->of", grad_full, act_low, preferred_element_type=jnp.float32
        )
        grad_hidden = act_pull(grad_act)[0].astype(jnp.bfloat16)
        up_grad = jnp.einsum("bld,blf->df", input2, grad_hidden, preferred_element_type=jnp.float32)
        grad_in2 = partial_sum(
            jnp.einsum("blf,df->bld", grad_hidden, full_up, preferred_element_type=jnp.float32)
        )
        second_grad = jnp.sum(grad_in2 * second_normed, axis=(0, 1))
        grad_residual = grad_rows_out.astype(jnp.float32) + row_back(
            grad_in2, second_normed, second_scale, second_gain
        )
        grad_branch = features(grad_residual.astype(jnp.bfloat16))
        grad_inner = jnp.einsum(
            "blo,oe->ble", grad_branch, full_out, preferred_element_type=jnp.float32
        )
        out_grad = jnp.einsum(
            "blo,ble->oe", grad_branch, inner_low, preferred_element_type=jnp.float32
        )
        grad_mixed = to_channels((grad_inner * gate_act).astype(jnp.bfloat16)).astype(jnp.float32)
        grad_real, grad_imag = spectrum(grad_mixed, padded_size, tables)
        grad_signal = signal_of(
            grad_real * kernel_real + grad_imag * kernel_imag,
            grad_imag * kernel_real - grad_real * kernel_imag,
            seq_length,
            tables,
        )
        kernel_grad = kernel_grad + jnp.sum(
            signal_of(
                grad_real * signal_real + grad_imag * signal_imag,
                grad_imag * signal_real - grad_real * signal_imag,
                tap_count,
                tables,
            ),
            axis=0,
        )
        grad_signal_rows = to_tokens(grad_signal.astype(jnp.bfloat16))
        grad_gate_rows = gate_pull(grad_inner * mixed_rows)[0].astype(jnp.bfloat16)
        value_grad = jnp.einsum(
            "bld,ble->de", input1, grad_signal_rows, preferred_element_type=jnp.float32
        )
        gate_grad = jnp.einsum(
            "bld,ble->de", input1, grad_gate_rows, preferred_element_type=jnp.float32
        )
        grad_in1 = partial_sum(
            jnp.einsum(
                "ble,de->bld", grad_signal_rows, full_value, preferred_element_type=jnp.float32
            )
            + jnp.einsum(
                "ble,de->bld", grad_gate_rows, full_gate, preferred_element_type=jnp.float32
            )
        )
        first_grad = jnp.sum(grad_in1 * first_normed, axis=(0, 1))
        input_grads.append(
            grad_residual + row_back(grad_in1, first_normed, first_scale, first_gain)
        )
        local_terms = (
            value_grad,
            gate_grad,
            out_grad,
            up_grad,
            down_grad,
            first_grad[:, None],
            second_grad[:, None],
        )
        totals = tuple((left + right for left, right in zip(totals, local_terms)))
    totals = lax.psum_scatter(totals, "freq", scatter_dimension=0, tiled=True)
    raw_grad = kernel_pull(kernel_grad)[0]
    grad_kernel = lax.all_to_all(raw_grad, "freq", split_axis=1, concat_axis=0, tiled=True)
    output = jnp.concatenate(outputs, axis=0)
    grad_input = jnp.concatenate(input_grads, axis=0)
    return (
        output,
        grad_input,
        totals[0],
        totals[1],
        totals[2],
        totals[3],
        totals[4],
        totals[5],
        totals[6],
        grad_kernel,
    )


def solution(mesh):
    specs = dict(
        mesh=mesh,
        in_specs=(
            P(None, "freq", "chan"),
            P(None, "freq", "chan"),
            P("chan"),
            P("chan"),
            P("freq", "chan"),
            P("freq", "chan"),
            P("freq", "chan"),
            P("freq", "chan"),
            P("freq", "chan"),
            P("chan", "freq"),
            P("chan"),
        ),
        out_specs=(
            P(None, "freq", "chan"),
            P(None, "freq", "chan"),
            P("freq", "chan"),
            P("freq", "chan"),
            P("freq", "chan"),
            P("freq", "chan"),
            P("freq", "chan"),
            P("freq", "chan"),
            P("freq", "chan"),
            P("chan", "freq"),
        ),
        check_vma=False,
    )

    def step(*args):
        whole = fits(mesh)(args[0], args[4], args[7], args[9])
        return jax.shard_map(one_sequence if whole else by_features, **specs)(*args)

    return step
```
